32 devices in a mesh: grp: 4 (over y, x), tile: 8 (over z, core).
Axes of the slice: x: 2, y: 2, z: 4, core: 2. Of those that a mesh axis runs over, the one named last changes fastest.
Arguments:
- jac_point: float32 [6, 32768], P(None, ('grp', 'tile')), may hold values from -6 to 6
- jac_cam: float32 [18, 32768], P(None, ('grp', 'tile')), may hold values from -3 to 3
- resid: float32 [2, 32768], P(None, ('grp', 'tile')), may hold values from -6 to 6
- point_index: int32 [32768], P(('grp', 'tile')), may hold values from 0 to 4095, as said below
- cam_index: int32 [32768], P(('grp', 'tile')), may hold values from 0 to 3071, as said below
Outputs:
- point_step: float32 [3, 131072], P(None, ('grp', 'tile'))
- camera_step: float32 [9, 12288], P(None, ('grp', 'tile'))
- point_resid: float32 [3, 131072], P(None, ('grp', 'tile'))
- camera_resid: float32 [9, 12288], P(None, ('grp', 'tile'))
The draws below stay inside these ranges and needn't reach their ends.
Inputs may be any that keep to these rules, and one draw needn't show every extreme that they name: `point_index`: index among the points of the observation's own device; every device names point 0 and point 4096 - 1. `cam_index`: block h of a device's observations (slots h * 256 to (h + 1) * 256 - 1) names cameras of group h by their index within the group; every block names camera 0 and camera 3072 - 1.
All inputs are finite; a program needn't handle non-finite values.
Results may differ from the reference program's by a relative error of at most 0.0002.
Values sent between devices are 32-bit elements; how exact they have to be, the bound alone decides.
No kernel may reach another device: no remote copies, remote signals or barrier semaphores. Data moves between devices by JAX's collectives and lax.ppermute only.
A program may use at most 64 MiB of HBM per device.

```python
import jax
import jax.numpy as jnp
from jax import lax

SLOT = 256
P_DEV = 4096
ITERS = 2
OBS_DEV = 1024
CAM_GRP = 3072
CAMS = 12288
OBS = 32768
N_GRP = 4
N_TILE = 8


def draw_point_index(key, part):
    values = jax.random.randint(key, (OBS,), 0, P_DEV, dtype=jnp.int32)
    blocks = values.reshape(-1, OBS_DEV)
    blocks = blocks.at[:, 0].set(0).at[:, 1].set(P_DEV - 1)
    return blocks.reshape(OBS)


def draw_cam_index(key, part):
    keys = jax.random.split(jax.random.fold_in(key, 7), 5)
    lowest = jax.random.randint(keys[0], (OBS,), 0, CAM_GRP, dtype=jnp.int32)
    for number in range(1, 4):
        lowest = jnp.minimum(lowest, jax.random.randint(keys[number], (OBS,), 0, CAM_GRP, dtype=jnp.int32))
    shuffle = jax.random.permutation(keys[4], CAM_GRP).astype(jnp.int32)
    values = shuffle[lowest]
    blocks = values.reshape(-1, SLOT)
    blocks = blocks.at[:, 0].set(0).at[:, 1].set(CAM_GRP - 1)
    return blocks.reshape(OBS)


def steps_of(key, shape, shards, low, top_value):
    loudness, own = 1.0, jax.random.fold_in(key, 6)
    for position, parts in shards:
        draws = jnp.exp(jax.random.uniform(jax.random.fold_in(own, position), (parts,), jnp.float32, low / len(shards), top_value / len(shards)))
        loudness = loudness * jnp.repeat(draws, shape[position] // parts).reshape([-1 if axis == position else 1 for axis in range(len(shape))])
    return loudness


def scatter_about(key, dims, width, bound, cuts=(), kind=jnp.bfloat16):
    values = jax.random.normal(key, dims, jnp.float32) * width
    if len(cuts) > 0:
        values = steps_of(key, dims, cuts, -0.22, 0.18) * values
    return jnp.clip(values, min=-bound, max=bound).astype(kind)


def setup_inputs(seed: int = 0) -> dict:
    key_list = jax.random.split(jax.random.key(seed), 6)
    jac_point = scatter_about(key_list[0], (6, OBS), 1.0, 6.0, ((1, 32),), jnp.float32)
    jac_cam = scatter_about(key_list[1], (18, OBS), 0.5, 3.0, ((1, 32),), jnp.float32)
    resid = scatter_about(key_list[2], (2, OBS), 1.0, 6.0, ((1, 32),), jnp.float32)
    point_index = draw_point_index(jax.random.fold_in(key_list[5], 71), 0)
    cam_index = draw_cam_index(jax.random.fold_in(key_list[5], 71), 0)
    return dict(jac_point=jac_point, jac_cam=jac_cam, resid=resid, point_index=point_index, cam_index=cam_index)


damping = 1.0


def segment_rows(data, ids, count):
    return jax.vmap(lambda row: jax.ops.segment_sum(row, ids, num_segments=count))(data)


def reference(jac_point, jac_cam, resid, point_index, cam_index):
    devices = N_GRP * N_TILE
    block_of = jnp.arange(OBS_DEV, dtype=jnp.int32) // SLOT
    device_ids = jnp.arange(devices, dtype=jnp.int32)

    def local(dev):
        start = dev * OBS_DEV
        jp = lax.dynamic_slice_in_dim(jac_point, start, OBS_DEV, 1).reshape(2, 3, OBS_DEV)
        jc = lax.dynamic_slice_in_dim(jac_cam, start, OBS_DEV, 1).reshape(2, 9, OBS_DEV)
        res = lax.dynamic_slice_in_dim(resid, start, OBS_DEV, 1)
        pts = lax.dynamic_slice_in_dim(point_index, start, OBS_DEV, 0)
        cams = block_of * CAM_GRP + lax.dynamic_slice_in_dim(cam_index, start, OBS_DEV, 0)
        return jp, jc, res, pts, cams

    def spread(stacked, rows):
        return jnp.transpose(stacked, (1, 0, 2)).reshape(rows, devices * P_DEV)

    def init_step(acc, dev):
        jp, jc, res, pts, cams = local(dev)
        point_terms = jnp.concatenate([-jnp.sum(jp * res[:, None], axis=0), jnp.sum(jp * jp, axis=0)], axis=0)
        cam_terms = jnp.concatenate([-jnp.sum(jc * res[:, None], axis=0), jnp.sum(jc * jc, axis=0)], axis=0)
        return acc + segment_rows(cam_terms, cams, CAMS), segment_rows(point_terms, pts, P_DEV)

    cam_init, point_init = lax.scan(init_step, jnp.zeros((18, CAMS), jnp.float32), device_ids)
    point_init = spread(point_init, 6)

    def apply(vp, vc):
        def step(acc, dev):
            jp, jc, res, pts, cams = local(dev)
            own = lax.dynamic_slice_in_dim(vp, dev * P_DEV, P_DEV, 1)
            error = jnp.sum(jp * own[:, pts][None], axis=1) + jnp.sum(jc * vc[:, cams][None], axis=1)
            acc = acc + segment_rows(jnp.sum(jc * error[:, None], axis=0), cams, CAMS)
            return acc, segment_rows(jnp.sum(jp * error[:, None], axis=0), pts, P_DEV)

        cam_out, point_out = lax.scan(step, jnp.zeros((9, CAMS), jnp.float32), device_ids)
        return spread(point_out, 3) + damping * vp, cam_out + damping * vc

    point_rhs, point_diag = point_init[:3], point_init[3:]
    camera_rhs, camera_diag = cam_init[:9], cam_init[9:]
    point_pre = point_diag + damping
    camera_pre = camera_diag + damping
    point_x = jnp.zeros_like(point_rhs)
    camera_x = jnp.zeros_like(camera_rhs)
    point_r, camera_r = point_rhs, camera_rhs
    point_z, camera_z = point_r / point_pre, camera_r / camera_pre
    point_dir, camera_dir = point_z, camera_z
    norm_now = jnp.sum(point_r * point_z) + jnp.sum(camera_r * camera_z)
    for step_number in range(ITERS):
        point_q, camera_q = apply(point_dir, camera_dir)
        alpha = norm_now / (jnp.sum(point_dir * point_q) + jnp.sum(camera_dir * camera_q))
        point_x = point_x + alpha * point_dir
        camera_x = camera_x + alpha * camera_dir
        point_r = point_r - alpha * point_q
        camera_r = camera_r - alpha * camera_q
        if step_number + 1 < ITERS:
            point_z, camera_z = point_r / point_pre, camera_r / camera_pre
            norm_next = jnp.sum(point_r * point_z) + jnp.sum(camera_r * camera_z)
            ratio = norm_next / norm_now
            point_dir = point_z + ratio * point_dir
            camera_dir = camera_z + ratio * camera_dir
            norm_now = norm_next
    return point_x, camera_x, point_r, camera_r
```

```python
import functools

import jax
import jax.numpy as jnp
from jax import lax
from jax.experimental import pallas as pl
from jax.experimental.pallas import tpu as pltpu
from jax.sharding import PartitionSpec as P

P_DEV = 4096
CAM_DEV = 384
LO_BITS = 8
LO = 1 << LO_BITS
PH = P_DEV // LO
DAMPING = 1.0
F32 = jnp.float32
BF16 = jnp.bfloat16
PARAMS = pltpu.CompilerParams(vmem_limit_bytes=48 * 1024 * 1024)


def halves(v):
    high = v.astype(BF16).astype(F32)
    return high, v - high


def one_hot_rows(index, rows):
    numbers = lax.broadcasted_iota(jnp.int32, (rows, index.shape[1]), 0)
    return jnp.where(numbers == index, 1.0, 0.0).astype(BF16)


def dot_nt(a, b):
    return lax.dot_general(a, b, (((1,), (1,)), ((), ())), preferred_element_type=F32)


def dot_nn(a, b):
    return lax.dot_general(a, b, (((1,), (0,)), ((), ())), preferred_element_type=F32)


def is_row(hi, rows):
    return lax.broadcasted_iota(jnp.int32, (rows, hi.shape[1]), 0) == hi


def spread_row(mask, row):
    return jnp.where(mask, jnp.broadcast_to(row, mask.shape), 0.0)


def scatter_mixed(hi, hot, mains, tails, count, tail_rows):
    total = None
    tail_mask = is_row(hi, tail_rows)
    hi8 = jnp.broadcast_to(hi, (8, hi.shape[1]))
    main_parts = [halves(v) for v in mains]
    tail_parts = [halves(v) for v in tails]
    for part in range(2):
        pieces = []
        for k in range(count):
            here = hi8 == k
            pieces += [jnp.where(here, v[part], 0.0) for v in main_parts]
        pieces += [spread_row(tail_mask, v[part]) for v in tail_parts]
        lhs = jnp.concatenate(pieces, axis=0).astype(BF16)
        product = dot_nt(lhs, hot)
        total = product if total is None else total + product
    return total


def gather_mixed(hi, hot, table_high, table_low, count, tail_rows):
    found = dot_nn(table_high, hot) + dot_nn(table_low, hot)
    hi8 = jnp.broadcast_to(hi, (8, hi.shape[1]))
    main = jnp.zeros(hi8.shape, F32)
    for k in range(count):
        main = main + jnp.where(hi8 == k, found[k * 8 : k * 8 + 8], 0.0)
    tail = jnp.sum(
        jnp.where(is_row(hi, tail_rows), found[count * 8 :], 0.0), axis=0, keepdims=True
    )
    return main, tail


def scatter_points(mask, hot, rows):
    parts = [halves(v) for v in rows]
    total = None
    for part in range(2):
        lhs = jnp.concatenate([spread_row(mask, v[part]) for v in parts], axis=0)
        product = dot_nt(lhs.astype(BF16), hot)
        total = product if total is None else total + product
    return total


def gather_points(mask, hot, table):
    high, low = halves(table)
    found = dot_nn(high.astype(BF16), hot) + dot_nn(low.astype(BF16), hot)
    return [
        jnp.sum(jnp.where(mask, found[i * PH : (i + 1) * PH], 0.0), axis=0, keepdims=True)
        for i in range(found.shape[0] // PH)
    ]


def total_of(v):
    return jnp.sum(jnp.sum(v, axis=0, keepdims=True), axis=1, keepdims=True)


def lanes(v, width):
    return jnp.broadcast_to(v, (v.shape[0], width))


def pack_kernel(n_grp, n_z, jp_ref, jc_ref, res_ref, pidx_ref, cidx_ref, out_ref, pb_ref, pd_ref):
    slot = out_ref.shape[2]
    index = pidx_ref[...]
    mask = is_row(index >> LO_BITS, PH)
    hot = one_hot_rows(index & (LO - 1), LO)
    jp = [jp_ref[k : k + 1, :] for k in range(6)]
    res = [res_ref[a : a + 1, :] for a in range(2)]
    grad = [-(jp[i] * res[0] + jp[3 + i] * res[1]) for i in range(3)]
    square = [jp[i] * jp[i] + jp[3 + i] * jp[3 + i] for i in range(3)]
    table = scatter_points(mask, hot, grad + square)
    rhs = table[: 3 * PH]
    diag = table[3 * PH :] + DAMPING
    pb_ref[...] = rhs
    pd_ref[...] = diag
    z = rhs / diag
    at = gather_points(mask, hot, z)
    u = [sum(jp[3 * a + i] * at[i] for i in range(3)) for a in range(2)]
    gamma = total_of(rhs * z)
    norm = total_of(z * z)
    scalars = jnp.concatenate([lanes(gamma, slot // 2), lanes(norm, slot // 2)], axis=1)
    cams = cidx_ref[...].astype(F32)
    for h in range(n_grp):
        cols = slice(h * slot, (h + 1) * slot)
        block = jnp.concatenate(
            [
                jc_ref[0:8, cols],
                jc_ref[9:17, cols],
                jc_ref[8:9, cols],
                jc_ref[17:18, cols],
                res[0][:, cols],
                res[1][:, cols],
                u[0][:, cols],
                u[1][:, cols],
                cams[:, cols],
                scalars,
            ],
            axis=0,
        )

        @pl.loop(0, n_z)
        def _(z_to, block=block, h=h):
            out_ref[h * n_z + z_to] = block


def read_chunk(ref, chunk, count):
    x = jnp.concatenate([ref[chunk * count + k] for k in range(count)], axis=1)
    index = x[22:23].astype(jnp.int32)
    return x, index


def camera_kernel(n_grp, n_z, a_ref, b_ref, back_ref, cb_ref, cd_ref, cs_ref, acc_ref, w_ref, zh_ref, zl_ref, tb_ref, td_ref, ts_ref):
    blocks, _, slot = a_ref.shape
    per = min(4, blocks)
    chunks = blocks // per
    count = CAM_DEV * 2 * n_z // LO
    tail_rows = tb_ref.shape[0] - 8 * count
    acc_ref[...] = jnp.zeros(acc_ref.shape, F32)

    def first(ref):
        def body(chunk, scalars):
            x, index = read_chunk(ref, chunk, per)
            hi, hot = index >> LO_BITS, one_hot_rows(index & (LO - 1), LO)
            j0, j1 = x[0:8], x[8:16]
            j08, j18, r0, r1 = x[16:17], x[17:18], x[18:19], x[19:20]
            acc_ref[...] += scatter_mixed(
                hi,
                hot,
                [-(j0 * r0 + j1 * r1), j0 * j0 + j1 * j1],
                [-(j08 * r0 + j18 * r1), j08 * j08 + j18 * j18],
                count,
                tail_rows,
            )
            for k in range(per):
                scalars = scalars + x[23:24, k * slot : (k + 1) * slot]
            return scalars

        return body

    scalars = lax.fori_loop(0, chunks, first(a_ref), jnp.zeros((1, slot), F32))
    scalars = lax.fori_loop(0, chunks, first(b_ref), scalars)
    main = 8 * count
    for k in range(count):
        tb_ref[8 * k : 8 * k + 8, :] = acc_ref[16 * k : 16 * k + 8, :]
        td_ref[8 * k : 8 * k + 8, :] = acc_ref[16 * k + 8 : 16 * k + 16, :] + DAMPING
    tb_ref[main:, :] = acc_ref[2 * main : 2 * main + tail_rows, :]
    td_ref[main:, :] = acc_ref[2 * main + tail_rows :, :] + DAMPING
    z = tb_ref[...] / td_ref[...]
    gamma = total_of(tb_ref[...] * z)
    norm = total_of(z * z)
    high, low = halves(z)
    zh_ref[...] = high.astype(BF16)
    zl_ref[...] = low.astype(BF16)
    ts_ref[...] = z

    def second(ref, offset):
        def body(chunk, energy):
            x, index = read_chunk(ref, chunk, per)
            hi, hot = index >> LO_BITS, one_hot_rows(index & (LO - 1), LO)
            j0, j1 = x[0:8], x[8:16]
            j08, j18, u0, u1 = x[16:17], x[17:18], x[20:21], x[21:22]
            at, at8 = gather_mixed(hi, hot, zh_ref[...], zl_ref[...], count, tail_rows)
            w0 = jnp.sum(j0 * at, axis=0, keepdims=True) + j08 * at8
            w1 = jnp.sum(j1 * at, axis=0, keepdims=True) + j18 * at8
            if offset == 0:
                for k in range(per):
                    cols = slice(k * slot, (k + 1) * slot)
                    w_ref[chunk * per + k, 0:1, :] = w0[:, cols]
                    w_ref[chunk * per + k, 1:2, :] = w1[:, cols]
            e0, e1 = u0 + w0, u1 + w1
            ts_ref[...] += scatter_mixed(
                hi, hot, [j0 * e0 + j1 * e1], [j08 * e0 + j18 * e1], count, tail_rows
            )
            return energy + e0 * e0 + e1 * e1

        return body

    energy = jnp.zeros((1, per * slot), F32)
    energy = lax.fori_loop(0, chunks, second(a_ref, 0), energy)
    energy = lax.fori_loop(0, chunks, second(b_ref, 1), energy)
    y = ts_ref[...] / td_ref[...]
    high, low = halves(y)
    zh_ref[...] = high.astype(BF16)
    zl_ref[...] = low.astype(BF16)
    share = 1.0 / n_grp
    gamma = gamma + share * scalars[:, 0:1]
    delta = norm + total_of(energy) + share * scalars[:, slot // 2 : slot // 2 + 1]
    tile = lax.axis_index("tile")
    mine, core = tile // 2, tile % 2
    for g in range(n_grp):
        block = g * n_z + mine
        x = a_ref[block]
        index = x[22:23].astype(jnp.int32)
        hi, hot = index >> LO_BITS, one_hot_rows(index & (LO - 1), LO)
        at, at8 = gather_mixed(hi, hot, zh_ref[...], zl_ref[...], count, tail_rows)
        v0 = jnp.sum(x[0:8] * at, axis=0, keepdims=True) + x[16:17] * at8
        v1 = jnp.sum(x[8:16] * at, axis=0, keepdims=True) + x[17:18] * at8
        back_ref[g, 0:2, 0:slot] = w_ref[block, 0:2, :]
        back_ref[g, 2:3, 0:slot] = v0
        back_ref[g, 3:4, 0:slot] = v1
        back_ref[g, :, slot:] = lanes(jnp.concatenate([gamma, delta, gamma, delta], axis=0), 128)
    for source, target in ((tb_ref, cb_ref), (td_ref, cd_ref), (ts_ref, cs_ref)):
        own, own8 = [], []
        for k in range(3):
            rows = source[pl.ds(pl.multiple_of(8 * (3 * mine + k), 8), 8), :]
            tail = source[pl.ds(main + 3 * mine + k, 1), :]
            own += [rows[:, :128], rows[:, 128:]]
            own8 += [tail[:, :128], tail[:, 128:]]
        for m in range(3):
            cols = slice(m * 128, (m + 1) * 128)
            target[0:8, cols] = jnp.where(core == 0, own[m], own[m + 3])
            target[8:9, cols] = jnp.where(core == 0, own8[m], own8[m + 3])


def point_kernel(
    n_grp, back_ref, jp_ref, pidx_ref, pb_ref, pd_ref, cb_ref, cd_ref, cs_ref, out_ref, ps_ref, pt_ref, sc_ref
):
    slot = back_ref.shape[2] - 128
    index = pidx_ref[...]
    mask = is_row(index >> LO_BITS, PH)
    hot = one_hot_rows(index & (LO - 1), LO)
    jp = [jp_ref[k : k + 1, :] for k in range(6)]
    scalars = back_ref[0, :, slot:]
    for h in range(1, n_grp):
        scalars = scalars + back_ref[h, :, slot:]
    gamma, delta = scalars[0:1, 0:1], scalars[1:2, 0:1]
    alpha = gamma / delta
    w = [
        jnp.concatenate([back_ref[h, r : r + 1, 0:slot] for h in range(n_grp)], axis=1) for r in range(4)
    ]
    rhs, diag = pb_ref[...], pd_ref[...]
    z = rhs / diag
    at = gather_points(mask, hot, z)
    error = [sum(jp[3 * a + i] * at[i] for i in range(3)) + w[a] for a in range(2)]
    s = z + scatter_points(mask, hot, [jp[i] * error[0] + jp[3 + i] * error[1] for i in range(3)])
    r1 = rhs - alpha * s
    z1 = r1 / diag
    at = gather_points(mask, hot, z1)
    error = [
        sum(jp[3 * a + i] * at[i] for i in range(3)) + (w[a] - alpha * w[2 + a]) for a in range(2)
    ]
    t = z1 + scatter_points(mask, hot, [jp[i] * error[0] + jp[3 + i] * error[1] for i in range(3)])
    ps_ref[...] = s
    pt_ref[...] = t
    cr1 = cb_ref[...] - alpha * cs_ref[...]
    cz1 = cr1 / cd_ref[...]
    gamma1 = total_of(r1 * z1) + total_of(cr1 * cz1)
    delta1 = (
        total_of(error[0] * error[0] + error[1] * error[1]) + total_of(z1 * z1) + total_of(cz1 * cz1)
    )
    sc_ref[...] = lanes(jnp.concatenate([gamma, alpha], axis=0), 128)
    tail = lanes(jnp.concatenate([gamma1, delta1], axis=0), 128)
    per = out_ref.shape[0] // n_grp
    for h in range(n_grp):
        cols = slice(h * slot, (h + 1) * slot)
        block = jnp.concatenate([jnp.concatenate([e[:, cols] for e in error], axis=0), tail], axis=1)

        @pl.loop(0, per)
        def _(tile, block=block, h=h):
            out_ref[h * per + tile] = block


def final_kernel(
    err_ref, a_ref, b_ref, pb_ref, pd_ref, ps_ref, pt_ref, cb_ref, cd_ref, cs_ref, sc_ref,
    px_ref, cx_ref, pr_ref, cr_ref, acc_ref,
):
    blocks, _, slot = a_ref.shape
    per = min(4, blocks)
    chunks = blocks // per
    tile = lax.axis_index("tile")
    core = tile % 2
    acc_ref[...] = jnp.zeros(acc_ref.shape, F32)

    def body(ref, parity):
        def step(chunk, scalars):
            x, index = read_chunk(ref, chunk, per)
            errs = [err_ref[2 * (chunk * per + k) + parity] for k in range(per)]
            e = jnp.concatenate([v[:, 0:slot] for v in errs], axis=1)
            for v in errs:
                scalars = scalars + v[:, slot:]
            index = index - tile * CAM_DEV
            hi = index >> 7
            hot = one_hot_rows(index & 127, 128)
            j0, j1 = x[0:8], x[8:16]
            e0, e1 = e[0:1], e[1:2]
            acc_ref[...] += scatter_mixed(
                hi, hot, [j0 * e0 + j1 * e1], [x[16:17] * e0 + x[17:18] * e1], 3, 8
            )
            return scalars

        return step

    scalars = lax.fori_loop(0, chunks, body(a_ref, core), jnp.zeros((2, 128), F32))
    scalars = lax.fori_loop(0, chunks, body(b_ref, 1 - core), scalars)
    gamma1, delta1 = scalars[0:1, 0:1], scalars[1:2, 0:1]
    gamma, alpha = sc_ref[0:1, 0:1], sc_ref[1:2, 0:1]
    ratio = gamma1 / gamma
    alpha1 = gamma1 / (delta1 - ratio * gamma1 / alpha)

    rhs, diag, s = pb_ref[...], pd_ref[...], ps_ref[...]
    z = rhs / diag
    r1 = rhs - alpha * s
    z1 = r1 / diag
    x = alpha * z + alpha1 * (z1 + ratio * z)
    r2 = r1 - alpha1 * (pt_ref[...] + ratio * s)
    for i in range(3):
        for hi in range(PH):
            row = i * PH + hi
            px_ref[i : i + 1, hi * LO : (hi + 1) * LO] = x[row : row + 1]
            pr_ref[i : i + 1, hi * LO : (hi + 1) * LO] = r2[row : row + 1]

    rhs, s = cb_ref[...], cs_ref[...]
    z = rhs / cd_ref[...]
    r1 = rhs - alpha * s
    z1 = r1 / cd_ref[...]
    cx_ref[...] = alpha * z + alpha1 * (z1 + ratio * z)
    base = r1 - alpha1 * (z1 + ratio * s)
    for k in range(3):
        cols = slice(k * 128, (k + 1) * 128)
        cr_ref[0:8, cols] = base[0:8, cols] - alpha1 * acc_ref[8 * k : 8 * k + 8, :]
        cr_ref[8:9, cols] = base[8:9, cols] - alpha1 * acc_ref[24 + k : 25 + k, :]


def shape(*dims):
    return jax.ShapeDtypeStruct(dims, F32)


def shards(jac_point, jac_cam, resid, point_index, cam_index):
    n_grp, n_tile = lax.axis_size("grp"), lax.axis_size("tile")
    n_z = n_tile // 2
    obs = jac_point.shape[1]
    slot = obs // n_grp
    blocks = n_grp * n_z
    count = CAM_DEV * n_tile // LO
    tail_rows = -(-count // 16) * 16
    rows = 8 * count + tail_rows
    groups = [[d * 2 + core for d in range(blocks)] for core in range(2)]
    swap = [(t, t ^ 1) for t in range(n_tile)]
    pidx, cidx = point_index.reshape(1, obs), cam_index.reshape(1, obs)

    packed, pb, pd = pl.pallas_call(
        functools.partial(pack_kernel, n_grp, n_z),
        out_shape=(shape(blocks, 24, slot), shape(3 * PH, LO), shape(3 * PH, LO)),
        compiler_params=PARAMS,
        name="pack",
    )(jac_point, jac_cam, resid, pidx, cidx)
    own = lax.all_to_all(packed, ("grp", "tile"), 0, 0, axis_index_groups=groups, tiled=True)
    other = lax.ppermute(own, "tile", swap)
    back, cb, cd, cs = pl.pallas_call(
        functools.partial(camera_kernel, n_grp, n_z),
        out_shape=(shape(n_grp, 4, slot + 128),) + (shape(9, CAM_DEV),) * 3,
        scratch_shapes=[
            pltpu.VMEM((2 * rows, LO), F32),
            pltpu.VMEM((blocks, 2, slot), F32),
            pltpu.VMEM((rows, LO), BF16),
            pltpu.VMEM((rows, LO), BF16),
            pltpu.VMEM((rows, LO), F32),
            pltpu.VMEM((rows, LO), F32),
            pltpu.VMEM((rows, LO), F32),
        ],
        compiler_params=PARAMS,
        name="cameras",
    )(own, other)
    back = lax.all_to_all(back, "grp", 0, 0, tiled=True)
    errors, ps, pt, sc = pl.pallas_call(
        functools.partial(point_kernel, n_grp),
        out_shape=(
            shape(n_grp * n_tile, 2, slot + 128),
            shape(3 * PH, LO),
            shape(3 * PH, LO),
            shape(2, 128),
        ),
        compiler_params=PARAMS,
        name="points",
    )(back, jac_point, pidx, pb, pd, cb, cd, cs)
    errors = lax.all_to_all(errors, ("grp", "tile"), 0, 0, tiled=True)
    return pl.pallas_call(
        final_kernel,
        out_shape=(shape(3, P_DEV), shape(9, CAM_DEV), shape(3, P_DEV), shape(9, CAM_DEV)),
        scratch_shapes=[pltpu.VMEM((32, 128), F32)],
        compiler_params=PARAMS,
        name="finish",
    )(errors, own, other, pb, pd, ps, pt, cb, cd, cs, sc)


def solution(mesh):
    placed = (
        P(None, ("grp", "tile")),
        P(None, ("grp", "tile")),
        P(None, ("grp", "tile")),
        P(("grp", "tile")),
        P(("grp", "tile")),
    )
    return jax.shard_map(
        shards,
        mesh=mesh,
        in_specs=placed,
        out_specs=(P(None, ("grp", "tile")),) * 4,
        check_vma=False,
    )
```

```python
import functools

import jax
import jax.numpy as jnp
from jax import lax
from jax.experimental import pallas as pl
from jax.experimental.pallas import tpu as pltpu
from jax.sharding import PartitionSpec as P

P_DEV = 4096
CAM_DEV = 384
LO_BITS = 8
LO = 1 << LO_BITS
PH = P_DEV // LO
DAMPING = 1.0
F32 = jnp.float32
BF16 = jnp.bfloat16
PARAMS = pltpu.CompilerParams(vmem_limit_bytes=48 * 1024 * 1024)


def halves(v):
    high = v.astype(BF16).astype(F32)
    return high, v - high


def rows16(width, step=1):
    numbers = lax.broadcasted_iota(jnp.int32, (16, width), 0)
    return (numbers // step if step > 1 else numbers).astype(F32).astype(BF16)


def sixteen(row):
    return jnp.broadcast_to(row.astype(F32), (16, row.shape[1])).astype(BF16)


def one_hot_rows(index, rows):
    wide, numbers = sixteen(index), rows16(index.shape[1])
    one, none = jnp.ones(wide.shape, BF16), jnp.zeros(wide.shape, BF16)
    return jnp.concatenate(
        [jnp.where(wide == numbers + BF16(16 * k), one, none) for k in range(rows // 16)], axis=0
    )


def dot_nt(a, b):
    return lax.dot_general(a, b, (((1,), (1,)), ((), ())), preferred_element_type=F32)


def dot_nn(a, b):
    return lax.dot_general(a, b, (((1,), (0,)), ((), ())), preferred_element_type=F32)


def is_row(hi, rows):
    return lax.broadcasted_iota(jnp.int32, (rows, hi.shape[1]), 0) == hi


def spread_row(mask, row):
    return jnp.where(mask, jnp.broadcast_to(row, mask.shape), 0.0)


def two_parts(v):
    high = v.astype(BF16)
    return high, (v - high.astype(F32)).astype(BF16)


def scatter_mixed(hi, hot, mains, tails, count, tail_rows):
    wide = sixteen(hi)
    none = jnp.zeros(wide.shape, BF16)
    single = len(mains) == 1
    numbers = rows16(hi.shape[1], 8) if single else none
    main_parts = two_parts(jnp.concatenate(mains * 2 if single else mains, axis=0))
    tail_parts = [two_parts(jnp.broadcast_to(v, wide.shape)) for v in tails]
    here = [wide == numbers + BF16(k) for k in range(0, count, 2 if single else 1)]
    tail_here = [wide == rows16(hi.shape[1]) + BF16(k) for k in range(0, tail_rows, 16)]
    pieces = []
    for part in range(2):
        pieces += [jnp.where(mask, main_parts[part], none) for mask in here]
        pieces += [jnp.where(mask, v[part], none) for v in tail_parts for mask in tail_here]
    return dot_nt(jnp.concatenate(pieces, axis=0), hot)


def both(v):
    half = v.shape[0] // 2
    return v[:half] + v[half:]


def gather_mixed(hi, hot, table, count, tail_rows):
    found = dot_nn(table, hot)
    hi8 = jnp.broadcast_to(hi, (8, hi.shape[1]))
    main = jnp.zeros(hi8.shape, F32)
    half = found.shape[0] // 2
    for k in range(count):
        rows = slice(k * 8, k * 8 + 8)
        low = slice(half + k * 8, half + k * 8 + 8)
        main = main + jnp.where(hi8 == k, found[rows] + found[low], 0.0)
    tail = found[count * 8 : half] + found[half + count * 8 :]
    tail = jnp.sum(jnp.where(is_row(hi, tail_rows), tail, 0.0), axis=0, keepdims=True)
    return main, tail


def stacked(table):
    high, low = halves(table)
    return jnp.concatenate([high, low], axis=0).astype(BF16)


def scatter_points(mask, hot, rows):
    parts = [halves(v) for v in rows]
    lhs = jnp.concatenate([spread_row(mask, v[k]) for k in range(2) for v in parts], axis=0)
    return both(dot_nt(lhs.astype(BF16), hot))


def gather_points(mask, hot, table):
    found = both(dot_nn(stacked(table), hot))
    return [
        jnp.sum(jnp.where(mask, found[i * PH : (i + 1) * PH], 0.0), axis=0, keepdims=True)
        for i in range(found.shape[0] // PH)
    ]


def total_of(v):
    return jnp.sum(jnp.sum(v, axis=0, keepdims=True), axis=1, keepdims=True)


def lanes(v, width):
    return jnp.broadcast_to(v, (v.shape[0], width))


def pack_kernel(
    n_grp, n_z, jp_hbm, jc_hbm, res_hbm, pidx_hbm, cidx_hbm,
    out_ref, pb_ref, pd_ref, pu_ref, jp_ref, pidx_ref,
    jc_ref, res_ref, cidx_ref, sems,
):
    copies = [
        pltpu.make_async_copy(source, target, sems.at[k])
        for k, (source, target) in enumerate(
            (
                (pidx_hbm, pidx_ref),
                (jp_hbm, jp_ref),
                (res_hbm, res_ref),
                (jc_hbm, jc_ref),
                (cidx_hbm, cidx_ref),
            )
        )
    ]
    for copy in copies:
        copy.start()
    for copy in copies:
        copy.wait()
    slot = out_ref.shape[2]
    index = pidx_ref[...]
    mask = is_row(index >> LO_BITS, PH)
    hot = one_hot_rows(index & (LO - 1), LO)
    jp = [jp_ref[k : k + 1, :] for k in range(6)]
    res = [res_ref[a : a + 1, :] for a in range(2)]
    grad = [-(jp[i] * res[0] + jp[3 + i] * res[1]) for i in range(3)]
    square = [jp[i] * jp[i] + jp[3 + i] * jp[3 + i] for i in range(3)]
    table = scatter_points(mask, hot, grad + square)
    rhs = table[: 3 * PH]
    diag = table[3 * PH :] + DAMPING
    pb_ref[...] = rhs
    pd_ref[...] = diag
    z = rhs / diag
    at = gather_points(mask, hot, z)
    u = [sum(jp[3 * a + i] * at[i] for i in range(3)) for a in range(2)]
    pu_ref[0:1, :] = u[0]
    pu_ref[1:2, :] = u[1]
    gamma = total_of(rhs * z)
    norm = total_of(z * z)
    scalars = jnp.concatenate([lanes(gamma, slot // 2), lanes(norm, slot // 2)], axis=1)
    cams = cidx_ref[...].astype(F32)
    for h in range(n_grp):
        cols = slice(h * slot, (h + 1) * slot)
        block = jnp.concatenate(
            [
                jc_ref[0:8, cols],
                jc_ref[9:17, cols],
                jc_ref[8:9, cols],
                jc_ref[17:18, cols],
                res[0][:, cols],
                res[1][:, cols],
                u[0][:, cols],
                u[1][:, cols],
                cams[:, cols],
                scalars,
            ],
            axis=0,
        )

        @pl.loop(0, n_z)
        def _(z_to, block=block, h=h):
            out_ref[h * n_z + z_to] = block


def read_blocks(ref, numbers):
    x = jnp.concatenate([ref[k] for k in numbers], axis=1)
    return x, x[22:23].astype(jnp.int32)


def chunk_of(chunk, per):
    return [chunk * per + k for k in range(per)]


def first_sums(ref, acc_ref, per, count, tail_rows):
    def body(chunk, carry):
        x, index = read_blocks(ref, chunk_of(chunk, per))
        hi, hot = index >> LO_BITS, one_hot_rows(index & (LO - 1), LO)
        j0, j1 = x[0:8], x[8:16]
        j08, j18, r0, r1 = x[16:17], x[17:18], x[18:19], x[19:20]
        acc_ref[...] += scatter_mixed(
            hi,
            hot,
            [-(j0 * r0 + j1 * r1), j0 * j0 + j1 * j1],
            [-(j08 * r0 + j18 * r1), j08 * j08 + j18 * j18],
            count,
            tail_rows,
        )
        return carry

    lax.fori_loop(0, ref.shape[0] // per, body, 0)


def own_sums_kernel(count, tail_rows, a_ref, acc_ref):
    acc_ref[...] = jnp.zeros(acc_ref.shape, F32)
    first_sums(a_ref, acc_ref, min(16, a_ref.shape[0]), count, tail_rows)


def camera_kernel(
    n_grp, n_z, count, tail_rows, a_ref, b_ref, start_ref,
    back_ref, tb_ref, td_ref, ts_ref,
    acc_ref, w_ref, zz_ref,
):
    blocks, _, slot = a_ref.shape
    per = min(8, blocks)
    chunks = blocks // per
    acc_ref[...] = start_ref[...]
    first_sums(b_ref, acc_ref, min(16, blocks), count, tail_rows)
    scalars = jnp.zeros((1, slot), F32)
    for ref in (a_ref, b_ref):
        scalars = scalars + jnp.sum(ref[:, 23, :], axis=0, keepdims=True)
    main = 8 * count
    half = acc_ref.shape[0] // 2
    for k in range(count):
        row = 16 * k
        tb_ref[8 * k : 8 * k + 8, :] = acc_ref[row : row + 8, :] + acc_ref[half + row : half + row + 8, :]
        row = 16 * k + 8
        td_ref[8 * k : 8 * k + 8, :] = (
            acc_ref[row : row + 8, :] + acc_ref[half + row : half + row + 8, :] + DAMPING
        )
    tb_ref[main:, :] = (
        acc_ref[2 * main : 2 * main + tail_rows, :]
        + acc_ref[half + 2 * main : half + 2 * main + tail_rows, :]
    )
    td_ref[main:, :] = (
        acc_ref[2 * main + tail_rows : half, :] + acc_ref[half + 2 * main + tail_rows :, :] + DAMPING
    )
    z = tb_ref[...] / td_ref[...]
    gamma = total_of(tb_ref[...] * z)
    norm = total_of(z * z)
    zz_ref[...] = stacked(z)
    ts_ref[...] = z
    acc_ref[0:half, :] = jnp.zeros((half, LO), F32)

    def second(ref, keep):
        def body(chunk, energy):
            numbers = chunk_of(chunk, per)
            x, index = read_blocks(ref, numbers)
            hi, hot = index >> LO_BITS, one_hot_rows(index & (LO - 1), LO)
            j0, j1 = x[0:8], x[8:16]
            j08, j18, u0, u1 = x[16:17], x[17:18], x[20:21], x[21:22]
            at, at8 = gather_mixed(hi, hot, zz_ref[...], count, tail_rows)
            w0 = jnp.sum(j0 * at, axis=0, keepdims=True) + j08 * at8
            w1 = jnp.sum(j1 * at, axis=0, keepdims=True) + j18 * at8
            if keep:
                for k, number in enumerate(numbers):
                    cols = slice(k * slot, (k + 1) * slot)
                    w_ref[number, 0:1, :] = w0[:, cols]
                    w_ref[number, 1:2, :] = w1[:, cols]
            e0, e1 = u0 + w0, u1 + w1
            acc_ref[0:half, :] += scatter_mixed(
                hi, hot, [j0 * e0 + j1 * e1], [j08 * e0 + j18 * e1], count, tail_rows
            )
            return energy + e0 * e0 + e1 * e1

        return body

    energy = jnp.zeros((1, per * slot), F32)
    energy = lax.fori_loop(0, chunks, second(a_ref, True), energy)
    energy = lax.fori_loop(0, chunks, second(b_ref, False), energy)
    ts_ref[...] += both(acc_ref[0:half, :])
    zz_ref[...] = stacked(ts_ref[...] / td_ref[...])
    share = 1.0 / n_grp
    gamma = gamma + share * scalars[:, 0:1]
    delta = norm + total_of(energy) + share * scalars[:, slot // 2 : slot // 2 + 1]
    mine = lax.axis_index("tile") // 2
    numbers = [g * n_z + mine for g in range(n_grp)]
    per = min(4, n_grp)
    for first in range(0, n_grp, per):
        some = numbers[first : first + per]
        x, index = read_blocks(a_ref, some)
        hi, hot = index >> LO_BITS, one_hot_rows(index & (LO - 1), LO)
        at, at8 = gather_mixed(hi, hot, zz_ref[...], count, tail_rows)
        v0 = jnp.sum(x[0:8] * at, axis=0, keepdims=True) + x[16:17] * at8
        v1 = jnp.sum(x[8:16] * at, axis=0, keepdims=True) + x[17:18] * at8
        for k in range(per):
            cols = slice(k * slot, (k + 1) * slot)
            g = first + k
            back_ref[g, 0:2, 0:slot] = w_ref[some[k], 0:2, :]
            back_ref[g, 2:3, 0:slot] = v0[:, cols]
            back_ref[g, 3:4, 0:slot] = v1[:, cols]
            back_ref[g, :, slot:] = lanes(jnp.concatenate([gamma, delta, gamma, delta], axis=0), 128)


def mine_kernel(main, tb_ref, td_ref, ts_ref, cb_ref, cd_ref, cs_ref):
    tile = lax.axis_index("tile")
    mine, core = tile // 2, tile % 2
    for source, target in ((tb_ref, cb_ref), (td_ref, cd_ref), (ts_ref, cs_ref)):
        own, own8 = [], []
        for k in range(3):
            rows = source[pl.ds(pl.multiple_of(8 * (3 * mine + k), 8), 8), :]
            tail = source[pl.ds(main + 3 * mine + k, 1), :]
            own += [rows[:, :128], rows[:, 128:]]
            own8 += [tail[:, :128], tail[:, 128:]]
        for m in range(3):
            cols = slice(m * 128, (m + 1) * 128)
            target[0:8, cols] = jnp.where(core == 0, own[m], own[m + 3])
            target[8:9, cols] = jnp.where(core == 0, own8[m], own8[m + 3])


def point_kernel(
    n_grp, back_ref, jp_ref, pidx_ref, pb_ref, pd_ref, pu_ref, cb_ref, cd_ref, cs_ref,
    out_ref, ps_ref, pe_ref, sc_ref,
):
    slot = back_ref.shape[2] - 128
    index = pidx_ref[...]
    mask = is_row(index >> LO_BITS, PH)
    hot = one_hot_rows(index & (LO - 1), LO)
    jp = [jp_ref[k : k + 1, :] for k in range(6)]
    scalars = back_ref[0, :, slot:]
    for h in range(1, n_grp):
        scalars = scalars + back_ref[h, :, slot:]
    gamma, delta = scalars[0:1, 0:1], scalars[1:2, 0:1]
    alpha = gamma / delta
    w = [
        jnp.concatenate([back_ref[h, r : r + 1, 0:slot] for h in range(n_grp)], axis=1) for r in range(4)
    ]
    rhs, diag = pb_ref[...], pd_ref[...]
    z = rhs / diag
    error = [pu_ref[a : a + 1, :] + w[a] for a in range(2)]
    s = z + scatter_points(mask, hot, [jp[i] * error[0] + jp[3 + i] * error[1] for i in range(3)])
    r1 = rhs - alpha * s
    z1 = r1 / diag
    at = gather_points(mask, hot, z1)
    error = [
        sum(jp[3 * a + i] * at[i] for i in range(3)) + (w[a] - alpha * w[2 + a]) for a in range(2)
    ]
    ps_ref[...] = s
    pe_ref[0:1, :] = error[0]
    pe_ref[1:2, :] = error[1]
    cr1 = cb_ref[...] - alpha * cs_ref[...]
    cz1 = cr1 / cd_ref[...]
    gamma1 = total_of(r1 * z1) + total_of(cr1 * cz1)
    delta1 = (
        total_of(error[0] * error[0] + error[1] * error[1]) + total_of(z1 * z1) + total_of(cz1 * cz1)
    )
    sc_ref[...] = lanes(jnp.concatenate([gamma, alpha], axis=0), 128)
    tail = lanes(jnp.concatenate([gamma1, delta1], axis=0), 128)
    per = out_ref.shape[0] // n_grp
    for h in range(n_grp):
        cols = slice(h * slot, (h + 1) * slot)
        block = jnp.concatenate([jnp.concatenate([e[:, cols] for e in error], axis=0), tail], axis=1)

        @pl.loop(0, per)
        def _(tile, block=block, h=h):
            out_ref[h * per + tile] = block


def last_point_sums_kernel(jp_ref, pidx_ref, pe_ref, pt_ref):
    index = pidx_ref[...]
    mask = is_row(index >> LO_BITS, PH)
    hot = one_hot_rows(index & (LO - 1), LO)
    jp = [jp_ref[k : k + 1, :] for k in range(6)]
    error = [pe_ref[a : a + 1, :] for a in range(2)]
    pt_ref[...] = scatter_points(
        mask, hot, [jp[i] * error[0] + jp[3 + i] * error[1] for i in range(3)]
    )


def final_kernel(
    err_ref, a_ref, b_ref, pb_ref, pd_ref, ps_ref, pt_ref, cb_ref, cd_ref, cs_ref, sc_ref,
    px_ref, cx_ref, pr_ref, cr_ref, acc_ref,
):
    blocks, _, slot = a_ref.shape
    per = min(8, blocks)
    chunks = blocks // per
    tile = lax.axis_index("tile")
    core = tile % 2
    acc_ref[...] = jnp.zeros(acc_ref.shape, F32)

    def body(ref, parity):
        def step(chunk, scalars):
            numbers = chunk_of(chunk, per)
            x, index = read_blocks(ref, numbers)
            errs = [err_ref[2 * k + parity] for k in numbers]
            e = jnp.concatenate([v[:, 0:slot] for v in errs], axis=1)
            for v in errs:
                scalars = scalars + v[:, slot:]
            index = index - tile * CAM_DEV
            hi = index >> 7
            hot = one_hot_rows(index & 127, 128)
            j0, j1 = x[0:8], x[8:16]
            e0, e1 = e[0:1], e[1:2]
            acc_ref[...] += scatter_mixed(
                hi, hot, [j0 * e0 + j1 * e1], [x[16:17] * e0 + x[17:18] * e1], 4, 16
            )
            return scalars

        return step

    scalars = lax.fori_loop(0, chunks, body(a_ref, core), jnp.zeros((2, 128), F32))
    scalars = lax.fori_loop(0, chunks, body(b_ref, 1 - core), scalars)
    gamma1, delta1 = scalars[0:1, 0:1], scalars[1:2, 0:1]
    gamma, alpha = sc_ref[0:1, 0:1], sc_ref[1:2, 0:1]
    ratio = gamma1 / gamma
    alpha1 = gamma1 / (delta1 - ratio * gamma1 / alpha)

    rhs, diag, s = pb_ref[...], pd_ref[...], ps_ref[...]
    z = rhs / diag
    r1 = rhs - alpha * s
    z1 = r1 / diag
    x = alpha * z + alpha1 * (z1 + ratio * z)
    r2 = r1 - alpha1 * (z1 + pt_ref[...] + ratio * s)
    for i in range(3):
        for hi in range(PH):
            row = i * PH + hi
            px_ref[i : i + 1, hi * LO : (hi + 1) * LO] = x[row : row + 1]
            pr_ref[i : i + 1, hi * LO : (hi + 1) * LO] = r2[row : row + 1]

    rhs, s = cb_ref[...], cs_ref[...]
    z = rhs / cd_ref[...]
    r1 = rhs - alpha * s
    z1 = r1 / cd_ref[...]
    cx_ref[...] = alpha * z + alpha1 * (z1 + ratio * z)
    sums = both(acc_ref[...])
    base = r1 - alpha1 * (z1 + ratio * s)
    for k in range(3):
        cols = slice(k * 128, (k + 1) * 128)
        cr_ref[0:8, cols] = base[0:8, cols] - alpha1 * sums[8 * k : 8 * k + 8, :]
        cr_ref[8:9, cols] = base[8:9, cols] - alpha1 * sums[32 + k : 33 + k, :]


def shape(*dims):
    return jax.ShapeDtypeStruct(dims, F32)


def shards(jac_point, jac_cam, resid, point_index, cam_index):
    n_grp, n_tile = lax.axis_size("grp"), lax.axis_size("tile")
    n_z = n_tile // 2
    obs = jac_point.shape[1]
    slot = obs // n_grp
    blocks = n_grp * n_z
    count = CAM_DEV * n_tile // LO
    tail_rows = -(-count // 16) * 16
    rows = 8 * count + tail_rows
    groups = [[d * 2 + core for d in range(blocks)] for core in range(2)]
    swap = [(t, t ^ 1) for t in range(n_tile)]
    pidx, cidx = point_index.reshape(1, obs), cam_index.reshape(1, obs)

    hbm = pl.BlockSpec(memory_space=pltpu.HBM)
    packed, pb, pd, pu, jp, pidx = pl.pallas_call(
        functools.partial(pack_kernel, n_grp, n_z),
        in_specs=[hbm] * 5,
        out_shape=(
            shape(blocks, 24, slot),
            shape(3 * PH, LO),
            shape(3 * PH, LO),
            shape(2, obs),
            shape(6, obs),
            jax.ShapeDtypeStruct((1, obs), jnp.int32),
        ),
        scratch_shapes=[
            pltpu.VMEM((18, obs), F32),
            pltpu.VMEM((2, obs), F32),
            pltpu.VMEM((1, obs), jnp.int32),
            pltpu.SemaphoreType.DMA((5,)),
        ],
        compiler_params=PARAMS,
        name="pack",
    )(*(pltpu.with_memory_space_constraint(x, pltpu.HBM) for x in (jac_point, jac_cam, resid, pidx, cidx)))
    own = lax.all_to_all(packed, ("grp", "tile"), 0, 0, axis_index_groups=groups, tiled=True)
    other = lax.ppermute(own, "tile", swap)
    sums = pl.pallas_call(
        functools.partial(own_sums_kernel, count, tail_rows),
        out_shape=shape(4 * rows, LO),
        compiler_params=PARAMS,
        name="own_sums",
        cost_estimate=pl.CostEstimate(flops=2 * 10**9, bytes_accessed=10**6, transcendentals=0),
    )(own)
    table = shape(rows, LO)
    back, tb, td, ts = pl.pallas_call(
        functools.partial(camera_kernel, n_grp, n_z, count, tail_rows),
        out_shape=(shape(n_grp, 4, slot + 128), table, table, table),
        scratch_shapes=[
            pltpu.VMEM((4 * rows, LO), F32),
            pltpu.VMEM((blocks, 2, slot), F32),
            pltpu.VMEM((2 * rows, LO), BF16),
        ],
        compiler_params=PARAMS,
        name="cameras",
    )(own, other, sums)
    back = lax.all_to_all(back, "grp", 0, 0, tiled=True)
    cb, cd, cs = pl.pallas_call(
        functools.partial(mine_kernel, 8 * count),
        out_shape=(shape(9, CAM_DEV),) * 3,
        compiler_params=PARAMS,
        name="mine",
    )(tb, td, ts)
    errors, ps, pe, sc = pl.pallas_call(
        functools.partial(point_kernel, n_grp),
        out_shape=(
            shape(n_grp * n_tile, 2, slot + 128),
            shape(3 * PH, LO),
            shape(2, obs),
            shape(2, 128),
        ),
        compiler_params=PARAMS,
        name="points",
    )(back, jp, pidx, pb, pd, pu, cb, cd, cs)
    errors = lax.all_to_all(errors, ("grp", "tile"), 0, 0, tiled=True)
    pt = pl.pallas_call(
        last_point_sums_kernel,
        out_shape=shape(3 * PH, LO),
        compiler_params=PARAMS,
        name="last_point_sums",
    )(jp, pidx, pe)
    return pl.pallas_call(
        final_kernel,
        out_shape=(shape(3, P_DEV), shape(9, CAM_DEV), shape(3, P_DEV), shape(9, CAM_DEV)),
        scratch_shapes=[pltpu.VMEM((96, 128), F32)],
        compiler_params=PARAMS,
        name="finish",
    )(errors, own, other, pb, pd, ps, pt, cb, cd, cs, sc)


def solution(mesh):
    placed = (
        P(None, ("grp", "tile")),
        P(None, ("grp", "tile")),
        P(None, ("grp", "tile")),
        P(("grp", "tile")),
        P(("grp", "tile")),
    )
    return jax.shard_map(
        shards,
        mesh=mesh,
        in_specs=placed,
        out_specs=(P(None, ("grp", "tile")),) * 4,
        check_vma=False,
    )
```

```python
import functools

import jax
import jax.numpy as jnp
from jax import lax
from jax.experimental import pallas as pl
from jax.experimental.pallas import tpu as pltpu
from jax.sharding import PartitionSpec as P

P_DEV = 4096
CAM_DEV = 384
LO_BITS = 8
LO = 1 << LO_BITS
PH = P_DEV // LO
DAMPING = 1.0
F32 = jnp.float32
BF16 = jnp.bfloat16
SLOTS = 64
HALF = 128
PARAMS = pltpu.CompilerParams(vmem_limit_bytes=48 * 1024 * 1024)


def halves(v):
    high = v.astype(BF16).astype(F32)
    return high, v - high


def rows16(width, step=1):
    numbers = lax.broadcasted_iota(jnp.int32, (16, width), 0)
    return (numbers // step if step > 1 else numbers).astype(F32).astype(BF16)


def sixteen(row):
    return jnp.broadcast_to(row.astype(F32), (16, row.shape[1])).astype(BF16)


def one_hot_rows(index, rows):
    numbers = rows16(index.shape[1])
    pieces = []
    for base in range(0, rows, 256):
        wide = sixteen(index - base)
        one, none = jnp.ones(wide.shape, BF16), jnp.zeros(wide.shape, BF16)
        pieces += [
            jnp.where(wide == numbers + BF16(16 * k), one, none)
            for k in range(min(256, rows - base) // 16)
        ]
    return jnp.concatenate(pieces, axis=0)


def dot_nt(a, b):
    return lax.dot_general(a, b, (((1,), (1,)), ((), ())), preferred_element_type=F32)


def dot_nn(a, b):
    return lax.dot_general(a, b, (((1,), (0,)), ((), ())), preferred_element_type=F32)


def is_row(hi, rows):
    return lax.broadcasted_iota(jnp.int32, (rows, hi.shape[1]), 0) == hi


def spread_row(mask, row):
    return jnp.where(mask, jnp.broadcast_to(row, mask.shape), 0.0)


def two_parts(v):
    high = v.astype(BF16)
    return high, (v - high.astype(F32)).astype(BF16)


def scatter_mixed(hi, hot, mains, tails, count, tail_rows):
    wide = sixteen(hi)
    none = jnp.zeros(wide.shape, BF16)
    single = len(mains) == 1
    numbers = rows16(hi.shape[1], 8) if single else none
    main_parts = two_parts(jnp.concatenate(mains * 2 if single else mains, axis=0))
    tail_parts = [two_parts(jnp.broadcast_to(v, wide.shape)) for v in tails]
    here = [wide == numbers + BF16(k) for k in range(0, count, 2 if single else 1)]
    tail_here = [wide == rows16(hi.shape[1]) + BF16(k) for k in range(0, tail_rows, 16)]
    pieces = []
    for part in range(2):
        pieces += [jnp.where(mask, main_parts[part], none) for mask in here]
        pieces += [jnp.where(mask, v[part], none) for v in tail_parts for mask in tail_here]
    return dot_nt(jnp.concatenate(pieces, axis=0), hot)


def both(v):
    half = v.shape[0] // 2
    return v[:half] + v[half:]


def gather_mixed(hi, hot, table, count, tail_rows):
    found = dot_nn(table, hot)
    hi8 = jnp.broadcast_to(hi, (8, hi.shape[1]))
    main = jnp.zeros(hi8.shape, F32)
    half = found.shape[0] // 2
    for k in range(count):
        rows = slice(k * 8, k * 8 + 8)
        low = slice(half + k * 8, half + k * 8 + 8)
        main = main + jnp.where(hi8 == k, found[rows] + found[low], 0.0)
    tail = found[count * 8 : half] + found[half + count * 8 :]
    tail = jnp.sum(jnp.where(is_row(hi, tail_rows), tail, 0.0), axis=0, keepdims=True)
    return main, tail


def stacked(table):
    high, low = halves(table)
    return jnp.concatenate([high, low], axis=0).astype(BF16)


def scatter_points(mask, hot, rows):
    parts = [halves(v) for v in rows]
    lhs = jnp.concatenate([spread_row(mask, v[k]) for k in range(2) for v in parts], axis=0)
    return both(dot_nt(lhs.astype(BF16), hot))


def gather_points(mask, hot, table):
    found = both(dot_nn(stacked(table), hot))
    return [
        jnp.sum(jnp.where(mask, found[i * PH : (i + 1) * PH], 0.0), axis=0, keepdims=True)
        for i in range(found.shape[0] // PH)
    ]


def total_of(v):
    return jnp.sum(jnp.sum(v, axis=0, keepdims=True), axis=1, keepdims=True)


def lanes(v, width):
    return jnp.broadcast_to(v, (v.shape[0], width))


def pack_kernel(
    n_grp, n_z, jp_hbm, jc_hbm, res_hbm, pidx_hbm, cidx_hbm,
    out_ref, pb_ref, pd_ref, pu_ref, jp_ref, pidx_ref,
    jc_ref, res_ref, cidx_ref, sems,
):
    copies = [
        pltpu.make_async_copy(source, target, sems.at[k])
        for k, (source, target) in enumerate(
            (
                (pidx_hbm, pidx_ref),
                (jp_hbm, jp_ref),
                (res_hbm, res_ref),
                (jc_hbm, jc_ref),
                (cidx_hbm, cidx_ref),
            )
        )
    ]
    for copy in copies:
        copy.start()
    for copy in copies:
        copy.wait()
    slot = out_ref.shape[2]
    index = pidx_ref[...]
    mask = is_row(index >> LO_BITS, PH)
    hot = one_hot_rows(index & (LO - 1), LO)
    jp = [jp_ref[k : k + 1, :] for k in range(6)]
    res = [res_ref[a : a + 1, :] for a in range(2)]
    grad = [-(jp[i] * res[0] + jp[3 + i] * res[1]) for i in range(3)]
    square = [jp[i] * jp[i] + jp[3 + i] * jp[3 + i] for i in range(3)]
    table = scatter_points(mask, hot, grad + square)
    rhs = table[: 3 * PH]
    diag = table[3 * PH :] + DAMPING
    pb_ref[...] = rhs
    pd_ref[...] = diag
    z = rhs / diag
    at = gather_points(mask, hot, z)
    u = [sum(jp[3 * a + i] * at[i] for i in range(3)) for a in range(2)]
    pu_ref[0:1, :] = u[0]
    pu_ref[1:2, :] = u[1]
    gamma = total_of(rhs * z)
    norm = total_of(z * z)
    scalars = jnp.concatenate([lanes(gamma, slot // 2), lanes(norm, slot // 2)], axis=1)
    cams = cidx_ref[...].astype(F32)
    for h in range(n_grp):
        cols = slice(h * slot, (h + 1) * slot)
        block = jnp.concatenate(
            [
                jc_ref[0:8, cols],
                jc_ref[9:17, cols],
                jc_ref[8:9, cols],
                jc_ref[17:18, cols],
                res[0][:, cols],
                res[1][:, cols],
                u[0][:, cols],
                u[1][:, cols],
                cams[:, cols],
                scalars,
            ],
            axis=0,
        )

        @pl.loop(0, n_z)
        def _(z_to, block=block, h=h):
            out_ref[h * n_z + z_to] = block


def read_blocks(ref, numbers):
    x = jnp.concatenate([ref[k] for k in numbers], axis=1)
    return x, x[22:23].astype(jnp.int32)


def chunk_of(chunk, per):
    return [chunk * per + k for k in range(per)]


def first_sums(ref, acc_ref, per, count, tail_rows):
    def body(chunk, carry):
        x, index = read_blocks(ref, chunk_of(chunk, per))
        hi, hot = index >> LO_BITS, one_hot_rows(index & (LO - 1), LO)
        j0, j1 = x[0:8], x[8:16]
        j08, j18, r0, r1 = x[16:17], x[17:18], x[18:19], x[19:20]
        acc_ref[...] += scatter_mixed(
            hi,
            hot,
            [-(j0 * r0 + j1 * r1), j0 * j0 + j1 * j1],
            [-(j08 * r0 + j18 * r1), j08 * j08 + j18 * j18],
            count,
            tail_rows,
        )
        return carry

    lax.fori_loop(0, ref.shape[0] // per, body, 0)


def own_sums_kernel(count, tail_rows, a_ref, acc_ref):
    acc_ref[...] = jnp.zeros(acc_ref.shape, F32)
    first_sums(a_ref, acc_ref, min(16, a_ref.shape[0]), count, tail_rows)


def camera_kernel(
    n_grp, n_z, count, tail_rows, a_ref, b_ref, start_ref,
    back_ref, tb_ref, td_ref, ts_ref,
    acc_ref, w_ref, zz_ref,
):
    blocks, _, slot = a_ref.shape
    per = min(8, blocks)
    chunks = blocks // per
    acc_ref[...] = start_ref[...]
    first_sums(b_ref, acc_ref, min(16, blocks), count, tail_rows)
    scalars = jnp.zeros((1, slot), F32)
    for ref in (a_ref, b_ref):
        scalars = scalars + jnp.sum(ref[:, 23, :], axis=0, keepdims=True)
    main = 8 * count
    half = acc_ref.shape[0] // 2
    for k in range(count):
        row = 16 * k
        tb_ref[8 * k : 8 * k + 8, :] = acc_ref[row : row + 8, :] + acc_ref[half + row : half + row + 8, :]
        row = 16 * k + 8
        td_ref[8 * k : 8 * k + 8, :] = (
            acc_ref[row : row + 8, :] + acc_ref[half + row : half + row + 8, :] + DAMPING
        )
    tb_ref[main:, :] = (
        acc_ref[2 * main : 2 * main + tail_rows, :]
        + acc_ref[half + 2 * main : half + 2 * main + tail_rows, :]
    )
    td_ref[main:, :] = (
        acc_ref[2 * main + tail_rows : half, :] + acc_ref[half + 2 * main + tail_rows :, :] + DAMPING
    )
    z = tb_ref[...] / td_ref[...]
    gamma = total_of(tb_ref[...] * z)
    norm = total_of(z * z)
    zz_ref[...] = stacked(z)
    ts_ref[...] = z
    acc_ref[0:half, :] = jnp.zeros((half, LO), F32)

    def second(ref, keep):
        def body(chunk, energy):
            numbers = chunk_of(chunk, per)
            x, index = read_blocks(ref, numbers)
            hi, hot = index >> LO_BITS, one_hot_rows(index & (LO - 1), LO)
            j0, j1 = x[0:8], x[8:16]
            j08, j18, u0, u1 = x[16:17], x[17:18], x[20:21], x[21:22]
            at, at8 = gather_mixed(hi, hot, zz_ref[...], count, tail_rows)
            w0 = jnp.sum(j0 * at, axis=0, keepdims=True) + j08 * at8
            w1 = jnp.sum(j1 * at, axis=0, keepdims=True) + j18 * at8
            if keep:
                for k, number in enumerate(numbers):
                    cols = slice(k * slot, (k + 1) * slot)
                    w_ref[number, 0:1, :] = w0[:, cols]
                    w_ref[number, 1:2, :] = w1[:, cols]
            e0, e1 = u0 + w0, u1 + w1
            acc_ref[0:half, :] += scatter_mixed(
                hi, hot, [j0 * e0 + j1 * e1], [j08 * e0 + j18 * e1], count, tail_rows
            )
            return energy + e0 * e0 + e1 * e1

        return body

    energy = jnp.zeros((1, per * slot), F32)
    energy = lax.fori_loop(0, chunks, second(a_ref, True), energy)
    energy = lax.fori_loop(0, chunks, second(b_ref, False), energy)
    ts_ref[...] += both(acc_ref[0:half, :])
    zz_ref[...] = stacked(ts_ref[...] / td_ref[...])
    share = 1.0 / n_grp
    gamma = gamma + share * scalars[:, 0:1]
    delta = norm + total_of(energy) + share * scalars[:, slot // 2 : slot // 2 + 1]
    mine = lax.axis_index("tile") // 2
    numbers = [g * n_z + mine for g in range(n_grp)]
    per = min(4, n_grp)
    for first in range(0, n_grp, per):
        some = numbers[first : first + per]
        x, index = read_blocks(a_ref, some)
        hi, hot = index >> LO_BITS, one_hot_rows(index & (LO - 1), LO)
        at, at8 = gather_mixed(hi, hot, zz_ref[...], count, tail_rows)
        v0 = jnp.sum(x[0:8] * at, axis=0, keepdims=True) + x[16:17] * at8
        v1 = jnp.sum(x[8:16] * at, axis=0, keepdims=True) + x[17:18] * at8
        for k in range(per):
            cols = slice(k * slot, (k + 1) * slot)
            g = first + k
            back_ref[g, 0:2, 0:slot] = w_ref[some[k], 0:2, :]
            back_ref[g, 2:3, 0:slot] = v0[:, cols]
            back_ref[g, 3:4, 0:slot] = v1[:, cols]
            back_ref[g, :, slot:] = lanes(jnp.concatenate([gamma, delta, gamma, delta], axis=0), 128)


def mine_kernel(main, tb_ref, td_ref, ts_ref, cb_ref, cd_ref, cs_ref):
    tile = lax.axis_index("tile")
    mine, core = tile // 2, tile % 2
    for source, target in ((tb_ref, cb_ref), (td_ref, cd_ref), (ts_ref, cs_ref)):
        own, own8 = [], []
        for k in range(3):
            rows = source[pl.ds(pl.multiple_of(8 * (3 * mine + k), 8), 8), :]
            tail = source[pl.ds(main + 3 * mine + k, 1), :]
            own += [rows[:, :128], rows[:, 128:]]
            own8 += [tail[:, :128], tail[:, 128:]]
        for m in range(3):
            cols = slice(m * 128, (m + 1) * 128)
            target[0:8, cols] = jnp.where(core == 0, own[m], own[m + 3])
            target[8:9, cols] = jnp.where(core == 0, own8[m], own8[m + 3])


def point_kernel(
    n_grp, back_ref, jp_ref, pidx_ref, pb_ref, pd_ref, pu_ref, cb_ref, cd_ref, cs_ref,
    out_ref, ps_ref, pe_ref, sc_ref,
):
    slot = back_ref.shape[2] - 128
    index = pidx_ref[...]
    mask = is_row(index >> LO_BITS, PH)
    hot = one_hot_rows(index & (LO - 1), LO)
    jp = [jp_ref[k : k + 1, :] for k in range(6)]
    scalars = back_ref[0, :, slot:]
    for h in range(1, n_grp):
        scalars = scalars + back_ref[h, :, slot:]
    gamma, delta = scalars[0:1, 0:1], scalars[1:2, 0:1]
    alpha = gamma / delta
    w = [
        jnp.concatenate([back_ref[h, r : r + 1, 0:slot] for h in range(n_grp)], axis=1) for r in range(4)
    ]
    rhs, diag = pb_ref[...], pd_ref[...]
    z = rhs / diag
    error = [pu_ref[a : a + 1, :] + w[a] for a in range(2)]
    s = z + scatter_points(mask, hot, [jp[i] * error[0] + jp[3 + i] * error[1] for i in range(3)])
    r1 = rhs - alpha * s
    z1 = r1 / diag
    at = gather_points(mask, hot, z1)
    error = [
        sum(jp[3 * a + i] * at[i] for i in range(3)) + (w[a] - alpha * w[2 + a]) for a in range(2)
    ]
    ps_ref[...] = s
    pe_ref[0:1, :] = error[0]
    pe_ref[1:2, :] = error[1]
    cr1 = cb_ref[...] - alpha * cs_ref[...]
    cz1 = cr1 / cd_ref[...]
    gamma1 = total_of(r1 * z1) + total_of(cr1 * cz1)
    delta1 = (
        total_of(error[0] * error[0] + error[1] * error[1]) + total_of(z1 * z1) + total_of(cz1 * cz1)
    )
    sc_ref[...] = lanes(jnp.concatenate([gamma, alpha], axis=0), 128)
    tail = lanes(jnp.concatenate([gamma1, delta1], axis=0), 128)
    per = out_ref.shape[0] // n_grp
    for h in range(n_grp):
        cols = slice(h * slot, (h + 1) * slot)
        block = jnp.concatenate([jnp.concatenate([e[:, cols] for e in error], axis=0), tail], axis=1)

        @pl.loop(0, per)
        def _(tile, block=block, h=h):
            out_ref[h * per + tile] = block


def last_point_sums_kernel(jp_ref, pidx_ref, pe_ref, pt_ref):
    index = pidx_ref[...]
    mask = is_row(index >> LO_BITS, PH)
    hot = one_hot_rows(index & (LO - 1), LO)
    jp = [jp_ref[k : k + 1, :] for k in range(6)]
    error = [pe_ref[a : a + 1, :] for a in range(2)]
    pt_ref[...] = scatter_points(
        mask, hot, [jp[i] * error[0] + jp[3 + i] * error[1] for i in range(3)]
    )


def final_kernel(
    err_ref, a_ref, b_ref, pb_ref, pd_ref, ps_ref, pt_ref, cb_ref, cd_ref, cs_ref, sc_ref,
    px_ref, cx_ref, pr_ref, cr_ref, acc_ref,
):
    blocks, _, slot = a_ref.shape
    per = min(8, blocks)
    chunks = blocks // per
    tile = lax.axis_index("tile")
    core = tile % 2
    acc_ref[...] = jnp.zeros(acc_ref.shape, F32)

    def body(ref, parity):
        def step(chunk, scalars):
            numbers = chunk_of(chunk, per)
            x, index = read_blocks(ref, numbers)
            errs = [err_ref[2 * k + parity] for k in numbers]
            e = jnp.concatenate([v[:, 0:slot] for v in errs], axis=1)
            for v in errs:
                scalars = scalars + v[:, slot:]
            index = index - tile * CAM_DEV
            hi = index >> 7
            hot = one_hot_rows(index & 127, 128)
            j0, j1 = x[0:8], x[8:16]
            e0, e1 = e[0:1], e[1:2]
            acc_ref[...] += scatter_mixed(
                hi, hot, [j0 * e0 + j1 * e1], [x[16:17] * e0 + x[17:18] * e1], 4, 16
            )
            return scalars

        return step

    scalars = lax.fori_loop(0, chunks, body(a_ref, core), jnp.zeros((2, 128), F32))
    scalars = lax.fori_loop(0, chunks, body(b_ref, 1 - core), scalars)
    gamma1, delta1 = scalars[0:1, 0:1], scalars[1:2, 0:1]
    gamma, alpha = sc_ref[0:1, 0:1], sc_ref[1:2, 0:1]
    ratio = gamma1 / gamma
    alpha1 = gamma1 / (delta1 - ratio * gamma1 / alpha)

    rhs, diag, s = pb_ref[...], pd_ref[...], ps_ref[...]
    z = rhs / diag
    r1 = rhs - alpha * s
    z1 = r1 / diag
    x = alpha * z + alpha1 * (z1 + ratio * z)
    r2 = r1 - alpha1 * (z1 + pt_ref[...] + ratio * s)
    for i in range(3):
        for hi in range(PH):
            row = i * PH + hi
            px_ref[i : i + 1, hi * LO : (hi + 1) * LO] = x[row : row + 1]
            pr_ref[i : i + 1, hi * LO : (hi + 1) * LO] = r2[row : row + 1]

    rhs, s = cb_ref[...], cs_ref[...]
    z = rhs / cd_ref[...]
    r1 = rhs - alpha * s
    z1 = r1 / cd_ref[...]
    cx_ref[...] = alpha * z + alpha1 * (z1 + ratio * z)
    sums = both(acc_ref[...])
    base = r1 - alpha1 * (z1 + ratio * s)
    for k in range(3):
        cols = slice(k * 128, (k + 1) * 128)
        cr_ref[0:8, cols] = base[0:8, cols] - alpha1 * sums[8 * k : 8 * k + 8, :]
        cr_ref[8:9, cols] = base[8:9, cols] - alpha1 * sums[32 + k : 33 + k, :]


def shape(*dims):
    return jax.ShapeDtypeStruct(dims, F32)


def replicated(jac_point, jac_cam, resid, point_index, cam_index):
    n_grp, n_tile = lax.axis_size("grp"), lax.axis_size("tile")
    n_z = n_tile // 2
    obs = jac_point.shape[1]
    slot = obs // n_grp
    blocks = n_grp * n_z
    count = CAM_DEV * n_tile // LO
    tail_rows = -(-count // 16) * 16
    rows = 8 * count + tail_rows
    groups = [[d * 2 + core for d in range(blocks)] for core in range(2)]
    swap = [(t, t ^ 1) for t in range(n_tile)]
    pidx, cidx = point_index.reshape(1, obs), cam_index.reshape(1, obs)

    hbm = pl.BlockSpec(memory_space=pltpu.HBM)
    packed, pb, pd, pu, jp, pidx = pl.pallas_call(
        functools.partial(pack_kernel, n_grp, n_z),
        in_specs=[hbm] * 5,
        out_shape=(
            shape(blocks, 24, slot),
            shape(3 * PH, LO),
            shape(3 * PH, LO),
            shape(2, obs),
            shape(6, obs),
            jax.ShapeDtypeStruct((1, obs), jnp.int32),
        ),
        scratch_shapes=[
            pltpu.VMEM((18, obs), F32),
            pltpu.VMEM((2, obs), F32),
            pltpu.VMEM((1, obs), jnp.int32),
            pltpu.SemaphoreType.DMA((5,)),
        ],
        compiler_params=PARAMS,
        name="pack",
    )(*(pltpu.with_memory_space_constraint(x, pltpu.HBM) for x in (jac_point, jac_cam, resid, pidx, cidx)))
    own = lax.all_to_all(packed, ("grp", "tile"), 0, 0, axis_index_groups=groups, tiled=True)
    other = lax.ppermute(own, "tile", swap)
    sums = pl.pallas_call(
        functools.partial(own_sums_kernel, count, tail_rows),
        out_shape=shape(4 * rows, LO),
        compiler_params=PARAMS,
        name="own_sums",
        cost_estimate=pl.CostEstimate(flops=2 * 10**9, bytes_accessed=10**6, transcendentals=0),
    )(own)
    table = shape(rows, LO)
    back, tb, td, ts = pl.pallas_call(
        functools.partial(camera_kernel, n_grp, n_z, count, tail_rows),
        out_shape=(shape(n_grp, 4, slot + 128), table, table, table),
        scratch_shapes=[
            pltpu.VMEM((4 * rows, LO), F32),
            pltpu.VMEM((blocks, 2, slot), F32),
            pltpu.VMEM((2 * rows, LO), BF16),
        ],
        compiler_params=PARAMS,
        name="cameras",
    )(own, other, sums)
    back = lax.all_to_all(back, "grp", 0, 0, tiled=True)
    cb, cd, cs = pl.pallas_call(
        functools.partial(mine_kernel, 8 * count),
        out_shape=(shape(9, CAM_DEV),) * 3,
        compiler_params=PARAMS,
        name="mine",
    )(tb, td, ts)
    errors, ps, pe, sc = pl.pallas_call(
        functools.partial(point_kernel, n_grp),
        out_shape=(
            shape(n_grp * n_tile, 2, slot + 128),
            shape(3 * PH, LO),
            shape(2, obs),
            shape(2, 128),
        ),
        compiler_params=PARAMS,
        name="points",
    )(back, jp, pidx, pb, pd, pu, cb, cd, cs)
    errors = lax.all_to_all(errors, ("grp", "tile"), 0, 0, tiled=True)
    pt = pl.pallas_call(
        last_point_sums_kernel,
        out_shape=shape(3 * PH, LO),
        compiler_params=PARAMS,
        name="last_point_sums",
    )(jp, pidx, pe)
    return pl.pallas_call(
        final_kernel,
        out_shape=(shape(3, P_DEV), shape(9, CAM_DEV), shape(3, P_DEV), shape(9, CAM_DEV)),
        scratch_shapes=[pltpu.VMEM((96, 128), F32)],
        compiler_params=PARAMS,
        name="finish",
    )(errors, own, other, pb, pd, ps, pt, cb, cd, cs, sc)


def three_parts(v):
    high = v.astype(BF16).astype(F32)
    rest = v - high
    middle = rest.astype(BF16).astype(F32)
    return jnp.concatenate([high, middle, rest - middle], axis=0).astype(BF16)


def thirds(v):
    rows = v.shape[0] // 3
    return v[:rows] + v[rows : 2 * rows] + v[2 * rows :]


def low_lanes(rows):
    return lax.broadcasted_iota(jnp.int32, (rows, HALF), 1) < SLOTS


def swap_lanes(v):
    return pltpu.roll(v, SLOTS, 1)


def point_start(pidx_ref, jp_ref, res_ref, pb_ref, pd_ref):
    index = pidx_ref[...]
    mask = is_row(index >> LO_BITS, PH)
    hot = one_hot_rows(index & (LO - 1), LO)
    jp = [jp_ref[k : k + 1, :] for k in range(6)]
    res = [res_ref[a : a + 1, :] for a in range(2)]
    grad = [-(jp[i] * res[0] + jp[3 + i] * res[1]) for i in range(3)]
    square = [jp[i] * jp[i] + jp[3 + i] * jp[3 + i] for i in range(3)]
    table = scatter_points(mask, hot, grad + square)
    rhs = table[: 3 * PH]
    diag = table[3 * PH :] + DAMPING
    pb_ref[...] = rhs
    pd_ref[...] = diag
    z = rhs / diag
    at = gather_points(mask, hot, z)
    u = [sum(jp[3 * a + i] * at[i] for i in range(3)) for a in range(2)]
    return u, total_of(rhs * z), total_of(z * z)


def start_copies(pairs, sems):
    copies = [pltpu.make_async_copy(a, b, sems.at[k]) for k, (a, b) in enumerate(pairs)]
    for copy in copies:
        copy.start()
    for copy in copies:
        copy.wait()


def route_kernel(
    n_grp, n_tile, jp_hbm, jc_hbm, res_hbm, pidx_hbm, cidx_hbm,
    out_ref, pb_ref, pd_ref, pu_ref, jp_ref, pidx_ref, place_ref, sc_ref,
    jc_ref, res_ref, cidx_ref, sems,
):
    start_copies(
        (
            (pidx_hbm, pidx_ref),
            (jp_hbm, jp_ref),
            (res_hbm, res_ref),
            (jc_hbm, jc_ref),
            (cidx_hbm, cidx_ref),
        ),
        sems,
    )
    slot = cidx_ref.shape[1] // n_grp
    cams = cidx_ref[...]
    owner = ((cams >> 7) * 171) >> 9
    local = (cams - owner * CAM_DEV).astype(F32)
    mine = is_row(owner, n_tile)
    ones = jnp.where(mine, 1.0, 0.0)
    stack = jnp.concatenate([ones[:, h * slot : (h + 1) * slot] for h in range(n_grp)], axis=0)
    before = lax.broadcasted_iota(jnp.int32, (slot, slot), 0)
    before = before < lax.broadcasted_iota(jnp.int32, (slot, slot), 1)
    counts = dot_nn(stack.astype(BF16), jnp.where(before, 1.0, 0.0).astype(BF16))
    counts = jnp.concatenate([counts[h * n_tile : (h + 1) * n_tile] for h in range(n_grp)], axis=1)
    rank = jnp.sum(jnp.where(mine, counts, 0.0), axis=0, keepdims=True)
    place = owner * SLOTS + rank.astype(jnp.int32)
    place_ref[...] = place
    over = jnp.max(jnp.where(rank >= SLOTS, 1.0, 0.0), axis=1, keepdims=True)
    u, gamma, norm = point_start(pidx_ref, jp_ref, res_ref, pb_ref, pd_ref)
    pu_ref[0:1, :] = u[0]
    pu_ref[1:2, :] = u[1]
    sc_ref[...] = lanes(jnp.concatenate([gamma, norm, over], axis=0), HALF)
    low = low_lanes(16)
    for h in range(n_grp):
        cols = slice(h * slot, (h + 1) * slot)
        rows = []
        for a in range(2):
            rows += [
                jc_ref[9 * a : 9 * a + 8, cols],
                jc_ref[9 * a + 8 : 9 * a + 9, cols],
                res_ref[a : a + 1, cols],
                u[a][:, cols],
                local[:, cols],
                jnp.zeros((4, slot), F32),
            ]
        hot = one_hot_rows(place[:, cols], n_tile * SLOTS)
        moved = thirds(dot_nt(three_parts(jnp.concatenate(rows, axis=0)), hot))
        for k in range(n_tile // 2):
            first = moved[0:16, k * HALF : (k + 1) * HALF]
            second = moved[16:32, k * HALF : (k + 1) * HALF]
            for t, block in (
                (2 * k, jnp.where(low, first, swap_lanes(second))),
                (2 * k + 1, jnp.where(low, swap_lanes(first), second)),
            ):
                for part in range(3):
                    out_ref[3 * (h * n_tile + t) + part] = block[4 * part : 4 * part + 4]


def read_routed(ref, sources):
    main = jnp.concatenate([jnp.concatenate([ref[3 * s], ref[3 * s + 1]], axis=0) for s in sources], axis=1)
    rest = jnp.concatenate([ref[3 * s + 2] for s in sources], axis=1)
    index = rest[3:4].astype(jnp.int32)
    return main, rest[0:1], rest[1:2], rest[2:3], index >> 7, one_hot_rows(index & 127, 128)


OWN_COUNT = 4
OWN_TAIL = 16
OWN_ROWS = 8 * OWN_COUNT + OWN_TAIL


def owner_kernel(in_ref, sc_ref, back_ref, tb_ref, td_ref, ts_ref, acc_ref, zz_ref):
    devices = back_ref.shape[0]
    per = min(32, devices)
    steps = devices // per
    acc_ref[...] = jnp.zeros(acc_ref.shape, F32)

    def loop(body, start):
        if steps == 1:
            return body(0, start)
        return lax.fori_loop(0, steps, body, start)

    def rhs_and_diag(step, carry):
        j, j8, r, _, hi, hot = read_routed(in_ref, chunk_of(step, per))
        acc_ref[...] += scatter_mixed(hi, hot, [-(j * r), j * j], [-(j8 * r), j8 * j8], OWN_COUNT, OWN_TAIL)
        return carry

    loop(rhs_and_diag, 0)
    sums = both(acc_ref[...])
    main = 8 * OWN_COUNT
    for k in range(OWN_COUNT):
        tb_ref[8 * k : 8 * k + 8, :] = sums[16 * k : 16 * k + 8]
        td_ref[8 * k : 8 * k + 8, :] = sums[16 * k + 8 : 16 * k + 16] + DAMPING
    tb_ref[main:, :] = sums[2 * main : 2 * main + OWN_TAIL]
    td_ref[main:, :] = sums[2 * main + OWN_TAIL :] + DAMPING
    z = tb_ref[...] / td_ref[...]
    zz_ref[...] = stacked(z)
    acc_ref[0 : 2 * OWN_ROWS, :] = jnp.zeros((2 * OWN_ROWS, 128), F32)

    def apply(step, energy):
        sources = chunk_of(step, per)
        j, j8, _, u, hi, hot = read_routed(in_ref, sources)
        at, at8 = gather_mixed(hi, hot, zz_ref[...], OWN_COUNT, OWN_TAIL)
        w = jnp.sum(j * at, axis=0, keepdims=True) + j8 * at8
        for k, s in enumerate(sources):
            back_ref[s, 0:1, :] = w[:, k * HALF : (k + 1) * HALF]
        e = u + w
        acc_ref[0 : 2 * OWN_ROWS, :] += scatter_mixed(hi, hot, [j * e], [j8 * e], OWN_COUNT, OWN_TAIL)
        return energy + e * e

    energy = loop(apply, jnp.zeros((1, per * HALF), F32))
    ts_ref[...] = z + both(acc_ref[0 : 2 * OWN_ROWS, :])
    zz_ref[...] = stacked(ts_ref[...] / td_ref[...])

    def gather_again(step, carry):
        sources = chunk_of(step, per)
        j, j8, _, _, hi, hot = read_routed(in_ref, sources)
        at, at8 = gather_mixed(hi, hot, zz_ref[...], OWN_COUNT, OWN_TAIL)
        v = jnp.sum(j * at, axis=0, keepdims=True) + j8 * at8
        for k, s in enumerate(sources):
            back_ref[s, 1:2, :] = v[:, k * HALF : (k + 1) * HALF]
        return carry

    loop(gather_again, 0)
    gamma = sc_ref[0:1, :] + total_of(tb_ref[...] * z)
    delta = sc_ref[1:2, :] + total_of(z * z) + total_of(energy)
    tail = jnp.concatenate([jnp.where(low_lanes(1), gamma, sc_ref[2:3, :]), delta], axis=0)
    back_ref[:, 2:4, :] = jnp.broadcast_to(tail[None], (devices, 2, HALF))


def routed_point_kernel(
    n_grp, n_tile, back_ref, jp_ref, pidx_ref, place_ref, pb_ref, pd_ref, pu_ref, cb_ref, cd_ref, cs_ref,
    out_ref, ps_ref, pe_ref, sc_ref, over_ref,
):
    slot = place_ref.shape[1] // n_grp
    index = pidx_ref[...]
    mask = is_row(index >> LO_BITS, PH)
    hot = one_hot_rows(index & (LO - 1), LO)
    jp = [jp_ref[k : k + 1, :] for k in range(6)]
    scalars = jnp.sum(back_ref[...], axis=0)
    gamma, delta = scalars[2:3, 0:1], scalars[3:4, 0:1]
    over_ref[...] = lanes(scalars[2:3, SLOTS : SLOTS + 1], HALF)
    alpha = gamma / delta
    low = low_lanes(4)
    places = [one_hot_rows(place_ref[:, h * slot : (h + 1) * slot], n_tile * SLOTS) for h in range(n_grp)]
    terms = []
    for h in range(n_grp):
        first, second = [], []
        for k in range(n_tile // 2):
            even, odd = back_ref[h * n_tile + 2 * k], back_ref[h * n_tile + 2 * k + 1]
            first.append(jnp.where(low, even, swap_lanes(odd)))
            second.append(jnp.where(low, swap_lanes(even), odd))
        both_rows = jnp.concatenate(
            [jnp.concatenate(first, axis=1), jnp.concatenate(second, axis=1)], axis=0
        )
        terms.append(thirds(dot_nn(three_parts(both_rows), places[h])))
    terms = jnp.concatenate(terms, axis=1)
    w0 = [terms[4 * a : 4 * a + 1] for a in range(2)]
    w1 = [terms[4 * a + 1 : 4 * a + 2] for a in range(2)]
    rhs, diag = pb_ref[...], pd_ref[...]
    z = rhs / diag
    error = [pu_ref[a : a + 1, :] + w0[a] for a in range(2)]
    s = z + scatter_points(mask, hot, [jp[i] * error[0] + jp[3 + i] * error[1] for i in range(3)])
    r1 = rhs - alpha * s
    z1 = r1 / diag
    at = gather_points(mask, hot, z1)
    error = [sum(jp[3 * a + i] * at[i] for i in range(3)) + (w0[a] - alpha * w1[a]) for a in range(2)]
    ps_ref[...] = s
    pe_ref[0:1, :] = error[0]
    pe_ref[1:2, :] = error[1]
    cr1 = cb_ref[...] - alpha * cs_ref[...]
    cz1 = cr1 / cd_ref[...]
    gamma1 = total_of(r1 * z1) + total_of(cr1 * cz1)
    delta1 = (
        total_of(error[0] * error[0] + error[1] * error[1]) + total_of(z1 * z1) + total_of(cz1 * cz1)
    )
    sc_ref[...] = lanes(jnp.concatenate([gamma, alpha], axis=0), HALF)
    tail = jnp.where(low_lanes(1), gamma1, delta1)
    low = low_lanes(8)
    for h in range(n_grp):
        rows = [jnp.broadcast_to(e[:, h * slot : (h + 1) * slot], (8, slot)) for e in error]
        moved = thirds(dot_nt(three_parts(jnp.concatenate(rows, axis=0)), places[h]))
        for k in range(n_tile // 2):
            first = moved[0:8, k * HALF : (k + 1) * HALF]
            second = moved[8:16, k * HALF : (k + 1) * HALF]
            out_ref[h * n_tile + 2 * k, 0:1, :] = jnp.where(low, first, swap_lanes(second))[0:1]
            out_ref[h * n_tile + 2 * k + 1, 0:1, :] = jnp.where(low, swap_lanes(first), second)[0:1]
    out_ref[:, 1:2, :] = jnp.broadcast_to(tail[None], (n_grp * n_tile, 1, HALF))


def point_results(alpha, alpha1, ratio, pb_ref, pd_ref, ps_ref, pt_ref, px_ref, pr_ref):
    rhs, diag, s = pb_ref[...], pd_ref[...], ps_ref[...]
    z = rhs / diag
    r1 = rhs - alpha * s
    z1 = r1 / diag
    x = alpha * z + alpha1 * (z1 + ratio * z)
    r2 = r1 - alpha1 * (z1 + pt_ref[...] + ratio * s)
    for i in range(3):
        for hi in range(PH):
            row = i * PH + hi
            px_ref[i : i + 1, hi * LO : (hi + 1) * LO] = x[row : row + 1]
            pr_ref[i : i + 1, hi * LO : (hi + 1) * LO] = r2[row : row + 1]


def routed_final_kernel(
    err_ref, in_ref, pb_ref, pd_ref, ps_ref, pt_ref, cb_ref, cd_ref, cs_ref, sc_ref,
    px_ref, cx_ref, pr_ref, cr_ref, acc_ref,
):
    devices = err_ref.shape[0]
    per = min(32, devices)
    steps = devices // per
    acc_ref[...] = jnp.zeros(acc_ref.shape, F32)

    def body(step, carry):
        sources = chunk_of(step, per)
        j, j8, _, _, hi, hot = read_routed(in_ref, sources)
        e = jnp.concatenate([err_ref[s, 0:1, :] for s in sources], axis=1)
        acc_ref[...] += scatter_mixed(hi, hot, [j * e], [j8 * e], OWN_COUNT, OWN_TAIL)
        return carry

    if steps == 1:
        body(0, 0)
    else:
        lax.fori_loop(0, steps, body, 0)
    scalars = jnp.sum(err_ref[...], axis=0)
    gamma1, delta1 = scalars[1:2, 0:1], scalars[1:2, SLOTS : SLOTS + 1]
    gamma, alpha = sc_ref[0:1, 0:1], sc_ref[1:2, 0:1]
    ratio = gamma1 / gamma
    alpha1 = gamma1 / (delta1 - ratio * gamma1 / alpha)
    point_results(alpha, alpha1, ratio, pb_ref, pd_ref, ps_ref, pt_ref, px_ref, pr_ref)
    rhs, s = cb_ref[...], cs_ref[...]
    z = rhs / cd_ref[...]
    r1 = rhs - alpha * s
    z1 = r1 / cd_ref[...]
    x = alpha * z + alpha1 * (z1 + ratio * z)
    r2 = r1 - alpha1 * (z1 + both(acc_ref[...]) + ratio * s)
    for table, target in ((x, cx_ref), (r2, cr_ref)):
        for k in range(CAM_DEV // 128):
            cols = slice(k * 128, (k + 1) * 128)
            target[0:8, cols] = table[8 * k : 8 * k + 8]
            row = 8 * OWN_COUNT + k
            target[8:9, cols] = table[row : row + 1]


def shards(jac_point, jac_cam, resid, point_index, cam_index):
    n_grp, n_tile = lax.axis_size("grp"), lax.axis_size("tile")
    devices = n_grp * n_tile
    obs = jac_point.shape[1]
    pidx, cidx = point_index.reshape(1, obs), cam_index.reshape(1, obs)
    hbm = pl.BlockSpec(memory_space=pltpu.HBM)
    ints = jax.ShapeDtypeStruct((1, obs), jnp.int32)
    points = shape(3 * PH, LO)
    cameras = shape(OWN_ROWS, 128)
    routed, pb, pd, pu, jp, pidx_here, place, sc = pl.pallas_call(
        functools.partial(route_kernel, n_grp, n_tile),
        in_specs=[hbm] * 5,
        out_shape=(shape(3 * devices, 4, HALF), points, points, shape(2, obs), shape(6, obs), ints, ints, shape(3, HALF)),
        scratch_shapes=[
            pltpu.VMEM((18, obs), F32),
            pltpu.VMEM((2, obs), F32),
            pltpu.VMEM((1, obs), jnp.int32),
            pltpu.SemaphoreType.DMA((5,)),
        ],
        compiler_params=PARAMS,
        name="route",
    )(*(pltpu.with_memory_space_constraint(x, pltpu.HBM) for x in (jac_point, jac_cam, resid, pidx, cidx)))
    routed = lax.all_to_all(routed, ("grp", "tile"), 0, 0, tiled=True)
    back, tb, td, ts = pl.pallas_call(
        owner_kernel,
        out_shape=(shape(devices, 4, HALF), cameras, cameras, cameras),
        scratch_shapes=[
            pltpu.VMEM((4 * OWN_ROWS, 128), F32),
            pltpu.VMEM((2 * OWN_ROWS, 128), BF16),
        ],
        compiler_params=PARAMS,
        name="owner",
    )(routed, sc)
    back = lax.all_to_all(back, ("grp", "tile"), 0, 0, tiled=True)
    errors, ps, pe, sc, over = pl.pallas_call(
        functools.partial(routed_point_kernel, n_grp, n_tile),
        out_shape=(shape(devices, 2, HALF), points, shape(2, obs), shape(2, HALF), shape(1, HALF)),
        compiler_params=PARAMS,
        name="points",
    )(back, jp, pidx_here, place, pb, pd, pu, tb, td, ts)
    errors = lax.all_to_all(errors, ("grp", "tile"), 0, 0, tiled=True)
    pt = pl.pallas_call(
        last_point_sums_kernel,
        out_shape=points,
        compiler_params=PARAMS,
        name="last_point_sums",
    )(jp, pidx_here, pe)
    outputs = (shape(3, P_DEV), shape(9, CAM_DEV), shape(3, P_DEV), shape(9, CAM_DEV))

    def fits(*operands):
        return pl.pallas_call(
            routed_final_kernel,
            out_shape=outputs,
            scratch_shapes=[pltpu.VMEM((2 * OWN_ROWS, 128), F32)],
            compiler_params=PARAMS,
            name="finish",
        )(*operands[5:])

    def overflows(*operands):
        return tuple(replicated(*operands[:5]))

    return lax.cond(
        over[0, 0] > 0,
        overflows,
        lambda *operands: tuple(fits(*operands)),
        jac_point, jac_cam, resid, point_index, cam_index,
        errors, routed, pb, pd, ps, pt, tb, td, ts, sc,
    )


def solution(mesh):
    placed = (
        P(None, ("grp", "tile")),
        P(None, ("grp", "tile")),
        P(None, ("grp", "tile")),
        P(("grp", "tile")),
        P(("grp", "tile")),
    )
    return jax.shard_map(
        shards,
        mesh=mesh,
        in_specs=placed,
        out_specs=(P(None, ("grp", "tile")),) * 4,
        check_vma=False,
    )
```

```python
import functools

import jax
import jax.numpy as jnp
from jax import lax
from jax.experimental import pallas as pl
from jax.experimental.pallas import tpu as pltpu
from jax.sharding import PartitionSpec as P

P_DEV = 4096
CAM_DEV = 384
LO_BITS = 8
LO = 1 << LO_BITS
PH = P_DEV // LO
DAMPING = 1.0
F32 = jnp.float32
BF16 = jnp.bfloat16
SLOTS = 64
HALF = 128
PARAMS = pltpu.CompilerParams(vmem_limit_bytes=48 * 1024 * 1024)


def halves(v):
    high = v.astype(BF16).astype(F32)
    return high, v - high


def rows16(width, step=1):
    numbers = lax.broadcasted_iota(jnp.int32, (16, width), 0)
    return (numbers // step if step > 1 else numbers).astype(F32).astype(BF16)


def sixteen(row):
    return jnp.broadcast_to(row.astype(F32), (16, row.shape[1])).astype(BF16)


def one_hot_rows(index, rows):
    numbers = rows16(index.shape[1])
    pieces = []
    for base in range(0, rows, 256):
        wide = sixteen(index - base)
        one, none = jnp.ones(wide.shape, BF16), jnp.zeros(wide.shape, BF16)
        pieces += [
            jnp.where(wide == numbers + BF16(16 * k), one, none)
            for k in range(min(256, rows - base) // 16)
        ]
    return jnp.concatenate(pieces, axis=0)


def dot_nt(a, b):
    return lax.dot_general(a, b, (((1,), (1,)), ((), ())), preferred_element_type=F32)


def dot_nn(a, b):
    return lax.dot_general(a, b, (((1,), (0,)), ((), ())), preferred_element_type=F32)


def is_row(hi, rows):
    return lax.broadcasted_iota(jnp.int32, (rows, hi.shape[1]), 0) == hi


def spread_row(mask, row):
    return jnp.where(mask, jnp.broadcast_to(row, mask.shape), 0.0)


def two_parts(v):
    high = v.astype(BF16)
    return high, (v - high.astype(F32)).astype(BF16)


def scatter_mixed(hi, hot, mains, tails, count, tail_rows):
    wide = sixteen(hi)
    none = jnp.zeros(wide.shape, BF16)
    single = len(mains) == 1
    numbers = rows16(hi.shape[1], 8) if single else none
    main_parts = two_parts(jnp.concatenate(mains * 2 if single else mains, axis=0))
    tail_parts = [two_parts(jnp.broadcast_to(v, wide.shape)) for v in tails]
    here = [wide == numbers + BF16(k) for k in range(0, count, 2 if single else 1)]
    tail_here = [wide == rows16(hi.shape[1]) + BF16(k) for k in range(0, tail_rows, 16)]
    pieces = []
    for part in range(2):
        pieces += [jnp.where(mask, main_parts[part], none) for mask in here]
        pieces += [jnp.where(mask, v[part], none) for v in tail_parts for mask in tail_here]
    return dot_nt(jnp.concatenate(pieces, axis=0), hot)


def both(v):
    half = v.shape[0] // 2
    return v[:half] + v[half:]


def gather_mixed(hi, hot, table, count, tail_rows):
    found = dot_nn(table, hot)
    hi8 = jnp.broadcast_to(hi, (8, hi.shape[1]))
    main = jnp.zeros(hi8.shape, F32)
    half = found.shape[0] // 2
    for k in range(count):
        rows = slice(k * 8, k * 8 + 8)
        low = slice(half + k * 8, half + k * 8 + 8)
        main = main + jnp.where(hi8 == k, found[rows] + found[low], 0.0)
    tail = found[count * 8 : half] + found[half + count * 8 :]
    tail = jnp.sum(jnp.where(is_row(hi, tail_rows), tail, 0.0), axis=0, keepdims=True)
    return main, tail


def stacked(table):
    high, low = halves(table)
    return jnp.concatenate([high, low], axis=0).astype(BF16)


def scatter_points(mask, hot, rows):
    parts = [halves(v) for v in rows]
    lhs = jnp.concatenate([spread_row(mask, v[k]) for k in range(2) for v in parts], axis=0)
    return both(dot_nt(lhs.astype(BF16), hot))


def gather_points(mask, hot, table):
    found = both(dot_nn(stacked(table), hot))
    return [
        jnp.sum(jnp.where(mask, found[i * PH : (i + 1) * PH], 0.0), axis=0, keepdims=True)
        for i in range(found.shape[0] // PH)
    ]


def total_of(v):
    return jnp.sum(jnp.sum(v, axis=0, keepdims=True), axis=1, keepdims=True)


def lanes(v, width):
    return jnp.broadcast_to(v, (v.shape[0], width))


def pack_kernel(
    n_grp, n_z, jp_hbm, jc_hbm, res_hbm, pidx_hbm, cidx_hbm,
    out_ref, pb_ref, pd_ref, pu_ref, jp_ref, pidx_ref,
    jc_ref, res_ref, cidx_ref, sems,
):
    copies = [
        pltpu.make_async_copy(source, target, sems.at[k])
        for k, (source, target) in enumerate(
            (
                (pidx_hbm, pidx_ref),
                (jp_hbm, jp_ref),
                (res_hbm, res_ref),
                (jc_hbm, jc_ref),
                (cidx_hbm, cidx_ref),
            )
        )
    ]
    for copy in copies:
        copy.start()
    for copy in copies:
        copy.wait()
    slot = out_ref.shape[2]
    index = pidx_ref[...]
    mask = is_row(index >> LO_BITS, PH)
    hot = one_hot_rows(index & (LO - 1), LO)
    jp = [jp_ref[k : k + 1, :] for k in range(6)]
    res = [res_ref[a : a + 1, :] for a in range(2)]
    grad = [-(jp[i] * res[0] + jp[3 + i] * res[1]) for i in range(3)]
    square = [jp[i] * jp[i] + jp[3 + i] * jp[3 + i] for i in range(3)]
    table = scatter_points(mask, hot, grad + square)
    rhs = table[: 3 * PH]
    diag = table[3 * PH :] + DAMPING
    pb_ref[...] = rhs
    pd_ref[...] = diag
    z = rhs / diag
    at = gather_points(mask, hot, z)
    u = [sum(jp[3 * a + i] * at[i] for i in range(3)) for a in range(2)]
    pu_ref[0:1, :] = u[0]
    pu_ref[1:2, :] = u[1]
    gamma = total_of(rhs * z)
    norm = total_of(z * z)
    scalars = jnp.concatenate([lanes(gamma, slot // 2), lanes(norm, slot // 2)], axis=1)
    cams = cidx_ref[...].astype(F32)
    for h in range(n_grp):
        cols = slice(h * slot, (h + 1) * slot)
        block = jnp.concatenate(
            [
                jc_ref[0:8, cols],
                jc_ref[9:17, cols],
                jc_ref[8:9, cols],
                jc_ref[17:18, cols],
                res[0][:, cols],
                res[1][:, cols],
                u[0][:, cols],
                u[1][:, cols],
                cams[:, cols],
                scalars,
            ],
            axis=0,
        )

        @pl.loop(0, n_z)
        def _(z_to, block=block, h=h):
            out_ref[h * n_z + z_to] = block


def read_blocks(ref, numbers):
    x = jnp.concatenate([ref[k] for k in numbers], axis=1)
    return x, x[22:23].astype(jnp.int32)


def chunk_of(chunk, per):
    return [chunk * per + k for k in range(per)]


def first_sums(ref, acc_ref, per, count, tail_rows):
    def body(chunk, carry):
        x, index = read_blocks(ref, chunk_of(chunk, per))
        hi, hot = index >> LO_BITS, one_hot_rows(index & (LO - 1), LO)
        j0, j1 = x[0:8], x[8:16]
        j08, j18, r0, r1 = x[16:17], x[17:18], x[18:19], x[19:20]
        acc_ref[...] += scatter_mixed(
            hi,
            hot,
            [-(j0 * r0 + j1 * r1), j0 * j0 + j1 * j1],
            [-(j08 * r0 + j18 * r1), j08 * j08 + j18 * j18],
            count,
            tail_rows,
        )
        return carry

    lax.fori_loop(0, ref.shape[0] // per, body, 0)


def own_sums_kernel(count, tail_rows, a_ref, acc_ref):
    acc_ref[...] = jnp.zeros(acc_ref.shape, F32)
    first_sums(a_ref, acc_ref, min(16, a_ref.shape[0]), count, tail_rows)


def camera_kernel(
    n_grp, n_z, count, tail_rows, a_ref, b_ref, start_ref,
    back_ref, tb_ref, td_ref, ts_ref,
    acc_ref, w_ref, zz_ref,
):
    blocks, _, slot = a_ref.shape
    per = min(8, blocks)
    chunks = blocks // per
    acc_ref[...] = start_ref[...]
    first_sums(b_ref, acc_ref, min(16, blocks), count, tail_rows)
    scalars = jnp.zeros((1, slot), F32)
    for ref in (a_ref, b_ref):
        scalars = scalars + jnp.sum(ref[:, 23, :], axis=0, keepdims=True)
    main = 8 * count
    half = acc_ref.shape[0] // 2
    for k in range(count):
        row = 16 * k
        tb_ref[8 * k : 8 * k + 8, :] = acc_ref[row : row + 8, :] + acc_ref[half + row : half + row + 8, :]
        row = 16 * k + 8
        td_ref[8 * k : 8 * k + 8, :] = (
            acc_ref[row : row + 8, :] + acc_ref[half + row : half + row + 8, :] + DAMPING
        )
    tb_ref[main:, :] = (
        acc_ref[2 * main : 2 * main + tail_rows, :]
        + acc_ref[half + 2 * main : half + 2 * main + tail_rows, :]
    )
    td_ref[main:, :] = (
        acc_ref[2 * main + tail_rows : half, :] + acc_ref[half + 2 * main + tail_rows :, :] + DAMPING
    )
    z = tb_ref[...] / td_ref[...]
    gamma = total_of(tb_ref[...] * z)
    norm = total_of(z * z)
    zz_ref[...] = stacked(z)
    ts_ref[...] = z
    acc_ref[0:half, :] = jnp.zeros((half, LO), F32)

    def second(ref, keep):
        def body(chunk, energy):
            numbers = chunk_of(chunk, per)
            x, index = read_blocks(ref, numbers)
            hi, hot = index >> LO_BITS, one_hot_rows(index & (LO - 1), LO)
            j0, j1 = x[0:8], x[8:16]
            j08, j18, u0, u1 = x[16:17], x[17:18], x[20:21], x[21:22]
            at, at8 = gather_mixed(hi, hot, zz_ref[...], count, tail_rows)
            w0 = jnp.sum(j0 * at, axis=0, keepdims=True) + j08 * at8
            w1 = jnp.sum(j1 * at, axis=0, keepdims=True) + j18 * at8
            if keep:
                for k, number in enumerate(numbers):
                    cols = slice(k * slot, (k + 1) * slot)
                    w_ref[number, 0:1, :] = w0[:, cols]
                    w_ref[number, 1:2, :] = w1[:, cols]
            e0, e1 = u0 + w0, u1 + w1
            acc_ref[0:half, :] += scatter_mixed(
                hi, hot, [j0 * e0 + j1 * e1], [j08 * e0 + j18 * e1], count, tail_rows
            )
            return energy + e0 * e0 + e1 * e1

        return body

    energy = jnp.zeros((1, per * slot), F32)
    energy = lax.fori_loop(0, chunks, second(a_ref, True), energy)
    energy = lax.fori_loop(0, chunks, second(b_ref, False), energy)
    ts_ref[...] += both(acc_ref[0:half, :])
    zz_ref[...] = stacked(ts_ref[...] / td_ref[...])
    share = 1.0 / n_grp
    gamma = gamma + share * scalars[:, 0:1]
    delta = norm + total_of(energy) + share * scalars[:, slot // 2 : slot // 2 + 1]
    mine = lax.axis_index("tile") // 2
    numbers = [g * n_z + mine for g in range(n_grp)]
    per = min(4, n_grp)
    for first in range(0, n_grp, per):
        some = numbers[first : first + per]
        x, index = read_blocks(a_ref, some)
        hi, hot = index >> LO_BITS, one_hot_rows(index & (LO - 1), LO)
        at, at8 = gather_mixed(hi, hot, zz_ref[...], count, tail_rows)
        v0 = jnp.sum(x[0:8] * at, axis=0, keepdims=True) + x[16:17] * at8
        v1 = jnp.sum(x[8:16] * at, axis=0, keepdims=True) + x[17:18] * at8
        for k in range(per):
            cols = slice(k * slot, (k + 1) * slot)
            g = first + k
            back_ref[g, 0:2, 0:slot] = w_ref[some[k], 0:2, :]
            back_ref[g, 2:3, 0:slot] = v0[:, cols]
            back_ref[g, 3:4, 0:slot] = v1[:, cols]
            back_ref[g, :, slot:] = lanes(jnp.concatenate([gamma, delta, gamma, delta], axis=0), 128)


def mine_kernel(main, tb_ref, td_ref, ts_ref, cb_ref, cd_ref, cs_ref):
    tile = lax.axis_index("tile")
    mine, core = tile // 2, tile % 2
    for source, target in ((tb_ref, cb_ref), (td_ref, cd_ref), (ts_ref, cs_ref)):
        own, own8 = [], []
        for k in range(3):
            rows = source[pl.ds(pl.multiple_of(8 * (3 * mine + k), 8), 8), :]
            tail = source[pl.ds(main + 3 * mine + k, 1), :]
            own += [rows[:, :128], rows[:, 128:]]
            own8 += [tail[:, :128], tail[:, 128:]]
        for m in range(3):
            cols = slice(m * 128, (m + 1) * 128)
            target[0:8, cols] = jnp.where(core == 0, own[m], own[m + 3])
            target[8:9, cols] = jnp.where(core == 0, own8[m], own8[m + 3])


def point_kernel(
    n_grp, back_ref, jp_ref, pidx_ref, pb_ref, pd_ref, pu_ref, cb_ref, cd_ref, cs_ref,
    out_ref, ps_ref, pe_ref, sc_ref,
):
    slot = back_ref.shape[2] - 128
    index = pidx_ref[...]
    mask = is_row(index >> LO_BITS, PH)
    hot = one_hot_rows(index & (LO - 1), LO)
    jp = [jp_ref[k : k + 1, :] for k in range(6)]
    scalars = back_ref[0, :, slot:]
    for h in range(1, n_grp):
        scalars = scalars + back_ref[h, :, slot:]
    gamma, delta = scalars[0:1, 0:1], scalars[1:2, 0:1]
    alpha = gamma / delta
    w = [
        jnp.concatenate([back_ref[h, r : r + 1, 0:slot] for h in range(n_grp)], axis=1) for r in range(4)
    ]
    rhs, diag = pb_ref[...], pd_ref[...]
    z = rhs / diag
    error = [pu_ref[a : a + 1, :] + w[a] for a in range(2)]
    s = z + scatter_points(mask, hot, [jp[i] * error[0] + jp[3 + i] * error[1] for i in range(3)])
    r1 = rhs - alpha * s
    z1 = r1 / diag
    at = gather_points(mask, hot, z1)
    error = [
        sum(jp[3 * a + i] * at[i] for i in range(3)) + (w[a] - alpha * w[2 + a]) for a in range(2)
    ]
    ps_ref[...] = s
    pe_ref[0:1, :] = error[0]
    pe_ref[1:2, :] = error[1]
    cr1 = cb_ref[...] - alpha * cs_ref[...]
    cz1 = cr1 / cd_ref[...]
    gamma1 = total_of(r1 * z1) + total_of(cr1 * cz1)
    delta1 = (
        total_of(error[0] * error[0] + error[1] * error[1]) + total_of(z1 * z1) + total_of(cz1 * cz1)
    )
    sc_ref[...] = lanes(jnp.concatenate([gamma, alpha], axis=0), 128)
    tail = lanes(jnp.concatenate([gamma1, delta1], axis=0), 128)
    per = out_ref.shape[0] // n_grp
    for h in range(n_grp):
        cols = slice(h * slot, (h + 1) * slot)
        block = jnp.concatenate([jnp.concatenate([e[:, cols] for e in error], axis=0), tail], axis=1)

        @pl.loop(0, per)
        def _(tile, block=block, h=h):
            out_ref[h * per + tile] = block


def last_point_sums_kernel(jp_ref, pidx_ref, pe_ref, pt_ref):
    index = pidx_ref[...]
    mask = is_row(index >> LO_BITS, PH)
    hot = one_hot_rows(index & (LO - 1), LO)
    jp = [jp_ref[k : k + 1, :] for k in range(6)]
    error = [pe_ref[a : a + 1, :] for a in range(2)]
    pt_ref[...] = scatter_points(
        mask, hot, [jp[i] * error[0] + jp[3 + i] * error[1] for i in range(3)]
    )


def final_kernel(
    err_ref, a_ref, b_ref, pb_ref, pd_ref, ps_ref, pt_ref, cb_ref, cd_ref, cs_ref, sc_ref,
    px_ref, cx_ref, pr_ref, cr_ref, acc_ref,
):
    blocks, _, slot = a_ref.shape
    per = min(8, blocks)
    chunks = blocks // per
    tile = lax.axis_index("tile")
    core = tile % 2
    acc_ref[...] = jnp.zeros(acc_ref.shape, F32)

    def body(ref, parity):
        def step(chunk, scalars):
            numbers = chunk_of(chunk, per)
            x, index = read_blocks(ref, numbers)
            errs = [err_ref[2 * k + parity] for k in numbers]
            e = jnp.concatenate([v[:, 0:slot] for v in errs], axis=1)
            for v in errs:
                scalars = scalars + v[:, slot:]
            index = index - tile * CAM_DEV
            hi = index >> 7
            hot = one_hot_rows(index & 127, 128)
            j0, j1 = x[0:8], x[8:16]
            e0, e1 = e[0:1], e[1:2]
            acc_ref[...] += scatter_mixed(
                hi, hot, [j0 * e0 + j1 * e1], [x[16:17] * e0 + x[17:18] * e1], 4, 16
            )
            return scalars

        return step

    scalars = lax.fori_loop(0, chunks, body(a_ref, core), jnp.zeros((2, 128), F32))
    scalars = lax.fori_loop(0, chunks, body(b_ref, 1 - core), scalars)
    gamma1, delta1 = scalars[0:1, 0:1], scalars[1:2, 0:1]
    gamma, alpha = sc_ref[0:1, 0:1], sc_ref[1:2, 0:1]
    ratio = gamma1 / gamma
    alpha1 = gamma1 / (delta1 - ratio * gamma1 / alpha)

    rhs, diag, s = pb_ref[...], pd_ref[...], ps_ref[...]
    z = rhs / diag
    r1 = rhs - alpha * s
    z1 = r1 / diag
    x = alpha * z + alpha1 * (z1 + ratio * z)
    r2 = r1 - alpha1 * (z1 + pt_ref[...] + ratio * s)
    for i in range(3):
        for hi in range(PH):
            row = i * PH + hi
            px_ref[i : i + 1, hi * LO : (hi + 1) * LO] = x[row : row + 1]
            pr_ref[i : i + 1, hi * LO : (hi + 1) * LO] = r2[row : row + 1]

    rhs, s = cb_ref[...], cs_ref[...]
    z = rhs / cd_ref[...]
    r1 = rhs - alpha * s
    z1 = r1 / cd_ref[...]
    cx_ref[...] = alpha * z + alpha1 * (z1 + ratio * z)
    sums = both(acc_ref[...])
    base = r1 - alpha1 * (z1 + ratio * s)
    for k in range(3):
        cols = slice(k * 128, (k + 1) * 128)
        cr_ref[0:8, cols] = base[0:8, cols] - alpha1 * sums[8 * k : 8 * k + 8, :]
        cr_ref[8:9, cols] = base[8:9, cols] - alpha1 * sums[32 + k : 33 + k, :]


def shape(*dims):
    return jax.ShapeDtypeStruct(dims, F32)


def replicated(jac_point, jac_cam, resid, point_index, cam_index):
    n_grp, n_tile = lax.axis_size("grp"), lax.axis_size("tile")
    n_z = n_tile // 2
    obs = jac_point.shape[1]
    slot = obs // n_grp
    blocks = n_grp * n_z
    count = CAM_DEV * n_tile // LO
    tail_rows = -(-count // 16) * 16
    rows = 8 * count + tail_rows
    groups = [[d * 2 + core for d in range(blocks)] for core in range(2)]
    swap = [(t, t ^ 1) for t in range(n_tile)]
    pidx, cidx = point_index.reshape(1, obs), cam_index.reshape(1, obs)

    hbm = pl.BlockSpec(memory_space=pltpu.HBM)
    packed, pb, pd, pu, jp, pidx = pl.pallas_call(
        functools.partial(pack_kernel, n_grp, n_z),
        in_specs=[hbm] * 5,
        out_shape=(
            shape(blocks, 24, slot),
            shape(3 * PH, LO),
            shape(3 * PH, LO),
            shape(2, obs),
            shape(6, obs),
            jax.ShapeDtypeStruct((1, obs), jnp.int32),
        ),
        scratch_shapes=[
            pltpu.VMEM((18, obs), F32),
            pltpu.VMEM((2, obs), F32),
            pltpu.VMEM((1, obs), jnp.int32),
            pltpu.SemaphoreType.DMA((5,)),
        ],
        compiler_params=PARAMS,
        name="pack",
    )(*(pltpu.with_memory_space_constraint(x, pltpu.HBM) for x in (jac_point, jac_cam, resid, pidx, cidx)))
    own = lax.all_to_all(packed, ("grp", "tile"), 0, 0, axis_index_groups=groups, tiled=True)
    other = lax.ppermute(own, "tile", swap)
    sums = pl.pallas_call(
        functools.partial(own_sums_kernel, count, tail_rows),
        out_shape=shape(4 * rows, LO),
        compiler_params=PARAMS,
        name="own_sums",
        cost_estimate=pl.CostEstimate(flops=2 * 10**9, bytes_accessed=10**6, transcendentals=0),
    )(own)
    table = shape(rows, LO)
    back, tb, td, ts = pl.pallas_call(
        functools.partial(camera_kernel, n_grp, n_z, count, tail_rows),
        out_shape=(shape(n_grp, 4, slot + 128), table, table, table),
        scratch_shapes=[
            pltpu.VMEM((4 * rows, LO), F32),
            pltpu.VMEM((blocks, 2, slot), F32),
            pltpu.VMEM((2 * rows, LO), BF16),
        ],
        compiler_params=PARAMS,
        name="cameras",
    )(own, other, sums)
    back = lax.all_to_all(back, "grp", 0, 0, tiled=True)
    cb, cd, cs = pl.pallas_call(
        functools.partial(mine_kernel, 8 * count),
        out_shape=(shape(9, CAM_DEV),) * 3,
        compiler_params=PARAMS,
        name="mine",
    )(tb, td, ts)
    errors, ps, pe, sc = pl.pallas_call(
        functools.partial(point_kernel, n_grp),
        out_shape=(
            shape(n_grp * n_tile, 2, slot + 128),
            shape(3 * PH, LO),
            shape(2, obs),
            shape(2, 128),
        ),
        compiler_params=PARAMS,
        name="points",
    )(back, jp, pidx, pb, pd, pu, cb, cd, cs)
    errors = lax.all_to_all(errors, ("grp", "tile"), 0, 0, tiled=True)
    pt = pl.pallas_call(
        last_point_sums_kernel,
        out_shape=shape(3 * PH, LO),
        compiler_params=PARAMS,
        name="last_point_sums",
    )(jp, pidx, pe)
    return pl.pallas_call(
        final_kernel,
        out_shape=(shape(3, P_DEV), shape(9, CAM_DEV), shape(3, P_DEV), shape(9, CAM_DEV)),
        scratch_shapes=[pltpu.VMEM((96, 128), F32)],
        compiler_params=PARAMS,
        name="finish",
    )(errors, own, other, pb, pd, ps, pt, cb, cd, cs, sc)


def three_parts(v):
    high = v.astype(BF16).astype(F32)
    rest = v - high
    middle = rest.astype(BF16).astype(F32)
    return jnp.concatenate([high, middle, rest - middle], axis=0).astype(BF16)


def thirds(v):
    rows = v.shape[0] // 3
    return v[:rows] + v[rows : 2 * rows] + v[2 * rows :]


def low_lanes(rows):
    return lax.broadcasted_iota(jnp.int32, (rows, HALF), 1) < SLOTS


def swap_lanes(v):
    return pltpu.roll(v, SLOTS, 1)


def point_start(pidx_ref, jp_ref, res_ref, pb_ref, pd_ref):
    index = pidx_ref[...]
    mask = is_row(index >> LO_BITS, PH)
    hot = one_hot_rows(index & (LO - 1), LO)
    jp = [jp_ref[k : k + 1, :] for k in range(6)]
    res = [res_ref[a : a + 1, :] for a in range(2)]
    grad = [-(jp[i] * res[0] + jp[3 + i] * res[1]) for i in range(3)]
    square = [jp[i] * jp[i] + jp[3 + i] * jp[3 + i] for i in range(3)]
    table = scatter_points(mask, hot, grad + square)
    rhs = table[: 3 * PH]
    diag = table[3 * PH :] + DAMPING
    pb_ref[...] = rhs
    pd_ref[...] = diag
    z = rhs / diag
    at = gather_points(mask, hot, z)
    u = [sum(jp[3 * a + i] * at[i] for i in range(3)) for a in range(2)]
    return u, total_of(rhs * z), total_of(z * z)


def start_copies(pairs, sems):
    copies = [pltpu.make_async_copy(a, b, sems.at[k]) for k, (a, b) in enumerate(pairs)]
    for copy in copies:
        copy.start()
    for copy in copies:
        copy.wait()


def route_kernel(
    n_grp, n_tile, jp_hbm, jc_hbm, res_hbm, pidx_hbm, cidx_hbm,
    out_ref, pb_ref, pd_ref, pu_ref, jp_ref, pidx_ref, place_ref, sc_ref,
    jc_ref, res_ref, cidx_ref, sems,
):
    start_copies(
        (
            (pidx_hbm, pidx_ref),
            (jp_hbm, jp_ref),
            (res_hbm, res_ref),
            (jc_hbm, jc_ref),
            (cidx_hbm, cidx_ref),
        ),
        sems,
    )
    slot = cidx_ref.shape[1] // n_grp
    cams = cidx_ref[...]
    owner = ((cams >> 7) * 171) >> 9
    local = (cams - owner * CAM_DEV).astype(F32)
    mine = is_row(owner, n_tile)
    ones = jnp.where(mine, 1.0, 0.0)
    stack = jnp.concatenate([ones[:, h * slot : (h + 1) * slot] for h in range(n_grp)], axis=0)
    before = lax.broadcasted_iota(jnp.int32, (slot, slot), 0)
    before = before < lax.broadcasted_iota(jnp.int32, (slot, slot), 1)
    counts = dot_nn(stack.astype(BF16), jnp.where(before, 1.0, 0.0).astype(BF16))
    counts = jnp.concatenate([counts[h * n_tile : (h + 1) * n_tile] for h in range(n_grp)], axis=1)
    rank = jnp.sum(jnp.where(mine, counts, 0.0), axis=0, keepdims=True)
    place = owner * SLOTS + rank.astype(jnp.int32)
    place_ref[...] = place
    over = jnp.max(jnp.where(rank >= SLOTS, 1.0, 0.0), axis=1, keepdims=True)
    u, gamma, norm = point_start(pidx_ref, jp_ref, res_ref, pb_ref, pd_ref)
    pu_ref[0:1, :] = u[0]
    pu_ref[1:2, :] = u[1]
    sc_ref[...] = lanes(jnp.concatenate([gamma, norm, over], axis=0), HALF)
    low = low_lanes(16)
    for h in range(n_grp):
        cols = slice(h * slot, (h + 1) * slot)
        rows = []
        for a in range(2):
            rows += [
                jc_ref[9 * a : 9 * a + 8, cols],
                jc_ref[9 * a + 8 : 9 * a + 9, cols],
                res_ref[a : a + 1, cols],
                u[a][:, cols],
                local[:, cols],
                jnp.zeros((4, slot), F32),
            ]
        hot = one_hot_rows(place[:, cols], n_tile * SLOTS)
        moved = thirds(dot_nt(three_parts(jnp.concatenate(rows, axis=0)), hot))
        for k in range(n_tile // 2):
            first = moved[0:16, k * HALF : (k + 1) * HALF]
            second = moved[16:32, k * HALF : (k + 1) * HALF]
            for t, block in (
                (2 * k, jnp.where(low, first, swap_lanes(second))),
                (2 * k + 1, jnp.where(low, swap_lanes(first), second)),
            ):
                for part in range(3):
                    out_ref[3 * (h * n_tile + t) + part] = block[4 * part : 4 * part + 4]


def unfold(even, odd):
    low = low_lanes(even.shape[0])
    return jnp.where(low, even, swap_lanes(odd)), jnp.where(low, swap_lanes(even), odd)


def side_by_side(even, odd):
    return jnp.where(low_lanes(even.shape[0]), even, swap_lanes(odd))


def read_routed(ref, sources):
    main, rest = ([], []), ([], [])
    for s, t in zip(sources[::2], sources[1::2]):
        pair = unfold(*(jnp.concatenate([ref[3 * k], ref[3 * k + 1]], axis=0) for k in (s, t)))
        pair_rest = unfold(ref[3 * s + 2], ref[3 * t + 2])
        for a in range(2):
            main[a].append(pair[a])
            rest[a].append(pair_rest[a])
    main = [jnp.concatenate(v, axis=1) for v in main]
    rest = [jnp.concatenate(v, axis=1) for v in rest]
    return main, rest, one_hot_rows(rest[0][3:4].astype(jnp.int32), CAM_DEV)


def padded(main, tail):
    below = lax.broadcasted_iota(jnp.int32, main.shape, 0) == 0
    return jnp.concatenate([main, jnp.where(below, jnp.broadcast_to(tail, main.shape), 0.0)], axis=0)


def scatter_own(hot, values):
    return both(dot_nt(stacked(values), hot))


def gather_own(hot, table, main, rest):
    at = both(dot_nn(table, hot))
    return [
        jnp.sum(main[a] * at[0:8], axis=0, keepdims=True) + rest[a][0:1] * at[8:9] for a in range(2)
    ]


def transposed_j(main, rest, e):
    return padded(main[0] * e[0] + main[1] * e[1], rest[0][0:1] * e[0] + rest[1][0:1] * e[1])


OWN_ROWS = 16
STEP = 32


def owner_kernel(in_ref, sc_ref, back_ref, tb_ref, td_ref, ts_ref, acc_ref, zz_ref, w_ref, *kept):
    devices = back_ref.shape[0]
    per = min(STEP, devices)
    steps = devices // per

    if steps == 1:
        main, rest, hot = read_routed(in_ref, range(devices))
        kept[0][...] = hot
        for a in range(2):
            kept[1][8 * a : 8 * a + 8, :] = main[a]
            kept[1][16 + a : 17 + a, :] = rest[a][0:1]

        def loop(body, start):
            return body((main, rest, hot), 0, start)
    else:

        def loop(body, start):
            def step(number, carry):
                return body(read_routed(in_ref, chunk_of(number, per)), number, carry)

            return lax.fori_loop(0, steps, step, start)

    def rhs_and_diag(slots, number, carry):
        main, rest, hot = slots
        r = [rest[a][1:2] for a in range(2)]
        rhs = padded(
            -(main[0] * r[0] + main[1] * r[1]), -(rest[0][0:1] * r[0] + rest[1][0:1] * r[1])
        )
        square = padded(
            main[0] * main[0] + main[1] * main[1],
            rest[0][0:1] * rest[0][0:1] + rest[1][0:1] * rest[1][0:1],
        )
        acc_ref[...] += scatter_own(hot, jnp.concatenate([rhs, square], axis=0))
        return carry

    acc_ref[...] = jnp.zeros(acc_ref.shape, F32)
    loop(rhs_and_diag, 0)
    rhs, diag = acc_ref[0:OWN_ROWS, :], acc_ref[OWN_ROWS:, :] + DAMPING
    tb_ref[...] = rhs
    td_ref[...] = diag
    z = rhs / diag
    zz_ref[...] = stacked(z)
    acc_ref[0:OWN_ROWS, :] = z

    def apply(slots, number, energy):
        main, rest, hot = slots
        w = gather_own(hot, zz_ref[...], main, rest)
        e = [rest[a][2:3] + w[a] for a in range(2)]
        for a in range(2):
            w_ref[number, a : a + 1, :] = w[a]
        acc_ref[0:OWN_ROWS, :] += scatter_own(hot, transposed_j(main, rest, e))
        return energy + e[0] * e[0] + e[1] * e[1]

    energy = loop(apply, jnp.zeros((1, per * SLOTS), F32))
    s = acc_ref[0:OWN_ROWS, :]
    ts_ref[...] = s
    zz_ref[...] = stacked(s / diag)
    gamma = sc_ref[0:1, :] + total_of(rhs * z)
    delta = sc_ref[1:2, :] + total_of(z * z) + total_of(energy)
    tail = jnp.concatenate([gamma, delta, sc_ref[2:3, :], sc_ref[2:3, :]], axis=0)

    def send(slots, number, carry):
        main, rest, hot = slots
        v = gather_own(hot, zz_ref[...], main, rest)
        for a in range(2):
            w_ref[number, 2 + a : 3 + a, :] = v[a]
        w = w_ref[number]
        low = low_lanes(4)
        for k in range(per // 2):
            pair = w[:, k * HALF : (k + 1) * HALF]
            back_ref[number * per + 2 * k] = jnp.where(low, pair, tail)
            back_ref[number * per + 2 * k + 1] = jnp.where(low, swap_lanes(pair), tail)
        return carry

    loop(send, 0)


def routed_point_kernel(
    n_grp, n_tile, back_ref, jp_ref, pidx_ref, place_ref, pb_ref, pd_ref, pu_ref, cb_ref, cd_ref, cs_ref,
    out_ref, ps_ref, pe_ref, sc_ref, over_ref,
):
    slot = place_ref.shape[1] // n_grp
    index = pidx_ref[...]
    mask = is_row(index >> LO_BITS, PH)
    hot = one_hot_rows(index & (LO - 1), LO)
    jp = [jp_ref[k : k + 1, :] for k in range(6)]
    scalars = jnp.sum(back_ref[...], axis=0)[:, SLOTS : SLOTS + 1]
    gamma, delta = scalars[0:1], scalars[1:2]
    over_ref[...] = lanes(scalars[2:3], HALF)
    alpha = gamma / delta
    places = [one_hot_rows(place_ref[:, h * slot : (h + 1) * slot], n_tile * SLOTS) for h in range(n_grp)]
    terms = []
    for h in range(n_grp):
        pairs = range(h * n_tile, (h + 1) * n_tile, 2)
        rows = jnp.concatenate([side_by_side(back_ref[k], back_ref[k + 1]) for k in pairs], axis=1)
        terms.append(thirds(dot_nn(three_parts(rows), places[h])))
    terms = jnp.concatenate(terms, axis=1)
    w0 = [terms[a : a + 1] for a in range(2)]
    w1 = [terms[2 + a : 3 + a] for a in range(2)]
    rhs, diag = pb_ref[...], pd_ref[...]
    z = rhs / diag
    error = [pu_ref[a : a + 1, :] + w0[a] for a in range(2)]
    s = z + scatter_points(mask, hot, [jp[i] * error[0] + jp[3 + i] * error[1] for i in range(3)])
    r1 = rhs - alpha * s
    z1 = r1 / diag
    at = gather_points(mask, hot, z1)
    error = [sum(jp[3 * a + i] * at[i] for i in range(3)) + (w0[a] - alpha * w1[a]) for a in range(2)]
    ps_ref[...] = s
    pe_ref[0:1, :] = error[0]
    pe_ref[1:2, :] = error[1]
    cr1 = cb_ref[...] - alpha * cs_ref[...]
    cz1 = cr1 / cd_ref[...]
    gamma1 = total_of(r1 * z1) + total_of(cr1 * cz1)
    delta1 = (
        total_of(error[0] * error[0] + error[1] * error[1]) + total_of(z1 * z1) + total_of(cz1 * cz1)
    )
    sc_ref[...] = lanes(jnp.concatenate([gamma, alpha], axis=0), HALF)
    tail = lanes(jnp.concatenate([gamma1, delta1], axis=0), HALF)
    low = low_lanes(2)
    for h in range(n_grp):
        rows = jnp.concatenate([e[:, h * slot : (h + 1) * slot] for e in error], axis=0)
        moved = thirds(dot_nt(three_parts(rows), places[h]))
        for k in range(n_tile // 2):
            pair = moved[:, k * HALF : (k + 1) * HALF]
            out_ref[h * n_tile + 2 * k] = jnp.where(low, pair, tail)
            out_ref[h * n_tile + 2 * k + 1] = jnp.where(low, swap_lanes(pair), tail)


def point_results(alpha, alpha1, ratio, pb_ref, pd_ref, ps_ref, pt_ref, px_ref, pr_ref):
    rhs, diag, s = pb_ref[...], pd_ref[...], ps_ref[...]
    z = rhs / diag
    r1 = rhs - alpha * s
    z1 = r1 / diag
    x = alpha * z + alpha1 * (z1 + ratio * z)
    r2 = r1 - alpha1 * (z1 + pt_ref[...] + ratio * s)
    for i in range(3):
        for hi in range(PH):
            row = i * PH + hi
            px_ref[i : i + 1, hi * LO : (hi + 1) * LO] = x[row : row + 1]
            pr_ref[i : i + 1, hi * LO : (hi + 1) * LO] = r2[row : row + 1]


def routed_final_kernel(
    err_ref, in_ref, pb_ref, pd_ref, ps_ref, pt_ref, cb_ref, cd_ref, cs_ref, sc_ref, *rest_refs
):
    kept, (px_ref, cx_ref, pr_ref, cr_ref, acc_ref) = rest_refs[:-5], rest_refs[-5:]
    devices = err_ref.shape[0]
    per = min(STEP, devices)
    steps = devices // per

    def body(step, carry):
        sources = chunk_of(step, per)
        if kept:
            hot, rows = kept[0][...], kept[1]
            main = [rows[8 * a : 8 * a + 8, :] for a in range(2)]
            rest = [rows[16 + a : 17 + a, :] for a in range(2)]
        else:
            main, rest, hot = read_routed(in_ref, sources)
        e = jnp.concatenate(
            [side_by_side(err_ref[s], err_ref[t]) for s, t in zip(sources[::2], sources[1::2])], axis=1
        )
        acc_ref[...] += scatter_own(hot, transposed_j(main, rest, [e[0:1], e[1:2]]))
        return carry

    acc_ref[...] = jnp.zeros(acc_ref.shape, F32)
    if steps == 1:
        body(0, 0)
    else:
        lax.fori_loop(0, steps, body, 0)
    scalars = jnp.sum(err_ref[...], axis=0)
    gamma1, delta1 = scalars[0:1, SLOTS : SLOTS + 1], scalars[1:2, SLOTS : SLOTS + 1]
    gamma, alpha = sc_ref[0:1, 0:1], sc_ref[1:2, 0:1]
    ratio = gamma1 / gamma
    alpha1 = gamma1 / (delta1 - ratio * gamma1 / alpha)
    point_results(alpha, alpha1, ratio, pb_ref, pd_ref, ps_ref, pt_ref, px_ref, pr_ref)
    rhs, s = cb_ref[...], cs_ref[...]
    z = rhs / cd_ref[...]
    r1 = rhs - alpha * s
    z1 = r1 / cd_ref[...]
    cx_ref[...] = (alpha * z + alpha1 * (z1 + ratio * z))[0:9]
    cr_ref[...] = (r1 - alpha1 * (z1 + acc_ref[...] + ratio * s))[0:9]


def shards(jac_point, jac_cam, resid, point_index, cam_index):
    n_grp, n_tile = lax.axis_size("grp"), lax.axis_size("tile")
    devices = n_grp * n_tile
    obs = jac_point.shape[1]
    pidx, cidx = point_index.reshape(1, obs), cam_index.reshape(1, obs)
    hbm = pl.BlockSpec(memory_space=pltpu.HBM)
    ints = jax.ShapeDtypeStruct((1, obs), jnp.int32)
    points = shape(3 * PH, LO)
    cameras = shape(OWN_ROWS, CAM_DEV)
    routed, pb, pd, pu, jp, pidx_here, place, sc = pl.pallas_call(
        functools.partial(route_kernel, n_grp, n_tile),
        in_specs=[hbm] * 5,
        out_shape=(shape(3 * devices, 4, HALF), points, points, shape(2, obs), shape(6, obs), ints, ints, shape(3, HALF)),
        scratch_shapes=[
            pltpu.VMEM((18, obs), F32),
            pltpu.VMEM((2, obs), F32),
            pltpu.VMEM((1, obs), jnp.int32),
            pltpu.SemaphoreType.DMA((5,)),
        ],
        compiler_params=PARAMS,
        name="route",
    )(*(pltpu.with_memory_space_constraint(x, pltpu.HBM) for x in (jac_point, jac_cam, resid, pidx, cidx)))
    routed = lax.all_to_all(routed, ("grp", "tile"), 0, 0, tiled=True)
    slots = devices * SLOTS
    per = min(STEP, devices)
    scratch = [
        pltpu.VMEM((2 * OWN_ROWS, CAM_DEV), F32),
        pltpu.VMEM((2 * OWN_ROWS, CAM_DEV), BF16),
        pltpu.VMEM((devices // per, 4, per * SLOTS), F32),
    ]
    kept_shapes = ()
    if devices == per:
        kept_shapes = (jax.ShapeDtypeStruct((CAM_DEV, slots), BF16), shape(24, slots))

    def owner(in_ref, sc_ref, back_ref, tb_ref, td_ref, ts_ref, *others):
        kept, work = others[: len(kept_shapes)], others[len(kept_shapes) :]
        owner_kernel(in_ref, sc_ref, back_ref, tb_ref, td_ref, ts_ref, *work, *kept)

    back, tb, td, ts, *kept = pl.pallas_call(
        owner,
        out_shape=(shape(devices, 4, HALF), cameras, cameras, cameras) + kept_shapes,
        scratch_shapes=scratch,
        compiler_params=PARAMS,
        name="owner",
    )(routed, sc)
    back = lax.all_to_all(back, ("grp", "tile"), 0, 0, tiled=True)
    errors, ps, pe, sc, over = pl.pallas_call(
        functools.partial(routed_point_kernel, n_grp, n_tile),
        out_shape=(shape(devices, 2, HALF), points, shape(2, obs), shape(2, HALF), shape(1, HALF)),
        compiler_params=PARAMS,
        name="points",
    )(back, jp, pidx_here, place, pb, pd, pu, tb, td, ts)
    errors = lax.all_to_all(errors, ("grp", "tile"), 0, 0, tiled=True)
    pt = pl.pallas_call(
        last_point_sums_kernel,
        out_shape=points,
        compiler_params=PARAMS,
        name="last_point_sums",
    )(jp, pidx_here, pe)
    outputs = (shape(3, P_DEV), shape(9, CAM_DEV), shape(3, P_DEV), shape(9, CAM_DEV))

    def fits(*operands):
        return pl.pallas_call(
            routed_final_kernel,
            out_shape=outputs,
            scratch_shapes=[pltpu.VMEM((OWN_ROWS, CAM_DEV), F32)],
            compiler_params=PARAMS,
            name="finish",
        )(*operands[5:])

    def overflows(*operands):
        return tuple(replicated(*operands[:5]))

    return lax.cond(
        over[0, 0] > 0,
        overflows,
        lambda *operands: tuple(fits(*operands)),
        jac_point, jac_cam, resid, point_index, cam_index,
        errors, routed, pb, pd, ps, pt, tb, td, ts, sc, *kept,
    )


def solution(mesh):
    placed = (
        P(None, ("grp", "tile")),
        P(None, ("grp", "tile")),
        P(None, ("grp", "tile")),
        P(("grp", "tile")),
        P(("grp", "tile")),
    )
    return jax.shard_map(
        shards,
        mesh=mesh,
        in_specs=placed,
        out_specs=(P(None, ("grp", "tile")),) * 4,
        check_vma=False,
    )
```

```python
import functools

import jax
import jax.numpy as jnp
from jax import lax
from jax.experimental import pallas as pl
from jax.experimental.pallas import tpu as pltpu
from jax.sharding import PartitionSpec as P

P_DEV = 4096
CAM_DEV = 384
LO_BITS = 8
LO = 1 << LO_BITS
PH = P_DEV // LO
DAMPING = 1.0
F32 = jnp.float32
BF16 = jnp.bfloat16
SLOTS = 64
HALF = 128
PARAMS = pltpu.CompilerParams(vmem_limit_bytes=48 * 1024 * 1024)


def halves(v):
    high = v.astype(BF16).astype(F32)
    return high, v - high


def rows16(width, step=1):
    numbers = lax.broadcasted_iota(jnp.int32, (16, width), 0)
    return (numbers // step if step > 1 else numbers).astype(F32).astype(BF16)


def sixteen(row):
    return jnp.broadcast_to(row.astype(F32), (16, row.shape[1])).astype(BF16)


def one_hot_rows(index, rows):
    numbers = rows16(index.shape[1])
    pieces = []
    for base in range(0, rows, 256):
        wide = sixteen(index - base)
        one, none = jnp.ones(wide.shape, BF16), jnp.zeros(wide.shape, BF16)
        pieces += [
            jnp.where(wide == numbers + BF16(16 * k), one, none)
            for k in range(min(256, rows - base) // 16)
        ]
    return jnp.concatenate(pieces, axis=0)


def dot_nt(a, b):
    return lax.dot_general(a, b, (((1,), (1,)), ((), ())), preferred_element_type=F32)


def dot_nn(a, b):
    return lax.dot_general(a, b, (((1,), (0,)), ((), ())), preferred_element_type=F32)


def is_row(hi, rows):
    return lax.broadcasted_iota(jnp.int32, (rows, hi.shape[1]), 0) == hi


def spread_row(mask, row):
    return jnp.where(mask, jnp.broadcast_to(row, mask.shape), 0.0)


def two_parts(v):
    high = v.astype(BF16)
    return high, (v - high.astype(F32)).astype(BF16)


def scatter_mixed(hi, hot, mains, tails, count, tail_rows):
    wide = sixteen(hi)
    none = jnp.zeros(wide.shape, BF16)
    single = len(mains) == 1
    numbers = rows16(hi.shape[1], 8) if single else none
    main_parts = two_parts(jnp.concatenate(mains * 2 if single else mains, axis=0))
    tail_parts = [two_parts(jnp.broadcast_to(v, wide.shape)) for v in tails]
    here = [wide == numbers + BF16(k) for k in range(0, count, 2 if single else 1)]
    tail_here = [wide == rows16(hi.shape[1]) + BF16(k) for k in range(0, tail_rows, 16)]
    pieces = []
    for part in range(2):
        pieces += [jnp.where(mask, main_parts[part], none) for mask in here]
        pieces += [jnp.where(mask, v[part], none) for v in tail_parts for mask in tail_here]
    return dot_nt(jnp.concatenate(pieces, axis=0), hot)


def both(v):
    half = v.shape[0] // 2
    return v[:half] + v[half:]


def gather_mixed(hi, hot, table, count, tail_rows):
    found = dot_nn(table, hot)
    hi8 = jnp.broadcast_to(hi, (8, hi.shape[1]))
    main = jnp.zeros(hi8.shape, F32)
    half = found.shape[0] // 2
    for k in range(count):
        rows = slice(k * 8, k * 8 + 8)
        low = slice(half + k * 8, half + k * 8 + 8)
        main = main + jnp.where(hi8 == k, found[rows] + found[low], 0.0)
    tail = found[count * 8 : half] + found[half + count * 8 :]
    tail = jnp.sum(jnp.where(is_row(hi, tail_rows), tail, 0.0), axis=0, keepdims=True)
    return main, tail


def stacked(table):
    high, low = halves(table)
    return jnp.concatenate([high, low], axis=0).astype(BF16)


def scatter_points(mask, hot, rows):
    parts = [halves(v) for v in rows]
    lhs = jnp.concatenate([spread_row(mask, v[k]) for k in range(2) for v in parts], axis=0)
    return both(dot_nt(lhs.astype(BF16), hot))


def gather_points(mask, hot, table):
    found = both(dot_nn(stacked(table), hot))
    return [
        jnp.sum(jnp.where(mask, found[i * PH : (i + 1) * PH], 0.0), axis=0, keepdims=True)
        for i in range(found.shape[0] // PH)
    ]


def total_of(v):
    return jnp.sum(jnp.sum(v, axis=0, keepdims=True), axis=1, keepdims=True)


def lanes(v, width):
    return jnp.broadcast_to(v, (v.shape[0], width))


def pack_kernel(
    n_grp, n_z, jp_hbm, jc_hbm, res_hbm, pidx_hbm, cidx_hbm,
    out_ref, pb_ref, pd_ref, pu_ref, jp_ref, pidx_ref,
    jc_ref, res_ref, cidx_ref, sems,
):
    copies = [
        pltpu.make_async_copy(source, target, sems.at[k])
        for k, (source, target) in enumerate(
            (
                (pidx_hbm, pidx_ref),
                (jp_hbm, jp_ref),
                (res_hbm, res_ref),
                (jc_hbm, jc_ref),
                (cidx_hbm, cidx_ref),
            )
        )
    ]
    for copy in copies:
        copy.start()
    for copy in copies:
        copy.wait()
    slot = out_ref.shape[2]
    index = pidx_ref[...]
    mask = is_row(index >> LO_BITS, PH)
    hot = one_hot_rows(index & (LO - 1), LO)
    jp = [jp_ref[k : k + 1, :] for k in range(6)]
    res = [res_ref[a : a + 1, :] for a in range(2)]
    grad = [-(jp[i] * res[0] + jp[3 + i] * res[1]) for i in range(3)]
    square = [jp[i] * jp[i] + jp[3 + i] * jp[3 + i] for i in range(3)]
    table = scatter_points(mask, hot, grad + square)
    rhs = table[: 3 * PH]
    diag = table[3 * PH :] + DAMPING
    pb_ref[...] = rhs
    pd_ref[...] = diag
    z = rhs / diag
    at = gather_points(mask, hot, z)
    u = [sum(jp[3 * a + i] * at[i] for i in range(3)) for a in range(2)]
    pu_ref[0:1, :] = u[0]
    pu_ref[1:2, :] = u[1]
    gamma = total_of(rhs * z)
    norm = total_of(z * z)
    scalars = jnp.concatenate([lanes(gamma, slot // 2), lanes(norm, slot // 2)], axis=1)
    cams = cidx_ref[...].astype(F32)
    for h in range(n_grp):
        cols = slice(h * slot, (h + 1) * slot)
        block = jnp.concatenate(
            [
                jc_ref[0:8, cols],
                jc_ref[9:17, cols],
                jc_ref[8:9, cols],
                jc_ref[17:18, cols],
                res[0][:, cols],
                res[1][:, cols],
                u[0][:, cols],
                u[1][:, cols],
                cams[:, cols],
                scalars,
            ],
            axis=0,
        )

        @pl.loop(0, n_z)
        def _(z_to, block=block, h=h):
            out_ref[h * n_z + z_to] = block


def read_blocks(ref, numbers):
    x = jnp.concatenate([ref[k] for k in numbers], axis=1)
    return x, x[22:23].astype(jnp.int32)


def chunk_of(chunk, per):
    return [chunk * per + k for k in range(per)]


def first_sums(ref, acc_ref, per, count, tail_rows):
    def body(chunk, carry):
        x, index = read_blocks(ref, chunk_of(chunk, per))
        hi, hot = index >> LO_BITS, one_hot_rows(index & (LO - 1), LO)
        j0, j1 = x[0:8], x[8:16]
        j08, j18, r0, r1 = x[16:17], x[17:18], x[18:19], x[19:20]
        acc_ref[...] += scatter_mixed(
            hi,
            hot,
            [-(j0 * r0 + j1 * r1), j0 * j0 + j1 * j1],
            [-(j08 * r0 + j18 * r1), j08 * j08 + j18 * j18],
            count,
            tail_rows,
        )
        return carry

    lax.fori_loop(0, ref.shape[0] // per, body, 0)


def own_sums_kernel(count, tail_rows, a_ref, acc_ref):
    acc_ref[...] = jnp.zeros(acc_ref.shape, F32)
    first_sums(a_ref, acc_ref, min(16, a_ref.shape[0]), count, tail_rows)


def camera_kernel(
    n_grp, n_z, count, tail_rows, a_ref, b_ref, start_ref,
    back_ref, tb_ref, td_ref, ts_ref,
    acc_ref, w_ref, zz_ref,
):
    blocks, _, slot = a_ref.shape
    per = min(8, blocks)
    chunks = blocks // per
    acc_ref[...] = start_ref[...]
    first_sums(b_ref, acc_ref, min(16, blocks), count, tail_rows)
    scalars = jnp.zeros((1, slot), F32)
    for ref in (a_ref, b_ref):
        scalars = scalars + jnp.sum(ref[:, 23, :], axis=0, keepdims=True)
    main = 8 * count
    half = acc_ref.shape[0] // 2
    for k in range(count):
        row = 16 * k
        tb_ref[8 * k : 8 * k + 8, :] = acc_ref[row : row + 8, :] + acc_ref[half + row : half + row + 8, :]
        row = 16 * k + 8
        td_ref[8 * k : 8 * k + 8, :] = (
            acc_ref[row : row + 8, :] + acc_ref[half + row : half + row + 8, :] + DAMPING
        )
    tb_ref[main:, :] = (
        acc_ref[2 * main : 2 * main + tail_rows, :]
        + acc_ref[half + 2 * main : half + 2 * main + tail_rows, :]
    )
    td_ref[main:, :] = (
        acc_ref[2 * main + tail_rows : half, :] + acc_ref[half + 2 * main + tail_rows :, :] + DAMPING
    )
    z = tb_ref[...] / td_ref[...]
    gamma = total_of(tb_ref[...] * z)
    norm = total_of(z * z)
    zz_ref[...] = stacked(z)
    ts_ref[...] = z
    acc_ref[0:half, :] = jnp.zeros((half, LO), F32)

    def second(ref, keep):
        def body(chunk, energy):
            numbers = chunk_of(chunk, per)
            x, index = read_blocks(ref, numbers)
            hi, hot = index >> LO_BITS, one_hot_rows(index & (LO - 1), LO)
            j0, j1 = x[0:8], x[8:16]
            j08, j18, u0, u1 = x[16:17], x[17:18], x[20:21], x[21:22]
            at, at8 = gather_mixed(hi, hot, zz_ref[...], count, tail_rows)
            w0 = jnp.sum(j0 * at, axis=0, keepdims=True) + j08 * at8
            w1 = jnp.sum(j1 * at, axis=0, keepdims=True) + j18 * at8
            if keep:
                for k, number in enumerate(numbers):
                    cols = slice(k * slot, (k + 1) * slot)
                    w_ref[number, 0:1, :] = w0[:, cols]
                    w_ref[number, 1:2, :] = w1[:, cols]
            e0, e1 = u0 + w0, u1 + w1
            acc_ref[0:half, :] += scatter_mixed(
                hi, hot, [j0 * e0 + j1 * e1], [j08 * e0 + j18 * e1], count, tail_rows
            )
            return energy + e0 * e0 + e1 * e1

        return body

    energy = jnp.zeros((1, per * slot), F32)
    energy = lax.fori_loop(0, chunks, second(a_ref, True), energy)
    energy = lax.fori_loop(0, chunks, second(b_ref, False), energy)
    ts_ref[...] += both(acc_ref[0:half, :])
    zz_ref[...] = stacked(ts_ref[...] / td_ref[...])
    share = 1.0 / n_grp
    gamma = gamma + share * scalars[:, 0:1]
    delta = norm + total_of(energy) + share * scalars[:, slot // 2 : slot // 2 + 1]
    mine = lax.axis_index("tile") // 2
    numbers = [g * n_z + mine for g in range(n_grp)]
    per = min(4, n_grp)
    for first in range(0, n_grp, per):
        some = numbers[first : first + per]
        x, index = read_blocks(a_ref, some)
        hi, hot = index >> LO_BITS, one_hot_rows(index & (LO - 1), LO)
        at, at8 = gather_mixed(hi, hot, zz_ref[...], count, tail_rows)
        v0 = jnp.sum(x[0:8] * at, axis=0, keepdims=True) + x[16:17] * at8
        v1 = jnp.sum(x[8:16] * at, axis=0, keepdims=True) + x[17:18] * at8
        for k in range(per):
            cols = slice(k * slot, (k + 1) * slot)
            g = first + k
            back_ref[g, 0:2, 0:slot] = w_ref[some[k], 0:2, :]
            back_ref[g, 2:3, 0:slot] = v0[:, cols]
            back_ref[g, 3:4, 0:slot] = v1[:, cols]
            back_ref[g, :, slot:] = lanes(jnp.concatenate([gamma, delta, gamma, delta], axis=0), 128)


def mine_kernel(main, tb_ref, td_ref, ts_ref, cb_ref, cd_ref, cs_ref):
    tile = lax.axis_index("tile")
    mine, core = tile // 2, tile % 2
    for source, target in ((tb_ref, cb_ref), (td_ref, cd_ref), (ts_ref, cs_ref)):
        own, own8 = [], []
        for k in range(3):
            rows = source[pl.ds(pl.multiple_of(8 * (3 * mine + k), 8), 8), :]
            tail = source[pl.ds(main + 3 * mine + k, 1), :]
            own += [rows[:, :128], rows[:, 128:]]
            own8 += [tail[:, :128], tail[:, 128:]]
        for m in range(3):
            cols = slice(m * 128, (m + 1) * 128)
            target[0:8, cols] = jnp.where(core == 0, own[m], own[m + 3])
            target[8:9, cols] = jnp.where(core == 0, own8[m], own8[m + 3])


def point_kernel(
    n_grp, back_ref, jp_ref, pidx_ref, pb_ref, pd_ref, pu_ref, cb_ref, cd_ref, cs_ref,
    out_ref, ps_ref, pe_ref, sc_ref,
):
    slot = back_ref.shape[2] - 128
    index = pidx_ref[...]
    mask = is_row(index >> LO_BITS, PH)
    hot = one_hot_rows(index & (LO - 1), LO)
    jp = [jp_ref[k : k + 1, :] for k in range(6)]
    scalars = back_ref[0, :, slot:]
    for h in range(1, n_grp):
        scalars = scalars + back_ref[h, :, slot:]
    gamma, delta = scalars[0:1, 0:1], scalars[1:2, 0:1]
    alpha = gamma / delta
    w = [
        jnp.concatenate([back_ref[h, r : r + 1, 0:slot] for h in range(n_grp)], axis=1) for r in range(4)
    ]
    rhs, diag = pb_ref[...], pd_ref[...]
    z = rhs / diag
    error = [pu_ref[a : a + 1, :] + w[a] for a in range(2)]
    s = z + scatter_points(mask, hot, [jp[i] * error[0] + jp[3 + i] * error[1] for i in range(3)])
    r1 = rhs - alpha * s
    z1 = r1 / diag
    at = gather_points(mask, hot, z1)
    error = [
        sum(jp[3 * a + i] * at[i] for i in range(3)) + (w[a] - alpha * w[2 + a]) for a in range(2)
    ]
    ps_ref[...] = s
    pe_ref[0:1, :] = error[0]
    pe_ref[1:2, :] = error[1]
    cr1 = cb_ref[...] - alpha * cs_ref[...]
    cz1 = cr1 / cd_ref[...]
    gamma1 = total_of(r1 * z1) + total_of(cr1 * cz1)
    delta1 = (
        total_of(error[0] * error[0] + error[1] * error[1]) + total_of(z1 * z1) + total_of(cz1 * cz1)
    )
    sc_ref[...] = lanes(jnp.concatenate([gamma, alpha], axis=0), 128)
    tail = lanes(jnp.concatenate([gamma1, delta1], axis=0), 128)
    per = out_ref.shape[0] // n_grp
    for h in range(n_grp):
        cols = slice(h * slot, (h + 1) * slot)
        block = jnp.concatenate([jnp.concatenate([e[:, cols] for e in error], axis=0), tail], axis=1)

        @pl.loop(0, per)
        def _(tile, block=block, h=h):
            out_ref[h * per + tile] = block


def last_point_sums_kernel(jp_ref, pidx_ref, pe_ref, pt_ref):
    index = pidx_ref[...]
    mask = is_row(index >> LO_BITS, PH)
    hot = one_hot_rows(index & (LO - 1), LO)
    jp = [jp_ref[k : k + 1, :] for k in range(6)]
    error = [pe_ref[a : a + 1, :] for a in range(2)]
    pt_ref[...] = scatter_points(
        mask, hot, [jp[i] * error[0] + jp[3 + i] * error[1] for i in range(3)]
    )


def final_kernel(
    err_ref, a_ref, b_ref, pb_ref, pd_ref, ps_ref, pt_ref, cb_ref, cd_ref, cs_ref, sc_ref,
    px_ref, cx_ref, pr_ref, cr_ref, acc_ref,
):
    blocks, _, slot = a_ref.shape
    per = min(8, blocks)
    chunks = blocks // per
    tile = lax.axis_index("tile")
    core = tile % 2
    acc_ref[...] = jnp.zeros(acc_ref.shape, F32)

    def body(ref, parity):
        def step(chunk, scalars):
            numbers = chunk_of(chunk, per)
            x, index = read_blocks(ref, numbers)
            errs = [err_ref[2 * k + parity] for k in numbers]
            e = jnp.concatenate([v[:, 0:slot] for v in errs], axis=1)
            for v in errs:
                scalars = scalars + v[:, slot:]
            index = index - tile * CAM_DEV
            hi = index >> 7
            hot = one_hot_rows(index & 127, 128)
            j0, j1 = x[0:8], x[8:16]
            e0, e1 = e[0:1], e[1:2]
            acc_ref[...] += scatter_mixed(
                hi, hot, [j0 * e0 + j1 * e1], [x[16:17] * e0 + x[17:18] * e1], 4, 16
            )
            return scalars

        return step

    scalars = lax.fori_loop(0, chunks, body(a_ref, core), jnp.zeros((2, 128), F32))
    scalars = lax.fori_loop(0, chunks, body(b_ref, 1 - core), scalars)
    gamma1, delta1 = scalars[0:1, 0:1], scalars[1:2, 0:1]
    gamma, alpha = sc_ref[0:1, 0:1], sc_ref[1:2, 0:1]
    ratio = gamma1 / gamma
    alpha1 = gamma1 / (delta1 - ratio * gamma1 / alpha)

    rhs, diag, s = pb_ref[...], pd_ref[...], ps_ref[...]
    z = rhs / diag
    r1 = rhs - alpha * s
    z1 = r1 / diag
    x = alpha * z + alpha1 * (z1 + ratio * z)
    r2 = r1 - alpha1 * (z1 + pt_ref[...] + ratio * s)
    for i in range(3):
        for hi in range(PH):
            row = i * PH + hi
            px_ref[i : i + 1, hi * LO : (hi + 1) * LO] = x[row : row + 1]
            pr_ref[i : i + 1, hi * LO : (hi + 1) * LO] = r2[row : row + 1]

    rhs, s = cb_ref[...], cs_ref[...]
    z = rhs / cd_ref[...]
    r1 = rhs - alpha * s
    z1 = r1 / cd_ref[...]
    cx_ref[...] = alpha * z + alpha1 * (z1 + ratio * z)
    sums = both(acc_ref[...])
    base = r1 - alpha1 * (z1 + ratio * s)
    for k in range(3):
        cols = slice(k * 128, (k + 1) * 128)
        cr_ref[0:8, cols] = base[0:8, cols] - alpha1 * sums[8 * k : 8 * k + 8, :]
        cr_ref[8:9, cols] = base[8:9, cols] - alpha1 * sums[32 + k : 33 + k, :]


def shape(*dims):
    return jax.ShapeDtypeStruct(dims, F32)


def replicated(jac_point, jac_cam, resid, point_index, cam_index):
    n_grp, n_tile = lax.axis_size("grp"), lax.axis_size("tile")
    n_z = n_tile // 2
    obs = jac_point.shape[1]
    slot = obs // n_grp
    blocks = n_grp * n_z
    count = CAM_DEV * n_tile // LO
    tail_rows = -(-count // 16) * 16
    rows = 8 * count + tail_rows
    groups = [[d * 2 + core for d in range(blocks)] for core in range(2)]
    swap = [(t, t ^ 1) for t in range(n_tile)]
    pidx, cidx = point_index.reshape(1, obs), cam_index.reshape(1, obs)

    hbm = pl.BlockSpec(memory_space=pltpu.HBM)
    packed, pb, pd, pu, jp, pidx = pl.pallas_call(
        functools.partial(pack_kernel, n_grp, n_z),
        in_specs=[hbm] * 5,
        out_shape=(
            shape(blocks, 24, slot),
            shape(3 * PH, LO),
            shape(3 * PH, LO),
            shape(2, obs),
            shape(6, obs),
            jax.ShapeDtypeStruct((1, obs), jnp.int32),
        ),
        scratch_shapes=[
            pltpu.VMEM((18, obs), F32),
            pltpu.VMEM((2, obs), F32),
            pltpu.VMEM((1, obs), jnp.int32),
            pltpu.SemaphoreType.DMA((5,)),
        ],
        compiler_params=PARAMS,
        name="pack",
    )(*(pltpu.with_memory_space_constraint(x, pltpu.HBM) for x in (jac_point, jac_cam, resid, pidx, cidx)))
    own = lax.all_to_all(packed, ("grp", "tile"), 0, 0, axis_index_groups=groups, tiled=True)
    other = lax.ppermute(own, "tile", swap)
    sums = pl.pallas_call(
        functools.partial(own_sums_kernel, count, tail_rows),
        out_shape=shape(4 * rows, LO),
        compiler_params=PARAMS,
        name="own_sums",
        cost_estimate=pl.CostEstimate(flops=2 * 10**9, bytes_accessed=10**6, transcendentals=0),
    )(own)
    table = shape(rows, LO)
    back, tb, td, ts = pl.pallas_call(
        functools.partial(camera_kernel, n_grp, n_z, count, tail_rows),
        out_shape=(shape(n_grp, 4, slot + 128), table, table, table),
        scratch_shapes=[
            pltpu.VMEM((4 * rows, LO), F32),
            pltpu.VMEM((blocks, 2, slot), F32),
            pltpu.VMEM((2 * rows, LO), BF16),
        ],
        compiler_params=PARAMS,
        name="cameras",
    )(own, other, sums)
    back = lax.all_to_all(back, "grp", 0, 0, tiled=True)
    cb, cd, cs = pl.pallas_call(
        functools.partial(mine_kernel, 8 * count),
        out_shape=(shape(9, CAM_DEV),) * 3,
        compiler_params=PARAMS,
        name="mine",
    )(tb, td, ts)
    errors, ps, pe, sc = pl.pallas_call(
        functools.partial(point_kernel, n_grp),
        out_shape=(
            shape(n_grp * n_tile, 2, slot + 128),
            shape(3 * PH, LO),
            shape(2, obs),
            shape(2, 128),
        ),
        compiler_params=PARAMS,
        name="points",
    )(back, jp, pidx, pb, pd, pu, cb, cd, cs)
    errors = lax.all_to_all(errors, ("grp", "tile"), 0, 0, tiled=True)
    pt = pl.pallas_call(
        last_point_sums_kernel,
        out_shape=shape(3 * PH, LO),
        compiler_params=PARAMS,
        name="last_point_sums",
    )(jp, pidx, pe)
    return pl.pallas_call(
        final_kernel,
        out_shape=(shape(3, P_DEV), shape(9, CAM_DEV), shape(3, P_DEV), shape(9, CAM_DEV)),
        scratch_shapes=[pltpu.VMEM((96, 128), F32)],
        compiler_params=PARAMS,
        name="finish",
    )(errors, own, other, pb, pd, ps, pt, cb, cd, cs, sc)


def eights(row):
    return jnp.broadcast_to(row, (8, row.shape[1]))


def row_numbers(width):
    return lax.broadcasted_iota(jnp.int32, (16, width), 0)


def as_16_bit(numbers):
    return numbers.astype(F32).astype(BF16)


def masked_rows(parts, masks):
    none = jnp.zeros(parts[0].shape, BF16)
    return jnp.concatenate([jnp.where(m, p, none) for p in parts for m in masks], axis=0)


def low_lanes(rows):
    return lax.broadcasted_iota(jnp.int32, (rows, HALF), 1) < SLOTS


def swap_lanes(v):
    return pltpu.roll(v, SLOTS, 1)


def point_sums(pidx_ref, jp_ref, res_ref):
    index = pidx_ref[...]
    mask = is_row(index >> LO_BITS, PH)
    hot = one_hot_rows(index & (LO - 1), LO)
    jp = [jp_ref[k : k + 1, :] for k in range(6)]
    res = [res_ref[a : a + 1, :] for a in range(2)]
    grad = [-(jp[i] * res[0] + jp[3 + i] * res[1]) for i in range(3)]
    square = [jp[i] * jp[i] + jp[3 + i] * jp[3 + i] for i in range(3)]
    return scatter_points(mask, hot, grad + square), mask, hot, jp


def start_copies(pairs, sems):
    copies = [pltpu.make_async_copy(a, b, sems.at[k]) for k, (a, b) in enumerate(pairs)]
    for copy in copies:
        copy.start()
    for copy in copies:
        copy.wait()


def route_kernel(
    n_grp, n_tile, jp_hbm, jc_hbm, res_hbm, pidx_hbm, cidx_hbm,
    out_ref, pb_ref, pd_ref, pu_ref, jp_ref, pidx_ref, place_ref, sc_ref,
    jc_ref, res_ref, cidx_ref, sems,
):
    start_copies(
        (
            (pidx_hbm, pidx_ref),
            (jp_hbm, jp_ref),
            (res_hbm, res_ref),
            (jc_hbm, jc_ref),
            (cidx_hbm, cidx_ref),
        ),
        sems,
    )
    slot = cidx_ref.shape[1] // n_grp
    cams = cidx_ref[...]
    owner = ((cams >> 7) * 171) >> 9
    local = (cams - owner * CAM_DEV).astype(F32)
    mine = is_row(owner, n_tile)
    ones = jnp.where(mine, 1.0, 0.0)
    stack = jnp.concatenate([ones[:, h * slot : (h + 1) * slot] for h in range(n_grp)], axis=0)
    before = lax.broadcasted_iota(jnp.int32, (slot, slot), 0)
    before = before < lax.broadcasted_iota(jnp.int32, (slot, slot), 1)
    counts = dot_nn(stack.astype(BF16), jnp.where(before, 1.0, 0.0).astype(BF16))
    counts = jnp.concatenate([counts[h * n_tile : (h + 1) * n_tile] for h in range(n_grp)], axis=1)
    rank = jnp.sum(jnp.where(mine, counts, 0.0), axis=0, keepdims=True)
    place_ref[0:1, :] = owner
    place_ref[1:2, :] = rank.astype(jnp.int32)
    over = jnp.max(jnp.where(rank >= SLOTS, 1.0, 0.0), axis=1, keepdims=True)
    rank = rank.astype(jnp.int32)
    hots = [one_hot_rows(rank + a * SLOTS, HALF) for a in range(2)]
    rights = [
        jnp.concatenate([hot[:, h * slot : (h + 1) * slot] for hot in hots], axis=1) for h in range(n_grp)
    ]
    def route_block(h):
        cols = slice(h * slot, (h + 1) * slot)
        here = [sixteen(owner[:, cols]) == BF16(t) for t in range(n_tile)]
        left = []
        for a in range(2):
            rows = [
                jc_ref[9 * a : 9 * a + 8, cols],
                jc_ref[9 * a + 8 : 9 * a + 9, cols],
                res_ref[a : a + 1, cols],
                local[:, cols],
                jnp.zeros((5, slot), F32),
            ]
            left.append(masked_rows(two_parts(jnp.concatenate(rows, axis=0)), here))
        moved = both(dot_nt(jnp.concatenate(left, axis=1), rights[h]))
        for t in range(n_tile):
            for part in range(3):
                row = 16 * t + 4 * part
                out_ref[3 * (h * n_tile + t) + part] = moved[row : row + 4]

    table, mask, hot, jp = point_sums(pidx_ref, jp_ref, res_ref)
    for h in range(n_grp // 2):
        route_block(h)
    rhs, diag = table[: 3 * PH], table[3 * PH :] + DAMPING
    z = rhs / diag
    at = gather_points(mask, hot, z)
    for h in range(n_grp // 2, n_grp):
        route_block(h)
    pb_ref[...] = rhs
    pd_ref[...] = diag
    u = [sum(jp[3 * a + i] * at[i] for i in range(3)) for a in range(2)]
    pu_ref[0:1, :] = u[0]
    pu_ref[1:2, :] = u[1]
    sc_ref[...] = lanes(jnp.concatenate([total_of(rhs * z), total_of(z * z), over], axis=0), HALF)
    masks = [sixteen(owner) == as_16_bit(row_numbers(owner.shape[1]) + t) for t in range(0, n_tile, 16)]
    left = [masked_rows(two_parts(jnp.broadcast_to(u[a], (16, u[a].shape[1]))), masks) for a in range(2)]
    for h in range(n_grp):
        cols = slice(h * slot, (h + 1) * slot)
        moved = both(dot_nt(jnp.concatenate([v[:, cols] for v in left], axis=1), rights[h]))
        for t in range(n_tile):
            out_ref[3 * (h * n_tile + t) + 2, 3:4, :] = moved[t : t + 1]


def unfold(even, odd):
    low = low_lanes(even.shape[0])
    return jnp.where(low, even, swap_lanes(odd)), jnp.where(low, swap_lanes(even), odd)


def side_by_side(even, odd):
    return jnp.where(low_lanes(even.shape[0]), even, swap_lanes(odd))


def read_routed(ref, sources):
    main, rest = ([], []), ([], [])
    for s, t in zip(sources[::2], sources[1::2]):
        pair = unfold(*(jnp.concatenate([ref[3 * k], ref[3 * k + 1]], axis=0) for k in (s, t)))
        pair_rest = unfold(ref[3 * s + 2], ref[3 * t + 2])
        for a in range(2):
            main[a].append(pair[a])
            rest[a].append(pair_rest[a])
    main = [jnp.concatenate(v, axis=1) for v in main]
    rest = [jnp.concatenate(v, axis=1) for v in rest]
    index = rest[0][2:3].astype(jnp.int32)
    return main, rest, (index >> 7).astype(F32), one_hot_rows(index & 127, 128)


OWN_ROWS = 32
STEP = 32


def scatter_two(hi, hot, first, second):
    wide, numbers = sixteen(hi), row_numbers(hi.shape[1])
    blocks = [wide == BF16(k) for k in range(3)]
    tail = wide == as_16_bit(numbers & 7)
    rows = two_parts(jnp.concatenate([first[0], second[0]], axis=0))
    tails = two_parts(jnp.concatenate([eights(first[1]), eights(second[1])], axis=0))
    none = jnp.zeros(wide.shape, BF16)
    pieces = []
    for part in range(2):
        pieces += [jnp.where(mask, rows[part], none) for mask in blocks]
        pieces.append(jnp.where(tail, tails[part], none))
    return both(dot_nt(jnp.concatenate(pieces, axis=0), hot))


def scatter_one(hi, hot, main, tail):
    wide, numbers = sixteen(hi), row_numbers(hi.shape[1])
    upper = wide == as_16_bit(numbers >> 3)
    lower = wide == as_16_bit(jnp.where(numbers < 8, 2, numbers - 8))
    rows = two_parts(jnp.concatenate([main, main], axis=0))
    tails = two_parts(jnp.concatenate([main, eights(tail)], axis=0))
    none = jnp.zeros(wide.shape, BF16)
    pieces = []
    for part in range(2):
        pieces += [jnp.where(upper, rows[part], none), jnp.where(lower, tails[part], none)]
    return both(dot_nt(jnp.concatenate(pieces, axis=0), hot))


def gather_own(hi, hot, table, main, rest):
    found = both(dot_nn(table, hot))
    block = eights(hi)
    at = jnp.where(block == 0, found[0:8], jnp.where(block == 1, found[8:16], found[16:24]))
    numbers = lax.broadcasted_iota(jnp.int32, block.shape, 0).astype(F32)
    tail = jnp.where(block == numbers, found[24:32], 0.0)
    return [
        jnp.sum(main[a] * at + eights(rest[a][0:1]) * tail, axis=0, keepdims=True) for a in range(2)
    ]


def scatter_j(hi, hot, main, rest, e):
    return scatter_one(
        hi, hot, main[0] * e[0] + main[1] * e[1], rest[0][0:1] * e[0] + rest[1][0:1] * e[1]
    )


def owner_kernel(in_ref, sc_ref, back_ref, tb_ref, td_ref, ts_ref, acc_ref, zz_ref, w_ref, *kept):
    devices = back_ref.shape[0]
    per = min(STEP, devices)
    steps = devices // per

    if steps == 1:
        main, rest, hi, hot = read_routed(in_ref, range(devices))
        kept[0][...] = hot
        for a in range(2):
            kept[1][8 * a : 8 * a + 8, :] = main[a]
            kept[1][16 + a : 17 + a, :] = rest[a][0:1]
        kept[1][18:19, :] = hi

        def loop(body, start):
            return body((main, rest, hi, hot), 0, start)
    else:

        def loop(body, start):
            def step(number, carry):
                return body(read_routed(in_ref, chunk_of(number, per)), number, carry)

            return lax.fori_loop(0, steps, step, start)

    def rhs_and_diag(slots, number, carry):
        main, rest, hi, hot = slots
        r = [rest[a][1:2] for a in range(2)]
        rhs = (-(main[0] * r[0] + main[1] * r[1]), -(rest[0][0:1] * r[0] + rest[1][0:1] * r[1]))
        square = (
            main[0] * main[0] + main[1] * main[1],
            rest[0][0:1] * rest[0][0:1] + rest[1][0:1] * rest[1][0:1],
        )
        acc_ref[...] += scatter_two(hi, hot, rhs, square)
        return carry

    acc_ref[...] = jnp.zeros(acc_ref.shape, F32)
    loop(rhs_and_diag, 0)
    rhs = jnp.concatenate([acc_ref[16 * k : 16 * k + 8, :] for k in range(4)], axis=0)
    diag = jnp.concatenate([acc_ref[16 * k + 8 : 16 * k + 16, :] for k in range(4)], axis=0) + DAMPING
    tb_ref[...] = rhs
    td_ref[...] = diag
    z = rhs / diag
    zz_ref[...] = stacked(z)
    acc_ref[0:OWN_ROWS, :] = z

    def apply(slots, number, energy):
        main, rest, hi, hot = slots
        w = gather_own(hi, hot, zz_ref[...], main, rest)
        e = [rest[a][3:4] + w[a] for a in range(2)]
        for a in range(2):
            w_ref[number, a : a + 1, :] = w[a]
        acc_ref[0:OWN_ROWS, :] += scatter_j(hi, hot, main, rest, e)
        return energy + e[0] * e[0] + e[1] * e[1]

    energy = loop(apply, jnp.zeros((1, per * SLOTS), F32))
    s = acc_ref[0:OWN_ROWS, :]
    ts_ref[...] = s
    zz_ref[...] = stacked(s / diag)
    gamma = sc_ref[0:1, :] + total_of(rhs * z)
    delta = sc_ref[1:2, :] + total_of(z * z) + total_of(energy)
    tail = jnp.concatenate([gamma, delta, sc_ref[2:3, :], sc_ref[2:3, :]], axis=0)

    def send(slots, number, carry):
        main, rest, hi, hot = slots
        v = gather_own(hi, hot, zz_ref[...], main, rest)
        for a in range(2):
            w_ref[number, 2 + a : 3 + a, :] = v[a]
        w = w_ref[number]
        low = low_lanes(4)
        for k in range(per // 2):
            pair = w[:, k * HALF : (k + 1) * HALF]
            back_ref[number * per + 2 * k] = jnp.where(low, pair, tail)
            back_ref[number * per + 2 * k + 1] = jnp.where(low, swap_lanes(pair), tail)
        return carry

    loop(send, 0)


def routed_point_kernel(
    n_grp, n_tile, back_ref, jp_ref, pidx_ref, place_ref, pb_ref, pd_ref, pu_ref, cb_ref, cd_ref, cs_ref,
    out_ref, ps_ref, pe_ref, sc_ref, over_ref,
):
    slot = place_ref.shape[1] // n_grp
    index = pidx_ref[...]
    mask = is_row(index >> LO_BITS, PH)
    hot = one_hot_rows(index & (LO - 1), LO)
    jp = [jp_ref[k : k + 1, :] for k in range(6)]
    scalars = jnp.sum(back_ref[...], axis=0)[:, SLOTS : SLOTS + 1]
    gamma, delta = scalars[0:1], scalars[1:2]
    over_ref[...] = lanes(scalars[2:3], HALF)
    alpha = gamma / delta
    owner = place_ref[0:1, :]
    slots = one_hot_rows(place_ref[1:2, :], HALF)
    numbers = lax.broadcasted_iota(jnp.int32, (4 * n_tile, slot), 0) >> 2
    terms = []
    for h in range(n_grp):
        cols = slice(h * slot, (h + 1) * slot)
        rows = jnp.concatenate([back_ref[h * n_tile + t] for t in range(n_tile)], axis=0)
        found = both(dot_nn(stacked(rows), slots[:, cols]))
        found = jnp.where(numbers == owner[:, cols], found, 0.0)
        found = sum(found[8 * k : 8 * k + 8] for k in range(n_tile // 2))
        terms.append(found[0:4] + found[4:8])
    terms = jnp.concatenate(terms, axis=1)
    w0 = [terms[a : a + 1] for a in range(2)]
    w1 = [terms[2 + a : 3 + a] for a in range(2)]
    rhs, diag = pb_ref[...], pd_ref[...]
    z = rhs / diag
    error = [pu_ref[a : a + 1, :] + w0[a] for a in range(2)]
    s = z + scatter_points(mask, hot, [jp[i] * error[0] + jp[3 + i] * error[1] for i in range(3)])
    r1 = rhs - alpha * s
    z1 = r1 / diag
    at = gather_points(mask, hot, z1)
    error = [sum(jp[3 * a + i] * at[i] for i in range(3)) + (w0[a] - alpha * w1[a]) for a in range(2)]
    ps_ref[...] = s
    pe_ref[0:1, :] = error[0]
    pe_ref[1:2, :] = error[1]
    cr1 = cb_ref[...] - alpha * cs_ref[...]
    cz1 = cr1 / cd_ref[...]
    gamma1 = total_of(r1 * z1) + total_of(cr1 * cz1)
    delta1 = (
        total_of(error[0] * error[0] + error[1] * error[1]) + total_of(z1 * z1) + total_of(cz1 * cz1)
    )
    sc_ref[...] = lanes(jnp.concatenate([gamma, alpha], axis=0), HALF)
    tail = lanes(jnp.concatenate([gamma1, delta1], axis=0), HALF)
    low = low_lanes(2)
    numbers = row_numbers(slot)
    for h in range(n_grp):
        cols = slice(h * slot, (h + 1) * slot)
        first, second = (jnp.broadcast_to(e[:, cols], (16, slot)) for e in error)
        parts = two_parts(jnp.where((numbers & 1) == 0, first, second))
        wide = sixteen(owner[:, cols])
        here = [wide == as_16_bit((numbers >> 1) + t) for t in range(0, n_tile, 8)]
        moved = both(dot_nt(masked_rows(parts, here), slots[:, cols]))
        for t in range(n_tile):
            out_ref[h * n_tile + t] = jnp.where(low, moved[2 * t : 2 * t + 2], tail)


def point_results(alpha, alpha1, ratio, pb_ref, pd_ref, ps_ref, pt_ref, px_ref, pr_ref):
    rhs, diag, s = pb_ref[...], pd_ref[...], ps_ref[...]
    z = rhs / diag
    r1 = rhs - alpha * s
    z1 = r1 / diag
    x = alpha * z + alpha1 * (z1 + ratio * z)
    r2 = r1 - alpha1 * (z1 + pt_ref[...] + ratio * s)
    for i in range(3):
        for hi in range(PH):
            row = i * PH + hi
            px_ref[i : i + 1, hi * LO : (hi + 1) * LO] = x[row : row + 1]
            pr_ref[i : i + 1, hi * LO : (hi + 1) * LO] = r2[row : row + 1]


def routed_final_kernel(
    err_ref, in_ref, pb_ref, pd_ref, ps_ref, pt_ref, cb_ref, cd_ref, cs_ref, sc_ref, *rest_refs
):
    kept, (px_ref, cx_ref, pr_ref, cr_ref, acc_ref) = rest_refs[:-5], rest_refs[-5:]
    devices = err_ref.shape[0]
    per = min(STEP, devices)
    steps = devices // per

    def body(step, carry):
        sources = chunk_of(step, per)
        if kept:
            hot, rows = kept[0][...], kept[1]
            main = [rows[8 * a : 8 * a + 8, :] for a in range(2)]
            rest = [rows[16 + a : 17 + a, :] for a in range(2)]
            hi = rows[18:19, :]
        else:
            main, rest, hi, hot = read_routed(in_ref, sources)
        e = jnp.concatenate(
            [side_by_side(err_ref[s], err_ref[t]) for s, t in zip(sources[::2], sources[1::2])], axis=1
        )
        acc_ref[...] += scatter_j(hi, hot, main, rest, [e[0:1], e[1:2]])
        return carry

    acc_ref[...] = jnp.zeros(acc_ref.shape, F32)
    if steps == 1:
        body(0, 0)
    else:
        lax.fori_loop(0, steps, body, 0)
    scalars = jnp.sum(err_ref[...], axis=0)
    gamma1, delta1 = scalars[0:1, SLOTS : SLOTS + 1], scalars[1:2, SLOTS : SLOTS + 1]
    gamma, alpha = sc_ref[0:1, 0:1], sc_ref[1:2, 0:1]
    ratio = gamma1 / gamma
    alpha1 = gamma1 / (delta1 - ratio * gamma1 / alpha)
    point_results(alpha, alpha1, ratio, pb_ref, pd_ref, ps_ref, pt_ref, px_ref, pr_ref)
    rhs, s = cb_ref[...], cs_ref[...]
    z = rhs / cd_ref[...]
    r1 = rhs - alpha * s
    z1 = r1 / cd_ref[...]
    x = alpha * z + alpha1 * (z1 + ratio * z)
    r2 = r1 - alpha1 * (z1 + acc_ref[...] + ratio * s)
    for table, target in ((x, cx_ref), (r2, cr_ref)):
        for k in range(3):
            cols = slice(k * 128, (k + 1) * 128)
            target[0:8, cols] = table[8 * k : 8 * k + 8]
            target[8:9, cols] = table[24 + k : 25 + k]


def shards(jac_point, jac_cam, resid, point_index, cam_index):
    n_grp, n_tile = lax.axis_size("grp"), lax.axis_size("tile")
    devices = n_grp * n_tile
    obs = jac_point.shape[1]
    pidx, cidx = point_index.reshape(1, obs), cam_index.reshape(1, obs)
    hbm = pl.BlockSpec(memory_space=pltpu.HBM)
    ints = jax.ShapeDtypeStruct((1, obs), jnp.int32)
    places = jax.ShapeDtypeStruct((2, obs), jnp.int32)
    points = shape(3 * PH, LO)
    cameras = shape(OWN_ROWS, 128)
    routed, pb, pd, pu, jp, pidx_here, place, sc = pl.pallas_call(
        functools.partial(route_kernel, n_grp, n_tile),
        in_specs=[hbm] * 5,
        out_shape=(shape(3 * devices, 4, HALF), points, points, shape(2, obs), shape(6, obs), ints, places, shape(3, HALF)),
        scratch_shapes=[
            pltpu.VMEM((18, obs), F32),
            pltpu.VMEM((2, obs), F32),
            pltpu.VMEM((1, obs), jnp.int32),
            pltpu.SemaphoreType.DMA((5,)),
        ],
        compiler_params=PARAMS,
        name="route",
    )(*(pltpu.with_memory_space_constraint(x, pltpu.HBM) for x in (jac_point, jac_cam, resid, pidx, cidx)))
    routed = lax.all_to_all(routed, ("grp", "tile"), 0, 0, tiled=True)
    slots = devices * SLOTS
    per = min(STEP, devices)
    scratch = [
        pltpu.VMEM((2 * OWN_ROWS, 128), F32),
        pltpu.VMEM((2 * OWN_ROWS, 128), BF16),
        pltpu.VMEM((devices // per, 4, per * SLOTS), F32),
    ]
    kept_shapes = ()
    if devices == per:
        kept_shapes = (jax.ShapeDtypeStruct((128, slots), BF16), shape(24, slots))

    def owner(in_ref, sc_ref, back_ref, tb_ref, td_ref, ts_ref, *others):
        kept, work = others[: len(kept_shapes)], others[len(kept_shapes) :]
        owner_kernel(in_ref, sc_ref, back_ref, tb_ref, td_ref, ts_ref, *work, *kept)

    back, tb, td, ts, *kept = pl.pallas_call(
        owner,
        out_shape=(shape(devices, 4, HALF), cameras, cameras, cameras) + kept_shapes,
        scratch_shapes=scratch,
        compiler_params=PARAMS,
        name="owner",
    )(routed, sc)
    back = lax.all_to_all(back, ("grp", "tile"), 0, 0, tiled=True)
    errors, ps, pe, sc, over = pl.pallas_call(
        functools.partial(routed_point_kernel, n_grp, n_tile),
        out_shape=(shape(devices, 2, HALF), points, shape(2, obs), shape(2, HALF), shape(1, HALF)),
        compiler_params=PARAMS,
        name="points",
    )(back, jp, pidx_here, place, pb, pd, pu, tb, td, ts)
    errors = lax.all_to_all(errors, ("grp", "tile"), 0, 0, tiled=True)
    pt = pl.pallas_call(
        last_point_sums_kernel,
        out_shape=points,
        compiler_params=PARAMS,
        name="last_point_sums",
    )(jp, pidx_here, pe)
    outputs = (shape(3, P_DEV), shape(9, CAM_DEV), shape(3, P_DEV), shape(9, CAM_DEV))

    def fits(*operands):
        return pl.pallas_call(
            routed_final_kernel,
            out_shape=outputs,
            scratch_shapes=[pltpu.VMEM((OWN_ROWS, 128), F32)],
            compiler_params=PARAMS,
            name="finish",
        )(*operands[5:])

    def overflows(*operands):
        return tuple(replicated(*operands[:5]))

    return lax.cond(
        over[0, 0] > 0,
        overflows,
        lambda *operands: tuple(fits(*operands)),
        jac_point, jac_cam, resid, point_index, cam_index,
        errors, routed, pb, pd, ps, pt, tb, td, ts, sc, *kept,
    )


def solution(mesh):
    placed = (
        P(None, ("grp", "tile")),
        P(None, ("grp", "tile")),
        P(None, ("grp", "tile")),
        P(("grp", "tile")),
        P(("grp", "tile")),
    )
    return jax.shard_map(
        shards,
        mesh=mesh,
        in_specs=placed,
        out_specs=(P(None, ("grp", "tile")),) * 4,
        check_vma=False,
    )
```

```python
import functools

import jax
import jax.numpy as jnp
from jax import lax
from jax.experimental import pallas as pl
from jax.experimental.pallas import tpu as pltpu
from jax.sharding import PartitionSpec as P

P_DEV = 4096
CAM_DEV = 384
LO_BITS = 8
LO = 1 << LO_BITS
PH = P_DEV // LO
DAMPING = 1.0
F32 = jnp.float32
BF16 = jnp.bfloat16
SLOTS = 64
HALF = 128
PARAMS = pltpu.CompilerParams(vmem_limit_bytes=48 * 1024 * 1024)


def halves(v):
    high = v.astype(BF16).astype(F32)
    return high, v - high


def rows16(width, step=1):
    numbers = lax.broadcasted_iota(jnp.int32, (16, width), 0)
    return (numbers // step if step > 1 else numbers).astype(F32).astype(BF16)


def sixteen(row):
    return jnp.broadcast_to(row.astype(F32), (16, row.shape[1])).astype(BF16)


def one_hot_rows(index, rows):
    numbers = rows16(index.shape[1])
    pieces = []
    for base in range(0, rows, 256):
        wide = sixteen(index - base)
        one, none = jnp.ones(wide.shape, BF16), jnp.zeros(wide.shape, BF16)
        pieces += [
            jnp.where(wide == numbers + BF16(16 * k), one, none)
            for k in range(min(256, rows - base) // 16)
        ]
    return jnp.concatenate(pieces, axis=0)


def dot_nt(a, b):
    return lax.dot_general(a, b, (((1,), (1,)), ((), ())), preferred_element_type=F32)


def dot_nn(a, b):
    return lax.dot_general(a, b, (((1,), (0,)), ((), ())), preferred_element_type=F32)


def is_row(hi, rows):
    return lax.broadcasted_iota(jnp.int32, (rows, hi.shape[1]), 0) == hi


def spread_row(mask, row):
    return jnp.where(mask, jnp.broadcast_to(row, mask.shape), 0.0)


def two_parts(v):
    high = v.astype(BF16)
    return high, (v - high.astype(F32)).astype(BF16)


def scatter_mixed(hi, hot, mains, tails, count, tail_rows):
    wide = sixteen(hi)
    none = jnp.zeros(wide.shape, BF16)
    single = len(mains) == 1
    numbers = rows16(hi.shape[1], 8) if single else none
    main_parts = two_parts(jnp.concatenate(mains * 2 if single else mains, axis=0))
    tail_parts = [two_parts(jnp.broadcast_to(v, wide.shape)) for v in tails]
    here = [wide == numbers + BF16(k) for k in range(0, count, 2 if single else 1)]
    tail_here = [wide == rows16(hi.shape[1]) + BF16(k) for k in range(0, tail_rows, 16)]
    pieces = []
    for part in range(2):
        pieces += [jnp.where(mask, main_parts[part], none) for mask in here]
        pieces += [jnp.where(mask, v[part], none) for v in tail_parts for mask in tail_here]
    return dot_nt(jnp.concatenate(pieces, axis=0), hot)


def both(v):
    half = v.shape[0] // 2
    return v[:half] + v[half:]


def gather_mixed(hi, hot, table, count, tail_rows):
    found = dot_nn(table, hot)
    hi8 = jnp.broadcast_to(hi, (8, hi.shape[1]))
    main = jnp.zeros(hi8.shape, F32)
    half = found.shape[0] // 2
    for k in range(count):
        rows = slice(k * 8, k * 8 + 8)
        low = slice(half + k * 8, half + k * 8 + 8)
        main = main + jnp.where(hi8 == k, found[rows] + found[low], 0.0)
    tail = found[count * 8 : half] + found[half + count * 8 :]
    tail = jnp.sum(jnp.where(is_row(hi, tail_rows), tail, 0.0), axis=0, keepdims=True)
    return main, tail


def stacked(table):
    high, low = halves(table)
    return jnp.concatenate([high, low], axis=0).astype(BF16)


def scatter_points(mask, hot, rows):
    parts = [halves(v) for v in rows]
    lhs = jnp.concatenate([spread_row(mask, v[k]) for k in range(2) for v in parts], axis=0)
    return both(dot_nt(lhs.astype(BF16), hot))


def gather_points(mask, hot, table):
    found = both(dot_nn(stacked(table), hot))
    return [
        jnp.sum(jnp.where(mask, found[i * PH : (i + 1) * PH], 0.0), axis=0, keepdims=True)
        for i in range(found.shape[0] // PH)
    ]


def total_of(v):
    return jnp.sum(jnp.sum(v, axis=0, keepdims=True), axis=1, keepdims=True)


def lanes(v, width):
    return jnp.broadcast_to(v, (v.shape[0], width))


def pack_kernel(
    n_grp, n_z, jp_hbm, jc_hbm, res_hbm, pidx_hbm, cidx_hbm,
    out_ref, pb_ref, pd_ref, pu_ref, jp_ref, pidx_ref,
    jc_ref, res_ref, cidx_ref, sems,
):
    copies = [
        pltpu.make_async_copy(source, target, sems.at[k])
        for k, (source, target) in enumerate(
            (
                (pidx_hbm, pidx_ref),
                (jp_hbm, jp_ref),
                (res_hbm, res_ref),
                (jc_hbm, jc_ref),
                (cidx_hbm, cidx_ref),
            )
        )
    ]
    for copy in copies:
        copy.start()
    for copy in copies:
        copy.wait()
    slot = out_ref.shape[2]
    index = pidx_ref[...]
    mask = is_row(index >> LO_BITS, PH)
    hot = one_hot_rows(index & (LO - 1), LO)
    jp = [jp_ref[k : k + 1, :] for k in range(6)]
    res = [res_ref[a : a + 1, :] for a in range(2)]
    grad = [-(jp[i] * res[0] + jp[3 + i] * res[1]) for i in range(3)]
    square = [jp[i] * jp[i] + jp[3 + i] * jp[3 + i] for i in range(3)]
    table = scatter_points(mask, hot, grad + square)
    rhs = table[: 3 * PH]
    diag = table[3 * PH :] + DAMPING
    pb_ref[...] = rhs
    pd_ref[...] = diag
    z = rhs / diag
    at = gather_points(mask, hot, z)
    u = [sum(jp[3 * a + i] * at[i] for i in range(3)) for a in range(2)]
    pu_ref[0:1, :] = u[0]
    pu_ref[1:2, :] = u[1]
    gamma = total_of(rhs * z)
    norm = total_of(z * z)
    scalars = jnp.concatenate([lanes(gamma, slot // 2), lanes(norm, slot // 2)], axis=1)
    cams = cidx_ref[...].astype(F32)
    for h in range(n_grp):
        cols = slice(h * slot, (h + 1) * slot)
        block = jnp.concatenate(
            [
                jc_ref[0:8, cols],
                jc_ref[9:17, cols],
                jc_ref[8:9, cols],
                jc_ref[17:18, cols],
                res[0][:, cols],
                res[1][:, cols],
                u[0][:, cols],
                u[1][:, cols],
                cams[:, cols],
                scalars,
            ],
            axis=0,
        )

        @pl.loop(0, n_z)
        def _(z_to, block=block, h=h):
            out_ref[h * n_z + z_to] = block


def read_blocks(ref, numbers):
    x = jnp.concatenate([ref[k] for k in numbers], axis=1)
    return x, x[22:23].astype(jnp.int32)


def chunk_of(chunk, per):
    return [chunk * per + k for k in range(per)]


def first_sums(ref, acc_ref, per, count, tail_rows):
    def body(chunk, carry):
        x, index = read_blocks(ref, chunk_of(chunk, per))
        hi, hot = index >> LO_BITS, one_hot_rows(index & (LO - 1), LO)
        j0, j1 = x[0:8], x[8:16]
        j08, j18, r0, r1 = x[16:17], x[17:18], x[18:19], x[19:20]
        acc_ref[...] += scatter_mixed(
            hi,
            hot,
            [-(j0 * r0 + j1 * r1), j0 * j0 + j1 * j1],
            [-(j08 * r0 + j18 * r1), j08 * j08 + j18 * j18],
            count,
            tail_rows,
        )
        return carry

    lax.fori_loop(0, ref.shape[0] // per, body, 0)


def own_sums_kernel(count, tail_rows, a_ref, acc_ref):
    acc_ref[...] = jnp.zeros(acc_ref.shape, F32)
    first_sums(a_ref, acc_ref, min(16, a_ref.shape[0]), count, tail_rows)


def camera_kernel(
    n_grp, n_z, count, tail_rows, a_ref, b_ref, start_ref,
    back_ref, tb_ref, td_ref, ts_ref,
    acc_ref, w_ref, zz_ref,
):
    blocks, _, slot = a_ref.shape
    per = min(8, blocks)
    chunks = blocks // per
    acc_ref[...] = start_ref[...]
    first_sums(b_ref, acc_ref, min(16, blocks), count, tail_rows)
    scalars = jnp.zeros((1, slot), F32)
    for ref in (a_ref, b_ref):
        scalars = scalars + jnp.sum(ref[:, 23, :], axis=0, keepdims=True)
    main = 8 * count
    half = acc_ref.shape[0] // 2
    for k in range(count):
        row = 16 * k
        tb_ref[8 * k : 8 * k + 8, :] = acc_ref[row : row + 8, :] + acc_ref[half + row : half + row + 8, :]
        row = 16 * k + 8
        td_ref[8 * k : 8 * k + 8, :] = (
            acc_ref[row : row + 8, :] + acc_ref[half + row : half + row + 8, :] + DAMPING
        )
    tb_ref[main:, :] = (
        acc_ref[2 * main : 2 * main + tail_rows, :]
        + acc_ref[half + 2 * main : half + 2 * main + tail_rows, :]
    )
    td_ref[main:, :] = (
        acc_ref[2 * main + tail_rows : half, :] + acc_ref[half + 2 * main + tail_rows :, :] + DAMPING
    )
    z = tb_ref[...] / td_ref[...]
    gamma = total_of(tb_ref[...] * z)
    norm = total_of(z * z)
    zz_ref[...] = stacked(z)
    ts_ref[...] = z
    acc_ref[0:half, :] = jnp.zeros((half, LO), F32)

    def second(ref, keep):
        def body(chunk, energy):
            numbers = chunk_of(chunk, per)
            x, index = read_blocks(ref, numbers)
            hi, hot = index >> LO_BITS, one_hot_rows(index & (LO - 1), LO)
            j0, j1 = x[0:8], x[8:16]
            j08, j18, u0, u1 = x[16:17], x[17:18], x[20:21], x[21:22]
            at, at8 = gather_mixed(hi, hot, zz_ref[...], count, tail_rows)
            w0 = jnp.sum(j0 * at, axis=0, keepdims=True) + j08 * at8
            w1 = jnp.sum(j1 * at, axis=0, keepdims=True) + j18 * at8
            if keep:
                for k, number in enumerate(numbers):
                    cols = slice(k * slot, (k + 1) * slot)
                    w_ref[number, 0:1, :] = w0[:, cols]
                    w_ref[number, 1:2, :] = w1[:, cols]
            e0, e1 = u0 + w0, u1 + w1
            acc_ref[0:half, :] += scatter_mixed(
                hi, hot, [j0 * e0 + j1 * e1], [j08 * e0 + j18 * e1], count, tail_rows
            )
            return energy + e0 * e0 + e1 * e1

        return body

    energy = jnp.zeros((1, per * slot), F32)
    energy = lax.fori_loop(0, chunks, second(a_ref, True), energy)
    energy = lax.fori_loop(0, chunks, second(b_ref, False), energy)
    ts_ref[...] += both(acc_ref[0:half, :])
    zz_ref[...] = stacked(ts_ref[...] / td_ref[...])
    share = 1.0 / n_grp
    gamma = gamma + share * scalars[:, 0:1]
    delta = norm + total_of(energy) + share * scalars[:, slot // 2 : slot // 2 + 1]
    mine = lax.axis_index("tile") // 2
    numbers = [g * n_z + mine for g in range(n_grp)]
    per = min(4, n_grp)
    for first in range(0, n_grp, per):
        some = numbers[first : first + per]
        x, index = read_blocks(a_ref, some)
        hi, hot = index >> LO_BITS, one_hot_rows(index & (LO - 1), LO)
        at, at8 = gather_mixed(hi, hot, zz_ref[...], count, tail_rows)
        v0 = jnp.sum(x[0:8] * at, axis=0, keepdims=True) + x[16:17] * at8
        v1 = jnp.sum(x[8:16] * at, axis=0, keepdims=True) + x[17:18] * at8
        for k in range(per):
            cols = slice(k * slot, (k + 1) * slot)
            g = first + k
            back_ref[g, 0:2, 0:slot] = w_ref[some[k], 0:2, :]
            back_ref[g, 2:3, 0:slot] = v0[:, cols]
            back_ref[g, 3:4, 0:slot] = v1[:, cols]
            back_ref[g, :, slot:] = lanes(jnp.concatenate([gamma, delta, gamma, delta], axis=0), 128)


def mine_kernel(main, tb_ref, td_ref, ts_ref, cb_ref, cd_ref, cs_ref):
    tile = lax.axis_index("tile")
    mine, core = tile // 2, tile % 2
    for source, target in ((tb_ref, cb_ref), (td_ref, cd_ref), (ts_ref, cs_ref)):
        own, own8 = [], []
        for k in range(3):
            rows = source[pl.ds(pl.multiple_of(8 * (3 * mine + k), 8), 8), :]
            tail = source[pl.ds(main + 3 * mine + k, 1), :]
            own += [rows[:, :128], rows[:, 128:]]
            own8 += [tail[:, :128], tail[:, 128:]]
        for m in range(3):
            cols = slice(m * 128, (m + 1) * 128)
            target[0:8, cols] = jnp.where(core == 0, own[m], own[m + 3])
            target[8:9, cols] = jnp.where(core == 0, own8[m], own8[m + 3])


def point_kernel(
    n_grp, back_ref, jp_ref, pidx_ref, pb_ref, pd_ref, pu_ref, cb_ref, cd_ref, cs_ref,
    out_ref, ps_ref, pe_ref, sc_ref,
):
    slot = back_ref.shape[2] - 128
    index = pidx_ref[...]
    mask = is_row(index >> LO_BITS, PH)
    hot = one_hot_rows(index & (LO - 1), LO)
    jp = [jp_ref[k : k + 1, :] for k in range(6)]
    scalars = back_ref[0, :, slot:]
    for h in range(1, n_grp):
        scalars = scalars + back_ref[h, :, slot:]
    gamma, delta = scalars[0:1, 0:1], scalars[1:2, 0:1]
    alpha = gamma / delta
    w = [
        jnp.concatenate([back_ref[h, r : r + 1, 0:slot] for h in range(n_grp)], axis=1) for r in range(4)
    ]
    rhs, diag = pb_ref[...], pd_ref[...]
    z = rhs / diag
    error = [pu_ref[a : a + 1, :] + w[a] for a in range(2)]
    s = z + scatter_points(mask, hot, [jp[i] * error[0] + jp[3 + i] * error[1] for i in range(3)])
    r1 = rhs - alpha * s
    z1 = r1 / diag
    at = gather_points(mask, hot, z1)
    error = [
        sum(jp[3 * a + i] * at[i] for i in range(3)) + (w[a] - alpha * w[2 + a]) for a in range(2)
    ]
    ps_ref[...] = s
    pe_ref[0:1, :] = error[0]
    pe_ref[1:2, :] = error[1]
    cr1 = cb_ref[...] - alpha * cs_ref[...]
    cz1 = cr1 / cd_ref[...]
    gamma1 = total_of(r1 * z1) + total_of(cr1 * cz1)
    delta1 = (
        total_of(error[0] * error[0] + error[1] * error[1]) + total_of(z1 * z1) + total_of(cz1 * cz1)
    )
    sc_ref[...] = lanes(jnp.concatenate([gamma, alpha], axis=0), 128)
    tail = lanes(jnp.concatenate([gamma1, delta1], axis=0), 128)
    per = out_ref.shape[0] // n_grp
    for h in range(n_grp):
        cols = slice(h * slot, (h + 1) * slot)
        block = jnp.concatenate([jnp.concatenate([e[:, cols] for e in error], axis=0), tail], axis=1)

        @pl.loop(0, per)
        def _(tile, block=block, h=h):
            out_ref[h * per + tile] = block


def last_point_sums_kernel(jp_ref, pidx_ref, pe_ref, pt_ref):
    index = pidx_ref[...]
    mask = is_row(index >> LO_BITS, PH)
    hot = one_hot_rows(index & (LO - 1), LO)
    jp = [jp_ref[k : k + 1, :] for k in range(6)]
    error = [pe_ref[a : a + 1, :] for a in range(2)]
    pt_ref[...] = scatter_points(
        mask, hot, [jp[i] * error[0] + jp[3 + i] * error[1] for i in range(3)]
    )


def final_kernel(
    err_ref, a_ref, b_ref, pb_ref, pd_ref, ps_ref, pt_ref, cb_ref, cd_ref, cs_ref, sc_ref,
    px_ref, cx_ref, pr_ref, cr_ref, acc_ref,
):
    blocks, _, slot = a_ref.shape
    per = min(8, blocks)
    chunks = blocks // per
    tile = lax.axis_index("tile")
    core = tile % 2
    acc_ref[...] = jnp.zeros(acc_ref.shape, F32)

    def body(ref, parity):
        def step(chunk, scalars):
            numbers = chunk_of(chunk, per)
            x, index = read_blocks(ref, numbers)
            errs = [err_ref[2 * k + parity] for k in numbers]
            e = jnp.concatenate([v[:, 0:slot] for v in errs], axis=1)
            for v in errs:
                scalars = scalars + v[:, slot:]
            index = index - tile * CAM_DEV
            hi = index >> 7
            hot = one_hot_rows(index & 127, 128)
            j0, j1 = x[0:8], x[8:16]
            e0, e1 = e[0:1], e[1:2]
            acc_ref[...] += scatter_mixed(
                hi, hot, [j0 * e0 + j1 * e1], [x[16:17] * e0 + x[17:18] * e1], 4, 16
            )
            return scalars

        return step

    scalars = lax.fori_loop(0, chunks, body(a_ref, core), jnp.zeros((2, 128), F32))
    scalars = lax.fori_loop(0, chunks, body(b_ref, 1 - core), scalars)
    gamma1, delta1 = scalars[0:1, 0:1], scalars[1:2, 0:1]
    gamma, alpha = sc_ref[0:1, 0:1], sc_ref[1:2, 0:1]
    ratio = gamma1 / gamma
    alpha1 = gamma1 / (delta1 - ratio * gamma1 / alpha)

    rhs, diag, s = pb_ref[...], pd_ref[...], ps_ref[...]
    z = rhs / diag
    r1 = rhs - alpha * s
    z1 = r1 / diag
    x = alpha * z + alpha1 * (z1 + ratio * z)
    r2 = r1 - alpha1 * (z1 + pt_ref[...] + ratio * s)
    for i in range(3):
        for hi in range(PH):
            row = i * PH + hi
            px_ref[i : i + 1, hi * LO : (hi + 1) * LO] = x[row : row + 1]
            pr_ref[i : i + 1, hi * LO : (hi + 1) * LO] = r2[row : row + 1]

    rhs, s = cb_ref[...], cs_ref[...]
    z = rhs / cd_ref[...]
    r1 = rhs - alpha * s
    z1 = r1 / cd_ref[...]
    cx_ref[...] = alpha * z + alpha1 * (z1 + ratio * z)
    sums = both(acc_ref[...])
    base = r1 - alpha1 * (z1 + ratio * s)
    for k in range(3):
        cols = slice(k * 128, (k + 1) * 128)
        cr_ref[0:8, cols] = base[0:8, cols] - alpha1 * sums[8 * k : 8 * k + 8, :]
        cr_ref[8:9, cols] = base[8:9, cols] - alpha1 * sums[32 + k : 33 + k, :]


def shape(*dims):
    return jax.ShapeDtypeStruct(dims, F32)


def replicated(jac_point, jac_cam, resid, point_index, cam_index):
    n_grp, n_tile = lax.axis_size("grp"), lax.axis_size("tile")
    n_z = n_tile // 2
    obs = jac_point.shape[1]
    slot = obs // n_grp
    blocks = n_grp * n_z
    count = CAM_DEV * n_tile // LO
    tail_rows = -(-count // 16) * 16
    rows = 8 * count + tail_rows
    groups = [[d * 2 + core for d in range(blocks)] for core in range(2)]
    swap = [(t, t ^ 1) for t in range(n_tile)]
    pidx, cidx = point_index.reshape(1, obs), cam_index.reshape(1, obs)

    hbm = pl.BlockSpec(memory_space=pltpu.HBM)
    packed, pb, pd, pu, jp, pidx = pl.pallas_call(
        functools.partial(pack_kernel, n_grp, n_z),
        in_specs=[hbm] * 5,
        out_shape=(
            shape(blocks, 24, slot),
            shape(3 * PH, LO),
            shape(3 * PH, LO),
            shape(2, obs),
            shape(6, obs),
            jax.ShapeDtypeStruct((1, obs), jnp.int32),
        ),
        scratch_shapes=[
            pltpu.VMEM((18, obs), F32),
            pltpu.VMEM((2, obs), F32),
            pltpu.VMEM((1, obs), jnp.int32),
            pltpu.SemaphoreType.DMA((5,)),
        ],
        compiler_params=PARAMS,
        name="pack",
    )(*(pltpu.with_memory_space_constraint(x, pltpu.HBM) for x in (jac_point, jac_cam, resid, pidx, cidx)))
    own = lax.all_to_all(packed, ("grp", "tile"), 0, 0, axis_index_groups=groups, tiled=True)
    other = lax.ppermute(own, "tile", swap)
    sums = pl.pallas_call(
        functools.partial(own_sums_kernel, count, tail_rows),
        out_shape=shape(4 * rows, LO),
        compiler_params=PARAMS,
        name="own_sums",
        cost_estimate=pl.CostEstimate(flops=2 * 10**9, bytes_accessed=10**6, transcendentals=0),
    )(own)
    table = shape(rows, LO)
    back, tb, td, ts = pl.pallas_call(
        functools.partial(camera_kernel, n_grp, n_z, count, tail_rows),
        out_shape=(shape(n_grp, 4, slot + 128), table, table, table),
        scratch_shapes=[
            pltpu.VMEM((4 * rows, LO), F32),
            pltpu.VMEM((blocks, 2, slot), F32),
            pltpu.VMEM((2 * rows, LO), BF16),
        ],
        compiler_params=PARAMS,
        name="cameras",
    )(own, other, sums)
    back = lax.all_to_all(back, "grp", 0, 0, tiled=True)
    cb, cd, cs = pl.pallas_call(
        functools.partial(mine_kernel, 8 * count),
        out_shape=(shape(9, CAM_DEV),) * 3,
        compiler_params=PARAMS,
        name="mine",
    )(tb, td, ts)
    errors, ps, pe, sc = pl.pallas_call(
        functools.partial(point_kernel, n_grp),
        out_shape=(
            shape(n_grp * n_tile, 2, slot + 128),
            shape(3 * PH, LO),
            shape(2, obs),
            shape(2, 128),
        ),
        compiler_params=PARAMS,
        name="points",
    )(back, jp, pidx, pb, pd, pu, cb, cd, cs)
    errors = lax.all_to_all(errors, ("grp", "tile"), 0, 0, tiled=True)
    pt = pl.pallas_call(
        last_point_sums_kernel,
        out_shape=shape(3 * PH, LO),
        compiler_params=PARAMS,
        name="last_point_sums",
    )(jp, pidx, pe)
    return pl.pallas_call(
        final_kernel,
        out_shape=(shape(3, P_DEV), shape(9, CAM_DEV), shape(3, P_DEV), shape(9, CAM_DEV)),
        scratch_shapes=[pltpu.VMEM((96, 128), F32)],
        compiler_params=PARAMS,
        name="finish",
    )(errors, own, other, pb, pd, ps, pt, cb, cd, cs, sc)


def eights(row):
    return jnp.broadcast_to(row, (8, row.shape[1]))


def row_numbers(width):
    return lax.broadcasted_iota(jnp.int32, (16, width), 0)


def as_16_bit(numbers):
    return numbers.astype(F32).astype(BF16)


def masked_rows(parts, masks):
    none = jnp.zeros(parts[0].shape, BF16)
    return jnp.concatenate([jnp.where(m, p, none) for p in parts for m in masks], axis=0)


def low_lanes(rows):
    return lax.broadcasted_iota(jnp.int32, (rows, HALF), 1) < SLOTS


def swap_lanes(v):
    return pltpu.roll(v, SLOTS, 1)


def point_sums(pidx_ref, jp_ref, res_ref):
    index = pidx_ref[...]
    mask = is_row(index >> LO_BITS, PH)
    hot = one_hot_rows(index & (LO - 1), LO)
    jp = [jp_ref[k : k + 1, :] for k in range(6)]
    res = [res_ref[a : a + 1, :] for a in range(2)]
    grad = [-(jp[i] * res[0] + jp[3 + i] * res[1]) for i in range(3)]
    square = [jp[i] * jp[i] + jp[3 + i] * jp[3 + i] for i in range(3)]
    return scatter_points(mask, hot, grad + square), mask, hot, jp


def start_copies(pairs, sems):
    copies = [pltpu.make_async_copy(a, b, sems.at[k]) for k, (a, b) in enumerate(pairs)]
    for copy in copies:
        copy.start()
    for copy in copies:
        copy.wait()


def route_kernel(
    n_grp, n_tile, jp_hbm, jc_hbm, res_hbm, pidx_hbm, cidx_hbm,
    out_ref, pb_ref, pd_ref, pu_ref, jp_ref, pidx_ref, place_ref, sc_ref,
    jc_ref, res_ref, cidx_ref, sems,
):
    start_copies(
        (
            (pidx_hbm, pidx_ref),
            (jp_hbm, jp_ref),
            (res_hbm, res_ref),
            (jc_hbm, jc_ref),
            (cidx_hbm, cidx_ref),
        ),
        sems,
    )
    slot = cidx_ref.shape[1] // n_grp
    cams = cidx_ref[...]
    owner = ((cams >> 7) * 171) >> 9
    local = (cams - owner * CAM_DEV).astype(F32)
    mine = is_row(owner, n_tile)
    ones = jnp.where(mine, 1.0, 0.0)
    stack = jnp.concatenate([ones[:, h * slot : (h + 1) * slot] for h in range(n_grp)], axis=0)
    before = lax.broadcasted_iota(jnp.int32, (slot, slot), 0)
    before = before < lax.broadcasted_iota(jnp.int32, (slot, slot), 1)
    counts = dot_nn(stack.astype(BF16), jnp.where(before, 1.0, 0.0).astype(BF16))
    counts = jnp.concatenate([counts[h * n_tile : (h + 1) * n_tile] for h in range(n_grp)], axis=1)
    rank = jnp.sum(jnp.where(mine, counts, 0.0), axis=0, keepdims=True)
    place_ref[0:1, :] = owner
    place_ref[1:2, :] = rank.astype(jnp.int32)
    over = jnp.max(jnp.where(rank >= SLOTS, 1.0, 0.0), axis=1, keepdims=True)
    rank = rank.astype(jnp.int32)
    hots = [one_hot_rows(rank + a * SLOTS, HALF) for a in range(2)]
    rights = [
        jnp.concatenate([hot[:, h * slot : (h + 1) * slot] for hot in hots], axis=1) for h in range(n_grp)
    ]
    def route_block(h):
        cols = slice(h * slot, (h + 1) * slot)
        here = [sixteen(owner[:, cols]) == BF16(t) for t in range(n_tile)]
        left = []
        for a in range(2):
            rows = [
                jc_ref[9 * a : 9 * a + 8, cols],
                jc_ref[9 * a + 8 : 9 * a + 9, cols],
                res_ref[a : a + 1, cols],
                local[:, cols],
                jnp.zeros((5, slot), F32),
            ]
            left.append(masked_rows(two_parts(jnp.concatenate(rows, axis=0)), here))
        moved = both(dot_nt(jnp.concatenate(left, axis=1), rights[h]))
        for t in range(n_tile):
            for part in range(3):
                row = 16 * t + 4 * part
                out_ref[3 * (h * n_tile + t) + part] = moved[row : row + 4]

    table, mask, hot, jp = point_sums(pidx_ref, jp_ref, res_ref)
    for h in range(n_grp // 2):
        route_block(h)
    rhs, diag = table[: 3 * PH], table[3 * PH :] + DAMPING
    z = rhs / diag
    at = gather_points(mask, hot, z)
    for h in range(n_grp // 2, n_grp):
        route_block(h)
    pb_ref[...] = rhs
    pd_ref[...] = diag
    u = [sum(jp[3 * a + i] * at[i] for i in range(3)) for a in range(2)]
    pu_ref[0:1, :] = u[0]
    pu_ref[1:2, :] = u[1]
    sc_ref[...] = lanes(jnp.concatenate([total_of(rhs * z), total_of(z * z), over], axis=0), HALF)
    masks = [sixteen(owner) == as_16_bit(row_numbers(owner.shape[1]) + t) for t in range(0, n_tile, 16)]
    left = [masked_rows(two_parts(jnp.broadcast_to(u[a], (16, u[a].shape[1]))), masks) for a in range(2)]
    for h in range(n_grp):
        cols = slice(h * slot, (h + 1) * slot)
        moved = both(dot_nt(jnp.concatenate([v[:, cols] for v in left], axis=1), rights[h]))
        for t in range(n_tile):
            out_ref[3 * (h * n_tile + t) + 2, 3:4, :] = moved[t : t + 1]


def unfold(even, odd):
    low = low_lanes(even.shape[0])
    return jnp.where(low, even, swap_lanes(odd)), jnp.where(low, swap_lanes(even), odd)


def side_by_side(even, odd):
    return jnp.where(low_lanes(even.shape[0]), even, swap_lanes(odd))


def read_routed(ref, sources):
    main, rest = ([], []), ([], [])
    for s, t in zip(sources[::2], sources[1::2]):
        pair = unfold(*(jnp.concatenate([ref[3 * k], ref[3 * k + 1]], axis=0) for k in (s, t)))
        pair_rest = unfold(ref[3 * s + 2], ref[3 * t + 2])
        for a in range(2):
            main[a].append(pair[a])
            rest[a].append(pair_rest[a])
    main = [jnp.concatenate(v, axis=1) for v in main]
    rest = [jnp.concatenate(v, axis=1) for v in rest]
    index = rest[0][2:3].astype(jnp.int32)
    return main, rest, (index >> 7).astype(F32), one_hot_rows(index & 127, 128)


OWN_ROWS = 32
STEP = 32


def scatter_two(hi, hot, first, second):
    wide, numbers = sixteen(hi), row_numbers(hi.shape[1])
    blocks = [wide == BF16(k) for k in range(3)]
    tail = wide == as_16_bit(numbers & 7)
    rows = two_parts(jnp.concatenate([first[0], second[0]], axis=0))
    tails = two_parts(jnp.concatenate([eights(first[1]), eights(second[1])], axis=0))
    none = jnp.zeros(wide.shape, BF16)
    pieces = []
    for part in range(2):
        pieces += [jnp.where(mask, rows[part], none) for mask in blocks]
        pieces.append(jnp.where(tail, tails[part], none))
    return both(dot_nt(jnp.concatenate(pieces, axis=0), hot))


def scatter_one(hi, hot, main, tail):
    wide, numbers = sixteen(hi), row_numbers(hi.shape[1])
    upper = wide == as_16_bit(numbers >> 3)
    lower = wide == as_16_bit(jnp.where(numbers < 8, 2, numbers - 8))
    rows = two_parts(jnp.concatenate([main, main], axis=0))
    tails = two_parts(jnp.concatenate([main, eights(tail)], axis=0))
    none = jnp.zeros(wide.shape, BF16)
    pieces = []
    for part in range(2):
        pieces += [jnp.where(upper, rows[part], none), jnp.where(lower, tails[part], none)]
    return both(dot_nt(jnp.concatenate(pieces, axis=0), hot))


def gather_own(hi, hot, table, main, rest):
    found = both(dot_nn(table, hot))
    block = eights(hi)
    at = jnp.where(block == 0, found[0:8], jnp.where(block == 1, found[8:16], found[16:24]))
    numbers = lax.broadcasted_iota(jnp.int32, block.shape, 0).astype(F32)
    tail = jnp.where(block == numbers, found[24:32], 0.0)
    return [
        jnp.sum(main[a] * at + eights(rest[a][0:1]) * tail, axis=0, keepdims=True) for a in range(2)
    ]


def scatter_j(hi, hot, main, rest, e):
    return scatter_one(
        hi, hot, main[0] * e[0] + main[1] * e[1], rest[0][0:1] * e[0] + rest[1][0:1] * e[1]
    )


def owner_kernel(in_ref, sc_ref, back_ref, tb_ref, td_ref, ts_ref, acc_ref, zz_ref, w_ref, *kept):
    devices = back_ref.shape[0]
    per = min(STEP, devices)
    steps = devices // per

    if steps == 1:
        main, rest, hi, hot = read_routed(in_ref, range(devices))
        kept[0][...] = hot
        for a in range(2):
            kept[1][8 * a : 8 * a + 8, :] = main[a]
            kept[1][16 + a : 17 + a, :] = rest[a][0:1]
        kept[1][18:19, :] = hi

        def loop(body, start):
            return body((main, rest, hi, hot), 0, start)
    else:

        def loop(body, start):
            def step(number, carry):
                return body(read_routed(in_ref, chunk_of(number, per)), number, carry)

            return lax.fori_loop(0, steps, step, start)

    def rhs_and_diag(slots, number, carry):
        main, rest, hi, hot = slots
        r = [rest[a][1:2] for a in range(2)]
        rhs = (-(main[0] * r[0] + main[1] * r[1]), -(rest[0][0:1] * r[0] + rest[1][0:1] * r[1]))
        square = (
            main[0] * main[0] + main[1] * main[1],
            rest[0][0:1] * rest[0][0:1] + rest[1][0:1] * rest[1][0:1],
        )
        acc_ref[...] += scatter_two(hi, hot, rhs, square)
        return carry

    acc_ref[...] = jnp.zeros(acc_ref.shape, F32)
    loop(rhs_and_diag, 0)
    rhs = jnp.concatenate([acc_ref[16 * k : 16 * k + 8, :] for k in range(4)], axis=0)
    diag = jnp.concatenate([acc_ref[16 * k + 8 : 16 * k + 16, :] for k in range(4)], axis=0) + DAMPING
    tb_ref[...] = rhs
    td_ref[...] = diag
    z = rhs / diag
    zz_ref[...] = stacked(z)
    acc_ref[0:OWN_ROWS, :] = z

    def apply(slots, number, energy):
        main, rest, hi, hot = slots
        w = gather_own(hi, hot, zz_ref[...], main, rest)
        e = [rest[a][3:4] + w[a] for a in range(2)]
        for a in range(2):
            w_ref[number, a : a + 1, :] = w[a]
        acc_ref[0:OWN_ROWS, :] += scatter_j(hi, hot, main, rest, e)
        return energy + e[0] * e[0] + e[1] * e[1]

    energy = loop(apply, jnp.zeros((1, per * SLOTS), F32))
    s = acc_ref[0:OWN_ROWS, :]
    ts_ref[...] = s
    zz_ref[...] = stacked(s / diag)
    gamma = sc_ref[0:1, :] + total_of(rhs * z)
    delta = sc_ref[1:2, :] + total_of(z * z) + total_of(energy)
    tail = jnp.concatenate([gamma, delta, sc_ref[2:3, :], sc_ref[2:3, :]], axis=0)

    def send(slots, number, carry):
        main, rest, hi, hot = slots
        v = gather_own(hi, hot, zz_ref[...], main, rest)
        for a in range(2):
            w_ref[number, 2 + a : 3 + a, :] = v[a]
        w = w_ref[number]
        low = low_lanes(4)
        for k in range(per // 2):
            pair = w[:, k * HALF : (k + 1) * HALF]
            back_ref[number * per + 2 * k] = jnp.where(low, pair, tail)
            back_ref[number * per + 2 * k + 1] = jnp.where(low, swap_lanes(pair), tail)
        return carry

    loop(send, 0)


def routed_point_kernel(
    n_grp, n_tile, back_ref, jp_ref, pidx_ref, place_ref, pb_ref, pd_ref, pu_ref, cb_ref, cd_ref, cs_ref,
    out_ref, ps_ref, pe_ref, sc_ref, over_ref,
):
    slot = place_ref.shape[1] // n_grp
    index = pidx_ref[...]
    mask = is_row(index >> LO_BITS, PH)
    hot = one_hot_rows(index & (LO - 1), LO)
    jp = [jp_ref[k : k + 1, :] for k in range(6)]
    scalars = jnp.sum(back_ref[...], axis=0)[:, SLOTS : SLOTS + 1]
    gamma, delta = scalars[0:1], scalars[1:2]
    over_ref[...] = lanes(scalars[2:3], HALF)
    alpha = gamma / delta
    owner = place_ref[0:1, :]
    slots = one_hot_rows(place_ref[1:2, :], HALF)
    numbers = lax.broadcasted_iota(jnp.int32, (4 * n_tile, slot), 0) >> 2
    terms = []
    for h in range(n_grp):
        cols = slice(h * slot, (h + 1) * slot)
        rows = jnp.concatenate([back_ref[h * n_tile + t] for t in range(n_tile)], axis=0)
        found = both(dot_nn(stacked(rows), slots[:, cols]))
        found = jnp.where(numbers == owner[:, cols], found, 0.0)
        found = sum(found[8 * k : 8 * k + 8] for k in range(n_tile // 2))
        terms.append(found[0:4] + found[4:8])
    terms = jnp.concatenate(terms, axis=1)
    w0 = [terms[a : a + 1] for a in range(2)]
    w1 = [terms[2 + a : 3 + a] for a in range(2)]
    rhs, diag = pb_ref[...], pd_ref[...]
    z = rhs / diag
    error = [pu_ref[a : a + 1, :] + w0[a] for a in range(2)]
    s = z + scatter_points(mask, hot, [jp[i] * error[0] + jp[3 + i] * error[1] for i in range(3)])
    r1 = rhs - alpha * s
    z1 = r1 / diag
    at = gather_points(mask, hot, z1)
    error = [sum(jp[3 * a + i] * at[i] for i in range(3)) + (w0[a] - alpha * w1[a]) for a in range(2)]
    ps_ref[...] = s
    pe_ref[0:1, :] = error[0]
    pe_ref[1:2, :] = error[1]
    cr1 = cb_ref[...] - alpha * cs_ref[...]
    cz1 = cr1 / cd_ref[...]
    gamma1 = total_of(r1 * z1) + total_of(cr1 * cz1)
    delta1 = (
        total_of(error[0] * error[0] + error[1] * error[1]) + total_of(z1 * z1) + total_of(cz1 * cz1)
    )
    sc_ref[...] = lanes(jnp.concatenate([gamma, alpha], axis=0), HALF)
    tail = lanes(jnp.concatenate([gamma1, delta1], axis=0), HALF)
    low = low_lanes(2)
    numbers = row_numbers(slot)
    for h in range(n_grp):
        cols = slice(h * slot, (h + 1) * slot)
        first, second = (jnp.broadcast_to(e[:, cols], (16, slot)) for e in error)
        parts = two_parts(jnp.where((numbers & 1) == 0, first, second))
        wide = sixteen(owner[:, cols])
        here = [wide == as_16_bit((numbers >> 1) + t) for t in range(0, n_tile, 8)]
        moved = both(dot_nt(masked_rows(parts, here), slots[:, cols]))
        for t in range(n_tile):
            out_ref[h * n_tile + t] = jnp.where(low, moved[2 * t : 2 * t + 2], tail)


def point_results(alpha, alpha1, ratio, pb_ref, pd_ref, ps_ref, pt_ref, px_ref, pr_ref):
    rhs, diag, s = pb_ref[...], pd_ref[...], ps_ref[...]
    z = rhs / diag
    r1 = rhs - alpha * s
    z1 = r1 / diag
    x = alpha * z + alpha1 * (z1 + ratio * z)
    r2 = r1 - alpha1 * (z1 + pt_ref[...] + ratio * s)
    for i in range(3):
        for hi in range(PH):
            row = i * PH + hi
            px_ref[i : i + 1, hi * LO : (hi + 1) * LO] = x[row : row + 1]
            pr_ref[i : i + 1, hi * LO : (hi + 1) * LO] = r2[row : row + 1]


def routed_final_kernel(
    err_ref, in_ref, jp_ref, pidx_ref, pe_ref, pb_ref, pd_ref, ps_ref, cb_ref, cd_ref, cs_ref, sc_ref, *rest_refs
):
    kept, outs, (px_ref, cx_ref, pr_ref, cr_ref, acc_ref, pt_ref, sems) = (
        rest_refs[:-11],
        rest_refs[-11:-7],
        rest_refs[-7:],
    )
    devices = err_ref.shape[0]
    per = min(STEP, devices)
    steps = devices // per

    def body(step, carry):
        sources = chunk_of(step, per)
        if kept:
            hot, rows = kept[0][...], kept[1]
            main = [rows[8 * a : 8 * a + 8, :] for a in range(2)]
            rest = [rows[16 + a : 17 + a, :] for a in range(2)]
            hi = rows[18:19, :]
        else:
            main, rest, hi, hot = read_routed(in_ref, sources)
        e = jnp.concatenate(
            [side_by_side(err_ref[s], err_ref[t]) for s, t in zip(sources[::2], sources[1::2])], axis=1
        )
        acc_ref[...] += scatter_j(hi, hot, main, rest, [e[0:1], e[1:2]])
        return carry

    acc_ref[...] = jnp.zeros(acc_ref.shape, F32)
    if steps == 1:
        body(0, 0)
    else:
        lax.fori_loop(0, steps, body, 0)
    last_point_sums_kernel(jp_ref, pidx_ref, pe_ref, pt_ref)
    scalars = jnp.sum(err_ref[...], axis=0)
    gamma1, delta1 = scalars[0:1, SLOTS : SLOTS + 1], scalars[1:2, SLOTS : SLOTS + 1]
    gamma, alpha = sc_ref[0:1, 0:1], sc_ref[1:2, 0:1]
    ratio = gamma1 / gamma
    alpha1 = gamma1 / (delta1 - ratio * gamma1 / alpha)
    point_results(alpha, alpha1, ratio, pb_ref, pd_ref, ps_ref, pt_ref, px_ref, pr_ref)
    copies = [
        pltpu.make_async_copy(here, there, sems.at[k])
        for k, (here, there) in enumerate(zip((px_ref, cx_ref, pr_ref, cr_ref), outs))
    ]
    copies[0].start()
    copies[2].start()
    rhs, s = cb_ref[...], cs_ref[...]
    z = rhs / cd_ref[...]
    r1 = rhs - alpha * s
    z1 = r1 / cd_ref[...]
    x = alpha * z + alpha1 * (z1 + ratio * z)
    r2 = r1 - alpha1 * (z1 + acc_ref[...] + ratio * s)
    for table, target in ((x, cx_ref), (r2, cr_ref)):
        for k in range(3):
            cols = slice(k * 128, (k + 1) * 128)
            target[0:8, cols] = table[8 * k : 8 * k + 8]
            target[8:9, cols] = table[24 + k : 25 + k]
    copies[1].start()
    copies[3].start()
    for copy in copies:
        copy.wait()


def shards(jac_point, jac_cam, resid, point_index, cam_index):
    n_grp, n_tile = lax.axis_size("grp"), lax.axis_size("tile")
    devices = n_grp * n_tile
    obs = jac_point.shape[1]
    pidx, cidx = point_index.reshape(1, obs), cam_index.reshape(1, obs)
    hbm = pl.BlockSpec(memory_space=pltpu.HBM)
    ints = jax.ShapeDtypeStruct((1, obs), jnp.int32)
    places = jax.ShapeDtypeStruct((2, obs), jnp.int32)
    points = shape(3 * PH, LO)
    cameras = shape(OWN_ROWS, 128)
    routed, pb, pd, pu, jp, pidx_here, place, sc = pl.pallas_call(
        functools.partial(route_kernel, n_grp, n_tile),
        in_specs=[hbm] * 5,
        out_shape=(shape(3 * devices, 4, HALF), points, points, shape(2, obs), shape(6, obs), ints, places, shape(3, HALF)),
        scratch_shapes=[
            pltpu.VMEM((18, obs), F32),
            pltpu.VMEM((2, obs), F32),
            pltpu.VMEM((1, obs), jnp.int32),
            pltpu.SemaphoreType.DMA((5,)),
        ],
        compiler_params=PARAMS,
        name="route",
    )(*(pltpu.with_memory_space_constraint(x, pltpu.HBM) for x in (jac_point, jac_cam, resid, pidx, cidx)))
    routed = lax.all_to_all(routed, ("grp", "tile"), 0, 0, tiled=True)
    slots = devices * SLOTS
    per = min(STEP, devices)
    scratch = [
        pltpu.VMEM((2 * OWN_ROWS, 128), F32),
        pltpu.VMEM((2 * OWN_ROWS, 128), BF16),
        pltpu.VMEM((devices // per, 4, per * SLOTS), F32),
    ]
    kept_shapes = ()
    if devices == per:
        kept_shapes = (jax.ShapeDtypeStruct((128, slots), BF16), shape(24, slots))

    def owner(in_ref, sc_ref, back_ref, tb_ref, td_ref, ts_ref, *others):
        kept, work = others[: len(kept_shapes)], others[len(kept_shapes) :]
        owner_kernel(in_ref, sc_ref, back_ref, tb_ref, td_ref, ts_ref, *work, *kept)

    back, tb, td, ts, *kept = pl.pallas_call(
        owner,
        out_shape=(shape(devices, 4, HALF), cameras, cameras, cameras) + kept_shapes,
        scratch_shapes=scratch,
        compiler_params=PARAMS,
        name="owner",
    )(routed, sc)
    back = lax.all_to_all(back, ("grp", "tile"), 0, 0, tiled=True)
    errors, ps, pe, sc, over = pl.pallas_call(
        functools.partial(routed_point_kernel, n_grp, n_tile),
        out_shape=(shape(devices, 2, HALF), points, shape(2, obs), shape(2, HALF), shape(1, HALF)),
        compiler_params=PARAMS,
        name="points",
    )(back, jp, pidx_here, place, pb, pd, pu, tb, td, ts)
    outputs = (shape(3, P_DEV), shape(9, CAM_DEV), shape(3, P_DEV), shape(9, CAM_DEV))

    def fits(*operands):
        errors = lax.all_to_all(operands[5], ("grp", "tile"), 0, 0, tiled=True)
        return pl.pallas_call(
            routed_final_kernel,
            out_shape=outputs,
            out_specs=[hbm] * 4,
            scratch_shapes=[pltpu.VMEM(v.shape, F32) for v in outputs]
            + [
                pltpu.VMEM((OWN_ROWS, 128), F32),
                pltpu.VMEM((3 * PH, LO), F32),
                pltpu.SemaphoreType.DMA((4,)),
            ],
            compiler_params=PARAMS,
            name="finish",
        )(errors, *operands[6:])

    def overflows(*operands):
        return tuple(replicated(*operands[:5]))

    return lax.cond(
        over[0, 0] > 0,
        overflows,
        lambda *operands: tuple(fits(*operands)),
        jac_point, jac_cam, resid, point_index, cam_index,
        errors, routed, jp, pidx_here, pe, pb, pd, ps, tb, td, ts, sc, *kept,
    )


def solution(mesh):
    placed = (
        P(None, ("grp", "tile")),
        P(None, ("grp", "tile")),
        P(None, ("grp", "tile")),
        P(("grp", "tile")),
        P(("grp", "tile")),
    )
    return jax.shard_map(
        shards,
        mesh=mesh,
        in_specs=placed,
        out_specs=(P(None, ("grp", "tile")),) * 4,
        check_vma=False,
    )
```

```python
import functools

import jax
import jax.numpy as jnp
from jax import lax
from jax.experimental import pallas as pl
from jax.experimental.pallas import tpu as pltpu
from jax.sharding import PartitionSpec as P

P_DEV = 4096
CAM_DEV = 384
LO_BITS = 8
LO = 1 << LO_BITS
PH = P_DEV // LO
DAMPING = 1.0
F32 = jnp.float32
BF16 = jnp.bfloat16
SLOTS = 64
HALF = 128
PARAMS = pltpu.CompilerParams(vmem_limit_bytes=48 * 1024 * 1024)


def halves(v):
    high = v.astype(BF16).astype(F32)
    return high, v - high


def rows16(width, step=1):
    numbers = lax.broadcasted_iota(jnp.int32, (16, width), 0)
    return (numbers // step if step > 1 else numbers).astype(F32).astype(BF16)


def sixteen(row):
    return jnp.broadcast_to(row.astype(F32), (16, row.shape[1])).astype(BF16)


def one_hot_rows(index, rows):
    numbers = rows16(index.shape[1])
    pieces = []
    for base in range(0, rows, 256):
        wide = sixteen(index - base)
        one, none = jnp.ones(wide.shape, BF16), jnp.zeros(wide.shape, BF16)
        pieces += [
            jnp.where(wide == numbers + BF16(16 * k), one, none)
            for k in range(min(256, rows - base) // 16)
        ]
    return jnp.concatenate(pieces, axis=0)


def dot_nt(a, b):
    return lax.dot_general(a, b, (((1,), (1,)), ((), ())), preferred_element_type=F32)


def dot_nn(a, b):
    return lax.dot_general(a, b, (((1,), (0,)), ((), ())), preferred_element_type=F32)


def is_row(hi, rows):
    return lax.broadcasted_iota(jnp.int32, (rows, hi.shape[1]), 0) == hi


def spread_row(mask, row):
    return jnp.where(mask, jnp.broadcast_to(row, mask.shape), 0.0)


def two_parts(v):
    high = v.astype(BF16)
    return high, (v - high.astype(F32)).astype(BF16)


def scatter_mixed(hi, hot, mains, tails, count, tail_rows):
    wide = sixteen(hi)
    none = jnp.zeros(wide.shape, BF16)
    single = len(mains) == 1
    numbers = rows16(hi.shape[1], 8) if single else none
    main_parts = two_parts(jnp.concatenate(mains * 2 if single else mains, axis=0))
    tail_parts = [two_parts(jnp.broadcast_to(v, wide.shape)) for v in tails]
    here = [wide == numbers + BF16(k) for k in range(0, count, 2 if single else 1)]
    tail_here = [wide == rows16(hi.shape[1]) + BF16(k) for k in range(0, tail_rows, 16)]
    pieces = []
    for part in range(2):
        pieces += [jnp.where(mask, main_parts[part], none) for mask in here]
        pieces += [jnp.where(mask, v[part], none) for v in tail_parts for mask in tail_here]
    return dot_nt(jnp.concatenate(pieces, axis=0), hot)


def both(v):
    half = v.shape[0] // 2
    return v[:half] + v[half:]


def gather_mixed(hi, hot, table, count, tail_rows):
    found = dot_nn(table, hot)
    hi8 = jnp.broadcast_to(hi, (8, hi.shape[1]))
    main = jnp.zeros(hi8.shape, F32)
    half = found.shape[0] // 2
    for k in range(count):
        rows = slice(k * 8, k * 8 + 8)
        low = slice(half + k * 8, half + k * 8 + 8)
        main = main + jnp.where(hi8 == k, found[rows] + found[low], 0.0)
    tail = found[count * 8 : half] + found[half + count * 8 :]
    tail = jnp.sum(jnp.where(is_row(hi, tail_rows), tail, 0.0), axis=0, keepdims=True)
    return main, tail


def stacked(table):
    high, low = halves(table)
    return jnp.concatenate([high, low], axis=0).astype(BF16)


def scatter_points(mask, hot, rows):
    parts = [halves(v) for v in rows]
    lhs = jnp.concatenate([spread_row(mask, v[k]) for k in range(2) for v in parts], axis=0)
    return both(dot_nt(lhs.astype(BF16), hot))


def gather_points(mask, hot, table):
    found = both(dot_nn(stacked(table), hot))
    return [
        jnp.sum(jnp.where(mask, found[i * PH : (i + 1) * PH], 0.0), axis=0, keepdims=True)
        for i in range(found.shape[0] // PH)
    ]


def total_of(v):
    return jnp.sum(jnp.sum(v, axis=0, keepdims=True), axis=1, keepdims=True)


def lanes(v, width):
    return jnp.broadcast_to(v, (v.shape[0], width))


def pack_kernel(
    n_grp, n_z, jp_hbm, jc_hbm, res_hbm, pidx_hbm, cidx_hbm,
    out_ref, pb_ref, pd_ref, pu_ref, jp_ref, pidx_ref,
    jc_ref, res_ref, cidx_ref, sems,
):
    copies = [
        pltpu.make_async_copy(source, target, sems.at[k])
        for k, (source, target) in enumerate(
            (
                (pidx_hbm, pidx_ref),
                (jp_hbm, jp_ref),
                (res_hbm, res_ref),
                (jc_hbm, jc_ref),
                (cidx_hbm, cidx_ref),
            )
        )
    ]
    for copy in copies:
        copy.start()
    for copy in copies:
        copy.wait()
    slot = out_ref.shape[2]
    index = pidx_ref[...]
    mask = is_row(index >> LO_BITS, PH)
    hot = one_hot_rows(index & (LO - 1), LO)
    jp = [jp_ref[k : k + 1, :] for k in range(6)]
    res = [res_ref[a : a + 1, :] for a in range(2)]
    grad = [-(jp[i] * res[0] + jp[3 + i] * res[1]) for i in range(3)]
    square = [jp[i] * jp[i] + jp[3 + i] * jp[3 + i] for i in range(3)]
    table = scatter_points(mask, hot, grad + square)
    rhs = table[: 3 * PH]
    diag = table[3 * PH :] + DAMPING
    pb_ref[...] = rhs
    pd_ref[...] = diag
    z = rhs / diag
    at = gather_points(mask, hot, z)
    u = [sum(jp[3 * a + i] * at[i] for i in range(3)) for a in range(2)]
    pu_ref[0:1, :] = u[0]
    pu_ref[1:2, :] = u[1]
    gamma = total_of(rhs * z)
    norm = total_of(z * z)
    scalars = jnp.concatenate([lanes(gamma, slot // 2), lanes(norm, slot // 2)], axis=1)
    cams = cidx_ref[...].astype(F32)
    for h in range(n_grp):
        cols = slice(h * slot, (h + 1) * slot)
        block = jnp.concatenate(
            [
                jc_ref[0:8, cols],
                jc_ref[9:17, cols],
                jc_ref[8:9, cols],
                jc_ref[17:18, cols],
                res[0][:, cols],
                res[1][:, cols],
                u[0][:, cols],
                u[1][:, cols],
                cams[:, cols],
                scalars,
            ],
            axis=0,
        )

        @pl.loop(0, n_z)
        def _(z_to, block=block, h=h):
            out_ref[h * n_z + z_to] = block


def read_blocks(ref, numbers):
    x = jnp.concatenate([ref[k] for k in numbers], axis=1)
    return x, x[22:23].astype(jnp.int32)


def chunk_of(chunk, per):
    return [chunk * per + k for k in range(per)]


def first_sums(ref, acc_ref, per, count, tail_rows):
    def body(chunk, carry):
        x, index = read_blocks(ref, chunk_of(chunk, per))
        hi, hot = index >> LO_BITS, one_hot_rows(index & (LO - 1), LO)
        j0, j1 = x[0:8], x[8:16]
        j08, j18, r0, r1 = x[16:17], x[17:18], x[18:19], x[19:20]
        acc_ref[...] += scatter_mixed(
            hi,
            hot,
            [-(j0 * r0 + j1 * r1), j0 * j0 + j1 * j1],
            [-(j08 * r0 + j18 * r1), j08 * j08 + j18 * j18],
            count,
            tail_rows,
        )
        return carry

    lax.fori_loop(0, ref.shape[0] // per, body, 0)


def own_sums_kernel(count, tail_rows, a_ref, acc_ref):
    acc_ref[...] = jnp.zeros(acc_ref.shape, F32)
    first_sums(a_ref, acc_ref, min(16, a_ref.shape[0]), count, tail_rows)


def camera_kernel(
    n_grp, n_z, count, tail_rows, a_ref, b_ref, start_ref,
    back_ref, tb_ref, td_ref, ts_ref,
    acc_ref, w_ref, zz_ref,
):
    blocks, _, slot = a_ref.shape
    per = min(8, blocks)
    chunks = blocks // per
    acc_ref[...] = start_ref[...]
    first_sums(b_ref, acc_ref, min(16, blocks), count, tail_rows)
    scalars = jnp.zeros((1, slot), F32)
    for ref in (a_ref, b_ref):
        scalars = scalars + jnp.sum(ref[:, 23, :], axis=0, keepdims=True)
    main = 8 * count
    half = acc_ref.shape[0] // 2
    for k in range(count):
        row = 16 * k
        tb_ref[8 * k : 8 * k + 8, :] = acc_ref[row : row + 8, :] + acc_ref[half + row : half + row + 8, :]
        row = 16 * k + 8
        td_ref[8 * k : 8 * k + 8, :] = (
            acc_ref[row : row + 8, :] + acc_ref[half + row : half + row + 8, :] + DAMPING
        )
    tb_ref[main:, :] = (
        acc_ref[2 * main : 2 * main + tail_rows, :]
        + acc_ref[half + 2 * main : half + 2 * main + tail_rows, :]
    )
    td_ref[main:, :] = (
        acc_ref[2 * main + tail_rows : half, :] + acc_ref[half + 2 * main + tail_rows :, :] + DAMPING
    )
    z = tb_ref[...] / td_ref[...]
    gamma = total_of(tb_ref[...] * z)
    norm = total_of(z * z)
    zz_ref[...] = stacked(z)
    ts_ref[...] = z
    acc_ref[0:half, :] = jnp.zeros((half, LO), F32)

    def second(ref, keep):
        def body(chunk, energy):
            numbers = chunk_of(chunk, per)
            x, index = read_blocks(ref, numbers)
            hi, hot = index >> LO_BITS, one_hot_rows(index & (LO - 1), LO)
            j0, j1 = x[0:8], x[8:16]
            j08, j18, u0, u1 = x[16:17], x[17:18], x[20:21], x[21:22]
            at, at8 = gather_mixed(hi, hot, zz_ref[...], count, tail_rows)
            w0 = jnp.sum(j0 * at, axis=0, keepdims=True) + j08 * at8
            w1 = jnp.sum(j1 * at, axis=0, keepdims=True) + j18 * at8
            if keep:
                for k, number in enumerate(numbers):
                    cols = slice(k * slot, (k + 1) * slot)
                    w_ref[number, 0:1, :] = w0[:, cols]
                    w_ref[number, 1:2, :] = w1[:, cols]
            e0, e1 = u0 + w0, u1 + w1
            acc_ref[0:half, :] += scatter_mixed(
                hi, hot, [j0 * e0 + j1 * e1], [j08 * e0 + j18 * e1], count, tail_rows
            )
            return energy + e0 * e0 + e1 * e1

        return body

    energy = jnp.zeros((1, per * slot), F32)
    energy = lax.fori_loop(0, chunks, second(a_ref, True), energy)
    energy = lax.fori_loop(0, chunks, second(b_ref, False), energy)
    ts_ref[...] += both(acc_ref[0:half, :])
    zz_ref[...] = stacked(ts_ref[...] / td_ref[...])
    share = 1.0 / n_grp
    gamma = gamma + share * scalars[:, 0:1]
    delta = norm + total_of(energy) + share * scalars[:, slot // 2 : slot // 2 + 1]
    mine = lax.axis_index("tile") // 2
    numbers = [g * n_z + mine for g in range(n_grp)]
    per = min(4, n_grp)
    for first in range(0, n_grp, per):
        some = numbers[first : first + per]
        x, index = read_blocks(a_ref, some)
        hi, hot = index >> LO_BITS, one_hot_rows(index & (LO - 1), LO)
        at, at8 = gather_mixed(hi, hot, zz_ref[...], count, tail_rows)
        v0 = jnp.sum(x[0:8] * at, axis=0, keepdims=True) + x[16:17] * at8
        v1 = jnp.sum(x[8:16] * at, axis=0, keepdims=True) + x[17:18] * at8
        for k in range(per):
            cols = slice(k * slot, (k + 1) * slot)
            g = first + k
            back_ref[g, 0:2, 0:slot] = w_ref[some[k], 0:2, :]
            back_ref[g, 2:3, 0:slot] = v0[:, cols]
            back_ref[g, 3:4, 0:slot] = v1[:, cols]
            back_ref[g, :, slot:] = lanes(jnp.concatenate([gamma, delta, gamma, delta], axis=0), 128)


def mine_kernel(main, tb_ref, td_ref, ts_ref, cb_ref, cd_ref, cs_ref):
    tile = lax.axis_index("tile")
    mine, core = tile // 2, tile % 2
    for source, target in ((tb_ref, cb_ref), (td_ref, cd_ref), (ts_ref, cs_ref)):
        own, own8 = [], []
        for k in range(3):
            rows = source[pl.ds(pl.multiple_of(8 * (3 * mine + k), 8), 8), :]
            tail = source[pl.ds(main + 3 * mine + k, 1), :]
            own += [rows[:, :128], rows[:, 128:]]
            own8 += [tail[:, :128], tail[:, 128:]]
        for m in range(3):
            cols = slice(m * 128, (m + 1) * 128)
            target[0:8, cols] = jnp.where(core == 0, own[m], own[m + 3])
            target[8:9, cols] = jnp.where(core == 0, own8[m], own8[m + 3])


def point_kernel(
    n_grp, back_ref, jp_ref, pidx_ref, pb_ref, pd_ref, pu_ref, cb_ref, cd_ref, cs_ref,
    out_ref, ps_ref, pe_ref, sc_ref,
):
    slot = back_ref.shape[2] - 128
    index = pidx_ref[...]
    mask = is_row(index >> LO_BITS, PH)
    hot = one_hot_rows(index & (LO - 1), LO)
    jp = [jp_ref[k : k + 1, :] for k in range(6)]
    scalars = back_ref[0, :, slot:]
    for h in range(1, n_grp):
        scalars = scalars + back_ref[h, :, slot:]
    gamma, delta = scalars[0:1, 0:1], scalars[1:2, 0:1]
    alpha = gamma / delta
    w = [
        jnp.concatenate([back_ref[h, r : r + 1, 0:slot] for h in range(n_grp)], axis=1) for r in range(4)
    ]
    rhs, diag = pb_ref[...], pd_ref[...]
    z = rhs / diag
    error = [pu_ref[a : a + 1, :] + w[a] for a in range(2)]
    s = z + scatter_points(mask, hot, [jp[i] * error[0] + jp[3 + i] * error[1] for i in range(3)])
    r1 = rhs - alpha * s
    z1 = r1 / diag
    at = gather_points(mask, hot, z1)
    error = [
        sum(jp[3 * a + i] * at[i] for i in range(3)) + (w[a] - alpha * w[2 + a]) for a in range(2)
    ]
    ps_ref[...] = s
    pe_ref[0:1, :] = error[0]
    pe_ref[1:2, :] = error[1]
    cr1 = cb_ref[...] - alpha * cs_ref[...]
    cz1 = cr1 / cd_ref[...]
    gamma1 = total_of(r1 * z1) + total_of(cr1 * cz1)
    delta1 = (
        total_of(error[0] * error[0] + error[1] * error[1]) + total_of(z1 * z1) + total_of(cz1 * cz1)
    )
    sc_ref[...] = lanes(jnp.concatenate([gamma, alpha], axis=0), 128)
    tail = lanes(jnp.concatenate([gamma1, delta1], axis=0), 128)
    per = out_ref.shape[0] // n_grp
    for h in range(n_grp):
        cols = slice(h * slot, (h + 1) * slot)
        block = jnp.concatenate([jnp.concatenate([e[:, cols] for e in error], axis=0), tail], axis=1)

        @pl.loop(0, per)
        def _(tile, block=block, h=h):
            out_ref[h * per + tile] = block


def last_point_sums_kernel(jp_ref, pidx_ref, pe_ref, pt_ref):
    index = pidx_ref[...]
    mask = is_row(index >> LO_BITS, PH)
    hot = one_hot_rows(index & (LO - 1), LO)
    jp = [jp_ref[k : k + 1, :] for k in range(6)]
    error = [pe_ref[a : a + 1, :] for a in range(2)]
    pt_ref[...] = scatter_points(
        mask, hot, [jp[i] * error[0] + jp[3 + i] * error[1] for i in range(3)]
    )


def final_kernel(
    err_ref, a_ref, b_ref, pb_ref, pd_ref, ps_ref, pt_ref, cb_ref, cd_ref, cs_ref, sc_ref,
    px_ref, cx_ref, pr_ref, cr_ref, acc_ref,
):
    blocks, _, slot = a_ref.shape
    per = min(8, blocks)
    chunks = blocks // per
    tile = lax.axis_index("tile")
    core = tile % 2
    acc_ref[...] = jnp.zeros(acc_ref.shape, F32)

    def body(ref, parity):
        def step(chunk, scalars):
            numbers = chunk_of(chunk, per)
            x, index = read_blocks(ref, numbers)
            errs = [err_ref[2 * k + parity] for k in numbers]
            e = jnp.concatenate([v[:, 0:slot] for v in errs], axis=1)
            for v in errs:
                scalars = scalars + v[:, slot:]
            index = index - tile * CAM_DEV
            hi = index >> 7
            hot = one_hot_rows(index & 127, 128)
            j0, j1 = x[0:8], x[8:16]
            e0, e1 = e[0:1], e[1:2]
            acc_ref[...] += scatter_mixed(
                hi, hot, [j0 * e0 + j1 * e1], [x[16:17] * e0 + x[17:18] * e1], 4, 16
            )
            return scalars

        return step

    scalars = lax.fori_loop(0, chunks, body(a_ref, core), jnp.zeros((2, 128), F32))
    scalars = lax.fori_loop(0, chunks, body(b_ref, 1 - core), scalars)
    gamma1, delta1 = scalars[0:1, 0:1], scalars[1:2, 0:1]
    gamma, alpha = sc_ref[0:1, 0:1], sc_ref[1:2, 0:1]
    ratio = gamma1 / gamma
    alpha1 = gamma1 / (delta1 - ratio * gamma1 / alpha)

    rhs, diag, s = pb_ref[...], pd_ref[...], ps_ref[...]
    z = rhs / diag
    r1 = rhs - alpha * s
    z1 = r1 / diag
    x = alpha * z + alpha1 * (z1 + ratio * z)
    r2 = r1 - alpha1 * (z1 + pt_ref[...] + ratio * s)
    for i in range(3):
        for hi in range(PH):
            row = i * PH + hi
            px_ref[i : i + 1, hi * LO : (hi + 1) * LO] = x[row : row + 1]
            pr_ref[i : i + 1, hi * LO : (hi + 1) * LO] = r2[row : row + 1]

    rhs, s = cb_ref[...], cs_ref[...]
    z = rhs / cd_ref[...]
    r1 = rhs - alpha * s
    z1 = r1 / cd_ref[...]
    cx_ref[...] = alpha * z + alpha1 * (z1 + ratio * z)
    sums = both(acc_ref[...])
    base = r1 - alpha1 * (z1 + ratio * s)
    for k in range(3):
        cols = slice(k * 128, (k + 1) * 128)
        cr_ref[0:8, cols] = base[0:8, cols] - alpha1 * sums[8 * k : 8 * k + 8, :]
        cr_ref[8:9, cols] = base[8:9, cols] - alpha1 * sums[32 + k : 33 + k, :]


def shape(*dims):
    return jax.ShapeDtypeStruct(dims, F32)


def replicated(jac_point, jac_cam, resid, point_index, cam_index):
    n_grp, n_tile = lax.axis_size("grp"), lax.axis_size("tile")
    n_z = n_tile // 2
    obs = jac_point.shape[1]
    slot = obs // n_grp
    blocks = n_grp * n_z
    count = CAM_DEV * n_tile // LO
    tail_rows = -(-count // 16) * 16
    rows = 8 * count + tail_rows
    groups = [[d * 2 + core for d in range(blocks)] for core in range(2)]
    swap = [(t, t ^ 1) for t in range(n_tile)]
    pidx, cidx = point_index.reshape(1, obs), cam_index.reshape(1, obs)

    hbm = pl.BlockSpec(memory_space=pltpu.HBM)
    packed, pb, pd, pu, jp, pidx = pl.pallas_call(
        functools.partial(pack_kernel, n_grp, n_z),
        in_specs=[hbm] * 5,
        out_shape=(
            shape(blocks, 24, slot),
            shape(3 * PH, LO),
            shape(3 * PH, LO),
            shape(2, obs),
            shape(6, obs),
            jax.ShapeDtypeStruct((1, obs), jnp.int32),
        ),
        scratch_shapes=[
            pltpu.VMEM((18, obs), F32),
            pltpu.VMEM((2, obs), F32),
            pltpu.VMEM((1, obs), jnp.int32),
            pltpu.SemaphoreType.DMA((5,)),
        ],
        compiler_params=PARAMS,
        name="pack",
    )(*(pltpu.with_memory_space_constraint(x, pltpu.HBM) for x in (jac_point, jac_cam, resid, pidx, cidx)))
    own = lax.all_to_all(packed, ("grp", "tile"), 0, 0, axis_index_groups=groups, tiled=True)
    other = lax.ppermute(own, "tile", swap)
    sums = pl.pallas_call(
        functools.partial(own_sums_kernel, count, tail_rows),
        out_shape=shape(4 * rows, LO),
        compiler_params=PARAMS,
        name="own_sums",
        cost_estimate=pl.CostEstimate(flops=2 * 10**9, bytes_accessed=10**6, transcendentals=0),
    )(own)
    table = shape(rows, LO)
    back, tb, td, ts = pl.pallas_call(
        functools.partial(camera_kernel, n_grp, n_z, count, tail_rows),
        out_shape=(shape(n_grp, 4, slot + 128), table, table, table),
        scratch_shapes=[
            pltpu.VMEM((4 * rows, LO), F32),
            pltpu.VMEM((blocks, 2, slot), F32),
            pltpu.VMEM((2 * rows, LO), BF16),
        ],
        compiler_params=PARAMS,
        name="cameras",
    )(own, other, sums)
    back = lax.all_to_all(back, "grp", 0, 0, tiled=True)
    cb, cd, cs = pl.pallas_call(
        functools.partial(mine_kernel, 8 * count),
        out_shape=(shape(9, CAM_DEV),) * 3,
        compiler_params=PARAMS,
        name="mine",
    )(tb, td, ts)
    errors, ps, pe, sc = pl.pallas_call(
        functools.partial(point_kernel, n_grp),
        out_shape=(
            shape(n_grp * n_tile, 2, slot + 128),
            shape(3 * PH, LO),
            shape(2, obs),
            shape(2, 128),
        ),
        compiler_params=PARAMS,
        name="points",
    )(back, jp, pidx, pb, pd, pu, cb, cd, cs)
    errors = lax.all_to_all(errors, ("grp", "tile"), 0, 0, tiled=True)
    pt = pl.pallas_call(
        last_point_sums_kernel,
        out_shape=shape(3 * PH, LO),
        compiler_params=PARAMS,
        name="last_point_sums",
    )(jp, pidx, pe)
    return pl.pallas_call(
        final_kernel,
        out_shape=(shape(3, P_DEV), shape(9, CAM_DEV), shape(3, P_DEV), shape(9, CAM_DEV)),
        scratch_shapes=[pltpu.VMEM((96, 128), F32)],
        compiler_params=PARAMS,
        name="finish",
    )(errors, own, other, pb, pd, ps, pt, cb, cd, cs, sc)


def eights(row):
    return jnp.broadcast_to(row, (8, row.shape[1]))


def row_numbers(width):
    return lax.broadcasted_iota(jnp.int32, (16, width), 0)


def as_16_bit(numbers):
    return numbers.astype(F32).astype(BF16)


def masked_rows(parts, masks):
    none = jnp.zeros(parts[0].shape, BF16)
    return jnp.concatenate([jnp.where(m, p, none) for p in parts for m in masks], axis=0)


def low_lanes(rows):
    return lax.broadcasted_iota(jnp.int32, (rows, HALF), 1) < SLOTS


def swap_lanes(v):
    return pltpu.roll(v, SLOTS, 1)


def point_sums(pidx_ref, jp_ref, res_ref):
    index = pidx_ref[...]
    mask = is_row(index >> LO_BITS, PH)
    hot = one_hot_rows(index & (LO - 1), LO)
    jp = [jp_ref[k : k + 1, :] for k in range(6)]
    res = [res_ref[a : a + 1, :] for a in range(2)]
    grad = [-(jp[i] * res[0] + jp[3 + i] * res[1]) for i in range(3)]
    square = [jp[i] * jp[i] + jp[3 + i] * jp[3 + i] for i in range(3)]
    return scatter_points(mask, hot, grad + square), mask, hot, jp


def start_copies(pairs, sems):
    copies = [pltpu.make_async_copy(a, b, sems.at[k]) for k, (a, b) in enumerate(pairs)]
    for copy in copies:
        copy.start()
    for copy in copies:
        copy.wait()


def route_kernel(
    n_grp, n_tile, jp_hbm, jc_hbm, res_hbm, pidx_hbm, cidx_hbm,
    out_ref, pb_ref, pd_ref, pu_ref, jp_ref, pidx_ref, place_ref, sc_ref,
    jc_ref, res_ref, cidx_ref, sems,
):
    start_copies(
        (
            (pidx_hbm, pidx_ref),
            (jp_hbm, jp_ref),
            (res_hbm, res_ref),
            (jc_hbm, jc_ref),
            (cidx_hbm, cidx_ref),
        ),
        sems,
    )
    slot = cidx_ref.shape[1] // n_grp
    cams = cidx_ref[...]
    owner = ((cams >> 7) * 171) >> 9
    local = (cams - owner * CAM_DEV).astype(F32)
    mine = is_row(owner, n_tile)
    ones = jnp.where(mine, 1.0, 0.0)
    stack = jnp.concatenate([ones[:, h * slot : (h + 1) * slot] for h in range(n_grp)], axis=0)
    before = lax.broadcasted_iota(jnp.int32, (slot, slot), 0)
    before = before < lax.broadcasted_iota(jnp.int32, (slot, slot), 1)
    counts = dot_nn(stack.astype(BF16), jnp.where(before, 1.0, 0.0).astype(BF16))
    counts = jnp.concatenate([counts[h * n_tile : (h + 1) * n_tile] for h in range(n_grp)], axis=1)
    rank = jnp.sum(jnp.where(mine, counts, 0.0), axis=0, keepdims=True)
    place_ref[0:1, :] = owner
    place_ref[1:2, :] = rank.astype(jnp.int32)
    over = jnp.max(jnp.where(rank >= SLOTS, 1.0, 0.0), axis=1, keepdims=True)
    rank = rank.astype(jnp.int32)
    hots = [one_hot_rows(rank + a * SLOTS, HALF) for a in range(2)]
    rights = [
        jnp.concatenate([hot[:, h * slot : (h + 1) * slot] for hot in hots], axis=1) for h in range(n_grp)
    ]
    def route_block(h):
        cols = slice(h * slot, (h + 1) * slot)
        here = [sixteen(owner[:, cols]) == BF16(t) for t in range(n_tile)]
        left = []
        for a in range(2):
            rows = [
                jc_ref[9 * a : 9 * a + 8, cols],
                jc_ref[9 * a + 8 : 9 * a + 9, cols],
                res_ref[a : a + 1, cols],
                local[:, cols],
                jnp.zeros((5, slot), F32),
            ]
            left.append(masked_rows(two_parts(jnp.concatenate(rows, axis=0)), here))
        moved = both(dot_nt(jnp.concatenate(left, axis=1), rights[h]))
        for t in range(n_tile):
            for part in range(3):
                row = 16 * t + 4 * part
                out_ref[3 * (h * n_tile + t) + part] = moved[row : row + 4]

    table, mask, hot, jp = point_sums(pidx_ref, jp_ref, res_ref)
    for h in range(n_grp // 2):
        route_block(h)
    rhs, diag = table[: 3 * PH], table[3 * PH :] + DAMPING
    z = rhs / diag
    at = gather_points(mask, hot, z)
    for h in range(n_grp // 2, n_grp):
        route_block(h)
    pb_ref[...] = rhs
    pd_ref[...] = diag
    u = [sum(jp[3 * a + i] * at[i] for i in range(3)) for a in range(2)]
    pu_ref[0:1, :] = u[0]
    pu_ref[1:2, :] = u[1]
    sc_ref[...] = lanes(jnp.concatenate([total_of(rhs * z), total_of(z * z), over], axis=0), HALF)
    masks = [sixteen(owner) == as_16_bit(row_numbers(owner.shape[1]) + t) for t in range(0, n_tile, 16)]
    left = [masked_rows(two_parts(jnp.broadcast_to(u[a], (16, u[a].shape[1]))), masks) for a in range(2)]
    for h in range(n_grp):
        cols = slice(h * slot, (h + 1) * slot)
        moved = both(dot_nt(jnp.concatenate([v[:, cols] for v in left], axis=1), rights[h]))
        for t in range(n_tile):
            out_ref[3 * (h * n_tile + t) + 2, 3:4, :] = moved[t : t + 1]


def unfold(even, odd):
    low = low_lanes(even.shape[0])
    return jnp.where(low, even, swap_lanes(odd)), jnp.where(low, swap_lanes(even), odd)


def side_by_side(even, odd):
    return jnp.where(low_lanes(even.shape[0]), even, swap_lanes(odd))


def read_routed(ref, sources):
    main, rest = ([], []), ([], [])
    for s, t in zip(sources[::2], sources[1::2]):
        pair = unfold(*(jnp.concatenate([ref[3 * k], ref[3 * k + 1]], axis=0) for k in (s, t)))
        pair_rest = unfold(ref[3 * s + 2], ref[3 * t + 2])
        for a in range(2):
            main[a].append(pair[a])
            rest[a].append(pair_rest[a])
    main = [jnp.concatenate(v, axis=1) for v in main]
    rest = [jnp.concatenate(v, axis=1) for v in rest]
    index = rest[0][2:3].astype(jnp.int32)
    return main, rest, (index >> 7).astype(F32), one_hot_rows(index & 127, 128)


OWN_ROWS = 32
STEP = 32


def scatter_two(hi, hot, first, second):
    wide, numbers = sixteen(hi), row_numbers(hi.shape[1])
    blocks = [wide == BF16(k) for k in range(3)]
    tail = wide == as_16_bit(numbers & 7)
    rows = two_parts(jnp.concatenate([first[0], second[0]], axis=0))
    tails = two_parts(jnp.concatenate([eights(first[1]), eights(second[1])], axis=0))
    none = jnp.zeros(wide.shape, BF16)
    pieces = []
    for part in range(2):
        pieces += [jnp.where(mask, rows[part], none) for mask in blocks]
        pieces.append(jnp.where(tail, tails[part], none))
    return both(dot_nt(jnp.concatenate(pieces, axis=0), hot))


def scatter_one(hi, hot, main, tail):
    wide, numbers = sixteen(hi), row_numbers(hi.shape[1])
    upper = wide == as_16_bit(numbers >> 3)
    lower = wide == as_16_bit(jnp.where(numbers < 8, 2, numbers - 8))
    rows = two_parts(jnp.concatenate([main, main], axis=0))
    tails = two_parts(jnp.concatenate([main, eights(tail)], axis=0))
    none = jnp.zeros(wide.shape, BF16)
    pieces = []
    for part in range(2):
        pieces += [jnp.where(upper, rows[part], none), jnp.where(lower, tails[part], none)]
    return both(dot_nt(jnp.concatenate(pieces, axis=0), hot))


def gather_own(hi, hot, table, main, rest):
    found = both(dot_nn(table, hot))
    block = eights(hi)
    at = jnp.where(block == 0, found[0:8], jnp.where(block == 1, found[8:16], found[16:24]))
    numbers = lax.broadcasted_iota(jnp.int32, block.shape, 0).astype(F32)
    tail = jnp.where(block == numbers, found[24:32], 0.0)
    return [
        jnp.sum(main[a] * at + eights(rest[a][0:1]) * tail, axis=0, keepdims=True) for a in range(2)
    ]


def scatter_j(hi, hot, main, rest, e):
    return scatter_one(
        hi, hot, main[0] * e[0] + main[1] * e[1], rest[0][0:1] * e[0] + rest[1][0:1] * e[1]
    )


def owner_kernel(in_ref, sc_ref, back_ref, tb_ref, td_ref, ts_ref, acc_ref, zz_ref, w_ref, *kept):
    devices = back_ref.shape[0]
    per = min(STEP, devices)
    steps = devices // per

    if steps == 1:
        main, rest, hi, hot = read_routed(in_ref, range(devices))
        kept[0][...] = hot
        for a in range(2):
            kept[1][8 * a : 8 * a + 8, :] = main[a]
            kept[1][16 + a : 17 + a, :] = rest[a][0:1]
        kept[1][18:19, :] = hi

        def loop(body, start):
            return body((main, rest, hi, hot), 0, start)
    else:

        def loop(body, start):
            def step(number, carry):
                return body(read_routed(in_ref, chunk_of(number, per)), number, carry)

            return lax.fori_loop(0, steps, step, start)

    def rhs_and_diag(slots, number, carry):
        main, rest, hi, hot = slots
        r = [rest[a][1:2] for a in range(2)]
        rhs = (-(main[0] * r[0] + main[1] * r[1]), -(rest[0][0:1] * r[0] + rest[1][0:1] * r[1]))
        square = (
            main[0] * main[0] + main[1] * main[1],
            rest[0][0:1] * rest[0][0:1] + rest[1][0:1] * rest[1][0:1],
        )
        acc_ref[...] += scatter_two(hi, hot, rhs, square)
        return carry

    acc_ref[...] = jnp.zeros(acc_ref.shape, F32)
    loop(rhs_and_diag, 0)
    rhs = jnp.concatenate([acc_ref[16 * k : 16 * k + 8, :] for k in range(4)], axis=0)
    diag = jnp.concatenate([acc_ref[16 * k + 8 : 16 * k + 16, :] for k in range(4)], axis=0) + DAMPING
    tb_ref[...] = rhs
    td_ref[...] = diag
    z = rhs / diag
    zz_ref[...] = stacked(z)
    acc_ref[0:OWN_ROWS, :] = z

    def apply(slots, number, energy):
        main, rest, hi, hot = slots
        w = gather_own(hi, hot, zz_ref[...], main, rest)
        e = [rest[a][3:4] + w[a] for a in range(2)]
        for a in range(2):
            w_ref[number, a : a + 1, :] = w[a]
        acc_ref[0:OWN_ROWS, :] += scatter_j(hi, hot, main, rest, e)
        return energy + e[0] * e[0] + e[1] * e[1]

    energy = loop(apply, jnp.zeros((1, per * SLOTS), F32))
    s = acc_ref[0:OWN_ROWS, :]
    ts_ref[...] = s
    zz_ref[...] = stacked(s / diag)
    gamma = sc_ref[0:1, :] + total_of(rhs * z)
    delta = sc_ref[1:2, :] + total_of(z * z) + total_of(energy)
    tail = jnp.concatenate([gamma, delta, sc_ref[2:3, :], sc_ref[2:3, :]], axis=0)

    def send(slots, number, carry):
        main, rest, hi, hot = slots
        v = gather_own(hi, hot, zz_ref[...], main, rest)
        for a in range(2):
            w_ref[number, 2 + a : 3 + a, :] = v[a]
        w = w_ref[number]
        low = low_lanes(4)
        for k in range(per // 2):
            pair = w[:, k * HALF : (k + 1) * HALF]
            back_ref[number * per + 2 * k] = jnp.where(low, pair, tail)
            back_ref[number * per + 2 * k + 1] = jnp.where(low, swap_lanes(pair), tail)
        return carry

    loop(send, 0)


def routed_point_kernel(
    n_grp, n_tile, back_ref, jp_ref, pidx_ref, place_ref, pb_ref, pd_ref, pu_ref, cb_ref, cd_ref, cs_ref,
    out_ref, ps_ref, pe_ref, sc_ref, over_ref,
):
    slot = place_ref.shape[1] // n_grp
    index = pidx_ref[...]
    mask = is_row(index >> LO_BITS, PH)
    hot = one_hot_rows(index & (LO - 1), LO)
    jp = [jp_ref[k : k + 1, :] for k in range(6)]
    scalars = jnp.sum(back_ref[...], axis=0)[:, SLOTS : SLOTS + 1]
    gamma, delta = scalars[0:1], scalars[1:2]
    over_ref[...] = lanes(scalars[2:3], HALF)
    alpha = gamma / delta
    owner = place_ref[0:1, :]
    slots = one_hot_rows(place_ref[1:2, :], HALF)
    numbers = lax.broadcasted_iota(jnp.int32, (4 * n_tile, slot), 0) >> 2
    terms = []
    for h in range(n_grp):
        cols = slice(h * slot, (h + 1) * slot)
        rows = jnp.concatenate([back_ref[h * n_tile + t] for t in range(n_tile)], axis=0)
        found = both(dot_nn(stacked(rows), slots[:, cols]))
        found = jnp.where(numbers == owner[:, cols], found, 0.0)
        found = sum(found[8 * k : 8 * k + 8] for k in range(n_tile // 2))
        terms.append(found[0:4] + found[4:8])
    terms = jnp.concatenate(terms, axis=1)
    w0 = [terms[a : a + 1] for a in range(2)]
    w1 = [terms[2 + a : 3 + a] for a in range(2)]
    rhs, diag = pb_ref[...], pd_ref[...]
    z = rhs / diag
    error = [pu_ref[a : a + 1, :] + w0[a] for a in range(2)]
    s = z + scatter_points(mask, hot, [jp[i] * error[0] + jp[3 + i] * error[1] for i in range(3)])
    r1 = rhs - alpha * s
    z1 = r1 / diag
    at = gather_points(mask, hot, z1)
    error = [sum(jp[3 * a + i] * at[i] for i in range(3)) + (w0[a] - alpha * w1[a]) for a in range(2)]
    ps_ref[...] = s
    pe_ref[0:1, :] = error[0]
    pe_ref[1:2, :] = error[1]
    cr1 = cb_ref[...] - alpha * cs_ref[...]
    cz1 = cr1 / cd_ref[...]
    gamma1 = total_of(r1 * z1) + total_of(cr1 * cz1)
    delta1 = (
        total_of(error[0] * error[0] + error[1] * error[1]) + total_of(z1 * z1) + total_of(cz1 * cz1)
    )
    sc_ref[...] = lanes(jnp.concatenate([gamma, alpha], axis=0), HALF)
    tail = lanes(jnp.concatenate([gamma1, delta1], axis=0), HALF)
    low = low_lanes(2)
    numbers = row_numbers(slot)
    for h in range(n_grp):
        cols = slice(h * slot, (h + 1) * slot)
        first, second = (jnp.broadcast_to(e[:, cols], (16, slot)) for e in error)
        parts = two_parts(jnp.where((numbers & 1) == 0, first, second))
        wide = sixteen(owner[:, cols])
        here = [wide == as_16_bit((numbers >> 1) + t) for t in range(0, n_tile, 8)]
        moved = both(dot_nt(masked_rows(parts, here), slots[:, cols]))
        for t in range(n_tile):
            out_ref[h * n_tile + t] = jnp.where(low, moved[2 * t : 2 * t + 2], tail)


def point_results(alpha, alpha1, ratio, pb_ref, pd_ref, ps_ref, pt_ref, px_ref, pr_ref):
    rhs, diag, s = pb_ref[...], pd_ref[...], ps_ref[...]
    z = rhs / diag
    r1 = rhs - alpha * s
    z1 = r1 / diag
    x = alpha * z + alpha1 * (z1 + ratio * z)
    r2 = r1 - alpha1 * (z1 + pt_ref[...] + ratio * s)
    for i in range(3):
        for hi in range(PH):
            row = i * PH + hi
            px_ref[i : i + 1, hi * LO : (hi + 1) * LO] = x[row : row + 1]
            pr_ref[i : i + 1, hi * LO : (hi + 1) * LO] = r2[row : row + 1]


def routed_final_kernel(
    err_ref, in_ref, jp_ref, pidx_ref, pe_ref, pb_ref, pd_ref, ps_ref, cb_ref, cd_ref, cs_ref, sc_ref, *rest_refs
):
    kept, outs, (px_ref, cx_ref, pr_ref, cr_ref, acc_ref, pt_ref, sems) = (
        rest_refs[:-11],
        rest_refs[-11:-7],
        rest_refs[-7:],
    )
    devices = err_ref.shape[0]
    per = min(STEP, devices)
    steps = devices // per

    def body(step, carry):
        sources = chunk_of(step, per)
        if kept:
            hot, rows = kept[0][...], kept[1]
            main = [rows[8 * a : 8 * a + 8, :] for a in range(2)]
            rest = [rows[16 + a : 17 + a, :] for a in range(2)]
            hi = rows[18:19, :]
        else:
            main, rest, hi, hot = read_routed(in_ref, sources)
        e = jnp.concatenate(
            [side_by_side(err_ref[s], err_ref[t]) for s, t in zip(sources[::2], sources[1::2])], axis=1
        )
        acc_ref[...] += scatter_j(hi, hot, main, rest, [e[0:1], e[1:2]])
        return carry

    acc_ref[...] = jnp.zeros(acc_ref.shape, F32)
    if steps == 1:
        body(0, 0)
    else:
        lax.fori_loop(0, steps, body, 0)
    last_point_sums_kernel(jp_ref, pidx_ref, pe_ref, pt_ref)
    scalars = jnp.sum(err_ref[...], axis=0)
    gamma1, delta1 = scalars[0:1, SLOTS : SLOTS + 1], scalars[1:2, SLOTS : SLOTS + 1]
    gamma, alpha = sc_ref[0:1, 0:1], sc_ref[1:2, 0:1]
    ratio = gamma1 / gamma
    alpha1 = gamma1 / (delta1 - ratio * gamma1 / alpha)
    point_results(alpha, alpha1, ratio, pb_ref, pd_ref, ps_ref, pt_ref, px_ref, pr_ref)
    copies = [
        pltpu.make_async_copy(here, there, sems.at[k])
        for k, (here, there) in enumerate(zip((px_ref, cx_ref, pr_ref, cr_ref), outs))
    ]
    copies[0].start()
    copies[2].start()
    rhs, s = cb_ref[...], cs_ref[...]
    z = rhs / cd_ref[...]
    r1 = rhs - alpha * s
    z1 = r1 / cd_ref[...]
    x = alpha * z + alpha1 * (z1 + ratio * z)
    r2 = r1 - alpha1 * (z1 + acc_ref[...] + ratio * s)
    for table, target in ((x, cx_ref), (r2, cr_ref)):
        for k in range(3):
            cols = slice(k * 128, (k + 1) * 128)
            target[0:8, cols] = table[8 * k : 8 * k + 8]
            target[8:9, cols] = table[24 + k : 25 + k]
    copies[1].start()
    copies[3].start()
    for copy in copies:
        copy.wait()


def shards(jac_point, jac_cam, resid, point_index, cam_index):
    n_grp, n_tile = lax.axis_size("grp"), lax.axis_size("tile")
    devices = n_grp * n_tile
    obs = jac_point.shape[1]
    pidx, cidx = point_index.reshape(1, obs), cam_index.reshape(1, obs)
    hbm = pl.BlockSpec(memory_space=pltpu.HBM)
    ints = jax.ShapeDtypeStruct((1, obs), jnp.int32)
    places = jax.ShapeDtypeStruct((2, obs), jnp.int32)
    points = shape(3 * PH, LO)
    cameras = shape(OWN_ROWS, 128)
    routed, pb, pd, pu, jp, pidx_here, place, sc = pl.pallas_call(
        functools.partial(route_kernel, n_grp, n_tile),
        in_specs=[hbm] * 5,
        out_shape=(shape(3 * devices, 4, HALF), points, points, shape(2, obs), shape(6, obs), ints, places, shape(3, HALF)),
        scratch_shapes=[
            pltpu.VMEM((18, obs), F32),
            pltpu.VMEM((2, obs), F32),
            pltpu.VMEM((1, obs), jnp.int32),
            pltpu.SemaphoreType.DMA((5,)),
        ],
        compiler_params=PARAMS,
        name="route",
    )(*(pltpu.with_memory_space_constraint(x, pltpu.HBM) for x in (jac_point, jac_cam, resid, pidx, cidx)))
    routed = lax.all_to_all(routed, ("grp", "tile"), 0, 0, tiled=True)
    slots = devices * SLOTS
    per = min(STEP, devices)
    scratch = [
        pltpu.VMEM((2 * OWN_ROWS, 128), F32),
        pltpu.VMEM((2 * OWN_ROWS, 128), BF16),
        pltpu.VMEM((devices // per, 4, per * SLOTS), F32),
    ]
    kept_shapes = ()
    if devices == per:
        kept_shapes = (jax.ShapeDtypeStruct((128, slots), BF16), shape(24, slots))

    def owner(in_ref, sc_ref, back_ref, tb_ref, td_ref, ts_ref, *others):
        kept, work = others[: len(kept_shapes)], others[len(kept_shapes) :]
        owner_kernel(in_ref, sc_ref, back_ref, tb_ref, td_ref, ts_ref, *work, *kept)

    back, tb, td, ts, *kept = pl.pallas_call(
        owner,
        out_shape=(shape(devices, 4, HALF), cameras, cameras, cameras) + kept_shapes,
        scratch_shapes=scratch,
        compiler_params=PARAMS,
        name="owner",
    )(routed, sc)
    back = lax.all_to_all(back, ("grp", "tile"), 0, 0, tiled=True)
    errors, ps, pe, sc, over = pl.pallas_call(
        functools.partial(routed_point_kernel, n_grp, n_tile),
        out_shape=(shape(devices, 2, HALF), points, shape(2, obs), shape(2, HALF), shape(1, HALF)),
        compiler_params=PARAMS,
        name="points",
    )(back, jp, pidx_here, place, pb, pd, pu, tb, td, ts)
    outputs = (shape(3, P_DEV), shape(9, CAM_DEV), shape(3, P_DEV), shape(9, CAM_DEV))

    def fits(*operands):
        errors = lax.all_to_all(operands[5], ("grp", "tile"), 0, 0, tiled=True)
        return pl.pallas_call(
            routed_final_kernel,
            out_shape=outputs,
            out_specs=[hbm] * 4,
            scratch_shapes=[pltpu.VMEM(v.shape, F32) for v in outputs]
            + [
                pltpu.VMEM((OWN_ROWS, 128), F32),
                pltpu.VMEM((3 * PH, LO), F32),
                pltpu.SemaphoreType.DMA((4,)),
            ],
            compiler_params=PARAMS,
            name="finish",
        )(errors, *operands[6:])

    def overflows(*operands):
        return tuple(replicated(*operands[:5]))

    over, *operands = lax.optimization_barrier(
        (
            over, jac_point, jac_cam, resid, point_index, cam_index,
            errors, routed, jp, pidx_here, pe, pb, pd, ps, tb, td, ts, sc, *kept,
        )
    )
    return lax.cond(over[0, 0] > 0, overflows, lambda *operands: tuple(fits(*operands)), *operands)


def solution(mesh):
    placed = (
        P(None, ("grp", "tile")),
        P(None, ("grp", "tile")),
        P(None, ("grp", "tile")),
        P(("grp", "tile")),
        P(("grp", "tile")),
    )
    return jax.shard_map(
        shards,
        mesh=mesh,
        in_specs=placed,
        out_specs=(P(None, ("grp", "tile")),) * 4,
        check_vma=False,
    )
```

```python
import functools

import jax
import jax.numpy as jnp
from jax import lax
from jax.experimental import pallas as pl
from jax.experimental.pallas import tpu as pltpu
from jax.sharding import PartitionSpec as P

P_DEV = 4096
CAM_DEV = 384
LO_BITS = 8
LO = 1 << LO_BITS
PH = P_DEV // LO
DAMPING = 1.0
F32 = jnp.float32
BF16 = jnp.bfloat16
SLOTS = 64
HALF = 128
PARAMS = pltpu.CompilerParams(vmem_limit_bytes=48 * 1024 * 1024)


def halves(v):
    high = v.astype(BF16).astype(F32)
    return high, v - high


def rows16(width, step=1):
    numbers = lax.broadcasted_iota(jnp.int32, (16, width), 0)
    return (numbers // step if step > 1 else numbers).astype(F32).astype(BF16)


def sixteen(row):
    return jnp.broadcast_to(row.astype(F32), (16, row.shape[1])).astype(BF16)


def one_hot_rows(index, rows):
    numbers = rows16(index.shape[1])
    pieces = []
    for base in range(0, rows, 256):
        wide = sixteen(index - base)
        one, none = jnp.ones(wide.shape, BF16), jnp.zeros(wide.shape, BF16)
        pieces += [
            jnp.where(wide == numbers + BF16(16 * k), one, none)
            for k in range(min(256, rows - base) // 16)
        ]
    return jnp.concatenate(pieces, axis=0)


def dot_nt(a, b):
    return lax.dot_general(a, b, (((1,), (1,)), ((), ())), preferred_element_type=F32)


def dot_nn(a, b):
    return lax.dot_general(a, b, (((1,), (0,)), ((), ())), preferred_element_type=F32)


def is_row(hi, rows):
    return lax.broadcasted_iota(jnp.int32, (rows, hi.shape[1]), 0) == hi


def spread_row(mask, row):
    return jnp.where(mask, jnp.broadcast_to(row, mask.shape), 0.0)


def two_parts(v):
    high = v.astype(BF16)
    return high, (v - high.astype(F32)).astype(BF16)


def scatter_mixed(hi, hot, mains, tails, count, tail_rows):
    wide = sixteen(hi)
    none = jnp.zeros(wide.shape, BF16)
    single = len(mains) == 1
    numbers = rows16(hi.shape[1], 8) if single else none
    main_parts = two_parts(jnp.concatenate(mains * 2 if single else mains, axis=0))
    tail_parts = [two_parts(jnp.broadcast_to(v, wide.shape)) for v in tails]
    here = [wide == numbers + BF16(k) for k in range(0, count, 2 if single else 1)]
    tail_here = [wide == rows16(hi.shape[1]) + BF16(k) for k in range(0, tail_rows, 16)]
    pieces = []
    for part in range(2):
        pieces += [jnp.where(mask, main_parts[part], none) for mask in here]
        pieces += [jnp.where(mask, v[part], none) for v in tail_parts for mask in tail_here]
    return dot_nt(jnp.concatenate(pieces, axis=0), hot)


def both(v):
    half = v.shape[0] // 2
    return v[:half] + v[half:]


def gather_mixed(hi, hot, table, count, tail_rows):
    found = dot_nn(table, hot)
    hi8 = jnp.broadcast_to(hi, (8, hi.shape[1]))
    main = jnp.zeros(hi8.shape, F32)
    half = found.shape[0] // 2
    for k in range(count):
        rows = slice(k * 8, k * 8 + 8)
        low = slice(half + k * 8, half + k * 8 + 8)
        main = main + jnp.where(hi8 == k, found[rows] + found[low], 0.0)
    tail = found[count * 8 : half] + found[half + count * 8 :]
    tail = jnp.sum(jnp.where(is_row(hi, tail_rows), tail, 0.0), axis=0, keepdims=True)
    return main, tail


def stacked(table):
    high, low = halves(table)
    return jnp.concatenate([high, low], axis=0).astype(BF16)


def scatter_points(mask, hot, rows):
    pieces = [spread_row(mask, v[k : k + 1]) for v in halves(rows) for k in range(rows.shape[0])]
    return both(dot_nt(jnp.concatenate(pieces, axis=0).astype(BF16), hot))


def gather_points(mask, hot, table):
    found = both(dot_nn(stacked(table), hot))
    return [
        jnp.sum(jnp.where(mask, found[i * PH : (i + 1) * PH], 0.0), axis=0, keepdims=True)
        for i in range(found.shape[0] // PH)
    ]


def total_of(v):
    return jnp.sum(jnp.sum(v, axis=0, keepdims=True), axis=1, keepdims=True)


def lanes(v, width):
    return jnp.broadcast_to(v, (v.shape[0], width))


def pack_kernel(
    n_grp, n_z, jp_hbm, jc_hbm, res_hbm, pidx_hbm, cidx_hbm,
    out_ref, pb_ref, pd_ref, pu_ref, jp_ref, pidx_ref,
    jc_ref, res_ref, cidx_ref, sems,
):
    copies = [
        pltpu.make_async_copy(source, target, sems.at[k])
        for k, (source, target) in enumerate(
            (
                (pidx_hbm, pidx_ref),
                (jp_hbm, jp_ref),
                (res_hbm, res_ref),
                (jc_hbm, jc_ref),
                (cidx_hbm, cidx_ref),
            )
        )
    ]
    for copy in copies:
        copy.start()
    for copy in copies:
        copy.wait()
    slot = out_ref.shape[2]
    index = pidx_ref[...]
    mask = is_row(index >> LO_BITS, PH)
    hot = one_hot_rows(index & (LO - 1), LO)
    jp = [jp_ref[k : k + 1, :] for k in range(6)]
    res = [res_ref[a : a + 1, :] for a in range(2)]
    grad = [-(jp[i] * res[0] + jp[3 + i] * res[1]) for i in range(3)]
    square = [jp[i] * jp[i] + jp[3 + i] * jp[3 + i] for i in range(3)]
    table = scatter_points(mask, hot, jnp.concatenate(grad + square, axis=0))
    rhs = table[: 3 * PH]
    diag = table[3 * PH :] + DAMPING
    pb_ref[...] = rhs
    pd_ref[...] = diag
    z = rhs / diag
    at = gather_points(mask, hot, z)
    u = [sum(jp[3 * a + i] * at[i] for i in range(3)) for a in range(2)]
    pu_ref[0:1, :] = u[0]
    pu_ref[1:2, :] = u[1]
    gamma = total_of(rhs * z)
    norm = total_of(z * z)
    scalars = jnp.concatenate([lanes(gamma, slot // 2), lanes(norm, slot // 2)], axis=1)
    cams = cidx_ref[...].astype(F32)
    for h in range(n_grp):
        cols = slice(h * slot, (h + 1) * slot)
        block = jnp.concatenate(
            [
                jc_ref[0:8, cols],
                jc_ref[9:17, cols],
                jc_ref[8:9, cols],
                jc_ref[17:18, cols],
                res[0][:, cols],
                res[1][:, cols],
                u[0][:, cols],
                u[1][:, cols],
                cams[:, cols],
                scalars,
            ],
            axis=0,
        )

        @pl.loop(0, n_z)
        def _(z_to, block=block, h=h):
            out_ref[h * n_z + z_to] = block


def read_blocks(ref, numbers):
    x = jnp.concatenate([ref[k] for k in numbers], axis=1)
    return x, x[22:23].astype(jnp.int32)


def chunk_of(chunk, per):
    return [chunk * per + k for k in range(per)]


def first_sums(ref, acc_ref, per, count, tail_rows):
    def body(chunk, carry):
        x, index = read_blocks(ref, chunk_of(chunk, per))
        hi, hot = index >> LO_BITS, one_hot_rows(index & (LO - 1), LO)
        j0, j1 = x[0:8], x[8:16]
        j08, j18, r0, r1 = x[16:17], x[17:18], x[18:19], x[19:20]
        acc_ref[...] += scatter_mixed(
            hi,
            hot,
            [-(j0 * r0 + j1 * r1), j0 * j0 + j1 * j1],
            [-(j08 * r0 + j18 * r1), j08 * j08 + j18 * j18],
            count,
            tail_rows,
        )
        return carry

    lax.fori_loop(0, ref.shape[0] // per, body, 0)


def own_sums_kernel(count, tail_rows, a_ref, acc_ref):
    acc_ref[...] = jnp.zeros(acc_ref.shape, F32)
    first_sums(a_ref, acc_ref, min(16, a_ref.shape[0]), count, tail_rows)


def camera_kernel(
    n_grp, n_z, count, tail_rows, a_ref, b_ref, start_ref,
    back_ref, tb_ref, td_ref, ts_ref,
    acc_ref, w_ref, zz_ref,
):
    blocks, _, slot = a_ref.shape
    per = min(8, blocks)
    chunks = blocks // per
    acc_ref[...] = start_ref[...]
    first_sums(b_ref, acc_ref, min(16, blocks), count, tail_rows)
    scalars = jnp.zeros((1, slot), F32)
    for ref in (a_ref, b_ref):
        scalars = scalars + jnp.sum(ref[:, 23, :], axis=0, keepdims=True)
    main = 8 * count
    half = acc_ref.shape[0] // 2
    for k in range(count):
        row = 16 * k
        tb_ref[8 * k : 8 * k + 8, :] = acc_ref[row : row + 8, :] + acc_ref[half + row : half + row + 8, :]
        row = 16 * k + 8
        td_ref[8 * k : 8 * k + 8, :] = (
            acc_ref[row : row + 8, :] + acc_ref[half + row : half + row + 8, :] + DAMPING
        )
    tb_ref[main:, :] = (
        acc_ref[2 * main : 2 * main + tail_rows, :]
        + acc_ref[half + 2 * main : half + 2 * main + tail_rows, :]
    )
    td_ref[main:, :] = (
        acc_ref[2 * main + tail_rows : half, :] + acc_ref[half + 2 * main + tail_rows :, :] + DAMPING
    )
    z = tb_ref[...] / td_ref[...]
    gamma = total_of(tb_ref[...] * z)
    norm = total_of(z * z)
    zz_ref[...] = stacked(z)
    ts_ref[...] = z
    acc_ref[0:half, :] = jnp.zeros((half, LO), F32)

    def second(ref, keep):
        def body(chunk, energy):
            numbers = chunk_of(chunk, per)
            x, index = read_blocks(ref, numbers)
            hi, hot = index >> LO_BITS, one_hot_rows(index & (LO - 1), LO)
            j0, j1 = x[0:8], x[8:16]
            j08, j18, u0, u1 = x[16:17], x[17:18], x[20:21], x[21:22]
            at, at8 = gather_mixed(hi, hot, zz_ref[...], count, tail_rows)
            w0 = jnp.sum(j0 * at, axis=0, keepdims=True) + j08 * at8
            w1 = jnp.sum(j1 * at, axis=0, keepdims=True) + j18 * at8
            if keep:
                for k, number in enumerate(numbers):
                    cols = slice(k * slot, (k + 1) * slot)
                    w_ref[number, 0:1, :] = w0[:, cols]
                    w_ref[number, 1:2, :] = w1[:, cols]
            e0, e1 = u0 + w0, u1 + w1
            acc_ref[0:half, :] += scatter_mixed(
                hi, hot, [j0 * e0 + j1 * e1], [j08 * e0 + j18 * e1], count, tail_rows
            )
            return energy + e0 * e0 + e1 * e1

        return body

    energy = jnp.zeros((1, per * slot), F32)
    energy = lax.fori_loop(0, chunks, second(a_ref, True), energy)
    energy = lax.fori_loop(0, chunks, second(b_ref, False), energy)
    ts_ref[...] += both(acc_ref[0:half, :])
    zz_ref[...] = stacked(ts_ref[...] / td_ref[...])
    share = 1.0 / n_grp
    gamma = gamma + share * scalars[:, 0:1]
    delta = norm + total_of(energy) + share * scalars[:, slot // 2 : slot // 2 + 1]
    mine = lax.axis_index("tile") // 2
    numbers = [g * n_z + mine for g in range(n_grp)]
    per = min(4, n_grp)
    for first in range(0, n_grp, per):
        some = numbers[first : first + per]
        x, index = read_blocks(a_ref, some)
        hi, hot = index >> LO_BITS, one_hot_rows(index & (LO - 1), LO)
        at, at8 = gather_mixed(hi, hot, zz_ref[...], count, tail_rows)
        v0 = jnp.sum(x[0:8] * at, axis=0, keepdims=True) + x[16:17] * at8
        v1 = jnp.sum(x[8:16] * at, axis=0, keepdims=True) + x[17:18] * at8
        for k in range(per):
            cols = slice(k * slot, (k + 1) * slot)
            g = first + k
            back_ref[g, 0:2, 0:slot] = w_ref[some[k], 0:2, :]
            back_ref[g, 2:3, 0:slot] = v0[:, cols]
            back_ref[g, 3:4, 0:slot] = v1[:, cols]
            back_ref[g, :, slot:] = lanes(jnp.concatenate([gamma, delta, gamma, delta], axis=0), 128)


def mine_kernel(main, tb_ref, td_ref, ts_ref, cb_ref, cd_ref, cs_ref):
    tile = lax.axis_index("tile")
    mine, core = tile // 2, tile % 2
    for source, target in ((tb_ref, cb_ref), (td_ref, cd_ref), (ts_ref, cs_ref)):
        own, own8 = [], []
        for k in range(3):
            rows = source[pl.ds(pl.multiple_of(8 * (3 * mine + k), 8), 8), :]
            tail = source[pl.ds(main + 3 * mine + k, 1), :]
            own += [rows[:, :128], rows[:, 128:]]
            own8 += [tail[:, :128], tail[:, 128:]]
        for m in range(3):
            cols = slice(m * 128, (m + 1) * 128)
            target[0:8, cols] = jnp.where(core == 0, own[m], own[m + 3])
            target[8:9, cols] = jnp.where(core == 0, own8[m], own8[m + 3])


def point_kernel(
    n_grp, back_ref, jp_ref, pidx_ref, pb_ref, pd_ref, pu_ref, cb_ref, cd_ref, cs_ref,
    out_ref, ps_ref, pe_ref, sc_ref,
):
    slot = back_ref.shape[2] - 128
    index = pidx_ref[...]
    mask = is_row(index >> LO_BITS, PH)
    hot = one_hot_rows(index & (LO - 1), LO)
    jp = [jp_ref[k : k + 1, :] for k in range(6)]
    scalars = back_ref[0, :, slot:]
    for h in range(1, n_grp):
        scalars = scalars + back_ref[h, :, slot:]
    gamma, delta = scalars[0:1, 0:1], scalars[1:2, 0:1]
    alpha = gamma / delta
    w = [
        jnp.concatenate([back_ref[h, r : r + 1, 0:slot] for h in range(n_grp)], axis=1) for r in range(4)
    ]
    rhs, diag = pb_ref[...], pd_ref[...]
    z = rhs / diag
    error = [pu_ref[a : a + 1, :] + w[a] for a in range(2)]
    s = z + scatter_points(mask, hot, jp_ref[0:3, :] * error[0] + jp_ref[3:6, :] * error[1])
    r1 = rhs - alpha * s
    z1 = r1 / diag
    at = gather_points(mask, hot, z1)
    error = [
        sum(jp[3 * a + i] * at[i] for i in range(3)) + (w[a] - alpha * w[2 + a]) for a in range(2)
    ]
    ps_ref[...] = s
    pe_ref[0:1, :] = error[0]
    pe_ref[1:2, :] = error[1]
    cr1 = cb_ref[...] - alpha * cs_ref[...]
    cz1 = cr1 / cd_ref[...]
    gamma1 = total_of(r1 * z1) + total_of(cr1 * cz1)
    delta1 = (
        total_of(error[0] * error[0] + error[1] * error[1]) + total_of(z1 * z1) + total_of(cz1 * cz1)
    )
    sc_ref[...] = lanes(jnp.concatenate([gamma, alpha], axis=0), 128)
    tail = lanes(jnp.concatenate([gamma1, delta1], axis=0), 128)
    per = out_ref.shape[0] // n_grp
    for h in range(n_grp):
        cols = slice(h * slot, (h + 1) * slot)
        block = jnp.concatenate([jnp.concatenate([e[:, cols] for e in error], axis=0), tail], axis=1)

        @pl.loop(0, per)
        def _(tile, block=block, h=h):
            out_ref[h * per + tile] = block


def last_point_sums_kernel(jp_ref, pidx_ref, pe_ref, pt_ref):
    index = pidx_ref[...]
    mask = is_row(index >> LO_BITS, PH)
    hot = one_hot_rows(index & (LO - 1), LO)
    terms = jp_ref[0:3, :] * pe_ref[0:1, :] + jp_ref[3:6, :] * pe_ref[1:2, :]
    pt_ref[...] = scatter_points(mask, hot, terms)


def final_kernel(
    err_ref, a_ref, b_ref, pb_ref, pd_ref, ps_ref, pt_ref, cb_ref, cd_ref, cs_ref, sc_ref,
    px_ref, cx_ref, pr_ref, cr_ref, acc_ref,
):
    blocks, _, slot = a_ref.shape
    per = min(8, blocks)
    chunks = blocks // per
    tile = lax.axis_index("tile")
    core = tile % 2
    acc_ref[...] = jnp.zeros(acc_ref.shape, F32)

    def body(ref, parity):
        def step(chunk, scalars):
            numbers = chunk_of(chunk, per)
            x, index = read_blocks(ref, numbers)
            errs = [err_ref[2 * k + parity] for k in numbers]
            e = jnp.concatenate([v[:, 0:slot] for v in errs], axis=1)
            for v in errs:
                scalars = scalars + v[:, slot:]
            index = index - tile * CAM_DEV
            hi = index >> 7
            hot = one_hot_rows(index & 127, 128)
            j0, j1 = x[0:8], x[8:16]
            e0, e1 = e[0:1], e[1:2]
            acc_ref[...] += scatter_mixed(
                hi, hot, [j0 * e0 + j1 * e1], [x[16:17] * e0 + x[17:18] * e1], 4, 16
            )
            return scalars

        return step

    scalars = lax.fori_loop(0, chunks, body(a_ref, core), jnp.zeros((2, 128), F32))
    scalars = lax.fori_loop(0, chunks, body(b_ref, 1 - core), scalars)
    gamma1, delta1 = scalars[0:1, 0:1], scalars[1:2, 0:1]
    gamma, alpha = sc_ref[0:1, 0:1], sc_ref[1:2, 0:1]
    ratio = gamma1 / gamma
    alpha1 = gamma1 / (delta1 - ratio * gamma1 / alpha)

    rhs, diag, s = pb_ref[...], pd_ref[...], ps_ref[...]
    z = rhs / diag
    r1 = rhs - alpha * s
    z1 = r1 / diag
    x = alpha * z + alpha1 * (z1 + ratio * z)
    r2 = r1 - alpha1 * (z1 + pt_ref[...] + ratio * s)
    for i in range(3):
        for hi in range(PH):
            row = i * PH + hi
            px_ref[i : i + 1, hi * LO : (hi + 1) * LO] = x[row : row + 1]
            pr_ref[i : i + 1, hi * LO : (hi + 1) * LO] = r2[row : row + 1]

    rhs, s = cb_ref[...], cs_ref[...]
    z = rhs / cd_ref[...]
    r1 = rhs - alpha * s
    z1 = r1 / cd_ref[...]
    cx_ref[...] = alpha * z + alpha1 * (z1 + ratio * z)
    sums = both(acc_ref[...])
    base = r1 - alpha1 * (z1 + ratio * s)
    for k in range(3):
        cols = slice(k * 128, (k + 1) * 128)
        cr_ref[0:8, cols] = base[0:8, cols] - alpha1 * sums[8 * k : 8 * k + 8, :]
        cr_ref[8:9, cols] = base[8:9, cols] - alpha1 * sums[32 + k : 33 + k, :]


def shape(*dims):
    return jax.ShapeDtypeStruct(dims, F32)


def replicated(jac_point, jac_cam, resid, point_index, cam_index):
    n_grp, n_tile = lax.axis_size("grp"), lax.axis_size("tile")
    n_z = n_tile // 2
    obs = jac_point.shape[1]
    slot = obs // n_grp
    blocks = n_grp * n_z
    count = CAM_DEV * n_tile // LO
    tail_rows = -(-count // 16) * 16
    rows = 8 * count + tail_rows
    groups = [[d * 2 + core for d in range(blocks)] for core in range(2)]
    swap = [(t, t ^ 1) for t in range(n_tile)]
    pidx, cidx = point_index.reshape(1, obs), cam_index.reshape(1, obs)

    hbm = pl.BlockSpec(memory_space=pltpu.HBM)
    packed, pb, pd, pu, jp, pidx = pl.pallas_call(
        functools.partial(pack_kernel, n_grp, n_z),
        in_specs=[hbm] * 5,
        out_shape=(
            shape(blocks, 24, slot),
            shape(3 * PH, LO),
            shape(3 * PH, LO),
            shape(2, obs),
            shape(6, obs),
            jax.ShapeDtypeStruct((1, obs), jnp.int32),
        ),
        scratch_shapes=[
            pltpu.VMEM((18, obs), F32),
            pltpu.VMEM((2, obs), F32),
            pltpu.VMEM((1, obs), jnp.int32),
            pltpu.SemaphoreType.DMA((5,)),
        ],
        compiler_params=PARAMS,
        name="pack",
    )(*(pltpu.with_memory_space_constraint(x, pltpu.HBM) for x in (jac_point, jac_cam, resid, pidx, cidx)))
    own = lax.all_to_all(packed, ("grp", "tile"), 0, 0, axis_index_groups=groups, tiled=True)
    other = lax.ppermute(own, "tile", swap)
    sums = pl.pallas_call(
        functools.partial(own_sums_kernel, count, tail_rows),
        out_shape=shape(4 * rows, LO),
        compiler_params=PARAMS,
        name="own_sums",
        cost_estimate=pl.CostEstimate(flops=2 * 10**9, bytes_accessed=10**6, transcendentals=0),
    )(own)
    table = shape(rows, LO)
    back, tb, td, ts = pl.pallas_call(
        functools.partial(camera_kernel, n_grp, n_z, count, tail_rows),
        out_shape=(shape(n_grp, 4, slot + 128), table, table, table),
        scratch_shapes=[
            pltpu.VMEM((4 * rows, LO), F32),
            pltpu.VMEM((blocks, 2, slot), F32),
            pltpu.VMEM((2 * rows, LO), BF16),
        ],
        compiler_params=PARAMS,
        name="cameras",
    )(own, other, sums)
    back = lax.all_to_all(back, "grp", 0, 0, tiled=True)
    cb, cd, cs = pl.pallas_call(
        functools.partial(mine_kernel, 8 * count),
        out_shape=(shape(9, CAM_DEV),) * 3,
        compiler_params=PARAMS,
        name="mine",
    )(tb, td, ts)
    errors, ps, pe, sc = pl.pallas_call(
        functools.partial(point_kernel, n_grp),
        out_shape=(
            shape(n_grp * n_tile, 2, slot + 128),
            shape(3 * PH, LO),
            shape(2, obs),
            shape(2, 128),
        ),
        compiler_params=PARAMS,
        name="points",
    )(back, jp, pidx, pb, pd, pu, cb, cd, cs)
    errors = lax.all_to_all(errors, ("grp", "tile"), 0, 0, tiled=True)
    pt = pl.pallas_call(
        last_point_sums_kernel,
        out_shape=shape(3 * PH, LO),
        compiler_params=PARAMS,
        name="last_point_sums",
    )(jp, pidx, pe)
    return pl.pallas_call(
        final_kernel,
        out_shape=(shape(3, P_DEV), shape(9, CAM_DEV), shape(3, P_DEV), shape(9, CAM_DEV)),
        scratch_shapes=[pltpu.VMEM((96, 128), F32)],
        compiler_params=PARAMS,
        name="finish",
    )(errors, own, other, pb, pd, ps, pt, cb, cd, cs, sc)


def eights(row):
    return jnp.broadcast_to(row, (8, row.shape[1]))


def row_numbers(width):
    return lax.broadcasted_iota(jnp.int32, (16, width), 0)


def as_16_bit(numbers):
    return numbers.astype(F32).astype(BF16)


def masked_rows(parts, masks):
    none = jnp.zeros(parts[0].shape, BF16)
    return jnp.concatenate([jnp.where(m, p, none) for p in parts for m in masks], axis=0)


def low_lanes(rows):
    return lax.broadcasted_iota(jnp.int32, (rows, HALF), 1) < SLOTS


def swap_lanes(v):
    return pltpu.roll(v, SLOTS, 1)


def point_sums(pidx_ref, jp_ref, res_ref):
    index = pidx_ref[...]
    mask = is_row(index >> LO_BITS, PH)
    hot = one_hot_rows(index & (LO - 1), LO)
    jp = jp_ref[0:3, :], jp_ref[3:6, :]
    grad = -(jp[0] * res_ref[0:1, :] + jp[1] * res_ref[1:2, :])
    square = jp[0] * jp[0] + jp[1] * jp[1]
    return scatter_points(mask, hot, jnp.concatenate([grad, square], axis=0)), mask, hot, jp


def start_copies(pairs, sems):
    copies = [pltpu.make_async_copy(a, b, sems.at[k]) for k, (a, b) in enumerate(pairs)]
    for copy in copies:
        copy.start()
    for copy in copies:
        copy.wait()


def route_kernel(
    n_grp, n_tile, jp_hbm, jc_hbm, res_hbm, pidx_hbm, cidx_hbm,
    out_ref, pb_ref, pd_ref, pu_ref, jp_ref, pidx_ref, place_ref, sc_ref,
    jc_ref, res_ref, cidx_ref, sems,
):
    start_copies(
        (
            (pidx_hbm, pidx_ref),
            (jp_hbm, jp_ref),
            (res_hbm, res_ref),
            (jc_hbm, jc_ref),
            (cidx_hbm, cidx_ref),
        ),
        sems,
    )
    slot = cidx_ref.shape[1] // n_grp
    cams = cidx_ref[...]
    owner = ((cams >> 7) * 171) >> 9
    local = (cams - owner * CAM_DEV).astype(F32)
    mine = is_row(owner, n_tile)
    ones = jnp.where(mine, 1.0, 0.0)
    stack = jnp.concatenate([ones[:, h * slot : (h + 1) * slot] for h in range(n_grp)], axis=0)
    before = lax.broadcasted_iota(jnp.int32, (slot, slot), 0)
    before = before < lax.broadcasted_iota(jnp.int32, (slot, slot), 1)
    counts = dot_nn(stack.astype(BF16), jnp.where(before, 1.0, 0.0).astype(BF16))
    counts = jnp.concatenate([counts[h * n_tile : (h + 1) * n_tile] for h in range(n_grp)], axis=1)
    rank = jnp.sum(jnp.where(mine, counts, 0.0), axis=0, keepdims=True)
    place_ref[0:1, :] = owner
    place_ref[1:2, :] = rank.astype(jnp.int32)
    over = jnp.max(jnp.where(rank >= SLOTS, 1.0, 0.0), axis=1, keepdims=True)
    rank = rank.astype(jnp.int32)
    hot_rank = one_hot_rows(rank, HALF)
    wide = sixteen(owner)
    numbers = row_numbers(owner.shape[1])
    core = lax.axis_index("tile") % 2
    upper, lower, others = core, 1 + core, 2 - 2 * core
    low = low_lanes(8)

    def route_main(h):
        cols = slice(h * slot, (h + 1) * slot)
        here = [wide[:, cols] == BF16(t) for t in range(n_tile)]
        parts = two_parts(jnp.concatenate([jc_ref[0:8, cols], jc_ref[9:17, cols]], axis=0))
        moved = both(dot_nt(masked_rows(parts, here), hot_rank[:, cols]))
        for t in range(n_tile):
            first, second = moved[16 * t : 16 * t + 8], moved[16 * t + 8 : 16 * t + 16]
            tile = jnp.where(low, first, swap_lanes(second))
            out_ref[3 * (h * n_tile + t) + upper] = tile[0:4]
            out_ref[3 * (h * n_tile + t) + lower] = tile[4:8]

    def route_rest(parts, here, h):
        cols = slice(h * slot, (h + 1) * slot)
        left = masked_rows([p[:, cols] for p in parts], [m[:, cols] for m in here])
        moved = both(dot_nt(left, hot_rank[:, cols]))
        for t in range(n_tile):
            rows = moved[8 * t : 8 * t + 8]
            tile = jnp.where(low[0:4], rows[0:4], swap_lanes(rows)[4:8])
            out_ref[3 * (h * n_tile + t) + others] = tile

    table, mask, hot, jp = point_sums(pidx_ref, jp_ref, res_ref)
    for h in range(n_grp // 2):
        route_main(h)
    rhs, diag = table[: 3 * PH], table[3 * PH :] + DAMPING
    z = rhs / diag
    at = gather_points(mask, hot, z)
    for h in range(n_grp // 2, n_grp):
        route_main(h)
    pb_ref[...] = rhs
    pd_ref[...] = diag
    u = [sum(jp[a][i : i + 1] * at[i] for i in range(3)) for a in range(2)]
    pu_ref[0:1, :] = u[0]
    pu_ref[1:2, :] = u[1]
    sc_ref[...] = lanes(jnp.concatenate([total_of(rhs * z), total_of(z * z), over], axis=0), HALF)
    rows = [jc_ref[8:9, :], res_ref[0:1, :], local, u[0], jc_ref[17:18, :], res_ref[1:2, :], local, u[1]]
    parts = two_parts(jnp.concatenate(rows * 2, axis=0))
    here = [wide == as_16_bit((numbers >> 3) + t) for t in range(0, n_tile, 2)]
    for h in range(n_grp):
        route_rest(parts, here, h)


def unfold(even, odd):
    low = low_lanes(even.shape[0])
    return jnp.where(low, even, swap_lanes(odd)), jnp.where(low, swap_lanes(even), odd)


def unfold_rest(both_rows):
    low, swapped = low_lanes(4), swap_lanes(both_rows)
    return (
        jnp.where(low, both_rows[0:4], swapped[4:8]),
        jnp.where(low, swapped[0:4], both_rows[4:8]),
    )


def side_by_side(even, odd):
    return jnp.where(low_lanes(even.shape[0]), even, swap_lanes(odd))


def read_routed(ref, sources):
    main, rest = ([], []), ([], [])
    for s in sources[::2]:
        tile = 3 * (s // 2)
        pair = unfold(ref[tile], ref[tile + 2])
        pair_rest = unfold_rest(ref[tile + 1])
        for a in range(2):
            main[a].append(pair[a])
            rest[a].append(pair_rest[a])
    main = [jnp.concatenate(v, axis=1) for v in main]
    rest = [jnp.concatenate(v, axis=1) for v in rest]
    index = rest[0][2:3].astype(jnp.int32)
    return main, rest, (index >> 7).astype(F32), one_hot_rows(index & 127, 128)


OWN_ROWS = 32
STEP = 32


def scatter_two(hi, hot, first, second):
    wide, numbers = sixteen(hi), row_numbers(hi.shape[1])
    blocks = [wide == BF16(k) for k in range(3)]
    tail = wide == as_16_bit(numbers & 7)
    rows = two_parts(jnp.concatenate([first[0], second[0]], axis=0))
    tails = two_parts(jnp.concatenate([eights(first[1]), eights(second[1])], axis=0))
    none = jnp.zeros(wide.shape, BF16)
    pieces = []
    for part in range(2):
        pieces += [jnp.where(mask, rows[part], none) for mask in blocks]
        pieces.append(jnp.where(tail, tails[part], none))
    return both(dot_nt(jnp.concatenate(pieces, axis=0), hot))


def scatter_one(hi, hot, main, tail):
    wide, numbers = sixteen(hi), row_numbers(hi.shape[1])
    upper = wide == as_16_bit(numbers >> 3)
    lower = wide == as_16_bit(jnp.where(numbers < 8, 2, numbers - 8))
    rows = two_parts(jnp.concatenate([main, main], axis=0))
    tails = two_parts(jnp.concatenate([main, eights(tail)], axis=0))
    none = jnp.zeros(wide.shape, BF16)
    pieces = []
    for part in range(2):
        pieces += [jnp.where(upper, rows[part], none), jnp.where(lower, tails[part], none)]
    return both(dot_nt(jnp.concatenate(pieces, axis=0), hot))


def gather_own(hi, hot, table, main, rest):
    found = both(dot_nn(table, hot))
    block = eights(hi)
    at = jnp.where(block == 0, found[0:8], jnp.where(block == 1, found[8:16], found[16:24]))
    numbers = lax.broadcasted_iota(jnp.int32, block.shape, 0).astype(F32)
    tail = jnp.where(block == numbers, found[24:32], 0.0)
    return [
        jnp.sum(main[a] * at + eights(rest[a][0:1]) * tail, axis=0, keepdims=True) for a in range(2)
    ]


def scatter_j(hi, hot, main, rest, e):
    return scatter_one(
        hi, hot, main[0] * e[0] + main[1] * e[1], rest[0][0:1] * e[0] + rest[1][0:1] * e[1]
    )


def owner_kernel(in_ref, sc_ref, back_ref, tb_ref, td_ref, ts_ref, acc_ref, zz_ref, w_ref, *kept):
    devices = back_ref.shape[0]
    per = min(STEP, devices)
    steps = devices // per

    if steps == 1:
        main, rest, hi, hot = read_routed(in_ref, range(devices))
        kept[0][...] = hot
        for a in range(2):
            kept[1][8 * a : 8 * a + 8, :] = main[a]
            kept[1][16 + a : 17 + a, :] = rest[a][0:1]
        kept[1][18:19, :] = hi

        def loop(body, start):
            return body((main, rest, hi, hot), 0, start)
    else:

        def loop(body, start):
            def step(number, carry):
                return body(read_routed(in_ref, chunk_of(number, per)), number, carry)

            return lax.fori_loop(0, steps, step, start)

    def rhs_and_diag(slots, number, carry):
        main, rest, hi, hot = slots
        r = [rest[a][1:2] for a in range(2)]
        rhs = (-(main[0] * r[0] + main[1] * r[1]), -(rest[0][0:1] * r[0] + rest[1][0:1] * r[1]))
        square = (
            main[0] * main[0] + main[1] * main[1],
            rest[0][0:1] * rest[0][0:1] + rest[1][0:1] * rest[1][0:1],
        )
        acc_ref[...] += scatter_two(hi, hot, rhs, square)
        return carry

    acc_ref[...] = jnp.zeros(acc_ref.shape, F32)
    loop(rhs_and_diag, 0)
    rhs = jnp.concatenate([acc_ref[16 * k : 16 * k + 8, :] for k in range(4)], axis=0)
    diag = jnp.concatenate([acc_ref[16 * k + 8 : 16 * k + 16, :] for k in range(4)], axis=0) + DAMPING
    tb_ref[...] = rhs
    td_ref[...] = diag
    z = rhs / diag
    zz_ref[...] = stacked(z)
    acc_ref[0:OWN_ROWS, :] = z

    def apply(slots, number, energy):
        main, rest, hi, hot = slots
        w = gather_own(hi, hot, zz_ref[...], main, rest)
        e = [rest[a][3:4] + w[a] for a in range(2)]
        for a in range(2):
            w_ref[number, a : a + 1, :] = w[a]
        acc_ref[0:OWN_ROWS, :] += scatter_j(hi, hot, main, rest, e)
        return energy + e[0] * e[0] + e[1] * e[1]

    energy = loop(apply, jnp.zeros((1, per * SLOTS), F32))
    s = acc_ref[0:OWN_ROWS, :]
    ts_ref[...] = s
    zz_ref[...] = stacked(s / diag)
    gamma = sc_ref[0:1, :] + total_of(rhs * z)
    delta = sc_ref[1:2, :] + total_of(z * z) + total_of(energy)
    tail = jnp.concatenate([gamma, delta, sc_ref[2:3, :], sc_ref[2:3, :]], axis=0)

    def send(slots, number, carry):
        main, rest, hi, hot = slots
        v = gather_own(hi, hot, zz_ref[...], main, rest)
        for a in range(2):
            w_ref[number, 2 + a : 3 + a, :] = v[a]
        w = w_ref[number]
        low = low_lanes(4)
        for k in range(per // 2):
            pair = w[:, k * HALF : (k + 1) * HALF]
            back_ref[number * per + 2 * k] = jnp.where(low, pair, tail)
            back_ref[number * per + 2 * k + 1] = jnp.where(low, swap_lanes(pair), tail)
        return carry

    loop(send, 0)


def routed_point_kernel(
    n_grp, n_tile, back_ref, jp_ref, pidx_ref, place_ref, pb_ref, pd_ref, pu_ref, cb_ref, cd_ref, cs_ref,
    out_ref, ps_ref, pe_ref, sc_ref, over_ref,
):
    slot = place_ref.shape[1] // n_grp
    index = pidx_ref[...]
    mask = is_row(index >> LO_BITS, PH)
    hot = one_hot_rows(index & (LO - 1), LO)
    jp = [jp_ref[k : k + 1, :] for k in range(6)]
    scalars = jnp.sum(back_ref[...], axis=0)[:, SLOTS : SLOTS + 1]
    scalars = scalars[0:4] + scalars[4:8]
    gamma, delta = scalars[0:1], scalars[1:2]
    over_ref[...] = lanes(scalars[2:3], HALF)
    alpha = gamma / delta
    owner = place_ref[0:1, :]
    slots = one_hot_rows(place_ref[1:2, :], HALF)
    numbers = lax.broadcasted_iota(jnp.int32, (4 * n_tile, slot), 0) >> 2
    terms = []
    for h in range(n_grp):
        cols = slice(h * slot, (h + 1) * slot)
        rows = jnp.concatenate([back_ref[h * n_tile // 2 + k] for k in range(n_tile // 2)], axis=0)
        found = both(dot_nn(stacked(rows), slots[:, cols]))
        found = jnp.where(numbers == owner[:, cols], found, 0.0)
        found = sum(found[8 * k : 8 * k + 8] for k in range(n_tile // 2))
        terms.append(found[0:4] + found[4:8])
    terms = jnp.concatenate(terms, axis=1)
    w0 = [terms[a : a + 1] for a in range(2)]
    w1 = [terms[2 + a : 3 + a] for a in range(2)]
    rhs, diag = pb_ref[...], pd_ref[...]
    z = rhs / diag
    error = [pu_ref[a : a + 1, :] + w0[a] for a in range(2)]
    s = z + scatter_points(mask, hot, jp_ref[0:3, :] * error[0] + jp_ref[3:6, :] * error[1])
    r1 = rhs - alpha * s
    z1 = r1 / diag
    at = gather_points(mask, hot, z1)
    error = [sum(jp[3 * a + i] * at[i] for i in range(3)) + (w0[a] - alpha * w1[a]) for a in range(2)]
    ps_ref[...] = s
    pe_ref[0:1, :] = error[0]
    pe_ref[1:2, :] = error[1]
    cr1 = cb_ref[...] - alpha * cs_ref[...]
    cz1 = cr1 / cd_ref[...]
    gamma1 = total_of(r1 * z1) + total_of(cr1 * cz1)
    delta1 = (
        total_of(error[0] * error[0] + error[1] * error[1]) + total_of(z1 * z1) + total_of(cz1 * cz1)
    )
    sc_ref[...] = lanes(jnp.concatenate([gamma, alpha], axis=0), HALF)
    tail = lanes(jnp.concatenate([gamma1, delta1], axis=0), HALF)
    low = low_lanes(2)
    numbers = row_numbers(slot)
    for h in range(n_grp):
        cols = slice(h * slot, (h + 1) * slot)
        first, second = (jnp.broadcast_to(e[:, cols], (16, slot)) for e in error)
        parts = two_parts(jnp.where((numbers & 1) == 0, first, second))
        wide = sixteen(owner[:, cols])
        here = [wide == as_16_bit((numbers >> 1) + t) for t in range(0, n_tile, 8)]
        moved = both(dot_nt(masked_rows(parts, here), slots[:, cols]))
        for t in range(n_tile):
            out_ref[h * n_tile + t] = jnp.where(low, moved[2 * t : 2 * t + 2], tail)


def point_results(alpha, alpha1, ratio, pb_ref, pd_ref, ps_ref, pt_ref, px_ref, pr_ref, copies):
    rhs, diag, s = pb_ref[...], pd_ref[...], ps_ref[...]
    z = rhs / diag
    r1 = rhs - alpha * s
    z1 = r1 / diag
    x = alpha * z + alpha1 * (z1 + ratio * z)
    r2 = r1 - alpha1 * (z1 + pt_ref[...] + ratio * s)
    for table, target, copy in ((x, px_ref, copies[0]), (r2, pr_ref, copies[1])):
        for i in range(3):
            for hi in range(PH):
                row = i * PH + hi
                target[i : i + 1, hi * LO : (hi + 1) * LO] = table[row : row + 1]
        copy.start()


def routed_final_kernel(
    err_ref, in_ref, jp_ref, pidx_ref, pe_ref, pb_ref, pd_ref, ps_ref, cb_ref, cd_ref, cs_ref, sc_ref, *rest_refs
):
    kept, outs, (px_ref, cx_ref, pr_ref, cr_ref, acc_ref, pt_ref, sems) = (
        rest_refs[:-11],
        rest_refs[-11:-7],
        rest_refs[-7:],
    )
    devices = err_ref.shape[0]
    per = min(STEP, devices)
    steps = devices // per

    def body(step, carry):
        sources = chunk_of(step, per)
        if kept:
            hot, rows = kept[0][...], kept[1]
            main = [rows[8 * a : 8 * a + 8, :] for a in range(2)]
            rest = [rows[16 + a : 17 + a, :] for a in range(2)]
            hi = rows[18:19, :]
        else:
            main, rest, hi, hot = read_routed(in_ref, sources)
        e = jnp.concatenate(
            [side_by_side(err_ref[s], err_ref[t]) for s, t in zip(sources[::2], sources[1::2])], axis=1
        )
        acc_ref[...] += scatter_j(hi, hot, main, rest, [e[0:1], e[1:2]])
        return carry

    acc_ref[...] = jnp.zeros(acc_ref.shape, F32)
    if steps == 1:
        body(0, 0)
    else:
        lax.fori_loop(0, steps, body, 0)
    last_point_sums_kernel(jp_ref, pidx_ref, pe_ref, pt_ref)
    scalars = jnp.sum(err_ref[...], axis=0)
    gamma1, delta1 = scalars[0:1, SLOTS : SLOTS + 1], scalars[1:2, SLOTS : SLOTS + 1]
    gamma, alpha = sc_ref[0:1, 0:1], sc_ref[1:2, 0:1]
    ratio = gamma1 / gamma
    alpha1 = gamma1 / (delta1 - ratio * gamma1 / alpha)
    copies = [
        pltpu.make_async_copy(here, there, sems.at[k])
        for k, (here, there) in enumerate(zip((px_ref, cx_ref, pr_ref, cr_ref), outs))
    ]
    point_results(
        alpha, alpha1, ratio, pb_ref, pd_ref, ps_ref, pt_ref, px_ref, pr_ref, (copies[0], copies[2])
    )
    rhs, s = cb_ref[...], cs_ref[...]
    z = rhs / cd_ref[...]
    r1 = rhs - alpha * s
    z1 = r1 / cd_ref[...]
    x = alpha * z + alpha1 * (z1 + ratio * z)
    r2 = r1 - alpha1 * (z1 + acc_ref[...] + ratio * s)
    for table, target in ((x, cx_ref), (r2, cr_ref)):
        for k in range(3):
            cols = slice(k * 128, (k + 1) * 128)
            target[0:8, cols] = table[8 * k : 8 * k + 8]
            target[8:9, cols] = table[24 + k : 25 + k]
    copies[1].start()
    copies[3].start()
    for copy in copies:
        copy.wait()


def shards(jac_point, jac_cam, resid, point_index, cam_index):
    n_grp, n_tile = lax.axis_size("grp"), lax.axis_size("tile")
    devices = n_grp * n_tile
    obs = jac_point.shape[1]
    pidx, cidx = point_index.reshape(1, obs), cam_index.reshape(1, obs)
    hbm = pl.BlockSpec(memory_space=pltpu.HBM)
    ints = jax.ShapeDtypeStruct((1, obs), jnp.int32)
    places = jax.ShapeDtypeStruct((2, obs), jnp.int32)
    points = shape(3 * PH, LO)
    cameras = shape(OWN_ROWS, 128)
    routed, pb, pd, pu, jp, pidx_here, place, sc = pl.pallas_call(
        functools.partial(route_kernel, n_grp, n_tile),
        in_specs=[hbm] * 5,
        out_shape=(shape(3 * devices, 4, HALF), points, points, shape(2, obs), shape(6, obs), ints, places, shape(3, HALF)),
        scratch_shapes=[
            pltpu.VMEM((18, obs), F32),
            pltpu.VMEM((2, obs), F32),
            pltpu.VMEM((1, obs), jnp.int32),
            pltpu.SemaphoreType.DMA((5,)),
        ],
        compiler_params=PARAMS,
        name="route",
    )(*(pltpu.with_memory_space_constraint(x, pltpu.HBM) for x in (jac_point, jac_cam, resid, pidx, cidx)))
    routed = lax.all_to_all(routed, ("grp", "tile"), 0, 0, tiled=True).reshape(3 * devices // 2, 8, HALF)
    slots = devices * SLOTS
    per = min(STEP, devices)
    scratch = [
        pltpu.VMEM((2 * OWN_ROWS, 128), F32),
        pltpu.VMEM((2 * OWN_ROWS, 128), BF16),
        pltpu.VMEM((devices // per, 4, per * SLOTS), F32),
    ]
    kept_shapes = ()
    if devices == per:
        kept_shapes = (jax.ShapeDtypeStruct((128, slots), BF16), shape(24, slots))

    def owner(in_ref, sc_ref, back_ref, tb_ref, td_ref, ts_ref, *others):
        kept, work = others[: len(kept_shapes)], others[len(kept_shapes) :]
        owner_kernel(in_ref, sc_ref, back_ref, tb_ref, td_ref, ts_ref, *work, *kept)

    back, tb, td, ts, *kept = pl.pallas_call(
        owner,
        out_shape=(shape(devices, 4, HALF), cameras, cameras, cameras) + kept_shapes,
        scratch_shapes=scratch,
        compiler_params=PARAMS,
        name="owner",
    )(routed, sc)
    back = lax.all_to_all(back, ("grp", "tile"), 0, 0, tiled=True).reshape(devices // 2, 8, HALF)
    errors, ps, pe, sc, over = pl.pallas_call(
        functools.partial(routed_point_kernel, n_grp, n_tile),
        out_shape=(shape(devices, 2, HALF), points, shape(2, obs), shape(2, HALF), shape(1, HALF)),
        compiler_params=PARAMS,
        name="points",
    )(back, jp, pidx_here, place, pb, pd, pu, tb, td, ts)
    outputs = (shape(3, P_DEV), shape(9, CAM_DEV), shape(3, P_DEV), shape(9, CAM_DEV))

    def fits(*operands):
        errors = lax.all_to_all(operands[5], ("grp", "tile"), 0, 0, tiled=True)
        return pl.pallas_call(
            routed_final_kernel,
            out_shape=outputs,
            out_specs=[hbm] * 4,
            scratch_shapes=[pltpu.VMEM(v.shape, F32) for v in outputs]
            + [
                pltpu.VMEM((OWN_ROWS, 128), F32),
                pltpu.VMEM((3 * PH, LO), F32),
                pltpu.SemaphoreType.DMA((4,)),
            ],
            compiler_params=PARAMS,
            name="finish",
        )(errors, *operands[6:])

    def overflows(*operands):
        return tuple(replicated(*operands[:5]))

    over, *operands = lax.optimization_barrier(
        (
            over, jac_point, jac_cam, resid, point_index, cam_index,
            errors, routed, jp, pidx_here, pe, pb, pd, ps, tb, td, ts, sc, *kept,
        )
    )
    return lax.cond(over[0, 0] > 0, overflows, lambda *operands: tuple(fits(*operands)), *operands)


def solution(mesh):
    placed = (
        P(None, ("grp", "tile")),
        P(None, ("grp", "tile")),
        P(None, ("grp", "tile")),
        P(("grp", "tile")),
        P(("grp", "tile")),
    )
    return jax.shard_map(
        shards,
        mesh=mesh,
        in_specs=placed,
        out_specs=(P(None, ("grp", "tile")),) * 4,
        check_vma=False,
    )
```

```python
import functools

import jax
import jax.numpy as jnp
from jax import lax
from jax.experimental import pallas as pl
from jax.experimental.pallas import tpu as pltpu
from jax.sharding import PartitionSpec as P

P_DEV = 4096
CAM_DEV = 384
LO_BITS = 8
LO = 1 << LO_BITS
PH = P_DEV // LO
DAMPING = 1.0
F32 = jnp.float32
BF16 = jnp.bfloat16
SLOTS = 64
FULL = SLOTS - 1
HALF = 128
PARAMS = pltpu.CompilerParams(vmem_limit_bytes=48 * 1024 * 1024)


def halves(v):
    high = v.astype(BF16).astype(F32)
    return high, v - high


def rows16(width, step=1):
    numbers = lax.broadcasted_iota(jnp.int32, (16, width), 0)
    return (numbers // step if step > 1 else numbers).astype(F32).astype(BF16)


def sixteen(row):
    return jnp.broadcast_to(row.astype(F32), (16, row.shape[1])).astype(BF16)


def one_hot_rows(index, rows):
    numbers = rows16(index.shape[1])
    pieces = []
    for base in range(0, rows, 256):
        wide = sixteen(index - base)
        one, none = jnp.ones(wide.shape, BF16), jnp.zeros(wide.shape, BF16)
        pieces += [
            jnp.where(wide == numbers + BF16(16 * k), one, none)
            for k in range(min(256, rows - base) // 16)
        ]
    return jnp.concatenate(pieces, axis=0)


def dot_nt(a, b):
    return lax.dot_general(a, b, (((1,), (1,)), ((), ())), preferred_element_type=F32)


def dot_nn(a, b):
    return lax.dot_general(a, b, (((1,), (0,)), ((), ())), preferred_element_type=F32)


def is_row(hi, rows):
    return lax.broadcasted_iota(jnp.int32, (rows, hi.shape[1]), 0) == hi


def spread_row(mask, row):
    return jnp.where(mask, jnp.broadcast_to(row, mask.shape), 0.0)


def two_parts(v):
    high = v.astype(BF16)
    return high, (v - high.astype(F32)).astype(BF16)


def scatter_mixed(hi, hot, mains, tails, count, tail_rows):
    wide = sixteen(hi)
    none = jnp.zeros(wide.shape, BF16)
    single = len(mains) == 1
    numbers = rows16(hi.shape[1], 8) if single else none
    main_parts = two_parts(jnp.concatenate(mains * 2 if single else mains, axis=0))
    tail_parts = [two_parts(jnp.broadcast_to(v, wide.shape)) for v in tails]
    here = [wide == numbers + BF16(k) for k in range(0, count, 2 if single else 1)]
    tail_here = [wide == rows16(hi.shape[1]) + BF16(k) for k in range(0, tail_rows, 16)]
    pieces = []
    for part in range(2):
        pieces += [jnp.where(mask, main_parts[part], none) for mask in here]
        pieces += [jnp.where(mask, v[part], none) for v in tail_parts for mask in tail_here]
    return dot_nt(jnp.concatenate(pieces, axis=0), hot)


def both(v):
    half = v.shape[0] // 2
    return v[:half] + v[half:]


def gather_mixed(hi, hot, table, count, tail_rows):
    found = dot_nn(table, hot)
    hi8 = jnp.broadcast_to(hi, (8, hi.shape[1]))
    main = jnp.zeros(hi8.shape, F32)
    half = found.shape[0] // 2
    for k in range(count):
        rows = slice(k * 8, k * 8 + 8)
        low = slice(half + k * 8, half + k * 8 + 8)
        main = main + jnp.where(hi8 == k, found[rows] + found[low], 0.0)
    tail = found[count * 8 : half] + found[half + count * 8 :]
    tail = jnp.sum(jnp.where(is_row(hi, tail_rows), tail, 0.0), axis=0, keepdims=True)
    return main, tail


def stacked(table):
    high, low = halves(table)
    return jnp.concatenate([high, low], axis=0).astype(BF16)


def scatter_points(mask, hot, rows):
    pieces = [spread_row(mask, v[k : k + 1]) for v in halves(rows) for k in range(rows.shape[0])]
    return both(dot_nt(jnp.concatenate(pieces, axis=0).astype(BF16), hot))


def gather_points(mask, hot, table):
    found = both(dot_nn(stacked(table), hot))
    return [
        jnp.sum(jnp.where(mask, found[i * PH : (i + 1) * PH], 0.0), axis=0, keepdims=True)
        for i in range(found.shape[0] // PH)
    ]


def total_of(v):
    return jnp.sum(jnp.sum(v, axis=0, keepdims=True), axis=1, keepdims=True)


def lanes(v, width):
    return jnp.broadcast_to(v, (v.shape[0], width))


def pack_kernel(
    n_grp, n_z, jp_hbm, jc_hbm, res_hbm, pidx_hbm, cidx_hbm,
    out_ref, pb_ref, pd_ref, pu_ref, jp_ref, pidx_ref,
    jc_ref, res_ref, cidx_ref, sems,
):
    copies = [
        pltpu.make_async_copy(source, target, sems.at[k])
        for k, (source, target) in enumerate(
            (
                (pidx_hbm, pidx_ref),
                (jp_hbm, jp_ref),
                (res_hbm, res_ref),
                (jc_hbm, jc_ref),
                (cidx_hbm, cidx_ref),
            )
        )
    ]
    for copy in copies:
        copy.start()
    for copy in copies:
        copy.wait()
    slot = out_ref.shape[2]
    index = pidx_ref[...]
    mask = is_row(index >> LO_BITS, PH)
    hot = one_hot_rows(index & (LO - 1), LO)
    jp = [jp_ref[k : k + 1, :] for k in range(6)]
    res = [res_ref[a : a + 1, :] for a in range(2)]
    grad = [-(jp[i] * res[0] + jp[3 + i] * res[1]) for i in range(3)]
    square = [jp[i] * jp[i] + jp[3 + i] * jp[3 + i] for i in range(3)]
    table = scatter_points(mask, hot, jnp.concatenate(grad + square, axis=0))
    rhs = table[: 3 * PH]
    diag = table[3 * PH :] + DAMPING
    pb_ref[...] = rhs
    pd_ref[...] = diag
    z = rhs / diag
    at = gather_points(mask, hot, z)
    u = [sum(jp[3 * a + i] * at[i] for i in range(3)) for a in range(2)]
    pu_ref[0:1, :] = u[0]
    pu_ref[1:2, :] = u[1]
    gamma = total_of(rhs * z)
    norm = total_of(z * z)
    scalars = jnp.concatenate([lanes(gamma, slot // 2), lanes(norm, slot // 2)], axis=1)
    cams = cidx_ref[...].astype(F32)
    for h in range(n_grp):
        cols = slice(h * slot, (h + 1) * slot)
        block = jnp.concatenate(
            [
                jc_ref[0:8, cols],
                jc_ref[9:17, cols],
                jc_ref[8:9, cols],
                jc_ref[17:18, cols],
                res[0][:, cols],
                res[1][:, cols],
                u[0][:, cols],
                u[1][:, cols],
                cams[:, cols],
                scalars,
            ],
            axis=0,
        )

        @pl.loop(0, n_z)
        def _(z_to, block=block, h=h):
            out_ref[h * n_z + z_to] = block


def read_blocks(ref, numbers):
    x = jnp.concatenate([ref[k] for k in numbers], axis=1)
    return x, x[22:23].astype(jnp.int32)


def chunk_of(chunk, per):
    return [chunk * per + k for k in range(per)]


def first_sums(ref, acc_ref, per, count, tail_rows):
    def body(chunk, carry):
        x, index = read_blocks(ref, chunk_of(chunk, per))
        hi, hot = index >> LO_BITS, one_hot_rows(index & (LO - 1), LO)
        j0, j1 = x[0:8], x[8:16]
        j08, j18, r0, r1 = x[16:17], x[17:18], x[18:19], x[19:20]
        acc_ref[...] += scatter_mixed(
            hi,
            hot,
            [-(j0 * r0 + j1 * r1), j0 * j0 + j1 * j1],
            [-(j08 * r0 + j18 * r1), j08 * j08 + j18 * j18],
            count,
            tail_rows,
        )
        return carry

    lax.fori_loop(0, ref.shape[0] // per, body, 0)


def own_sums_kernel(count, tail_rows, a_ref, acc_ref):
    acc_ref[...] = jnp.zeros(acc_ref.shape, F32)
    first_sums(a_ref, acc_ref, min(16, a_ref.shape[0]), count, tail_rows)


def camera_kernel(
    n_grp, n_z, count, tail_rows, a_ref, b_ref, start_ref,
    back_ref, tb_ref, td_ref, ts_ref,
    acc_ref, w_ref, zz_ref,
):
    blocks, _, slot = a_ref.shape
    per = min(8, blocks)
    chunks = blocks // per
    acc_ref[...] = start_ref[...]
    first_sums(b_ref, acc_ref, min(16, blocks), count, tail_rows)
    scalars = jnp.zeros((1, slot), F32)
    for ref in (a_ref, b_ref):
        scalars = scalars + jnp.sum(ref[:, 23, :], axis=0, keepdims=True)
    main = 8 * count
    half = acc_ref.shape[0] // 2
    for k in range(count):
        row = 16 * k
        tb_ref[8 * k : 8 * k + 8, :] = acc_ref[row : row + 8, :] + acc_ref[half + row : half + row + 8, :]
        row = 16 * k + 8
        td_ref[8 * k : 8 * k + 8, :] = (
            acc_ref[row : row + 8, :] + acc_ref[half + row : half + row + 8, :] + DAMPING
        )
    tb_ref[main:, :] = (
        acc_ref[2 * main : 2 * main + tail_rows, :]
        + acc_ref[half + 2 * main : half + 2 * main + tail_rows, :]
    )
    td_ref[main:, :] = (
        acc_ref[2 * main + tail_rows : half, :] + acc_ref[half + 2 * main + tail_rows :, :] + DAMPING
    )
    z = tb_ref[...] / td_ref[...]
    gamma = total_of(tb_ref[...] * z)
    norm = total_of(z * z)
    zz_ref[...] = stacked(z)
    ts_ref[...] = z
    acc_ref[0:half, :] = jnp.zeros((half, LO), F32)

    def second(ref, keep):
        def body(chunk, energy):
            numbers = chunk_of(chunk, per)
            x, index = read_blocks(ref, numbers)
            hi, hot = index >> LO_BITS, one_hot_rows(index & (LO - 1), LO)
            j0, j1 = x[0:8], x[8:16]
            j08, j18, u0, u1 = x[16:17], x[17:18], x[20:21], x[21:22]
            at, at8 = gather_mixed(hi, hot, zz_ref[...], count, tail_rows)
            w0 = jnp.sum(j0 * at, axis=0, keepdims=True) + j08 * at8
            w1 = jnp.sum(j1 * at, axis=0, keepdims=True) + j18 * at8
            if keep:
                for k, number in enumerate(numbers):
                    cols = slice(k * slot, (k + 1) * slot)
                    w_ref[number, 0:1, :] = w0[:, cols]
                    w_ref[number, 1:2, :] = w1[:, cols]
            e0, e1 = u0 + w0, u1 + w1
            acc_ref[0:half, :] += scatter_mixed(
                hi, hot, [j0 * e0 + j1 * e1], [j08 * e0 + j18 * e1], count, tail_rows
            )
            return energy + e0 * e0 + e1 * e1

        return body

    energy = jnp.zeros((1, per * slot), F32)
    energy = lax.fori_loop(0, chunks, second(a_ref, True), energy)
    energy = lax.fori_loop(0, chunks, second(b_ref, False), energy)
    ts_ref[...] += both(acc_ref[0:half, :])
    zz_ref[...] = stacked(ts_ref[...] / td_ref[...])
    share = 1.0 / n_grp
    gamma = gamma + share * scalars[:, 0:1]
    delta = norm + total_of(energy) + share * scalars[:, slot // 2 : slot // 2 + 1]
    mine = lax.axis_index("tile") // 2
    numbers = [g * n_z + mine for g in range(n_grp)]
    per = min(4, n_grp)
    for first in range(0, n_grp, per):
        some = numbers[first : first + per]
        x, index = read_blocks(a_ref, some)
        hi, hot = index >> LO_BITS, one_hot_rows(index & (LO - 1), LO)
        at, at8 = gather_mixed(hi, hot, zz_ref[...], count, tail_rows)
        v0 = jnp.sum(x[0:8] * at, axis=0, keepdims=True) + x[16:17] * at8
        v1 = jnp.sum(x[8:16] * at, axis=0, keepdims=True) + x[17:18] * at8
        for k in range(per):
            cols = slice(k * slot, (k + 1) * slot)
            g = first + k
            back_ref[g, 0:2, 0:slot] = w_ref[some[k], 0:2, :]
            back_ref[g, 2:3, 0:slot] = v0[:, cols]
            back_ref[g, 3:4, 0:slot] = v1[:, cols]
            back_ref[g, :, slot:] = lanes(jnp.concatenate([gamma, delta, gamma, delta], axis=0), 128)


def mine_kernel(main, tb_ref, td_ref, ts_ref, cb_ref, cd_ref, cs_ref):
    tile = lax.axis_index("tile")
    mine, core = tile // 2, tile % 2
    for source, target in ((tb_ref, cb_ref), (td_ref, cd_ref), (ts_ref, cs_ref)):
        own, own8 = [], []
        for k in range(3):
            rows = source[pl.ds(pl.multiple_of(8 * (3 * mine + k), 8), 8), :]
            tail = source[pl.ds(main + 3 * mine + k, 1), :]
            own += [rows[:, :128], rows[:, 128:]]
            own8 += [tail[:, :128], tail[:, 128:]]
        for m in range(3):
            cols = slice(m * 128, (m + 1) * 128)
            target[0:8, cols] = jnp.where(core == 0, own[m], own[m + 3])
            target[8:9, cols] = jnp.where(core == 0, own8[m], own8[m + 3])


def point_kernel(
    n_grp, back_ref, jp_ref, pidx_ref, pb_ref, pd_ref, pu_ref, cb_ref, cd_ref, cs_ref,
    out_ref, ps_ref, pe_ref, sc_ref,
):
    slot = back_ref.shape[2] - 128
    index = pidx_ref[...]
    mask = is_row(index >> LO_BITS, PH)
    hot = one_hot_rows(index & (LO - 1), LO)
    jp = [jp_ref[k : k + 1, :] for k in range(6)]
    scalars = back_ref[0, :, slot:]
    for h in range(1, n_grp):
        scalars = scalars + back_ref[h, :, slot:]
    gamma, delta = scalars[0:1, 0:1], scalars[1:2, 0:1]
    alpha = gamma / delta
    w = [
        jnp.concatenate([back_ref[h, r : r + 1, 0:slot] for h in range(n_grp)], axis=1) for r in range(4)
    ]
    rhs, diag = pb_ref[...], pd_ref[...]
    z = rhs / diag
    error = [pu_ref[a : a + 1, :] + w[a] for a in range(2)]
    s = z + scatter_points(mask, hot, jp_ref[0:3, :] * error[0] + jp_ref[3:6, :] * error[1])
    r1 = rhs - alpha * s
    z1 = r1 / diag
    at = gather_points(mask, hot, z1)
    error = [
        sum(jp[3 * a + i] * at[i] for i in range(3)) + (w[a] - alpha * w[2 + a]) for a in range(2)
    ]
    ps_ref[...] = s
    pe_ref[0:1, :] = error[0]
    pe_ref[1:2, :] = error[1]
    cr1 = cb_ref[...] - alpha * cs_ref[...]
    cz1 = cr1 / cd_ref[...]
    gamma1 = total_of(r1 * z1) + total_of(cr1 * cz1)
    delta1 = (
        total_of(error[0] * error[0] + error[1] * error[1]) + total_of(z1 * z1) + total_of(cz1 * cz1)
    )
    sc_ref[...] = lanes(jnp.concatenate([gamma, alpha], axis=0), 128)
    tail = lanes(jnp.concatenate([gamma1, delta1], axis=0), 128)
    per = out_ref.shape[0] // n_grp
    for h in range(n_grp):
        cols = slice(h * slot, (h + 1) * slot)
        block = jnp.concatenate([jnp.concatenate([e[:, cols] for e in error], axis=0), tail], axis=1)

        @pl.loop(0, per)
        def _(tile, block=block, h=h):
            out_ref[h * per + tile] = block


def last_point_sums_kernel(jp_ref, pidx_ref, pe_ref, pt_ref):
    index = pidx_ref[...]
    mask = is_row(index >> LO_BITS, PH)
    hot = one_hot_rows(index & (LO - 1), LO)
    terms = jp_ref[0:3, :] * pe_ref[0:1, :] + jp_ref[3:6, :] * pe_ref[1:2, :]
    pt_ref[...] = scatter_points(mask, hot, terms)


def final_kernel(
    err_ref, a_ref, b_ref, pb_ref, pd_ref, ps_ref, pt_ref, cb_ref, cd_ref, cs_ref, sc_ref,
    px_ref, cx_ref, pr_ref, cr_ref, acc_ref,
):
    blocks, _, slot = a_ref.shape
    per = min(8, blocks)
    chunks = blocks // per
    tile = lax.axis_index("tile")
    core = tile % 2
    acc_ref[...] = jnp.zeros(acc_ref.shape, F32)

    def body(ref, parity):
        def step(chunk, scalars):
            numbers = chunk_of(chunk, per)
            x, index = read_blocks(ref, numbers)
            errs = [err_ref[2 * k + parity] for k in numbers]
            e = jnp.concatenate([v[:, 0:slot] for v in errs], axis=1)
            for v in errs:
                scalars = scalars + v[:, slot:]
            index = index - tile * CAM_DEV
            hi = index >> 7
            hot = one_hot_rows(index & 127, 128)
            j0, j1 = x[0:8], x[8:16]
            e0, e1 = e[0:1], e[1:2]
            acc_ref[...] += scatter_mixed(
                hi, hot, [j0 * e0 + j1 * e1], [x[16:17] * e0 + x[17:18] * e1], 4, 16
            )
            return scalars

        return step

    scalars = lax.fori_loop(0, chunks, body(a_ref, core), jnp.zeros((2, 128), F32))
    scalars = lax.fori_loop(0, chunks, body(b_ref, 1 - core), scalars)
    gamma1, delta1 = scalars[0:1, 0:1], scalars[1:2, 0:1]
    gamma, alpha = sc_ref[0:1, 0:1], sc_ref[1:2, 0:1]
    ratio = gamma1 / gamma
    alpha1 = gamma1 / (delta1 - ratio * gamma1 / alpha)

    rhs, diag, s = pb_ref[...], pd_ref[...], ps_ref[...]
    z = rhs / diag
    r1 = rhs - alpha * s
    z1 = r1 / diag
    x = alpha * z + alpha1 * (z1 + ratio * z)
    r2 = r1 - alpha1 * (z1 + pt_ref[...] + ratio * s)
    for i in range(3):
        for hi in range(PH):
            row = i * PH + hi
            px_ref[i : i + 1, hi * LO : (hi + 1) * LO] = x[row : row + 1]
            pr_ref[i : i + 1, hi * LO : (hi + 1) * LO] = r2[row : row + 1]

    rhs, s = cb_ref[...], cs_ref[...]
    z = rhs / cd_ref[...]
    r1 = rhs - alpha * s
    z1 = r1 / cd_ref[...]
    cx_ref[...] = alpha * z + alpha1 * (z1 + ratio * z)
    sums = both(acc_ref[...])
    base = r1 - alpha1 * (z1 + ratio * s)
    for k in range(3):
        cols = slice(k * 128, (k + 1) * 128)
        cr_ref[0:8, cols] = base[0:8, cols] - alpha1 * sums[8 * k : 8 * k + 8, :]
        cr_ref[8:9, cols] = base[8:9, cols] - alpha1 * sums[32 + k : 33 + k, :]


def shape(*dims):
    return jax.ShapeDtypeStruct(dims, F32)


def replicated(jac_point, jac_cam, resid, point_index, cam_index):
    n_grp, n_tile = lax.axis_size("grp"), lax.axis_size("tile")
    n_z = n_tile // 2
    obs = jac_point.shape[1]
    slot = obs // n_grp
    blocks = n_grp * n_z
    count = CAM_DEV * n_tile // LO
    tail_rows = -(-count // 16) * 16
    rows = 8 * count + tail_rows
    groups = [[d * 2 + core for d in range(blocks)] for core in range(2)]
    swap = [(t, t ^ 1) for t in range(n_tile)]
    pidx, cidx = point_index.reshape(1, obs), cam_index.reshape(1, obs)

    hbm = pl.BlockSpec(memory_space=pltpu.HBM)
    packed, pb, pd, pu, jp, pidx = pl.pallas_call(
        functools.partial(pack_kernel, n_grp, n_z),
        in_specs=[hbm] * 5,
        out_shape=(
            shape(blocks, 24, slot),
            shape(3 * PH, LO),
            shape(3 * PH, LO),
            shape(2, obs),
            shape(6, obs),
            jax.ShapeDtypeStruct((1, obs), jnp.int32),
        ),
        scratch_shapes=[
            pltpu.VMEM((18, obs), F32),
            pltpu.VMEM((2, obs), F32),
            pltpu.VMEM((1, obs), jnp.int32),
            pltpu.SemaphoreType.DMA((5,)),
        ],
        compiler_params=PARAMS,
        name="pack",
    )(*(pltpu.with_memory_space_constraint(x, pltpu.HBM) for x in (jac_point, jac_cam, resid, pidx, cidx)))
    own = lax.all_to_all(packed, ("grp", "tile"), 0, 0, axis_index_groups=groups, tiled=True)
    other = lax.ppermute(own, "tile", swap)
    sums = pl.pallas_call(
        functools.partial(own_sums_kernel, count, tail_rows),
        out_shape=shape(4 * rows, LO),
        compiler_params=PARAMS,
        name="own_sums",
        cost_estimate=pl.CostEstimate(flops=2 * 10**9, bytes_accessed=10**6, transcendentals=0),
    )(own)
    table = shape(rows, LO)
    back, tb, td, ts = pl.pallas_call(
        functools.partial(camera_kernel, n_grp, n_z, count, tail_rows),
        out_shape=(shape(n_grp, 4, slot + 128), table, table, table),
        scratch_shapes=[
            pltpu.VMEM((4 * rows, LO), F32),
            pltpu.VMEM((blocks, 2, slot), F32),
            pltpu.VMEM((2 * rows, LO), BF16),
        ],
        compiler_params=PARAMS,
        name="cameras",
    )(own, other, sums)
    back = lax.all_to_all(back, "grp", 0, 0, tiled=True)
    cb, cd, cs = pl.pallas_call(
        functools.partial(mine_kernel, 8 * count),
        out_shape=(shape(9, CAM_DEV),) * 3,
        compiler_params=PARAMS,
        name="mine",
    )(tb, td, ts)
    errors, ps, pe, sc = pl.pallas_call(
        functools.partial(point_kernel, n_grp),
        out_shape=(
            shape(n_grp * n_tile, 2, slot + 128),
            shape(3 * PH, LO),
            shape(2, obs),
            shape(2, 128),
        ),
        compiler_params=PARAMS,
        name="points",
    )(back, jp, pidx, pb, pd, pu, cb, cd, cs)
    errors = lax.all_to_all(errors, ("grp", "tile"), 0, 0, tiled=True)
    pt = pl.pallas_call(
        last_point_sums_kernel,
        out_shape=shape(3 * PH, LO),
        compiler_params=PARAMS,
        name="last_point_sums",
    )(jp, pidx, pe)
    return pl.pallas_call(
        final_kernel,
        out_shape=(shape(3, P_DEV), shape(9, CAM_DEV), shape(3, P_DEV), shape(9, CAM_DEV)),
        scratch_shapes=[pltpu.VMEM((96, 128), F32)],
        compiler_params=PARAMS,
        name="finish",
    )(errors, own, other, pb, pd, ps, pt, cb, cd, cs, sc)


def eights(row):
    return jnp.broadcast_to(row, (8, row.shape[1]))


def row_numbers(width):
    return lax.broadcasted_iota(jnp.int32, (16, width), 0)


def as_16_bit(numbers):
    return numbers.astype(F32).astype(BF16)


def masked_rows(parts, masks):
    none = jnp.zeros(parts[0].shape, BF16)
    return jnp.concatenate([jnp.where(m, p, none) for p in parts for m in masks], axis=0)


def low_lanes(rows):
    return lax.broadcasted_iota(jnp.int32, (rows, HALF), 1) < SLOTS


def swap_lanes(v):
    return pltpu.roll(v, SLOTS, 1)


def point_sums(pidx_ref, jp_ref, res_ref):
    index = pidx_ref[...]
    mask = is_row(index >> LO_BITS, PH)
    hot = one_hot_rows(index & (LO - 1), LO)
    jp = jp_ref[0:3, :], jp_ref[3:6, :]
    grad = -(jp[0] * res_ref[0:1, :] + jp[1] * res_ref[1:2, :])
    square = jp[0] * jp[0] + jp[1] * jp[1]
    return scatter_points(mask, hot, jnp.concatenate([grad, square], axis=0)), mask, hot, jp


def start_copies(pairs, sems):
    copies = [pltpu.make_async_copy(a, b, sems.at[k]) for k, (a, b) in enumerate(pairs)]
    for copy in copies:
        copy.start()
    for copy in copies:
        copy.wait()


def route_kernel(
    n_grp, n_tile, jp_hbm, jc_hbm, res_hbm, pidx_hbm, cidx_hbm,
    out_ref, pb_ref, pd_ref, pu_ref, jp_ref, pidx_ref, place_ref, sc_ref,
    jc_ref, res_ref, cidx_ref, sems,
):
    start_copies(
        (
            (pidx_hbm, pidx_ref),
            (jp_hbm, jp_ref),
            (res_hbm, res_ref),
            (jc_hbm, jc_ref),
            (cidx_hbm, cidx_ref),
        ),
        sems,
    )
    slot = cidx_ref.shape[1] // n_grp
    cams = cidx_ref[...]
    owner = ((cams >> 7) * 171) >> 9
    local = (cams - owner * CAM_DEV).astype(F32)
    mine = is_row(owner, n_tile)
    ones = jnp.where(mine, 1.0, 0.0)
    stack = jnp.concatenate([ones[:, h * slot : (h + 1) * slot] for h in range(n_grp)], axis=0)
    before = lax.broadcasted_iota(jnp.int32, (slot, slot), 0)
    before = before < lax.broadcasted_iota(jnp.int32, (slot, slot), 1)
    counts = dot_nn(stack.astype(BF16), jnp.where(before, 1.0, 0.0).astype(BF16))
    counts = jnp.concatenate([counts[h * n_tile : (h + 1) * n_tile] for h in range(n_grp)], axis=1)
    rank = jnp.sum(jnp.where(mine, counts, 0.0), axis=0, keepdims=True)
    place_ref[0:1, :] = owner
    place_ref[1:2, :] = rank.astype(jnp.int32)
    over = jnp.max(jnp.where(rank >= FULL, 1.0, 0.0), axis=1, keepdims=True)
    rank = rank.astype(jnp.int32)
    hot_rank = one_hot_rows(rank, HALF)
    wide = sixteen(owner)
    numbers = row_numbers(owner.shape[1])
    core = lax.axis_index("tile") % 2
    upper, lower, others = core, 1 + core, 2 - 2 * core
    low = low_lanes(8)

    def route_main(h):
        cols = slice(h * slot, (h + 1) * slot)
        here = [wide[:, cols] == BF16(t) for t in range(n_tile)]
        parts = two_parts(jnp.concatenate([jc_ref[0:8, cols], jc_ref[9:17, cols]], axis=0))
        moved = both(dot_nt(masked_rows(parts, here), hot_rank[:, cols]))
        for t in range(n_tile):
            first, second = moved[16 * t : 16 * t + 8], moved[16 * t + 8 : 16 * t + 16]
            tile = jnp.where(low, first, swap_lanes(second))
            out_ref[3 * (h * n_tile + t) + upper] = tile[0:4]
            out_ref[3 * (h * n_tile + t) + lower] = tile[4:8]

    def route_rest(parts, here, h):
        cols = slice(h * slot, (h + 1) * slot)
        left = masked_rows([p[:, cols] for p in parts], [m[:, cols] for m in here])
        moved = both(dot_nt(left, hot_rank[:, cols]))
        for t in range(n_tile):
            rows = moved[8 * t : 8 * t + 8]
            tile = jnp.where(low[0:4], rows[0:4], swap_lanes(rows)[4:8])
            out_ref[3 * (h * n_tile + t) + others] = tile

    table, mask, hot, jp = point_sums(pidx_ref, jp_ref, res_ref)
    for h in range(n_grp // 2):
        route_main(h)
    rhs, diag = table[: 3 * PH], table[3 * PH :] + DAMPING
    z = rhs / diag
    at = gather_points(mask, hot, z)
    for h in range(n_grp // 2, n_grp):
        route_main(h)
    pb_ref[...] = rhs
    pd_ref[...] = diag
    u = [sum(jp[a][i : i + 1] * at[i] for i in range(3)) for a in range(2)]
    pu_ref[0:1, :] = u[0]
    pu_ref[1:2, :] = u[1]
    sc_ref[...] = lanes(jnp.concatenate([total_of(rhs * z), total_of(z * z), over], axis=0), HALF)
    rows = [jc_ref[8:9, :], res_ref[0:1, :], local, u[0], jc_ref[17:18, :], res_ref[1:2, :], local, u[1]]
    parts = two_parts(jnp.concatenate(rows * 2, axis=0))
    here = [wide == as_16_bit((numbers >> 3) + t) for t in range(0, n_tile, 2)]
    for h in range(n_grp):
        route_rest(parts, here, h)


def unfold(even, odd):
    low = low_lanes(even.shape[0])
    return jnp.where(low, even, swap_lanes(odd)), jnp.where(low, swap_lanes(even), odd)


def unfold_rest(both_rows):
    low, swapped = low_lanes(4), swap_lanes(both_rows)
    return (
        jnp.where(low, both_rows[0:4], swapped[4:8]),
        jnp.where(low, swapped[0:4], both_rows[4:8]),
    )


def last_slot(v):
    return (lax.broadcasted_iota(jnp.int32, v.shape, 1) & (SLOTS - 1)) == FULL


def read_routed(ref, sources):
    main, rest = ([], []), ([], [])
    for s in sources[::2]:
        tile = 3 * (s // 2)
        pair = unfold(ref[tile], ref[tile + 2])
        pair_rest = unfold_rest(ref[tile + 1])
        for a in range(2):
            main[a].append(pair[a])
            rest[a].append(pair_rest[a])
    main = [jnp.concatenate(v, axis=1) for v in main]
    rest = [jnp.concatenate(v, axis=1) for v in rest]
    index = rest[0][2:3].astype(jnp.int32)
    return main, rest, (index >> 7).astype(F32), one_hot_rows(index & 127, 128)


OWN_ROWS = 32
STEP = 32


def scatter_two(hi, hot, first, second):
    wide, numbers = sixteen(hi), row_numbers(hi.shape[1])
    blocks = [wide == BF16(k) for k in range(3)]
    tail = wide == as_16_bit(numbers & 7)
    rows = two_parts(jnp.concatenate([first[0], second[0]], axis=0))
    tails = two_parts(jnp.concatenate([eights(first[1]), eights(second[1])], axis=0))
    none = jnp.zeros(wide.shape, BF16)
    pieces = []
    for part in range(2):
        pieces += [jnp.where(mask, rows[part], none) for mask in blocks]
        pieces.append(jnp.where(tail, tails[part], none))
    return both(dot_nt(jnp.concatenate(pieces, axis=0), hot))


def scatter_one(hi, hot, main, tail):
    wide, numbers = sixteen(hi), row_numbers(hi.shape[1])
    upper = wide == as_16_bit(numbers >> 3)
    lower = wide == as_16_bit(jnp.where(numbers < 8, 2, numbers - 8))
    rows = two_parts(jnp.concatenate([main, main], axis=0))
    tails = two_parts(jnp.concatenate([main, eights(tail)], axis=0))
    none = jnp.zeros(wide.shape, BF16)
    pieces = []
    for part in range(2):
        pieces += [jnp.where(upper, rows[part], none), jnp.where(lower, tails[part], none)]
    return both(dot_nt(jnp.concatenate(pieces, axis=0), hot))


def gather_own(hi, hot, table, main, rest):
    found = both(dot_nn(table, hot))
    block = eights(hi)
    at = jnp.where(block == 0, found[0:8], jnp.where(block == 1, found[8:16], found[16:24]))
    numbers = lax.broadcasted_iota(jnp.int32, block.shape, 0).astype(F32)
    tail = jnp.where(block == numbers, found[24:32], 0.0)
    return [
        jnp.sum(main[a] * at + eights(rest[a][0:1]) * tail, axis=0, keepdims=True) for a in range(2)
    ]


def scatter_j(hi, hot, main, rest, e):
    return scatter_one(
        hi, hot, main[0] * e[0] + main[1] * e[1], rest[0][0:1] * e[0] + rest[1][0:1] * e[1]
    )


def owner_kernel(in_ref, sc_ref, back_ref, tb_ref, td_ref, ts_ref, acc_ref, zz_ref, w_ref, *kept):
    devices = back_ref.shape[0]
    per = min(STEP, devices)
    steps = devices // per

    if steps == 1:
        main, rest, hi, hot = read_routed(in_ref, range(devices))
        kept[0][...] = hot
        for a in range(2):
            kept[1][8 * a : 8 * a + 8, :] = main[a]
            kept[1][16 + a : 17 + a, :] = rest[a][0:1]
        kept[1][18:19, :] = hi

        def loop(body, start):
            return body((main, rest, hi, hot), 0, start)
    else:

        def loop(body, start):
            def step(number, carry):
                return body(read_routed(in_ref, chunk_of(number, per)), number, carry)

            return lax.fori_loop(0, steps, step, start)

    def rhs_and_diag(slots, number, carry):
        main, rest, hi, hot = slots
        r = [rest[a][1:2] for a in range(2)]
        rhs = (-(main[0] * r[0] + main[1] * r[1]), -(rest[0][0:1] * r[0] + rest[1][0:1] * r[1]))
        square = (
            main[0] * main[0] + main[1] * main[1],
            rest[0][0:1] * rest[0][0:1] + rest[1][0:1] * rest[1][0:1],
        )
        acc_ref[...] += scatter_two(hi, hot, rhs, square)
        return carry

    acc_ref[...] = jnp.zeros(acc_ref.shape, F32)
    loop(rhs_and_diag, 0)
    rhs = jnp.concatenate([acc_ref[16 * k : 16 * k + 8, :] for k in range(4)], axis=0)
    diag = jnp.concatenate([acc_ref[16 * k + 8 : 16 * k + 16, :] for k in range(4)], axis=0) + DAMPING
    tb_ref[...] = rhs
    td_ref[...] = diag
    z = rhs / diag
    zz_ref[...] = stacked(z)
    acc_ref[0:OWN_ROWS, :] = z

    def apply(slots, number, energy):
        main, rest, hi, hot = slots
        w = gather_own(hi, hot, zz_ref[...], main, rest)
        e = [rest[a][3:4] + w[a] for a in range(2)]
        for a in range(2):
            w_ref[number, 2 * a : 2 * a + 1, :] = w[a]
        acc_ref[0:OWN_ROWS, :] += scatter_j(hi, hot, main, rest, e)
        return energy + e[0] * e[0] + e[1] * e[1]

    energy = loop(apply, jnp.zeros((1, per * SLOTS), F32))
    s = acc_ref[0:OWN_ROWS, :]
    ts_ref[...] = s
    zz_ref[...] = stacked(s / diag)
    gamma = sc_ref[0:1, :] + total_of(rhs * z)
    delta = sc_ref[1:2, :] + total_of(z * z) + total_of(energy)
    over = sc_ref[2:3, :]
    low = low_lanes(2)
    tail = jnp.where(
        low, jnp.concatenate([gamma, over], axis=0), jnp.concatenate([delta, over], axis=0)
    )

    def send(slots, number, carry):
        main, rest, hi, hot = slots
        v = gather_own(hi, hot, zz_ref[...], main, rest)
        for a in range(2):
            w_ref[number, 2 * a + 1 : 2 * a + 2, :] = v[a]
        w = w_ref[number]
        for k in range(per // 2):
            cols = slice(k * HALF, (k + 1) * HALF)
            first, second = w[0:2, cols], w[2:4, cols]
            even = jnp.where(low, first, swap_lanes(second))
            odd = jnp.where(low, swap_lanes(first), second)
            for t, tile in ((2 * k, even), (2 * k + 1, odd)):
                back_ref[number * per + t] = jnp.where(last_slot(tile), tail, tile)
        return carry

    loop(send, 0)


def routed_point_kernel(
    n_grp, n_tile, back_ref, jp_ref, pidx_ref, place_ref, pb_ref, pd_ref, pu_ref, cb_ref, cd_ref, cs_ref,
    out_ref, ps_ref, pe_ref, sc_ref, over_ref,
):
    slot = place_ref.shape[1] // n_grp
    index = pidx_ref[...]
    mask = is_row(index >> LO_BITS, PH)
    hot = one_hot_rows(index & (LO - 1), LO)
    jp = [jp_ref[k : k + 1, :] for k in range(6)]
    scalars = jnp.sum(back_ref[...], axis=0)
    scalars = scalars[0:4] + scalars[4:8]
    scalars = scalars[0:2] + scalars[2:4]
    gamma, delta = scalars[0:1, FULL : FULL + 1], scalars[0:1, HALF - 1 : HALF]
    over_ref[...] = lanes(scalars[1:2, FULL : FULL + 1], HALF)
    alpha = gamma / delta
    owner = place_ref[0:1, :]
    hot_rank = one_hot_rows(place_ref[1:2, :], HALF)
    numbers = lax.broadcasted_iota(jnp.int32, (2 * n_tile, slot), 0) >> 1
    terms = []
    for h in range(n_grp):
        cols = slice(h * slot, (h + 1) * slot)
        rows = jnp.concatenate([back_ref[h * n_tile // 4 + k] for k in range(n_tile // 4)], axis=0)
        rows = jnp.concatenate([rows, swap_lanes(rows)], axis=0)
        found = both(dot_nn(stacked(rows), hot_rank[:, cols]))
        here = numbers == owner[:, cols]
        of_a = []
        for a in range(2):
            mine = jnp.where(here, found[2 * n_tile * a : 2 * n_tile * (a + 1)], 0.0)
            mine = sum(mine[8 * k : 8 * k + 8] for k in range(n_tile // 4))
            mine = mine[0:4] + mine[4:8]
            of_a.append(mine[0:2] + mine[2:4])
        terms.append(jnp.concatenate(of_a, axis=0))
    terms = jnp.concatenate(terms, axis=1)
    w0 = [terms[2 * a : 2 * a + 1] for a in range(2)]
    w1 = [terms[2 * a + 1 : 2 * a + 2] for a in range(2)]
    rhs, diag = pb_ref[...], pd_ref[...]
    z = rhs / diag
    error = [pu_ref[a : a + 1, :] + w0[a] for a in range(2)]
    s = z + scatter_points(mask, hot, jp_ref[0:3, :] * error[0] + jp_ref[3:6, :] * error[1])
    r1 = rhs - alpha * s
    z1 = r1 / diag
    at = gather_points(mask, hot, z1)
    error = [sum(jp[3 * a + i] * at[i] for i in range(3)) + (w0[a] - alpha * w1[a]) for a in range(2)]
    ps_ref[...] = s
    pe_ref[0:1, :] = error[0]
    pe_ref[1:2, :] = error[1]
    cr1 = cb_ref[...] - alpha * cs_ref[...]
    cz1 = cr1 / cd_ref[...]
    gamma1 = total_of(r1 * z1) + total_of(cr1 * cz1)
    delta1 = (
        total_of(error[0] * error[0] + error[1] * error[1]) + total_of(z1 * z1) + total_of(cz1 * cz1)
    )
    sc_ref[...] = lanes(jnp.concatenate([gamma, alpha], axis=0), HALF)
    tail = jnp.where(low_lanes(1), gamma1, delta1)
    wide, numbers = sixteen(owner), row_numbers(owner.shape[1])
    parts = two_parts(jnp.concatenate([eights(e) for e in error], axis=0))
    here = [wide == as_16_bit((numbers & 7) + t) for t in range(0, n_tile, 8)]
    left = masked_rows(parts, here)
    low = low_lanes(8)
    for h in range(n_grp):
        moved = both(dot_nt(left[:, h * slot : (h + 1) * slot], hot_rank[:, h * slot : (h + 1) * slot]))
        for t in range(0, n_tile, 8):
            tile = jnp.where(low, moved[2 * t : 2 * t + 8], swap_lanes(moved[2 * t + 8 : 2 * t + 16]))
            tile = jnp.where(last_slot(tile), tail, tile)
            for k in range(8):
                out_ref[h * n_tile + t + k] = tile[k : k + 1]


def point_results(alpha, alpha1, ratio, pb_ref, pd_ref, ps_ref, pt_ref, px_ref, pr_ref, copies):
    rhs, diag, s = pb_ref[...], pd_ref[...], ps_ref[...]
    z = rhs / diag
    r1 = rhs - alpha * s
    z1 = r1 / diag
    x = alpha * z + alpha1 * (z1 + ratio * z)
    r2 = r1 - alpha1 * (z1 + pt_ref[...] + ratio * s)
    for table, target, copy in ((x, px_ref, copies[0]), (r2, pr_ref, copies[1])):
        for i in range(3):
            for hi in range(PH):
                row = i * PH + hi
                target[i : i + 1, hi * LO : (hi + 1) * LO] = table[row : row + 1]
        copy.start()


def routed_final_kernel(
    err_ref, in_ref, jp_ref, pidx_ref, pe_ref, pb_ref, pd_ref, ps_ref, cb_ref, cd_ref, cs_ref, sc_ref, *rest_refs
):
    kept, outs, (px_ref, cx_ref, pr_ref, cr_ref, acc_ref, pt_ref, sems) = (
        rest_refs[:-11],
        rest_refs[-11:-7],
        rest_refs[-7:],
    )
    devices = err_ref.shape[0]
    per = min(STEP, devices)
    steps = devices // per

    def body(step, carry):
        sources = chunk_of(step, per)
        if kept:
            hot, rows = kept[0][...], kept[1]
            main = [rows[8 * a : 8 * a + 8, :] for a in range(2)]
            rest = [rows[16 + a : 17 + a, :] for a in range(2)]
            hi = rows[18:19, :]
        else:
            main, rest, hi, hot = read_routed(in_ref, sources)
        pairs = [unfold(err_ref[s], err_ref[t]) for s, t in zip(sources[::2], sources[1::2])]
        e = [jnp.concatenate([pair[a] for pair in pairs], axis=1) for a in range(2)]
        acc_ref[...] += scatter_j(hi, hot, main, rest, e)
        return carry

    acc_ref[...] = jnp.zeros(acc_ref.shape, F32)
    if steps == 1:
        body(0, 0)
    else:
        lax.fori_loop(0, steps, body, 0)
    last_point_sums_kernel(jp_ref, pidx_ref, pe_ref, pt_ref)
    scalars = jnp.sum(err_ref[...], axis=0)
    gamma1, delta1 = scalars[:, FULL : FULL + 1], scalars[:, HALF - 1 : HALF]
    gamma, alpha = sc_ref[0:1, 0:1], sc_ref[1:2, 0:1]
    ratio = gamma1 / gamma
    alpha1 = gamma1 / (delta1 - ratio * gamma1 / alpha)
    copies = [
        pltpu.make_async_copy(here, there, sems.at[k])
        for k, (here, there) in enumerate(zip((px_ref, cx_ref, pr_ref, cr_ref), outs))
    ]
    point_results(
        alpha, alpha1, ratio, pb_ref, pd_ref, ps_ref, pt_ref, px_ref, pr_ref, (copies[0], copies[2])
    )
    rhs, s = cb_ref[...], cs_ref[...]
    z = rhs / cd_ref[...]
    r1 = rhs - alpha * s
    z1 = r1 / cd_ref[...]
    x = alpha * z + alpha1 * (z1 + ratio * z)
    r2 = r1 - alpha1 * (z1 + acc_ref[...] + ratio * s)
    for table, target in ((x, cx_ref), (r2, cr_ref)):
        for k in range(3):
            cols = slice(k * 128, (k + 1) * 128)
            target[0:8, cols] = table[8 * k : 8 * k + 8]
            target[8:9, cols] = table[24 + k : 25 + k]
    copies[1].start()
    copies[3].start()
    for copy in copies:
        copy.wait()


def shards(jac_point, jac_cam, resid, point_index, cam_index):
    n_grp, n_tile = lax.axis_size("grp"), lax.axis_size("tile")
    devices = n_grp * n_tile
    obs = jac_point.shape[1]
    pidx, cidx = point_index.reshape(1, obs), cam_index.reshape(1, obs)
    hbm = pl.BlockSpec(memory_space=pltpu.HBM)
    ints = jax.ShapeDtypeStruct((1, obs), jnp.int32)
    places = jax.ShapeDtypeStruct((2, obs), jnp.int32)
    points = shape(3 * PH, LO)
    cameras = shape(OWN_ROWS, 128)
    routed, pb, pd, pu, jp, pidx_here, place, sc = pl.pallas_call(
        functools.partial(route_kernel, n_grp, n_tile),
        in_specs=[hbm] * 5,
        out_shape=(shape(3 * devices, 4, HALF), points, points, shape(2, obs), shape(6, obs), ints, places, shape(3, HALF)),
        scratch_shapes=[
            pltpu.VMEM((18, obs), F32),
            pltpu.VMEM((2, obs), F32),
            pltpu.VMEM((1, obs), jnp.int32),
            pltpu.SemaphoreType.DMA((5,)),
        ],
        compiler_params=PARAMS,
        name="route",
    )(*(pltpu.with_memory_space_constraint(x, pltpu.HBM) for x in (jac_point, jac_cam, resid, pidx, cidx)))
    routed = lax.all_to_all(routed, ("grp", "tile"), 0, 0, tiled=True).reshape(3 * devices // 2, 8, HALF)
    slots = devices * SLOTS
    per = min(STEP, devices)
    scratch = [
        pltpu.VMEM((2 * OWN_ROWS, 128), F32),
        pltpu.VMEM((2 * OWN_ROWS, 128), BF16),
        pltpu.VMEM((devices // per, 4, per * SLOTS), F32),
    ]
    kept_shapes = ()
    if devices == per:
        kept_shapes = (jax.ShapeDtypeStruct((128, slots), BF16), shape(24, slots))

    def owner(in_ref, sc_ref, back_ref, tb_ref, td_ref, ts_ref, *others):
        kept, work = others[: len(kept_shapes)], others[len(kept_shapes) :]
        owner_kernel(in_ref, sc_ref, back_ref, tb_ref, td_ref, ts_ref, *work, *kept)

    back, tb, td, ts, *kept = pl.pallas_call(
        owner,
        out_shape=(shape(devices, 2, HALF), cameras, cameras, cameras) + kept_shapes,
        scratch_shapes=scratch,
        compiler_params=PARAMS,
        name="owner",
    )(routed, sc)
    back = lax.all_to_all(back, ("grp", "tile"), 0, 0, tiled=True).reshape(devices // 4, 8, HALF)
    errors, ps, pe, sc, over = pl.pallas_call(
        functools.partial(routed_point_kernel, n_grp, n_tile),
        out_shape=(shape(devices, 1, HALF), points, shape(2, obs), shape(2, HALF), shape(1, HALF)),
        compiler_params=PARAMS,
        name="points",
    )(back, jp, pidx_here, place, pb, pd, pu, tb, td, ts)
    outputs = (shape(3, P_DEV), shape(9, CAM_DEV), shape(3, P_DEV), shape(9, CAM_DEV))

    def fits(*operands):
        errors = lax.all_to_all(operands[5], ("grp", "tile"), 0, 0, tiled=True)
        return pl.pallas_call(
            routed_final_kernel,
            out_shape=outputs,
            out_specs=[hbm] * 4,
            scratch_shapes=[pltpu.VMEM(v.shape, F32) for v in outputs]
            + [
                pltpu.VMEM((OWN_ROWS, 128), F32),
                pltpu.VMEM((3 * PH, LO), F32),
                pltpu.SemaphoreType.DMA((4,)),
            ],
            compiler_params=PARAMS,
            name="finish",
        )(errors, *operands[6:])

    def overflows(*operands):
        return tuple(replicated(*operands[:5]))

    over, *operands = lax.optimization_barrier(
        (
            over, jac_point, jac_cam, resid, point_index, cam_index,
            errors, routed, jp, pidx_here, pe, pb, pd, ps, tb, td, ts, sc, *kept,
        )
    )
    return lax.cond(over[0, 0] > 0, overflows, lambda *operands: tuple(fits(*operands)), *operands)


def solution(mesh):
    placed = (
        P(None, ("grp", "tile")),
        P(None, ("grp", "tile")),
        P(None, ("grp", "tile")),
        P(("grp", "tile")),
        P(("grp", "tile")),
    )
    return jax.shard_map(
        shards,
        mesh=mesh,
        in_specs=placed,
        out_specs=(P(None, ("grp", "tile")),) * 4,
        check_vma=False,
    )
```

```python
import functools

import jax
import jax.numpy as jnp
from jax import lax
from jax.experimental import pallas as pl
from jax.experimental.pallas import tpu as pltpu
from jax.sharding import PartitionSpec as P

P_DEV = 4096
CAM_DEV = 384
LO_BITS = 8
LO = 1 << LO_BITS
PH = P_DEV // LO
DAMPING = 1.0
F32 = jnp.float32
BF16 = jnp.bfloat16
SLOTS = 64
FULL = SLOTS - 1
HALF = 128
PARAMS = pltpu.CompilerParams(vmem_limit_bytes=48 * 1024 * 1024)


def halves(v):
    high = v.astype(BF16).astype(F32)
    return high, v - high


def rows16(width, step=1):
    numbers = lax.broadcasted_iota(jnp.int32, (16, width), 0)
    return (numbers // step if step > 1 else numbers).astype(F32).astype(BF16)


def sixteen(row):
    return jnp.broadcast_to(row.astype(F32), (16, row.shape[1])).astype(BF16)


def one_hot_rows(index, rows):
    numbers = rows16(index.shape[1])
    pieces = []
    for base in range(0, rows, 256):
        wide = sixteen(index - base)
        one, none = jnp.ones(wide.shape, BF16), jnp.zeros(wide.shape, BF16)
        pieces += [
            jnp.where(wide == numbers + BF16(16 * k), one, none)
            for k in range(min(256, rows - base) // 16)
        ]
    return jnp.concatenate(pieces, axis=0)


def dot_nt(a, b):
    return lax.dot_general(a, b, (((1,), (1,)), ((), ())), preferred_element_type=F32)


def dot_nn(a, b):
    return lax.dot_general(a, b, (((1,), (0,)), ((), ())), preferred_element_type=F32)


def is_row(hi, rows):
    return lax.broadcasted_iota(jnp.int32, (rows, hi.shape[1]), 0) == hi


def spread_row(mask, row):
    return jnp.where(mask, jnp.broadcast_to(row, mask.shape), 0.0)


def two_parts(v):
    high = v.astype(BF16)
    return high, (v - high.astype(F32)).astype(BF16)


def scatter_mixed(hi, hot, mains, tails, count, tail_rows):
    wide = sixteen(hi)
    none = jnp.zeros(wide.shape, BF16)
    single = len(mains) == 1
    numbers = rows16(hi.shape[1], 8) if single else none
    main_parts = two_parts(jnp.concatenate(mains * 2 if single else mains, axis=0))
    tail_parts = [two_parts(jnp.broadcast_to(v, wide.shape)) for v in tails]
    here = [wide == numbers + BF16(k) for k in range(0, count, 2 if single else 1)]
    tail_here = [wide == rows16(hi.shape[1]) + BF16(k) for k in range(0, tail_rows, 16)]
    pieces = []
    for part in range(2):
        pieces += [jnp.where(mask, main_parts[part], none) for mask in here]
        pieces += [jnp.where(mask, v[part], none) for v in tail_parts for mask in tail_here]
    return dot_nt(jnp.concatenate(pieces, axis=0), hot)


def both(v):
    half = v.shape[0] // 2
    return v[:half] + v[half:]


def gather_mixed(hi, hot, table, count, tail_rows):
    found = dot_nn(table, hot)
    hi8 = jnp.broadcast_to(hi, (8, hi.shape[1]))
    main = jnp.zeros(hi8.shape, F32)
    half = found.shape[0] // 2
    for k in range(count):
        rows = slice(k * 8, k * 8 + 8)
        low = slice(half + k * 8, half + k * 8 + 8)
        main = main + jnp.where(hi8 == k, found[rows] + found[low], 0.0)
    tail = found[count * 8 : half] + found[half + count * 8 :]
    tail = jnp.sum(jnp.where(is_row(hi, tail_rows), tail, 0.0), axis=0, keepdims=True)
    return main, tail


def stacked(table):
    high, low = halves(table)
    return jnp.concatenate([high, low], axis=0).astype(BF16)


def scatter_points(mask, hot, rows):
    pieces = [spread_row(mask, v[k : k + 1]) for v in halves(rows) for k in range(rows.shape[0])]
    return both(dot_nt(jnp.concatenate(pieces, axis=0).astype(BF16), hot))


def gather_points(mask, hot, table):
    found = both(dot_nn(stacked(table), hot))
    return [
        jnp.sum(jnp.where(mask, found[i * PH : (i + 1) * PH], 0.0), axis=0, keepdims=True)
        for i in range(found.shape[0] // PH)
    ]


def total_of(v):
    return jnp.sum(jnp.sum(v, axis=0, keepdims=True), axis=1, keepdims=True)


def lanes(v, width):
    return jnp.broadcast_to(v, (v.shape[0], width))


def pack_kernel(
    n_grp, n_z, jp_hbm, jc_hbm, res_hbm, pidx_hbm, cidx_hbm,
    out_ref, pb_ref, pd_ref, pu_ref, jp_ref, pidx_ref,
    jc_ref, res_ref, cidx_ref, sems,
):
    copies = [
        pltpu.make_async_copy(source, target, sems.at[k])
        for k, (source, target) in enumerate(
            (
                (pidx_hbm, pidx_ref),
                (jp_hbm, jp_ref),
                (res_hbm, res_ref),
                (jc_hbm, jc_ref),
                (cidx_hbm, cidx_ref),
            )
        )
    ]
    for copy in copies:
        copy.start()
    for copy in copies:
        copy.wait()
    slot = out_ref.shape[2]
    index = pidx_ref[...]
    mask = is_row(index >> LO_BITS, PH)
    hot = one_hot_rows(index & (LO - 1), LO)
    jp = [jp_ref[k : k + 1, :] for k in range(6)]
    res = [res_ref[a : a + 1, :] for a in range(2)]
    grad = [-(jp[i] * res[0] + jp[3 + i] * res[1]) for i in range(3)]
    square = [jp[i] * jp[i] + jp[3 + i] * jp[3 + i] for i in range(3)]
    table = scatter_points(mask, hot, jnp.concatenate(grad + square, axis=0))
    rhs = table[: 3 * PH]
    diag = table[3 * PH :] + DAMPING
    pb_ref[...] = rhs
    pd_ref[...] = diag
    z = rhs / diag
    at = gather_points(mask, hot, z)
    u = [sum(jp[3 * a + i] * at[i] for i in range(3)) for a in range(2)]
    pu_ref[0:1, :] = u[0]
    pu_ref[1:2, :] = u[1]
    gamma = total_of(rhs * z)
    norm = total_of(z * z)
    scalars = jnp.concatenate([lanes(gamma, slot // 2), lanes(norm, slot // 2)], axis=1)
    cams = cidx_ref[...].astype(F32)
    for h in range(n_grp):
        cols = slice(h * slot, (h + 1) * slot)
        block = jnp.concatenate(
            [
                jc_ref[0:8, cols],
                jc_ref[9:17, cols],
                jc_ref[8:9, cols],
                jc_ref[17:18, cols],
                res[0][:, cols],
                res[1][:, cols],
                u[0][:, cols],
                u[1][:, cols],
                cams[:, cols],
                scalars,
            ],
            axis=0,
        )

        @pl.loop(0, n_z)
        def _(z_to, block=block, h=h):
            out_ref[h * n_z + z_to] = block


def read_blocks(ref, numbers):
    x = jnp.concatenate([ref[k] for k in numbers], axis=1)
    return x, x[22:23].astype(jnp.int32)


def chunk_of(chunk, per):
    return [chunk * per + k for k in range(per)]


def first_sums(ref, acc_ref, per, count, tail_rows):
    def body(chunk, carry):
        x, index = read_blocks(ref, chunk_of(chunk, per))
        hi, hot = index >> LO_BITS, one_hot_rows(index & (LO - 1), LO)
        j0, j1 = x[0:8], x[8:16]
        j08, j18, r0, r1 = x[16:17], x[17:18], x[18:19], x[19:20]
        acc_ref[...] += scatter_mixed(
            hi,
            hot,
            [-(j0 * r0 + j1 * r1), j0 * j0 + j1 * j1],
            [-(j08 * r0 + j18 * r1), j08 * j08 + j18 * j18],
            count,
            tail_rows,
        )
        return carry

    lax.fori_loop(0, ref.shape[0] // per, body, 0)


def own_sums_kernel(count, tail_rows, a_ref, acc_ref):
    acc_ref[...] = jnp.zeros(acc_ref.shape, F32)
    first_sums(a_ref, acc_ref, min(16, a_ref.shape[0]), count, tail_rows)


def camera_kernel(
    n_grp, n_z, count, tail_rows, a_ref, b_ref, start_ref,
    back_ref, tb_ref, td_ref, ts_ref,
    acc_ref, w_ref, zz_ref,
):
    blocks, _, slot = a_ref.shape
    per = min(8, blocks)
    chunks = blocks // per
    acc_ref[...] = start_ref[...]
    first_sums(b_ref, acc_ref, min(16, blocks), count, tail_rows)
    scalars = jnp.zeros((1, slot), F32)
    for ref in (a_ref, b_ref):
        scalars = scalars + jnp.sum(ref[:, 23, :], axis=0, keepdims=True)
    main = 8 * count
    half = acc_ref.shape[0] // 2
    for k in range(count):
        row = 16 * k
        tb_ref[8 * k : 8 * k + 8, :] = acc_ref[row : row + 8, :] + acc_ref[half + row : half + row + 8, :]
        row = 16 * k + 8
        td_ref[8 * k : 8 * k + 8, :] = (
            acc_ref[row : row + 8, :] + acc_ref[half + row : half + row + 8, :] + DAMPING
        )
    tb_ref[main:, :] = (
        acc_ref[2 * main : 2 * main + tail_rows, :]
        + acc_ref[half + 2 * main : half + 2 * main + tail_rows, :]
    )
    td_ref[main:, :] = (
        acc_ref[2 * main + tail_rows : half, :] + acc_ref[half + 2 * main + tail_rows :, :] + DAMPING
    )
    z = tb_ref[...] / td_ref[...]
    gamma = total_of(tb_ref[...] * z)
    norm = total_of(z * z)
    zz_ref[...] = stacked(z)
    ts_ref[...] = z
    acc_ref[0:half, :] = jnp.zeros((half, LO), F32)

    def second(ref, keep):
        def body(chunk, energy):
            numbers = chunk_of(chunk, per)
            x, index = read_blocks(ref, numbers)
            hi, hot = index >> LO_BITS, one_hot_rows(index & (LO - 1), LO)
            j0, j1 = x[0:8], x[8:16]
            j08, j18, u0, u1 = x[16:17], x[17:18], x[20:21], x[21:22]
            at, at8 = gather_mixed(hi, hot, zz_ref[...], count, tail_rows)
            w0 = jnp.sum(j0 * at, axis=0, keepdims=True) + j08 * at8
            w1 = jnp.sum(j1 * at, axis=0, keepdims=True) + j18 * at8
            if keep:
                for k, number in enumerate(numbers):
                    cols = slice(k * slot, (k + 1) * slot)
                    w_ref[number, 0:1, :] = w0[:, cols]
                    w_ref[number, 1:2, :] = w1[:, cols]
            e0, e1 = u0 + w0, u1 + w1
            acc_ref[0:half, :] += scatter_mixed(
                hi, hot, [j0 * e0 + j1 * e1], [j08 * e0 + j18 * e1], count, tail_rows
            )
            return energy + e0 * e0 + e1 * e1

        return body

    energy = jnp.zeros((1, per * slot), F32)
    energy = lax.fori_loop(0, chunks, second(a_ref, True), energy)
    energy = lax.fori_loop(0, chunks, second(b_ref, False), energy)
    ts_ref[...] += both(acc_ref[0:half, :])
    zz_ref[...] = stacked(ts_ref[...] / td_ref[...])
    share = 1.0 / n_grp
    gamma = gamma + share * scalars[:, 0:1]
    delta = norm + total_of(energy) + share * scalars[:, slot // 2 : slot // 2 + 1]
    mine = lax.axis_index("tile") // 2
    numbers = [g * n_z + mine for g in range(n_grp)]
    per = min(4, n_grp)
    for first in range(0, n_grp, per):
        some = numbers[first : first + per]
        x, index = read_blocks(a_ref, some)
        hi, hot = index >> LO_BITS, one_hot_rows(index & (LO - 1), LO)
        at, at8 = gather_mixed(hi, hot, zz_ref[...], count, tail_rows)
        v0 = jnp.sum(x[0:8] * at, axis=0, keepdims=True) + x[16:17] * at8
        v1 = jnp.sum(x[8:16] * at, axis=0, keepdims=True) + x[17:18] * at8
        for k in range(per):
            cols = slice(k * slot, (k + 1) * slot)
            g = first + k
            back_ref[g, 0:2, 0:slot] = w_ref[some[k], 0:2, :]
            back_ref[g, 2:3, 0:slot] = v0[:, cols]
            back_ref[g, 3:4, 0:slot] = v1[:, cols]
            back_ref[g, :, slot:] = lanes(jnp.concatenate([gamma, delta, gamma, delta], axis=0), 128)


def mine_kernel(main, tb_ref, td_ref, ts_ref, cb_ref, cd_ref, cs_ref):
    tile = lax.axis_index("tile")
    mine, core = tile // 2, tile % 2
    for source, target in ((tb_ref, cb_ref), (td_ref, cd_ref), (ts_ref, cs_ref)):
        own, own8 = [], []
        for k in range(3):
            rows = source[pl.ds(pl.multiple_of(8 * (3 * mine + k), 8), 8), :]
            tail = source[pl.ds(main + 3 * mine + k, 1), :]
            own += [rows[:, :128], rows[:, 128:]]
            own8 += [tail[:, :128], tail[:, 128:]]
        for m in range(3):
            cols = slice(m * 128, (m + 1) * 128)
            target[0:8, cols] = jnp.where(core == 0, own[m], own[m + 3])
            target[8:9, cols] = jnp.where(core == 0, own8[m], own8[m + 3])


def point_kernel(
    n_grp, back_ref, jp_ref, pidx_ref, pb_ref, pd_ref, pu_ref, cb_ref, cd_ref, cs_ref,
    out_ref, ps_ref, pe_ref, sc_ref,
):
    slot = back_ref.shape[2] - 128
    index = pidx_ref[...]
    mask = is_row(index >> LO_BITS, PH)
    hot = one_hot_rows(index & (LO - 1), LO)
    jp = [jp_ref[k : k + 1, :] for k in range(6)]
    scalars = back_ref[0, :, slot:]
    for h in range(1, n_grp):
        scalars = scalars + back_ref[h, :, slot:]
    gamma, delta = scalars[0:1, 0:1], scalars[1:2, 0:1]
    alpha = gamma / delta
    w = [
        jnp.concatenate([back_ref[h, r : r + 1, 0:slot] for h in range(n_grp)], axis=1) for r in range(4)
    ]
    rhs, diag = pb_ref[...], pd_ref[...]
    z = rhs / diag
    error = [pu_ref[a : a + 1, :] + w[a] for a in range(2)]
    s = z + scatter_points(mask, hot, jp_ref[0:3, :] * error[0] + jp_ref[3:6, :] * error[1])
    r1 = rhs - alpha * s
    z1 = r1 / diag
    at = gather_points(mask, hot, z1)
    error = [
        sum(jp[3 * a + i] * at[i] for i in range(3)) + (w[a] - alpha * w[2 + a]) for a in range(2)
    ]
    ps_ref[...] = s
    pe_ref[0:1, :] = error[0]
    pe_ref[1:2, :] = error[1]
    cr1 = cb_ref[...] - alpha * cs_ref[...]
    cz1 = cr1 / cd_ref[...]
    gamma1 = total_of(r1 * z1) + total_of(cr1 * cz1)
    delta1 = (
        total_of(error[0] * error[0] + error[1] * error[1]) + total_of(z1 * z1) + total_of(cz1 * cz1)
    )
    sc_ref[...] = lanes(jnp.concatenate([gamma, alpha], axis=0), 128)
    tail = lanes(jnp.concatenate([gamma1, delta1], axis=0), 128)
    per = out_ref.shape[0] // n_grp
    for h in range(n_grp):
        cols = slice(h * slot, (h + 1) * slot)
        block = jnp.concatenate([jnp.concatenate([e[:, cols] for e in error], axis=0), tail], axis=1)

        @pl.loop(0, per)
        def _(tile, block=block, h=h):
            out_ref[h * per + tile] = block


def last_point_sums_kernel(jp_ref, pidx_ref, pe_ref, pt_ref):
    index = pidx_ref[...]
    mask = is_row(index >> LO_BITS, PH)
    hot = one_hot_rows(index & (LO - 1), LO)
    terms = jp_ref[0:3, :] * pe_ref[0:1, :] + jp_ref[3:6, :] * pe_ref[1:2, :]
    pt_ref[...] = scatter_points(mask, hot, terms)


def final_kernel(
    err_ref, a_ref, b_ref, pb_ref, pd_ref, ps_ref, pt_ref, cb_ref, cd_ref, cs_ref, sc_ref,
    px_ref, cx_ref, pr_ref, cr_ref, acc_ref,
):
    blocks, _, slot = a_ref.shape
    per = min(8, blocks)
    chunks = blocks // per
    tile = lax.axis_index("tile")
    core = tile % 2
    acc_ref[...] = jnp.zeros(acc_ref.shape, F32)

    def body(ref, parity):
        def step(chunk, scalars):
            numbers = chunk_of(chunk, per)
            x, index = read_blocks(ref, numbers)
            errs = [err_ref[2 * k + parity] for k in numbers]
            e = jnp.concatenate([v[:, 0:slot] for v in errs], axis=1)
            for v in errs:
                scalars = scalars + v[:, slot:]
            index = index - tile * CAM_DEV
            hi = index >> 7
            hot = one_hot_rows(index & 127, 128)
            j0, j1 = x[0:8], x[8:16]
            e0, e1 = e[0:1], e[1:2]
            acc_ref[...] += scatter_mixed(
                hi, hot, [j0 * e0 + j1 * e1], [x[16:17] * e0 + x[17:18] * e1], 4, 16
            )
            return scalars

        return step

    scalars = lax.fori_loop(0, chunks, body(a_ref, core), jnp.zeros((2, 128), F32))
    scalars = lax.fori_loop(0, chunks, body(b_ref, 1 - core), scalars)
    gamma1, delta1 = scalars[0:1, 0:1], scalars[1:2, 0:1]
    gamma, alpha = sc_ref[0:1, 0:1], sc_ref[1:2, 0:1]
    ratio = gamma1 / gamma
    alpha1 = gamma1 / (delta1 - ratio * gamma1 / alpha)

    rhs, diag, s = pb_ref[...], pd_ref[...], ps_ref[...]
    z = rhs / diag
    r1 = rhs - alpha * s
    z1 = r1 / diag
    x = alpha * z + alpha1 * (z1 + ratio * z)
    r2 = r1 - alpha1 * (z1 + pt_ref[...] + ratio * s)
    for i in range(3):
        for hi in range(PH):
            row = i * PH + hi
            px_ref[i : i + 1, hi * LO : (hi + 1) * LO] = x[row : row + 1]
            pr_ref[i : i + 1, hi * LO : (hi + 1) * LO] = r2[row : row + 1]

    rhs, s = cb_ref[...], cs_ref[...]
    z = rhs / cd_ref[...]
    r1 = rhs - alpha * s
    z1 = r1 / cd_ref[...]
    cx_ref[...] = alpha * z + alpha1 * (z1 + ratio * z)
    sums = both(acc_ref[...])
    base = r1 - alpha1 * (z1 + ratio * s)
    for k in range(3):
        cols = slice(k * 128, (k + 1) * 128)
        cr_ref[0:8, cols] = base[0:8, cols] - alpha1 * sums[8 * k : 8 * k + 8, :]
        cr_ref[8:9, cols] = base[8:9, cols] - alpha1 * sums[32 + k : 33 + k, :]


def shape(*dims):
    return jax.ShapeDtypeStruct(dims, F32)


def replicated(jac_point, jac_cam, resid, point_index, cam_index):
    n_grp, n_tile = lax.axis_size("grp"), lax.axis_size("tile")
    n_z = n_tile // 2
    obs = jac_point.shape[1]
    slot = obs // n_grp
    blocks = n_grp * n_z
    count = CAM_DEV * n_tile // LO
    tail_rows = -(-count // 16) * 16
    rows = 8 * count + tail_rows
    groups = [[d * 2 + core for d in range(blocks)] for core in range(2)]
    swap = [(t, t ^ 1) for t in range(n_tile)]
    pidx, cidx = point_index.reshape(1, obs), cam_index.reshape(1, obs)

    hbm = pl.BlockSpec(memory_space=pltpu.HBM)
    packed, pb, pd, pu, jp, pidx = pl.pallas_call(
        functools.partial(pack_kernel, n_grp, n_z),
        in_specs=[hbm] * 5,
        out_shape=(
            shape(blocks, 24, slot),
            shape(3 * PH, LO),
            shape(3 * PH, LO),
            shape(2, obs),
            shape(6, obs),
            jax.ShapeDtypeStruct((1, obs), jnp.int32),
        ),
        scratch_shapes=[
            pltpu.VMEM((18, obs), F32),
            pltpu.VMEM((2, obs), F32),
            pltpu.VMEM((1, obs), jnp.int32),
            pltpu.SemaphoreType.DMA((5,)),
        ],
        compiler_params=PARAMS,
        name="pack",
    )(*(pltpu.with_memory_space_constraint(x, pltpu.HBM) for x in (jac_point, jac_cam, resid, pidx, cidx)))
    own = lax.all_to_all(packed, ("grp", "tile"), 0, 0, axis_index_groups=groups, tiled=True)
    other = lax.ppermute(own, "tile", swap)
    sums = pl.pallas_call(
        functools.partial(own_sums_kernel, count, tail_rows),
        out_shape=shape(4 * rows, LO),
        compiler_params=PARAMS,
        name="own_sums",
        cost_estimate=pl.CostEstimate(flops=2 * 10**9, bytes_accessed=10**6, transcendentals=0),
    )(own)
    table = shape(rows, LO)
    back, tb, td, ts = pl.pallas_call(
        functools.partial(camera_kernel, n_grp, n_z, count, tail_rows),
        out_shape=(shape(n_grp, 4, slot + 128), table, table, table),
        scratch_shapes=[
            pltpu.VMEM((4 * rows, LO), F32),
            pltpu.VMEM((blocks, 2, slot), F32),
            pltpu.VMEM((2 * rows, LO), BF16),
        ],
        compiler_params=PARAMS,
        name="cameras",
    )(own, other, sums)
    back = lax.all_to_all(back, "grp", 0, 0, tiled=True)
    cb, cd, cs = pl.pallas_call(
        functools.partial(mine_kernel, 8 * count),
        out_shape=(shape(9, CAM_DEV),) * 3,
        compiler_params=PARAMS,
        name="mine",
    )(tb, td, ts)
    errors, ps, pe, sc = pl.pallas_call(
        functools.partial(point_kernel, n_grp),
        out_shape=(
            shape(n_grp * n_tile, 2, slot + 128),
            shape(3 * PH, LO),
            shape(2, obs),
            shape(2, 128),
        ),
        compiler_params=PARAMS,
        name="points",
    )(back, jp, pidx, pb, pd, pu, cb, cd, cs)
    errors = lax.all_to_all(errors, ("grp", "tile"), 0, 0, tiled=True)
    pt = pl.pallas_call(
        last_point_sums_kernel,
        out_shape=shape(3 * PH, LO),
        compiler_params=PARAMS,
        name="last_point_sums",
    )(jp, pidx, pe)
    return pl.pallas_call(
        final_kernel,
        out_shape=(shape(3, P_DEV), shape(9, CAM_DEV), shape(3, P_DEV), shape(9, CAM_DEV)),
        scratch_shapes=[pltpu.VMEM((96, 128), F32)],
        compiler_params=PARAMS,
        name="finish",
    )(errors, own, other, pb, pd, ps, pt, cb, cd, cs, sc)


def eights(row):
    return jnp.broadcast_to(row, (8, row.shape[1]))


def row_numbers(width):
    return lax.broadcasted_iota(jnp.int32, (16, width), 0)


def as_16_bit(numbers):
    return numbers.astype(F32).astype(BF16)


def masked_rows(parts, masks):
    none = jnp.zeros(parts[0].shape, BF16)
    return jnp.concatenate([jnp.where(m, p, none) for p in parts for m in masks], axis=0)


def low_lanes(rows):
    return lax.broadcasted_iota(jnp.int32, (rows, HALF), 1) < SLOTS


def swap_lanes(v):
    return pltpu.roll(v, SLOTS, 1)


def point_sums(pidx_ref, jp_ref, res_ref):
    index = pidx_ref[...]
    mask = is_row(index >> LO_BITS, PH)
    hot = one_hot_rows(index & (LO - 1), LO)
    jp = jp_ref[0:3, :], jp_ref[3:6, :]
    grad = -(jp[0] * res_ref[0:1, :] + jp[1] * res_ref[1:2, :])
    square = jp[0] * jp[0] + jp[1] * jp[1]
    return scatter_points(mask, hot, jnp.concatenate([grad, square], axis=0)), mask, hot, jp


def start_copies(pairs, sems):
    copies = [pltpu.make_async_copy(a, b, sems.at[k]) for k, (a, b) in enumerate(pairs)]
    for copy in copies:
        copy.start()
    for copy in copies:
        copy.wait()


def route_kernel(
    n_grp, n_tile, jp_hbm, jc_hbm, res_hbm, pidx_hbm, cidx_hbm,
    out_ref, pb_ref, pd_ref, pu_ref, jp_ref, pidx_ref, place_ref, sc_ref,
    jc_ref, res_ref, cidx_ref, sems,
):
    width = cidx_ref.shape[1] // 4
    pairs = [(pidx_hbm, pidx_ref), (jp_hbm, jp_ref), (res_hbm, res_ref), (cidx_hbm, cidx_ref)]
    for k in range(4):
        part = pl.ds(k * width, width)
        pairs.append((jc_hbm.at[:, part], jc_ref.at[:, part]))
    start_copies(pairs, sems)
    slot = cidx_ref.shape[1] // n_grp
    cams = cidx_ref[...]
    owner = ((cams >> 7) * 171) >> 9
    local = (cams - owner * CAM_DEV).astype(F32)
    mine = is_row(owner, n_tile)
    ones = jnp.where(mine, 1.0, 0.0)
    stack = jnp.concatenate([ones[:, h * slot : (h + 1) * slot] for h in range(n_grp)], axis=0)
    before = lax.broadcasted_iota(jnp.int32, (slot, slot), 0)
    before = before < lax.broadcasted_iota(jnp.int32, (slot, slot), 1)
    counts = dot_nn(stack.astype(BF16), jnp.where(before, 1.0, 0.0).astype(BF16))
    counts = jnp.concatenate([counts[h * n_tile : (h + 1) * n_tile] for h in range(n_grp)], axis=1)
    rank = jnp.sum(jnp.where(mine, counts, 0.0), axis=0, keepdims=True)
    place_ref[0:1, :] = owner
    place_ref[1:2, :] = rank.astype(jnp.int32)
    over = jnp.max(jnp.where(rank >= FULL, 1.0, 0.0), axis=1, keepdims=True)
    rank = rank.astype(jnp.int32)
    hot_rank = one_hot_rows(rank, HALF)
    wide = sixteen(owner)
    numbers = row_numbers(owner.shape[1])
    core = lax.axis_index("tile") % 2
    upper, lower, others = core, 1 + core, 2 - 2 * core
    low = low_lanes(8)

    def route_main(h):
        cols = slice(h * slot, (h + 1) * slot)
        here = [wide[:, cols] == BF16(t) for t in range(n_tile)]
        parts = two_parts(jnp.concatenate([jc_ref[0:8, cols], jc_ref[9:17, cols]], axis=0))
        moved = both(dot_nt(masked_rows(parts, here), hot_rank[:, cols]))
        for t in range(n_tile):
            first, second = moved[16 * t : 16 * t + 8], moved[16 * t + 8 : 16 * t + 16]
            tile = jnp.where(low, first, swap_lanes(second))
            out_ref[3 * (h * n_tile + t) + upper] = tile[0:4]
            out_ref[3 * (h * n_tile + t) + lower] = tile[4:8]

    def route_rest(parts, here, h):
        cols = slice(h * slot, (h + 1) * slot)
        left = masked_rows([p[:, cols] for p in parts], [m[:, cols] for m in here])
        moved = both(dot_nt(left, hot_rank[:, cols]))
        for t in range(n_tile):
            rows = moved[8 * t : 8 * t + 8]
            tile = jnp.where(low[0:4], rows[0:4], swap_lanes(rows)[4:8])
            out_ref[3 * (h * n_tile + t) + others] = tile

    table, mask, hot, jp = point_sums(pidx_ref, jp_ref, res_ref)
    for h in range(n_grp):
        route_main(h)
    rhs, diag = table[: 3 * PH], table[3 * PH :] + DAMPING
    z = rhs / diag
    at = gather_points(mask, hot, z)
    pb_ref[...] = rhs
    pd_ref[...] = diag
    u = [sum(jp[a][i : i + 1] * at[i] for i in range(3)) for a in range(2)]
    pu_ref[0:1, :] = u[0]
    pu_ref[1:2, :] = u[1]
    sc_ref[...] = lanes(jnp.concatenate([total_of(rhs * z), total_of(z * z), over], axis=0), HALF)
    rows = [jc_ref[8:9, :], res_ref[0:1, :], local, u[0], jc_ref[17:18, :], res_ref[1:2, :], local, u[1]]
    parts = two_parts(jnp.concatenate(rows * 2, axis=0))
    here = [wide == as_16_bit((numbers >> 3) + t) for t in range(0, n_tile, 2)]
    for h in range(n_grp):
        route_rest(parts, here, h)


def unfold(even, odd):
    low = low_lanes(even.shape[0])
    return jnp.where(low, even, swap_lanes(odd)), jnp.where(low, swap_lanes(even), odd)


def unfold_rest(both_rows):
    low, swapped = low_lanes(4), swap_lanes(both_rows)
    return (
        jnp.where(low, both_rows[0:4], swapped[4:8]),
        jnp.where(low, swapped[0:4], both_rows[4:8]),
    )


def last_slot(v):
    return (lax.broadcasted_iota(jnp.int32, v.shape, 1) & (SLOTS - 1)) == FULL


def read_routed(ref, sources):
    main, rest = ([], []), ([], [])
    for s in sources[::2]:
        tile = 3 * (s // 2)
        pair = unfold(ref[tile], ref[tile + 2])
        pair_rest = unfold_rest(ref[tile + 1])
        for a in range(2):
            main[a].append(pair[a])
            rest[a].append(pair_rest[a])
    main = [jnp.concatenate(v, axis=1) for v in main]
    rest = [jnp.concatenate(v, axis=1) for v in rest]
    index = rest[0][2:3].astype(jnp.int32)
    return main, rest, (index >> 7).astype(F32), one_hot_rows(index & 127, 128)


OWN_ROWS = 32
STEP = 32


def scatter_two(hi, hot, first, second):
    wide, numbers = sixteen(hi), row_numbers(hi.shape[1])
    blocks = [wide == BF16(k) for k in range(3)]
    tail = wide == as_16_bit(numbers & 7)
    rows = two_parts(jnp.concatenate([first[0], second[0]], axis=0))
    tails = two_parts(jnp.concatenate([eights(first[1]), eights(second[1])], axis=0))
    none = jnp.zeros(wide.shape, BF16)
    pieces = []
    for part in range(2):
        pieces += [jnp.where(mask, rows[part], none) for mask in blocks]
        pieces.append(jnp.where(tail, tails[part], none))
    return both(dot_nt(jnp.concatenate(pieces, axis=0), hot))


def scatter_one(hi, hot, main, tail):
    wide, numbers = sixteen(hi), row_numbers(hi.shape[1])
    upper = wide == as_16_bit(numbers >> 3)
    lower = wide == as_16_bit(jnp.where(numbers < 8, 2, numbers - 8))
    rows = two_parts(jnp.concatenate([main, main], axis=0))
    tails = two_parts(jnp.concatenate([main, eights(tail)], axis=0))
    none = jnp.zeros(wide.shape, BF16)
    pieces = []
    for part in range(2):
        pieces += [jnp.where(upper, rows[part], none), jnp.where(lower, tails[part], none)]
    return both(dot_nt(jnp.concatenate(pieces, axis=0), hot))


def gather_own(hi, hot, table, main, rest):
    found = both(dot_nn(table, hot))
    block = eights(hi)
    at = jnp.where(block == 0, found[0:8], jnp.where(block == 1, found[8:16], found[16:24]))
    numbers = lax.broadcasted_iota(jnp.int32, block.shape, 0).astype(F32)
    tail = jnp.where(block == numbers, found[24:32], 0.0)
    return [
        jnp.sum(main[a] * at + eights(rest[a][0:1]) * tail, axis=0, keepdims=True) for a in range(2)
    ]


def scatter_j(hi, hot, main, rest, e):
    return scatter_one(
        hi, hot, main[0] * e[0] + main[1] * e[1], rest[0][0:1] * e[0] + rest[1][0:1] * e[1]
    )


def owner_kernel(in_ref, sc_ref, back_ref, tb_ref, td_ref, ts_ref, acc_ref, zz_ref, w_ref, *kept):
    devices = back_ref.shape[0]
    per = min(STEP, devices)
    steps = devices // per

    if steps == 1:
        main, rest, hi, hot = read_routed(in_ref, range(devices))
        kept[0][...] = hot
        for a in range(2):
            kept[1][8 * a : 8 * a + 8, :] = main[a]
            kept[1][16 + a : 17 + a, :] = rest[a][0:1]
        kept[1][18:19, :] = hi

        def loop(body, start):
            return body((main, rest, hi, hot), 0, start)
    else:

        def loop(body, start):
            def step(number, carry):
                return body(read_routed(in_ref, chunk_of(number, per)), number, carry)

            return lax.fori_loop(0, steps, step, start)

    def rhs_and_diag(slots, number, carry):
        main, rest, hi, hot = slots
        r = [rest[a][1:2] for a in range(2)]
        rhs = (-(main[0] * r[0] + main[1] * r[1]), -(rest[0][0:1] * r[0] + rest[1][0:1] * r[1]))
        square = (
            main[0] * main[0] + main[1] * main[1],
            rest[0][0:1] * rest[0][0:1] + rest[1][0:1] * rest[1][0:1],
        )
        acc_ref[...] += scatter_two(hi, hot, rhs, square)
        return carry

    acc_ref[...] = jnp.zeros(acc_ref.shape, F32)
    loop(rhs_and_diag, 0)
    rhs = jnp.concatenate([acc_ref[16 * k : 16 * k + 8, :] for k in range(4)], axis=0)
    diag = jnp.concatenate([acc_ref[16 * k + 8 : 16 * k + 16, :] for k in range(4)], axis=0) + DAMPING
    tb_ref[...] = rhs
    td_ref[...] = diag
    z = rhs / diag
    zz_ref[...] = stacked(z)
    acc_ref[0:OWN_ROWS, :] = z

    def apply(slots, number, energy):
        main, rest, hi, hot = slots
        w = gather_own(hi, hot, zz_ref[...], main, rest)
        e = [rest[a][3:4] + w[a] for a in range(2)]
        for a in range(2):
            w_ref[number, 2 * a : 2 * a + 1, :] = w[a]
        acc_ref[0:OWN_ROWS, :] += scatter_j(hi, hot, main, rest, e)
        return energy + e[0] * e[0] + e[1] * e[1]

    energy = loop(apply, jnp.zeros((1, per * SLOTS), F32))
    s = acc_ref[0:OWN_ROWS, :]
    ts_ref[...] = s
    zz_ref[...] = stacked(s / diag)
    gamma = sc_ref[0:1, :] + total_of(rhs * z)
    delta = sc_ref[1:2, :] + total_of(z * z) + total_of(energy)
    over = sc_ref[2:3, :]
    low = low_lanes(2)
    tail = jnp.where(
        low, jnp.concatenate([gamma, over], axis=0), jnp.concatenate([delta, over], axis=0)
    )

    def send(slots, number, carry):
        main, rest, hi, hot = slots
        v = gather_own(hi, hot, zz_ref[...], main, rest)
        for a in range(2):
            w_ref[number, 2 * a + 1 : 2 * a + 2, :] = v[a]
        w = w_ref[number]
        for k in range(per // 2):
            cols = slice(k * HALF, (k + 1) * HALF)
            first, second = w[0:2, cols], w[2:4, cols]
            even = jnp.where(low, first, swap_lanes(second))
            odd = jnp.where(low, swap_lanes(first), second)
            for t, tile in ((2 * k, even), (2 * k + 1, odd)):
                back_ref[number * per + t] = jnp.where(last_slot(tile), tail, tile)
        return carry

    loop(send, 0)


def routed_point_kernel(
    n_grp, n_tile, back_ref, jp_ref, pidx_ref, place_ref, pb_ref, pd_ref, pu_ref, cb_ref, cd_ref, cs_ref,
    out_ref, ps_ref, pe_ref, sc_ref, over_ref,
):
    slot = place_ref.shape[1] // n_grp
    index = pidx_ref[...]
    mask = is_row(index >> LO_BITS, PH)
    hot = one_hot_rows(index & (LO - 1), LO)
    jp = [jp_ref[k : k + 1, :] for k in range(6)]
    scalars = jnp.sum(back_ref[...], axis=0)
    scalars = scalars[0:4] + scalars[4:8]
    scalars = scalars[0:2] + scalars[2:4]
    gamma, delta = scalars[0:1, FULL : FULL + 1], scalars[0:1, HALF - 1 : HALF]
    over_ref[...] = lanes(scalars[1:2, FULL : FULL + 1], HALF)
    alpha = gamma / delta
    owner = place_ref[0:1, :]
    hot_rank = one_hot_rows(place_ref[1:2, :], HALF)
    numbers = lax.broadcasted_iota(jnp.int32, (2 * n_tile, slot), 0) >> 1
    terms = []
    for h in range(n_grp):
        cols = slice(h * slot, (h + 1) * slot)
        rows = jnp.concatenate([back_ref[h * n_tile // 4 + k] for k in range(n_tile // 4)], axis=0)
        rows = jnp.concatenate([rows, swap_lanes(rows)], axis=0)
        found = both(dot_nn(stacked(rows), hot_rank[:, cols]))
        here = numbers == owner[:, cols]
        of_a = []
        for a in range(2):
            mine = jnp.where(here, found[2 * n_tile * a : 2 * n_tile * (a + 1)], 0.0)
            mine = sum(mine[8 * k : 8 * k + 8] for k in range(n_tile // 4))
            mine = mine[0:4] + mine[4:8]
            of_a.append(mine[0:2] + mine[2:4])
        terms.append(jnp.concatenate(of_a, axis=0))
    terms = jnp.concatenate(terms, axis=1)
    w0 = [terms[2 * a : 2 * a + 1] for a in range(2)]
    w1 = [terms[2 * a + 1 : 2 * a + 2] for a in range(2)]
    rhs, diag = pb_ref[...], pd_ref[...]
    z = rhs / diag
    error = [pu_ref[a : a + 1, :] + w0[a] for a in range(2)]
    s = z + scatter_points(mask, hot, jp_ref[0:3, :] * error[0] + jp_ref[3:6, :] * error[1])
    r1 = rhs - alpha * s
    z1 = r1 / diag
    at = gather_points(mask, hot, z1)
    error = [sum(jp[3 * a + i] * at[i] for i in range(3)) + (w0[a] - alpha * w1[a]) for a in range(2)]
    ps_ref[...] = s
    pe_ref[0:1, :] = error[0]
    pe_ref[1:2, :] = error[1]
    cr1 = cb_ref[...] - alpha * cs_ref[...]
    cz1 = cr1 / cd_ref[...]
    gamma1 = total_of(r1 * z1) + total_of(cr1 * cz1)
    delta1 = (
        total_of(error[0] * error[0] + error[1] * error[1]) + total_of(z1 * z1) + total_of(cz1 * cz1)
    )
    sc_ref[...] = lanes(jnp.concatenate([gamma, alpha], axis=0), HALF)
    tail = jnp.where(low_lanes(1), gamma1, delta1)
    wide, numbers = sixteen(owner), row_numbers(owner.shape[1])
    parts = two_parts(jnp.concatenate([eights(e) for e in error], axis=0))
    here = [wide == as_16_bit((numbers & 7) + t) for t in range(0, n_tile, 8)]
    left = masked_rows(parts, here)
    low = low_lanes(8)
    for h in range(n_grp):
        moved = both(dot_nt(left[:, h * slot : (h + 1) * slot], hot_rank[:, h * slot : (h + 1) * slot]))
        for t in range(0, n_tile, 8):
            tile = jnp.where(low, moved[2 * t : 2 * t + 8], swap_lanes(moved[2 * t + 8 : 2 * t + 16]))
            tile = jnp.where(last_slot(tile), tail, tile)
            for k in range(8):
                out_ref[h * n_tile + t + k] = tile[k : k + 1]


def point_results(alpha, alpha1, ratio, pb_ref, pd_ref, ps_ref, pt_ref, px_ref, pr_ref, copies):
    rhs, diag, s = pb_ref[...], pd_ref[...], ps_ref[...]
    z = rhs / diag
    r1 = rhs - alpha * s
    z1 = r1 / diag
    x = alpha * z + alpha1 * (z1 + ratio * z)
    r2 = r1 - alpha1 * (z1 + pt_ref[...] + ratio * s)
    for table, target, copy in ((x, px_ref, copies[0]), (r2, pr_ref, copies[1])):
        for i in range(3):
            for hi in range(PH):
                row = i * PH + hi
                target[i : i + 1, hi * LO : (hi + 1) * LO] = table[row : row + 1]
        copy.start()


def routed_final_kernel(
    err_ref, in_ref, jp_ref, pidx_ref, pe_ref, pb_ref, pd_ref, ps_ref, cb_ref, cd_ref, cs_ref, sc_ref, *rest_refs
):
    kept, outs, (px_ref, cx_ref, pr_ref, cr_ref, acc_ref, pt_ref, sems) = (
        rest_refs[:-11],
        rest_refs[-11:-7],
        rest_refs[-7:],
    )
    devices = err_ref.shape[0]
    per = min(STEP, devices)
    steps = devices // per

    def body(step, carry):
        sources = chunk_of(step, per)
        if kept:
            hot, rows = kept[0][...], kept[1]
            main = [rows[8 * a : 8 * a + 8, :] for a in range(2)]
            rest = [rows[16 + a : 17 + a, :] for a in range(2)]
            hi = rows[18:19, :]
        else:
            main, rest, hi, hot = read_routed(in_ref, sources)
        pairs = [unfold(err_ref[s], err_ref[t]) for s, t in zip(sources[::2], sources[1::2])]
        e = [jnp.concatenate([pair[a] for pair in pairs], axis=1) for a in range(2)]
        acc_ref[...] += scatter_j(hi, hot, main, rest, e)
        return carry

    acc_ref[...] = jnp.zeros(acc_ref.shape, F32)
    if steps == 1:
        body(0, 0)
    else:
        lax.fori_loop(0, steps, body, 0)
    last_point_sums_kernel(jp_ref, pidx_ref, pe_ref, pt_ref)
    scalars = jnp.sum(err_ref[...], axis=0)
    gamma1, delta1 = scalars[:, FULL : FULL + 1], scalars[:, HALF - 1 : HALF]
    gamma, alpha = sc_ref[0:1, 0:1], sc_ref[1:2, 0:1]
    ratio = gamma1 / gamma
    alpha1 = gamma1 / (delta1 - ratio * gamma1 / alpha)
    copies = [
        pltpu.make_async_copy(here, there, sems.at[k])
        for k, (here, there) in enumerate(zip((px_ref, cx_ref, pr_ref, cr_ref), outs))
    ]
    point_results(
        alpha, alpha1, ratio, pb_ref, pd_ref, ps_ref, pt_ref, px_ref, pr_ref, (copies[0], copies[2])
    )
    rhs, s = cb_ref[...], cs_ref[...]
    z = rhs / cd_ref[...]
    r1 = rhs - alpha * s
    z1 = r1 / cd_ref[...]
    x = alpha * z + alpha1 * (z1 + ratio * z)
    r2 = r1 - alpha1 * (z1 + acc_ref[...] + ratio * s)
    for table, target in ((x, cx_ref), (r2, cr_ref)):
        for k in range(3):
            cols = slice(k * 128, (k + 1) * 128)
            target[0:8, cols] = table[8 * k : 8 * k + 8]
            target[8:9, cols] = table[24 + k : 25 + k]
    copies[1].start()
    copies[3].start()
    for copy in copies:
        copy.wait()


def shards(jac_point, jac_cam, resid, point_index, cam_index):
    n_grp, n_tile = lax.axis_size("grp"), lax.axis_size("tile")
    devices = n_grp * n_tile
    obs = jac_point.shape[1]
    pidx, cidx = point_index.reshape(1, obs), cam_index.reshape(1, obs)
    hbm = pl.BlockSpec(memory_space=pltpu.HBM)
    ints = jax.ShapeDtypeStruct((1, obs), jnp.int32)
    places = jax.ShapeDtypeStruct((2, obs), jnp.int32)
    points = shape(3 * PH, LO)
    cameras = shape(OWN_ROWS, 128)
    routed, pb, pd, pu, jp, pidx_here, place, sc = pl.pallas_call(
        functools.partial(route_kernel, n_grp, n_tile),
        in_specs=[hbm] * 5,
        out_shape=(shape(3 * devices, 4, HALF), points, points, shape(2, obs), shape(6, obs), ints, places, shape(3, HALF)),
        scratch_shapes=[
            pltpu.VMEM((18, obs), F32),
            pltpu.VMEM((2, obs), F32),
            pltpu.VMEM((1, obs), jnp.int32),
            pltpu.SemaphoreType.DMA((8,)),
        ],
        compiler_params=PARAMS,
        name="route",
    )(*(pltpu.with_memory_space_constraint(x, pltpu.HBM) for x in (jac_point, jac_cam, resid, pidx, cidx)))
    routed = lax.all_to_all(routed, ("grp", "tile"), 0, 0, tiled=True).reshape(3 * devices // 2, 8, HALF)
    slots = devices * SLOTS
    per = min(STEP, devices)
    scratch = [
        pltpu.VMEM((2 * OWN_ROWS, 128), F32),
        pltpu.VMEM((2 * OWN_ROWS, 128), BF16),
        pltpu.VMEM((devices // per, 4, per * SLOTS), F32),
    ]
    kept_shapes = ()
    if devices == per:
        kept_shapes = (jax.ShapeDtypeStruct((128, slots), BF16), shape(24, slots))

    def owner(in_ref, sc_ref, back_ref, tb_ref, td_ref, ts_ref, *others):
        kept, work = others[: len(kept_shapes)], others[len(kept_shapes) :]
        owner_kernel(in_ref, sc_ref, back_ref, tb_ref, td_ref, ts_ref, *work, *kept)

    back, tb, td, ts, *kept = pl.pallas_call(
        owner,
        out_shape=(shape(devices, 2, HALF), cameras, cameras, cameras) + kept_shapes,
        scratch_shapes=scratch,
        compiler_params=PARAMS,
        name="owner",
    )(routed, sc)
    back = lax.all_to_all(back, ("grp", "tile"), 0, 0, tiled=True).reshape(devices // 4, 8, HALF)
    errors, ps, pe, sc, over = pl.pallas_call(
        functools.partial(routed_point_kernel, n_grp, n_tile),
        out_shape=(shape(devices, 1, HALF), points, shape(2, obs), shape(2, HALF), shape(1, HALF)),
        compiler_params=PARAMS,
        name="points",
    )(back, jp, pidx_here, place, pb, pd, pu, tb, td, ts)
    outputs = (shape(3, P_DEV), shape(9, CAM_DEV), shape(3, P_DEV), shape(9, CAM_DEV))

    def fits(*operands):
        errors = lax.all_to_all(operands[5], ("grp", "tile"), 0, 0, tiled=True)
        return pl.pallas_call(
            routed_final_kernel,
            out_shape=outputs,
            out_specs=[hbm] * 4,
            scratch_shapes=[pltpu.VMEM(v.shape, F32) for v in outputs]
            + [
                pltpu.VMEM((OWN_ROWS, 128), F32),
                pltpu.VMEM((3 * PH, LO), F32),
                pltpu.SemaphoreType.DMA((4,)),
            ],
            compiler_params=PARAMS,
            name="finish",
        )(errors, *operands[6:])

    def overflows(*operands):
        return tuple(replicated(*operands[:5]))

    over, *operands = lax.optimization_barrier(
        (
            over, jac_point, jac_cam, resid, point_index, cam_index,
            errors, routed, jp, pidx_here, pe, pb, pd, ps, tb, td, ts, sc, *kept,
        )
    )
    return lax.cond(over[0, 0] > 0, overflows, lambda *operands: tuple(fits(*operands)), *operands)


def solution(mesh):
    placed = (
        P(None, ("grp", "tile")),
        P(None, ("grp", "tile")),
        P(None, ("grp", "tile")),
        P(("grp", "tile")),
        P(("grp", "tile")),
    )
    return jax.shard_map(
        shards,
        mesh=mesh,
        in_specs=placed,
        out_specs=(P(None, ("grp", "tile")),) * 4,
        check_vma=False,
    )
```

```python
import functools

import jax
import jax.numpy as jnp
from jax import lax
from jax.experimental import pallas as pl
from jax.experimental.pallas import tpu as pltpu
from jax.sharding import PartitionSpec as P

P_DEV = 4096
CAM_DEV = 384
LO_BITS = 8
LO = 1 << LO_BITS
PH = P_DEV // LO
DAMPING = 1.0
F32 = jnp.float32
BF16 = jnp.bfloat16
SLOTS = 64
FULL = SLOTS - 1
HALF = 128
PARAMS = pltpu.CompilerParams(vmem_limit_bytes=48 * 1024 * 1024)


def halves(v):
    high = v.astype(BF16).astype(F32)
    return high, v - high


def rows16(width, step=1):
    numbers = lax.broadcasted_iota(jnp.int32, (16, width), 0)
    return (numbers // step if step > 1 else numbers).astype(F32).astype(BF16)


def sixteen(row):
    return jnp.broadcast_to(row.astype(F32), (16, row.shape[1])).astype(BF16)


def one_hot_rows(index, rows):
    numbers = rows16(index.shape[1])
    pieces = []
    for base in range(0, rows, 256):
        wide = sixteen(index - base)
        one, none = jnp.ones(wide.shape, BF16), jnp.zeros(wide.shape, BF16)
        pieces += [
            jnp.where(wide == numbers + BF16(16 * k), one, none)
            for k in range(min(256, rows - base) // 16)
        ]
    return jnp.concatenate(pieces, axis=0)


def dot_nt(a, b):
    return lax.dot_general(a, b, (((1,), (1,)), ((), ())), preferred_element_type=F32)


def dot_nn(a, b):
    return lax.dot_general(a, b, (((1,), (0,)), ((), ())), preferred_element_type=F32)


def is_row(hi, rows):
    return lax.broadcasted_iota(jnp.int32, (rows, hi.shape[1]), 0) == hi


def spread_row(mask, row):
    return jnp.where(mask, jnp.broadcast_to(row, mask.shape), 0.0)


def two_parts(v):
    high = v.astype(BF16)
    return high, (v - high.astype(F32)).astype(BF16)


def scatter_mixed(hi, hot, mains, tails, count, tail_rows):
    wide = sixteen(hi)
    none = jnp.zeros(wide.shape, BF16)
    single = len(mains) == 1
    numbers = rows16(hi.shape[1], 8) if single else none
    main_parts = two_parts(jnp.concatenate(mains * 2 if single else mains, axis=0))
    tail_parts = [two_parts(jnp.broadcast_to(v, wide.shape)) for v in tails]
    here = [wide == numbers + BF16(k) for k in range(0, count, 2 if single else 1)]
    tail_here = [wide == rows16(hi.shape[1]) + BF16(k) for k in range(0, tail_rows, 16)]
    pieces = []
    for part in range(2):
        pieces += [jnp.where(mask, main_parts[part], none) for mask in here]
        pieces += [jnp.where(mask, v[part], none) for v in tail_parts for mask in tail_here]
    return dot_nt(jnp.concatenate(pieces, axis=0), hot)


def both(v):
    half = v.shape[0] // 2
    return v[:half] + v[half:]


def gather_mixed(hi, hot, table, count, tail_rows):
    found = dot_nn(table, hot)
    hi8 = jnp.broadcast_to(hi, (8, hi.shape[1]))
    main = jnp.zeros(hi8.shape, F32)
    half = found.shape[0] // 2
    for k in range(count):
        rows = slice(k * 8, k * 8 + 8)
        low = slice(half + k * 8, half + k * 8 + 8)
        main = main + jnp.where(hi8 == k, found[rows] + found[low], 0.0)
    tail = found[count * 8 : half] + found[half + count * 8 :]
    tail = jnp.sum(jnp.where(is_row(hi, tail_rows), tail, 0.0), axis=0, keepdims=True)
    return main, tail


def stacked(table):
    high, low = halves(table)
    return jnp.concatenate([high, low], axis=0).astype(BF16)


def scatter_points(mask, hot, rows):
    pieces = [spread_row(mask, v[k : k + 1]) for v in halves(rows) for k in range(rows.shape[0])]
    return both(dot_nt(jnp.concatenate(pieces, axis=0).astype(BF16), hot))


def gather_points(mask, hot, table):
    found = both(dot_nn(stacked(table), hot))
    rows = mask.shape[0]
    return [
        jnp.sum(jnp.where(mask, found[i * rows : (i + 1) * rows], 0.0), axis=0, keepdims=True)
        for i in range(found.shape[0] // rows)
    ]


def total_of(v):
    return jnp.sum(jnp.sum(v, axis=0, keepdims=True), axis=1, keepdims=True)


def lanes(v, width):
    return jnp.broadcast_to(v, (v.shape[0], width))


def pack_kernel(
    n_grp, n_z, jp_hbm, jc_hbm, res_hbm, pidx_hbm, cidx_hbm,
    out_ref, pb_ref, pd_ref, pu_ref, jp_ref, pidx_ref,
    jc_ref, res_ref, cidx_ref, sems,
):
    copies = [
        pltpu.make_async_copy(source, target, sems.at[k])
        for k, (source, target) in enumerate(
            (
                (pidx_hbm, pidx_ref),
                (jp_hbm, jp_ref),
                (res_hbm, res_ref),
                (jc_hbm, jc_ref),
                (cidx_hbm, cidx_ref),
            )
        )
    ]
    for copy in copies:
        copy.start()
    for copy in copies:
        copy.wait()
    slot = out_ref.shape[2]
    index = pidx_ref[...]
    mask = is_row(index >> LO_BITS, PH)
    hot = one_hot_rows(index & (LO - 1), LO)
    jp = [jp_ref[k : k + 1, :] for k in range(6)]
    res = [res_ref[a : a + 1, :] for a in range(2)]
    grad = [-(jp[i] * res[0] + jp[3 + i] * res[1]) for i in range(3)]
    square = [jp[i] * jp[i] + jp[3 + i] * jp[3 + i] for i in range(3)]
    table = scatter_points(mask, hot, jnp.concatenate(grad + square, axis=0))
    rhs = table[: 3 * PH]
    diag = table[3 * PH :] + DAMPING
    pb_ref[...] = rhs
    pd_ref[...] = diag
    z = rhs / diag
    at = gather_points(mask, hot, z)
    u = [sum(jp[3 * a + i] * at[i] for i in range(3)) for a in range(2)]
    pu_ref[0:1, :] = u[0]
    pu_ref[1:2, :] = u[1]
    gamma = total_of(rhs * z)
    norm = total_of(z * z)
    scalars = jnp.concatenate([lanes(gamma, slot // 2), lanes(norm, slot // 2)], axis=1)
    cams = cidx_ref[...].astype(F32)
    for h in range(n_grp):
        cols = slice(h * slot, (h + 1) * slot)
        block = jnp.concatenate(
            [
                jc_ref[0:8, cols],
                jc_ref[9:17, cols],
                jc_ref[8:9, cols],
                jc_ref[17:18, cols],
                res[0][:, cols],
                res[1][:, cols],
                u[0][:, cols],
                u[1][:, cols],
                cams[:, cols],
                scalars,
            ],
            axis=0,
        )

        @pl.loop(0, n_z)
        def _(z_to, block=block, h=h):
            out_ref[h * n_z + z_to] = block


def read_blocks(ref, numbers):
    x = jnp.concatenate([ref[k] for k in numbers], axis=1)
    return x, x[22:23].astype(jnp.int32)


def chunk_of(chunk, per):
    return [chunk * per + k for k in range(per)]


def first_sums(ref, acc_ref, per, count, tail_rows):
    def body(chunk, carry):
        x, index = read_blocks(ref, chunk_of(chunk, per))
        hi, hot = index >> LO_BITS, one_hot_rows(index & (LO - 1), LO)
        j0, j1 = x[0:8], x[8:16]
        j08, j18, r0, r1 = x[16:17], x[17:18], x[18:19], x[19:20]
        acc_ref[...] += scatter_mixed(
            hi,
            hot,
            [-(j0 * r0 + j1 * r1), j0 * j0 + j1 * j1],
            [-(j08 * r0 + j18 * r1), j08 * j08 + j18 * j18],
            count,
            tail_rows,
        )
        return carry

    lax.fori_loop(0, ref.shape[0] // per, body, 0)


def own_sums_kernel(count, tail_rows, a_ref, acc_ref):
    acc_ref[...] = jnp.zeros(acc_ref.shape, F32)
    first_sums(a_ref, acc_ref, min(16, a_ref.shape[0]), count, tail_rows)


def camera_kernel(
    n_grp, n_z, count, tail_rows, a_ref, b_ref, start_ref,
    back_ref, tb_ref, td_ref, ts_ref,
    acc_ref, w_ref, zz_ref,
):
    blocks, _, slot = a_ref.shape
    per = min(8, blocks)
    chunks = blocks // per
    acc_ref[...] = start_ref[...]
    first_sums(b_ref, acc_ref, min(16, blocks), count, tail_rows)
    scalars = jnp.zeros((1, slot), F32)
    for ref in (a_ref, b_ref):
        scalars = scalars + jnp.sum(ref[:, 23, :], axis=0, keepdims=True)
    main = 8 * count
    half = acc_ref.shape[0] // 2
    for k in range(count):
        row = 16 * k
        tb_ref[8 * k : 8 * k + 8, :] = acc_ref[row : row + 8, :] + acc_ref[half + row : half + row + 8, :]
        row = 16 * k + 8
        td_ref[8 * k : 8 * k + 8, :] = (
            acc_ref[row : row + 8, :] + acc_ref[half + row : half + row + 8, :] + DAMPING
        )
    tb_ref[main:, :] = (
        acc_ref[2 * main : 2 * main + tail_rows, :]
        + acc_ref[half + 2 * main : half + 2 * main + tail_rows, :]
    )
    td_ref[main:, :] = (
        acc_ref[2 * main + tail_rows : half, :] + acc_ref[half + 2 * main + tail_rows :, :] + DAMPING
    )
    z = tb_ref[...] / td_ref[...]
    gamma = total_of(tb_ref[...] * z)
    norm = total_of(z * z)
    zz_ref[...] = stacked(z)
    ts_ref[...] = z
    acc_ref[0:half, :] = jnp.zeros((half, LO), F32)

    def second(ref, keep):
        def body(chunk, energy):
            numbers = chunk_of(chunk, per)
            x, index = read_blocks(ref, numbers)
            hi, hot = index >> LO_BITS, one_hot_rows(index & (LO - 1), LO)
            j0, j1 = x[0:8], x[8:16]
            j08, j18, u0, u1 = x[16:17], x[17:18], x[20:21], x[21:22]
            at, at8 = gather_mixed(hi, hot, zz_ref[...], count, tail_rows)
            w0 = jnp.sum(j0 * at, axis=0, keepdims=True) + j08 * at8
            w1 = jnp.sum(j1 * at, axis=0, keepdims=True) + j18 * at8
            if keep:
                for k, number in enumerate(numbers):
                    cols = slice(k * slot, (k + 1) * slot)
                    w_ref[number, 0:1, :] = w0[:, cols]
                    w_ref[number, 1:2, :] = w1[:, cols]
            e0, e1 = u0 + w0, u1 + w1
            acc_ref[0:half, :] += scatter_mixed(
                hi, hot, [j0 * e0 + j1 * e1], [j08 * e0 + j18 * e1], count, tail_rows
            )
            return energy + e0 * e0 + e1 * e1

        return body

    energy = jnp.zeros((1, per * slot), F32)
    energy = lax.fori_loop(0, chunks, second(a_ref, True), energy)
    energy = lax.fori_loop(0, chunks, second(b_ref, False), energy)
    ts_ref[...] += both(acc_ref[0:half, :])
    zz_ref[...] = stacked(ts_ref[...] / td_ref[...])
    share = 1.0 / n_grp
    gamma = gamma + share * scalars[:, 0:1]
    delta = norm + total_of(energy) + share * scalars[:, slot // 2 : slot // 2 + 1]
    mine = lax.axis_index("tile") // 2
    numbers = [g * n_z + mine for g in range(n_grp)]
    per = min(4, n_grp)
    for first in range(0, n_grp, per):
        some = numbers[first : first + per]
        x, index = read_blocks(a_ref, some)
        hi, hot = index >> LO_BITS, one_hot_rows(index & (LO - 1), LO)
        at, at8 = gather_mixed(hi, hot, zz_ref[...], count, tail_rows)
        v0 = jnp.sum(x[0:8] * at, axis=0, keepdims=True) + x[16:17] * at8
        v1 = jnp.sum(x[8:16] * at, axis=0, keepdims=True) + x[17:18] * at8
        for k in range(per):
            cols = slice(k * slot, (k + 1) * slot)
            g = first + k
            back_ref[g, 0:2, 0:slot] = w_ref[some[k], 0:2, :]
            back_ref[g, 2:3, 0:slot] = v0[:, cols]
            back_ref[g, 3:4, 0:slot] = v1[:, cols]
            back_ref[g, :, slot:] = lanes(jnp.concatenate([gamma, delta, gamma, delta], axis=0), 128)


def mine_kernel(main, tb_ref, td_ref, ts_ref, cb_ref, cd_ref, cs_ref):
    tile = lax.axis_index("tile")
    mine, core = tile // 2, tile % 2
    for source, target in ((tb_ref, cb_ref), (td_ref, cd_ref), (ts_ref, cs_ref)):
        own, own8 = [], []
        for k in range(3):
            rows = source[pl.ds(pl.multiple_of(8 * (3 * mine + k), 8), 8), :]
            tail = source[pl.ds(main + 3 * mine + k, 1), :]
            own += [rows[:, :128], rows[:, 128:]]
            own8 += [tail[:, :128], tail[:, 128:]]
        for m in range(3):
            cols = slice(m * 128, (m + 1) * 128)
            target[0:8, cols] = jnp.where(core == 0, own[m], own[m + 3])
            target[8:9, cols] = jnp.where(core == 0, own8[m], own8[m + 3])


def point_kernel(
    n_grp, back_ref, jp_ref, pidx_ref, pb_ref, pd_ref, pu_ref, cb_ref, cd_ref, cs_ref,
    out_ref, ps_ref, pe_ref, sc_ref,
):
    slot = back_ref.shape[2] - 128
    index = pidx_ref[...]
    mask = is_row(index >> LO_BITS, PH)
    hot = one_hot_rows(index & (LO - 1), LO)
    jp = [jp_ref[k : k + 1, :] for k in range(6)]
    scalars = back_ref[0, :, slot:]
    for h in range(1, n_grp):
        scalars = scalars + back_ref[h, :, slot:]
    gamma, delta = scalars[0:1, 0:1], scalars[1:2, 0:1]
    alpha = gamma / delta
    w = [
        jnp.concatenate([back_ref[h, r : r + 1, 0:slot] for h in range(n_grp)], axis=1) for r in range(4)
    ]
    rhs, diag = pb_ref[...], pd_ref[...]
    z = rhs / diag
    error = [pu_ref[a : a + 1, :] + w[a] for a in range(2)]
    s = z + scatter_points(mask, hot, jp_ref[0:3, :] * error[0] + jp_ref[3:6, :] * error[1])
    r1 = rhs - alpha * s
    z1 = r1 / diag
    at = gather_points(mask, hot, z1)
    error = [
        sum(jp[3 * a + i] * at[i] for i in range(3)) + (w[a] - alpha * w[2 + a]) for a in range(2)
    ]
    ps_ref[...] = s
    pe_ref[0:1, :] = error[0]
    pe_ref[1:2, :] = error[1]
    cr1 = cb_ref[...] - alpha * cs_ref[...]
    cz1 = cr1 / cd_ref[...]
    gamma1 = total_of(r1 * z1) + total_of(cr1 * cz1)
    delta1 = (
        total_of(error[0] * error[0] + error[1] * error[1]) + total_of(z1 * z1) + total_of(cz1 * cz1)
    )
    sc_ref[...] = lanes(jnp.concatenate([gamma, alpha], axis=0), 128)
    tail = lanes(jnp.concatenate([gamma1, delta1], axis=0), 128)
    per = out_ref.shape[0] // n_grp
    for h in range(n_grp):
        cols = slice(h * slot, (h + 1) * slot)
        block = jnp.concatenate([jnp.concatenate([e[:, cols] for e in error], axis=0), tail], axis=1)

        @pl.loop(0, per)
        def _(tile, block=block, h=h):
            out_ref[h * per + tile] = block


def last_point_sums_kernel(jp_ref, pidx_ref, pe_ref, pt_ref):
    index = pidx_ref[...]
    mask = is_row(index >> LO_BITS, PH)
    hot = one_hot_rows(index & (LO - 1), LO)
    terms = jp_ref[0:3, :] * pe_ref[0:1, :] + jp_ref[3:6, :] * pe_ref[1:2, :]
    pt_ref[...] = scatter_points(mask, hot, terms)


def final_kernel(
    err_ref, a_ref, b_ref, pb_ref, pd_ref, ps_ref, pt_ref, cb_ref, cd_ref, cs_ref, sc_ref,
    px_ref, cx_ref, pr_ref, cr_ref, acc_ref,
):
    blocks, _, slot = a_ref.shape
    per = min(8, blocks)
    chunks = blocks // per
    tile = lax.axis_index("tile")
    core = tile % 2
    acc_ref[...] = jnp.zeros(acc_ref.shape, F32)

    def body(ref, parity):
        def step(chunk, scalars):
            numbers = chunk_of(chunk, per)
            x, index = read_blocks(ref, numbers)
            errs = [err_ref[2 * k + parity] for k in numbers]
            e = jnp.concatenate([v[:, 0:slot] for v in errs], axis=1)
            for v in errs:
                scalars = scalars + v[:, slot:]
            index = index - tile * CAM_DEV
            hi = index >> 7
            hot = one_hot_rows(index & 127, 128)
            j0, j1 = x[0:8], x[8:16]
            e0, e1 = e[0:1], e[1:2]
            acc_ref[...] += scatter_mixed(
                hi, hot, [j0 * e0 + j1 * e1], [x[16:17] * e0 + x[17:18] * e1], 4, 16
            )
            return scalars

        return step

    scalars = lax.fori_loop(0, chunks, body(a_ref, core), jnp.zeros((2, 128), F32))
    scalars = lax.fori_loop(0, chunks, body(b_ref, 1 - core), scalars)
    gamma1, delta1 = scalars[0:1, 0:1], scalars[1:2, 0:1]
    gamma, alpha = sc_ref[0:1, 0:1], sc_ref[1:2, 0:1]
    ratio = gamma1 / gamma
    alpha1 = gamma1 / (delta1 - ratio * gamma1 / alpha)

    rhs, diag, s = pb_ref[...], pd_ref[...], ps_ref[...]
    z = rhs / diag
    r1 = rhs - alpha * s
    z1 = r1 / diag
    x = alpha * z + alpha1 * (z1 + ratio * z)
    r2 = r1 - alpha1 * (z1 + pt_ref[...] + ratio * s)
    for i in range(3):
        for hi in range(PH):
            row = i * PH + hi
            px_ref[i : i + 1, hi * LO : (hi + 1) * LO] = x[row : row + 1]
            pr_ref[i : i + 1, hi * LO : (hi + 1) * LO] = r2[row : row + 1]

    rhs, s = cb_ref[...], cs_ref[...]
    z = rhs / cd_ref[...]
    r1 = rhs - alpha * s
    z1 = r1 / cd_ref[...]
    cx_ref[...] = alpha * z + alpha1 * (z1 + ratio * z)
    sums = both(acc_ref[...])
    base = r1 - alpha1 * (z1 + ratio * s)
    for k in range(3):
        cols = slice(k * 128, (k + 1) * 128)
        cr_ref[0:8, cols] = base[0:8, cols] - alpha1 * sums[8 * k : 8 * k + 8, :]
        cr_ref[8:9, cols] = base[8:9, cols] - alpha1 * sums[32 + k : 33 + k, :]


def shape(*dims):
    return jax.ShapeDtypeStruct(dims, F32)


def replicated(jac_point, jac_cam, resid, point_index, cam_index):
    n_grp, n_tile = lax.axis_size("grp"), lax.axis_size("tile")
    n_z = n_tile // 2
    obs = jac_point.shape[1]
    slot = obs // n_grp
    blocks = n_grp * n_z
    count = CAM_DEV * n_tile // LO
    tail_rows = -(-count // 16) * 16
    rows = 8 * count + tail_rows
    groups = [[d * 2 + core for d in range(blocks)] for core in range(2)]
    swap = [(t, t ^ 1) for t in range(n_tile)]
    pidx, cidx = point_index.reshape(1, obs), cam_index.reshape(1, obs)

    hbm = pl.BlockSpec(memory_space=pltpu.HBM)
    packed, pb, pd, pu, jp, pidx = pl.pallas_call(
        functools.partial(pack_kernel, n_grp, n_z),
        in_specs=[hbm] * 5,
        out_shape=(
            shape(blocks, 24, slot),
            shape(3 * PH, LO),
            shape(3 * PH, LO),
            shape(2, obs),
            shape(6, obs),
            jax.ShapeDtypeStruct((1, obs), jnp.int32),
        ),
        scratch_shapes=[
            pltpu.VMEM((18, obs), F32),
            pltpu.VMEM((2, obs), F32),
            pltpu.VMEM((1, obs), jnp.int32),
            pltpu.SemaphoreType.DMA((5,)),
        ],
        compiler_params=PARAMS,
        name="pack",
    )(*(pltpu.with_memory_space_constraint(x, pltpu.HBM) for x in (jac_point, jac_cam, resid, pidx, cidx)))
    own = lax.all_to_all(packed, ("grp", "tile"), 0, 0, axis_index_groups=groups, tiled=True)
    other = lax.ppermute(own, "tile", swap)
    sums = pl.pallas_call(
        functools.partial(own_sums_kernel, count, tail_rows),
        out_shape=shape(4 * rows, LO),
        compiler_params=PARAMS,
        name="own_sums",
        cost_estimate=pl.CostEstimate(flops=2 * 10**9, bytes_accessed=10**6, transcendentals=0),
    )(own)
    table = shape(rows, LO)
    back, tb, td, ts = pl.pallas_call(
        functools.partial(camera_kernel, n_grp, n_z, count, tail_rows),
        out_shape=(shape(n_grp, 4, slot + 128), table, table, table),
        scratch_shapes=[
            pltpu.VMEM((4 * rows, LO), F32),
            pltpu.VMEM((blocks, 2, slot), F32),
            pltpu.VMEM((2 * rows, LO), BF16),
        ],
        compiler_params=PARAMS,
        name="cameras",
    )(own, other, sums)
    back = lax.all_to_all(back, "grp", 0, 0, tiled=True)
    cb, cd, cs = pl.pallas_call(
        functools.partial(mine_kernel, 8 * count),
        out_shape=(shape(9, CAM_DEV),) * 3,
        compiler_params=PARAMS,
        name="mine",
    )(tb, td, ts)
    errors, ps, pe, sc = pl.pallas_call(
        functools.partial(point_kernel, n_grp),
        out_shape=(
            shape(n_grp * n_tile, 2, slot + 128),
            shape(3 * PH, LO),
            shape(2, obs),
            shape(2, 128),
        ),
        compiler_params=PARAMS,
        name="points",
    )(back, jp, pidx, pb, pd, pu, cb, cd, cs)
    errors = lax.all_to_all(errors, ("grp", "tile"), 0, 0, tiled=True)
    pt = pl.pallas_call(
        last_point_sums_kernel,
        out_shape=shape(3 * PH, LO),
        compiler_params=PARAMS,
        name="last_point_sums",
    )(jp, pidx, pe)
    return pl.pallas_call(
        final_kernel,
        out_shape=(shape(3, P_DEV), shape(9, CAM_DEV), shape(3, P_DEV), shape(9, CAM_DEV)),
        scratch_shapes=[pltpu.VMEM((96, 128), F32)],
        compiler_params=PARAMS,
        name="finish",
    )(errors, own, other, pb, pd, ps, pt, cb, cd, cs, sc)


def eights(row):
    return jnp.broadcast_to(row, (8, row.shape[1]))


def row_numbers(width):
    return lax.broadcasted_iota(jnp.int32, (16, width), 0)


def as_16_bit(numbers):
    return numbers.astype(F32).astype(BF16)


def masked_rows(parts, masks):
    none = jnp.zeros(parts[0].shape, BF16)
    return jnp.concatenate([jnp.where(m, p, none) for p in parts for m in masks], axis=0)


def low_lanes(rows):
    return lax.broadcasted_iota(jnp.int32, (rows, HALF), 1) < SLOTS


def swap_lanes(v):
    return pltpu.roll(v, SLOTS, 1)


def point_sums(pidx_ref, jp_ref, res_ref):
    index = pidx_ref[...]
    mask = is_row(index >> LO_BITS, PH)
    hot = one_hot_rows(index & (LO - 1), LO)
    jp = jp_ref[0:3, :], jp_ref[3:6, :]
    grad = -(jp[0] * res_ref[0:1, :] + jp[1] * res_ref[1:2, :])
    square = jp[0] * jp[0] + jp[1] * jp[1]
    return scatter_points(mask, hot, jnp.concatenate([grad, square], axis=0)), mask, hot, jp


def start_copies(pairs, sems):
    copies = [pltpu.make_async_copy(a, b, sems.at[k]) for k, (a, b) in enumerate(pairs)]
    for copy in copies:
        copy.start()
    for copy in copies:
        copy.wait()


def route_kernel(
    n_grp, n_tile, jp_hbm, jc_hbm, res_hbm, pidx_hbm, cidx_hbm,
    out_ref, pb_ref, pd_ref, pu_ref, jp_ref, pidx_ref, place_ref, sc_ref,
    jc_ref, res_ref, cidx_ref, sems,
):
    width = cidx_ref.shape[1] // 4
    pairs = [(pidx_hbm, pidx_ref), (jp_hbm, jp_ref), (res_hbm, res_ref), (cidx_hbm, cidx_ref)]
    for k in range(4):
        part = pl.ds(k * width, width)
        pairs.append((jc_hbm.at[:, part], jc_ref.at[:, part]))
    start_copies(pairs, sems)
    slot = cidx_ref.shape[1] // n_grp
    cams = cidx_ref[...]
    owner = ((cams >> 7) * 171) >> 9
    local = (cams - owner * CAM_DEV).astype(F32)
    mine = is_row(owner, n_tile)
    ones = jnp.where(mine, 1.0, 0.0)
    stack = jnp.concatenate([ones[:, h * slot : (h + 1) * slot] for h in range(n_grp)], axis=0)
    before = lax.broadcasted_iota(jnp.int32, (slot, slot), 0)
    before = before < lax.broadcasted_iota(jnp.int32, (slot, slot), 1)
    counts = dot_nn(stack.astype(BF16), jnp.where(before, 1.0, 0.0).astype(BF16))
    counts = jnp.concatenate([counts[h * n_tile : (h + 1) * n_tile] for h in range(n_grp)], axis=1)
    rank = jnp.sum(jnp.where(mine, counts, 0.0), axis=0, keepdims=True)
    place_ref[0:1, :] = owner
    place_ref[1:2, :] = rank.astype(jnp.int32)
    over = jnp.max(jnp.where(rank >= FULL, 1.0, 0.0), axis=1, keepdims=True)
    rank = rank.astype(jnp.int32)
    hot_rank = one_hot_rows(rank, HALF)
    wide = sixteen(owner)
    numbers = row_numbers(owner.shape[1])
    core = lax.axis_index("tile") % 2
    upper, lower, others = core, 1 + core, 2 - 2 * core
    low = low_lanes(8)

    def route_main(h):
        cols = slice(h * slot, (h + 1) * slot)
        here = [wide[:, cols] == BF16(t) for t in range(n_tile)]
        parts = two_parts(jnp.concatenate([jc_ref[0:8, cols], jc_ref[9:17, cols]], axis=0))
        moved = both(dot_nt(masked_rows(parts, here), hot_rank[:, cols]))
        for t in range(n_tile):
            first, second = moved[16 * t : 16 * t + 8], moved[16 * t + 8 : 16 * t + 16]
            tile = jnp.where(low, first, swap_lanes(second))
            out_ref[3 * (h * n_tile + t) + upper] = tile[0:4]
            out_ref[3 * (h * n_tile + t) + lower] = tile[4:8]

    def route_rest(parts, here, h):
        cols = slice(h * slot, (h + 1) * slot)
        left = masked_rows([p[:, cols] for p in parts], [m[:, cols] for m in here])
        moved = both(dot_nt(left, hot_rank[:, cols]))
        for t in range(n_tile):
            rows = moved[8 * t : 8 * t + 8]
            tile = jnp.where(low[0:4], rows[0:4], swap_lanes(rows)[4:8])
            out_ref[3 * (h * n_tile + t) + others] = tile

    table, mask, hot, jp = point_sums(pidx_ref, jp_ref, res_ref)
    for h in range(n_grp):
        route_main(h)
    rhs, diag = table[: 3 * PH], table[3 * PH :] + DAMPING
    z = rhs / diag
    at = gather_points(mask, hot, z)
    pb_ref[...] = rhs
    pd_ref[...] = diag
    u = [sum(jp[a][i : i + 1] * at[i] for i in range(3)) for a in range(2)]
    pu_ref[0:1, :] = u[0]
    pu_ref[1:2, :] = u[1]
    sc_ref[...] = lanes(jnp.concatenate([total_of(rhs * z), total_of(z * z), over], axis=0), HALF)
    rows = [jc_ref[8:9, :], res_ref[0:1, :], local, u[0], jc_ref[17:18, :], res_ref[1:2, :], local, u[1]]
    parts = two_parts(jnp.concatenate(rows * 2, axis=0))
    here = [wide == as_16_bit((numbers >> 3) + t) for t in range(0, n_tile, 2)]
    for h in range(n_grp):
        route_rest(parts, here, h)


def unfold(even, odd):
    low = low_lanes(even.shape[0])
    return jnp.where(low, even, swap_lanes(odd)), jnp.where(low, swap_lanes(even), odd)


def unfold_rest(both_rows):
    low, swapped = low_lanes(4), swap_lanes(both_rows)
    return (
        jnp.where(low, both_rows[0:4], swapped[4:8]),
        jnp.where(low, swapped[0:4], both_rows[4:8]),
    )


def last_slot(v):
    return (lax.broadcasted_iota(jnp.int32, v.shape, 1) & (SLOTS - 1)) == FULL


def read_routed(ref, sources):
    main, rest = ([], []), ([], [])
    for s in sources[::2]:
        tile = 3 * (s // 2)
        pair = unfold(ref[tile], ref[tile + 2])
        pair_rest = unfold_rest(ref[tile + 1])
        for a in range(2):
            main[a].append(pair[a])
            rest[a].append(pair_rest[a])
    main = [jnp.concatenate(v, axis=1) for v in main]
    rest = [jnp.concatenate(v, axis=1) for v in rest]
    index = rest[0][2:3].astype(jnp.int32)
    return main, rest, (index >> 7).astype(F32), one_hot_rows(index & 127, 128)


OWN_ROWS = 32
STEP = 32


def scatter_two(hi, hot, first, second):
    wide, numbers = sixteen(hi), row_numbers(hi.shape[1])
    blocks = [wide == BF16(k) for k in range(3)]
    tail = wide == as_16_bit(numbers & 7)
    rows = two_parts(jnp.concatenate([first[0], second[0]], axis=0))
    tails = two_parts(jnp.concatenate([eights(first[1]), eights(second[1])], axis=0))
    none = jnp.zeros(wide.shape, BF16)
    pieces = []
    for part in range(2):
        pieces += [jnp.where(mask, rows[part], none) for mask in blocks]
        pieces.append(jnp.where(tail, tails[part], none))
    return both(dot_nt(jnp.concatenate(pieces, axis=0), hot))


def scatter_one(hi, hot, main, tail):
    wide, numbers = sixteen(hi), row_numbers(hi.shape[1])
    upper = wide == as_16_bit(numbers >> 3)
    lower = wide == as_16_bit(jnp.where(numbers < 8, 2, numbers - 8))
    rows = two_parts(jnp.concatenate([main, main], axis=0))
    tails = two_parts(jnp.concatenate([main, eights(tail)], axis=0))
    none = jnp.zeros(wide.shape, BF16)
    pieces = []
    for part in range(2):
        pieces += [jnp.where(upper, rows[part], none), jnp.where(lower, tails[part], none)]
    return both(dot_nt(jnp.concatenate(pieces, axis=0), hot))


def gather_own(hi, hot, table, main, rest):
    found = both(dot_nn(table, hot))
    block = eights(hi)
    at = jnp.where(block == 0, found[0:8], jnp.where(block == 1, found[8:16], found[16:24]))
    numbers = lax.broadcasted_iota(jnp.int32, block.shape, 0).astype(F32)
    tail = jnp.where(block == numbers, found[24:32], 0.0)
    return [
        jnp.sum(main[a] * at + eights(rest[a][0:1]) * tail, axis=0, keepdims=True) for a in range(2)
    ]


def scatter_j(hi, hot, main, rest, e):
    return scatter_one(
        hi, hot, main[0] * e[0] + main[1] * e[1], rest[0][0:1] * e[0] + rest[1][0:1] * e[1]
    )


def owner_kernel(in_ref, sc_ref, back_ref, tb_ref, td_ref, ts_ref, acc_ref, zz_ref, w_ref, *kept):
    devices = back_ref.shape[0]
    per = min(STEP, devices)
    steps = devices // per

    if steps == 1:
        main, rest, hi, hot = read_routed(in_ref, range(devices))
        kept[0][...] = hot
        for a in range(2):
            kept[1][8 * a : 8 * a + 8, :] = main[a]
            kept[1][16 + a : 17 + a, :] = rest[a][0:1]
        kept[1][18:19, :] = hi

        def loop(body, start):
            return body((main, rest, hi, hot), 0, start)
    else:

        def loop(body, start):
            def step(number, carry):
                return body(read_routed(in_ref, chunk_of(number, per)), number, carry)

            return lax.fori_loop(0, steps, step, start)

    def rhs_and_diag(slots, number, carry):
        main, rest, hi, hot = slots
        r = [rest[a][1:2] for a in range(2)]
        rhs = (-(main[0] * r[0] + main[1] * r[1]), -(rest[0][0:1] * r[0] + rest[1][0:1] * r[1]))
        square = (
            main[0] * main[0] + main[1] * main[1],
            rest[0][0:1] * rest[0][0:1] + rest[1][0:1] * rest[1][0:1],
        )
        acc_ref[...] += scatter_two(hi, hot, rhs, square)
        return carry

    acc_ref[...] = jnp.zeros(acc_ref.shape, F32)
    loop(rhs_and_diag, 0)
    rhs = jnp.concatenate([acc_ref[16 * k : 16 * k + 8, :] for k in range(4)], axis=0)
    diag = jnp.concatenate([acc_ref[16 * k + 8 : 16 * k + 16, :] for k in range(4)], axis=0) + DAMPING
    tb_ref[...] = rhs
    td_ref[...] = diag
    z = rhs / diag
    zz_ref[...] = stacked(z)
    acc_ref[0:OWN_ROWS, :] = z

    def apply(slots, number, energy):
        main, rest, hi, hot = slots
        w = gather_own(hi, hot, zz_ref[...], main, rest)
        e = [rest[a][3:4] + w[a] for a in range(2)]
        for a in range(2):
            w_ref[number, 2 * a : 2 * a + 1, :] = w[a]
        acc_ref[0:OWN_ROWS, :] += scatter_j(hi, hot, main, rest, e)
        return energy + e[0] * e[0] + e[1] * e[1]

    energy = loop(apply, jnp.zeros((1, per * SLOTS), F32))
    s = acc_ref[0:OWN_ROWS, :]
    ts_ref[...] = s
    zz_ref[...] = stacked(s / diag)
    gamma = sc_ref[0:1, :] + total_of(rhs * z)
    delta = sc_ref[1:2, :] + total_of(z * z) + total_of(energy)
    over = sc_ref[2:3, :]
    low = low_lanes(2)
    tail = jnp.where(
        low, jnp.concatenate([gamma, over], axis=0), jnp.concatenate([delta, over], axis=0)
    )

    def send(slots, number, carry):
        main, rest, hi, hot = slots
        v = gather_own(hi, hot, zz_ref[...], main, rest)
        for a in range(2):
            w_ref[number, 2 * a + 1 : 2 * a + 2, :] = v[a]
        w = w_ref[number]
        for k in range(per // 2):
            cols = slice(k * HALF, (k + 1) * HALF)
            first, second = w[0:2, cols], w[2:4, cols]
            even = jnp.where(low, first, swap_lanes(second))
            odd = jnp.where(low, swap_lanes(first), second)
            for t, tile in ((2 * k, even), (2 * k + 1, odd)):
                back_ref[number * per + t] = jnp.where(last_slot(tile), tail, tile)
        return carry

    loop(send, 0)


def halved(ref):
    return jnp.concatenate(
        [
            ref[i * PH : (i + 1) * PH, half * HALF : (half + 1) * HALF]
            for i in range(3)
            for half in range(2)
        ],
        axis=0,
    )


def routed_point_kernel(
    n_grp, n_tile, back_ref, jp_ref, pidx_ref, place_ref, pb_ref, pd_ref, pu_ref, cb_ref, cd_ref, cs_ref,
    out_ref, ps_ref, pe_ref, sc_ref, over_ref,
):
    slot = place_ref.shape[1] // n_grp
    index = pidx_ref[...]
    mask = is_row(((index >> 7) & 1) * PH + (index >> LO_BITS), 2 * PH)
    hot = one_hot_rows(index & (HALF - 1), HALF)
    jp = [jp_ref[k : k + 1, :] for k in range(6)]
    scalars = jnp.sum(back_ref[...], axis=0)
    scalars = scalars[0:4] + scalars[4:8]
    scalars = scalars[0:2] + scalars[2:4]
    gamma, delta = scalars[0:1, FULL : FULL + 1], scalars[0:1, HALF - 1 : HALF]
    over_ref[...] = lanes(scalars[1:2, FULL : FULL + 1], HALF)
    alpha = gamma / delta
    owner = place_ref[0:1, :]
    hot_rank = one_hot_rows(place_ref[1:2, :], HALF)
    numbers = lax.broadcasted_iota(jnp.int32, (2 * n_tile, slot), 0) >> 1
    terms = []
    for h in range(n_grp):
        cols = slice(h * slot, (h + 1) * slot)
        rows = jnp.concatenate([back_ref[h * n_tile // 4 + k] for k in range(n_tile // 4)], axis=0)
        rows = jnp.concatenate([rows, swap_lanes(rows)], axis=0)
        found = both(dot_nn(stacked(rows), hot_rank[:, cols]))
        here = numbers == owner[:, cols]
        of_a = []
        for a in range(2):
            mine = jnp.where(here, found[2 * n_tile * a : 2 * n_tile * (a + 1)], 0.0)
            mine = sum(mine[8 * k : 8 * k + 8] for k in range(n_tile // 4))
            mine = mine[0:4] + mine[4:8]
            of_a.append(mine[0:2] + mine[2:4])
        terms.append(jnp.concatenate(of_a, axis=0))
    terms = jnp.concatenate(terms, axis=1)
    w0 = [terms[2 * a : 2 * a + 1] for a in range(2)]
    w1 = [terms[2 * a + 1 : 2 * a + 2] for a in range(2)]
    rhs, diag = halved(pb_ref), halved(pd_ref)
    z = rhs / diag
    error = [pu_ref[a : a + 1, :] + w0[a] for a in range(2)]
    s = z + scatter_points(mask, hot, jp_ref[0:3, :] * error[0] + jp_ref[3:6, :] * error[1])
    r1 = rhs - alpha * s
    z1 = r1 / diag
    at = gather_points(mask, hot, z1)
    error = [sum(jp[3 * a + i] * at[i] for i in range(3)) + (w0[a] - alpha * w1[a]) for a in range(2)]
    for i in range(3):
        for half in range(2):
            row = (2 * i + half) * PH
            ps_ref[i * PH : (i + 1) * PH, half * HALF : (half + 1) * HALF] = s[row : row + PH]
    pe_ref[0:1, :] = error[0]
    pe_ref[1:2, :] = error[1]
    cr1 = cb_ref[...] - alpha * cs_ref[...]
    cz1 = cr1 / cd_ref[...]
    gamma1 = total_of(r1 * z1) + total_of(cr1 * cz1)
    delta1 = (
        total_of(error[0] * error[0] + error[1] * error[1]) + total_of(z1 * z1) + total_of(cz1 * cz1)
    )
    sc_ref[...] = lanes(jnp.concatenate([gamma, alpha], axis=0), HALF)
    tail = jnp.where(low_lanes(1), gamma1, delta1)
    wide, numbers = sixteen(owner), row_numbers(owner.shape[1])
    parts = two_parts(jnp.concatenate([eights(e) for e in error], axis=0))
    here = [wide == as_16_bit((numbers & 7) + t) for t in range(0, n_tile, 8)]
    left = masked_rows(parts, here)
    low = low_lanes(8)
    for h in range(n_grp):
        moved = both(dot_nt(left[:, h * slot : (h + 1) * slot], hot_rank[:, h * slot : (h + 1) * slot]))
        for t in range(0, n_tile, 8):
            tile = jnp.where(low, moved[2 * t : 2 * t + 8], swap_lanes(moved[2 * t + 8 : 2 * t + 16]))
            tile = jnp.where(last_slot(tile), tail, tile)
            for k in range(8):
                out_ref[h * n_tile + t + k] = tile[k : k + 1]


def point_results(alpha, alpha1, ratio, pb_ref, pd_ref, ps_ref, pt_ref, px_ref, pr_ref, copies):
    rhs, diag, s = pb_ref[...], pd_ref[...], ps_ref[...]
    z = rhs / diag
    r1 = rhs - alpha * s
    z1 = r1 / diag
    x = alpha * z + alpha1 * (z1 + ratio * z)
    r2 = r1 - alpha1 * (z1 + pt_ref[...] + ratio * s)
    for table, target, copy in ((x, px_ref, copies[0]), (r2, pr_ref, copies[1])):
        for i in range(3):
            for hi in range(PH):
                row = i * PH + hi
                target[i : i + 1, hi * LO : (hi + 1) * LO] = table[row : row + 1]
        copy.start()


def routed_final_kernel(
    err_ref, in_ref, jp_ref, pidx_ref, pe_ref, pb_ref, pd_ref, ps_ref, cb_ref, cd_ref, cs_ref, sc_ref, *rest_refs
):
    kept, outs, (px_ref, cx_ref, pr_ref, cr_ref, acc_ref, pt_ref, sems) = (
        rest_refs[:-11],
        rest_refs[-11:-7],
        rest_refs[-7:],
    )
    devices = err_ref.shape[0]
    per = min(STEP, devices)
    steps = devices // per

    def body(step, carry):
        sources = chunk_of(step, per)
        if kept:
            hot, rows = kept[0][...], kept[1]
            main = [rows[8 * a : 8 * a + 8, :] for a in range(2)]
            rest = [rows[16 + a : 17 + a, :] for a in range(2)]
            hi = rows[18:19, :]
        else:
            main, rest, hi, hot = read_routed(in_ref, sources)
        pairs = [unfold(err_ref[s], err_ref[t]) for s, t in zip(sources[::2], sources[1::2])]
        e = [jnp.concatenate([pair[a] for pair in pairs], axis=1) for a in range(2)]
        acc_ref[...] += scatter_j(hi, hot, main, rest, e)
        return carry

    acc_ref[...] = jnp.zeros(acc_ref.shape, F32)
    if steps == 1:
        body(0, 0)
    else:
        lax.fori_loop(0, steps, body, 0)
    last_point_sums_kernel(jp_ref, pidx_ref, pe_ref, pt_ref)
    scalars = jnp.sum(err_ref[...], axis=0)
    gamma1, delta1 = scalars[:, FULL : FULL + 1], scalars[:, HALF - 1 : HALF]
    gamma, alpha = sc_ref[0:1, 0:1], sc_ref[1:2, 0:1]
    ratio = gamma1 / gamma
    alpha1 = gamma1 / (delta1 - ratio * gamma1 / alpha)
    copies = [
        pltpu.make_async_copy(here, there, sems.at[k])
        for k, (here, there) in enumerate(zip((px_ref, cx_ref, pr_ref, cr_ref), outs))
    ]
    point_results(
        alpha, alpha1, ratio, pb_ref, pd_ref, ps_ref, pt_ref, px_ref, pr_ref, (copies[0], copies[2])
    )
    rhs, s = cb_ref[...], cs_ref[...]
    z = rhs / cd_ref[...]
    r1 = rhs - alpha * s
    z1 = r1 / cd_ref[...]
    x = alpha * z + alpha1 * (z1 + ratio * z)
    r2 = r1 - alpha1 * (z1 + acc_ref[...] + ratio * s)
    for table, target in ((x, cx_ref), (r2, cr_ref)):
        for k in range(3):
            cols = slice(k * 128, (k + 1) * 128)
            target[0:8, cols] = table[8 * k : 8 * k + 8]
            target[8:9, cols] = table[24 + k : 25 + k]
    copies[1].start()
    copies[3].start()
    for copy in copies:
        copy.wait()


def shards(jac_point, jac_cam, resid, point_index, cam_index):
    n_grp, n_tile = lax.axis_size("grp"), lax.axis_size("tile")
    devices = n_grp * n_tile
    obs = jac_point.shape[1]
    pidx, cidx = point_index.reshape(1, obs), cam_index.reshape(1, obs)
    hbm = pl.BlockSpec(memory_space=pltpu.HBM)
    ints = jax.ShapeDtypeStruct((1, obs), jnp.int32)
    places = jax.ShapeDtypeStruct((2, obs), jnp.int32)
    points = shape(3 * PH, LO)
    cameras = shape(OWN_ROWS, 128)
    routed, pb, pd, pu, jp, pidx_here, place, sc = pl.pallas_call(
        functools.partial(route_kernel, n_grp, n_tile),
        in_specs=[hbm] * 5,
        out_shape=(shape(3 * devices, 4, HALF), points, points, shape(2, obs), shape(6, obs), ints, places, shape(3, HALF)),
        scratch_shapes=[
            pltpu.VMEM((18, obs), F32),
            pltpu.VMEM((2, obs), F32),
            pltpu.VMEM((1, obs), jnp.int32),
            pltpu.SemaphoreType.DMA((8,)),
        ],
        compiler_params=PARAMS,
        name="route",
    )(*(pltpu.with_memory_space_constraint(x, pltpu.HBM) for x in (jac_point, jac_cam, resid, pidx, cidx)))
    routed = lax.all_to_all(routed, ("grp", "tile"), 0, 0, tiled=True).reshape(3 * devices // 2, 8, HALF)
    slots = devices * SLOTS
    per = min(STEP, devices)
    scratch = [
        pltpu.VMEM((2 * OWN_ROWS, 128), F32),
        pltpu.VMEM((2 * OWN_ROWS, 128), BF16),
        pltpu.VMEM((devices // per, 4, per * SLOTS), F32),
    ]
    kept_shapes = ()
    if devices == per:
        kept_shapes = (jax.ShapeDtypeStruct((128, slots), BF16), shape(24, slots))

    def owner(in_ref, sc_ref, back_ref, tb_ref, td_ref, ts_ref, *others):
        kept, work = others[: len(kept_shapes)], others[len(kept_shapes) :]
        owner_kernel(in_ref, sc_ref, back_ref, tb_ref, td_ref, ts_ref, *work, *kept)

    back, tb, td, ts, *kept = pl.pallas_call(
        owner,
        out_shape=(shape(devices, 2, HALF), cameras, cameras, cameras) + kept_shapes,
        scratch_shapes=scratch,
        compiler_params=PARAMS,
        name="owner",
    )(routed, sc)
    back = lax.all_to_all(back, ("grp", "tile"), 0, 0, tiled=True).reshape(devices // 4, 8, HALF)
    errors, ps, pe, sc, over = pl.pallas_call(
        functools.partial(routed_point_kernel, n_grp, n_tile),
        out_shape=(shape(devices, 1, HALF), points, shape(2, obs), shape(2, HALF), shape(1, HALF)),
        compiler_params=PARAMS,
        name="points",
    )(back, jp, pidx_here, place, pb, pd, pu, tb, td, ts)
    outputs = (shape(3, P_DEV), shape(9, CAM_DEV), shape(3, P_DEV), shape(9, CAM_DEV))

    def fits(*operands):
        errors = lax.all_to_all(operands[5], ("grp", "tile"), 0, 0, tiled=True)
        return pl.pallas_call(
            routed_final_kernel,
            out_shape=outputs,
            out_specs=[hbm] * 4,
            scratch_shapes=[pltpu.VMEM(v.shape, F32) for v in outputs]
            + [
                pltpu.VMEM((OWN_ROWS, 128), F32),
                pltpu.VMEM((3 * PH, LO), F32),
                pltpu.SemaphoreType.DMA((4,)),
            ],
            compiler_params=PARAMS,
            name="finish",
        )(errors, *operands[6:])

    def overflows(*operands):
        return tuple(replicated(*operands[:5]))

    over, *operands = lax.optimization_barrier(
        (
            over, jac_point, jac_cam, resid, point_index, cam_index,
            errors, routed, jp, pidx_here, pe, pb, pd, ps, tb, td, ts, sc, *kept,
        )
    )
    return lax.cond(over[0, 0] > 0, overflows, lambda *operands: tuple(fits(*operands)), *operands)


def solution(mesh):
    placed = (
        P(None, ("grp", "tile")),
        P(None, ("grp", "tile")),
        P(None, ("grp", "tile")),
        P(("grp", "tile")),
        P(("grp", "tile")),
    )
    return jax.shard_map(
        shards,
        mesh=mesh,
        in_specs=placed,
        out_specs=(P(None, ("grp", "tile")),) * 4,
        check_vma=False,
    )
```

```python
import functools

import jax
import jax.numpy as jnp
from jax import lax
from jax.experimental import pallas as pl
from jax.experimental.pallas import tpu as pltpu
from jax.sharding import PartitionSpec as P

P_DEV = 4096
CAM_DEV = 384
LO_BITS = 8
LO = 1 << LO_BITS
PH = P_DEV // LO
DAMPING = 1.0
F32 = jnp.float32
BF16 = jnp.bfloat16
SLOTS = 64
FULL = SLOTS - 1
HALF = 128
PARAMS = pltpu.CompilerParams(vmem_limit_bytes=48 * 1024 * 1024)


def halves(v):
    high = v.astype(BF16).astype(F32)
    return high, v - high


def rows16(width, step=1):
    numbers = lax.broadcasted_iota(jnp.int32, (16, width), 0)
    return (numbers // step if step > 1 else numbers).astype(F32).astype(BF16)


def sixteen(row):
    return jnp.broadcast_to(row.astype(F32), (16, row.shape[1])).astype(BF16)


def one_hot_rows(index, rows):
    numbers = rows16(index.shape[1])
    pieces = []
    for base in range(0, rows, 256):
        wide = sixteen(index - base)
        one, none = jnp.ones(wide.shape, BF16), jnp.zeros(wide.shape, BF16)
        pieces += [
            jnp.where(wide == numbers + BF16(16 * k), one, none)
            for k in range(min(256, rows - base) // 16)
        ]
    return jnp.concatenate(pieces, axis=0)


def dot_nt(a, b):
    return lax.dot_general(a, b, (((1,), (1,)), ((), ())), preferred_element_type=F32)


def dot_nn(a, b):
    return lax.dot_general(a, b, (((1,), (0,)), ((), ())), preferred_element_type=F32)


def is_row(hi, rows):
    return lax.broadcasted_iota(jnp.int32, (rows, hi.shape[1]), 0) == hi


def spread_row(mask, row):
    return jnp.where(mask, jnp.broadcast_to(row, mask.shape), 0.0)


def two_parts(v):
    high = v.astype(BF16)
    return high, (v - high.astype(F32)).astype(BF16)


def scatter_mixed(hi, hot, mains, tails, count, tail_rows):
    wide = sixteen(hi)
    none = jnp.zeros(wide.shape, BF16)
    single = len(mains) == 1
    numbers = rows16(hi.shape[1], 8) if single else none
    main_parts = two_parts(jnp.concatenate(mains * 2 if single else mains, axis=0))
    tail_parts = [two_parts(jnp.broadcast_to(v, wide.shape)) for v in tails]
    here = [wide == numbers + BF16(k) for k in range(0, count, 2 if single else 1)]
    tail_here = [wide == rows16(hi.shape[1]) + BF16(k) for k in range(0, tail_rows, 16)]
    pieces = []
    for part in range(2):
        pieces += [jnp.where(mask, main_parts[part], none) for mask in here]
        pieces += [jnp.where(mask, v[part], none) for v in tail_parts for mask in tail_here]
    return dot_nt(jnp.concatenate(pieces, axis=0), hot)


def both(v):
    half = v.shape[0] // 2
    return v[:half] + v[half:]


def gather_mixed(hi, hot, table, count, tail_rows):
    found = dot_nn(table, hot)
    hi8 = jnp.broadcast_to(hi, (8, hi.shape[1]))
    main = jnp.zeros(hi8.shape, F32)
    half = found.shape[0] // 2
    for k in range(count):
        rows = slice(k * 8, k * 8 + 8)
        low = slice(half + k * 8, half + k * 8 + 8)
        main = main + jnp.where(hi8 == k, found[rows] + found[low], 0.0)
    tail = found[count * 8 : half] + found[half + count * 8 :]
    tail = jnp.sum(jnp.where(is_row(hi, tail_rows), tail, 0.0), axis=0, keepdims=True)
    return main, tail


def stacked(table):
    high, low = halves(table)
    return jnp.concatenate([high, low], axis=0).astype(BF16)


def scatter_points(mask, hot, rows):
    pieces = [spread_row(mask, v[k : k + 1]) for v in halves(rows) for k in range(rows.shape[0])]
    return both(dot_nt(jnp.concatenate(pieces, axis=0).astype(BF16), hot))


def gather_points(mask, hot, table):
    found = both(dot_nn(stacked(table), hot))
    rows = mask.shape[0]
    return [
        jnp.sum(jnp.where(mask, found[i * rows : (i + 1) * rows], 0.0), axis=0, keepdims=True)
        for i in range(found.shape[0] // rows)
    ]


def total_of(v):
    return jnp.sum(jnp.sum(v, axis=0, keepdims=True), axis=1, keepdims=True)


def lanes(v, width):
    return jnp.broadcast_to(v, (v.shape[0], width))


def pack_kernel(
    n_grp, n_z, jp_hbm, jc_hbm, res_hbm, pidx_hbm, cidx_hbm,
    out_ref, pb_ref, pd_ref, pu_ref, jp_ref, pidx_ref,
    jc_ref, res_ref, cidx_ref, sems,
):
    copies = [
        pltpu.make_async_copy(source, target, sems.at[k])
        for k, (source, target) in enumerate(
            (
                (pidx_hbm, pidx_ref),
                (jp_hbm, jp_ref),
                (res_hbm, res_ref),
                (jc_hbm, jc_ref),
                (cidx_hbm, cidx_ref),
            )
        )
    ]
    for copy in copies:
        copy.start()
    for copy in copies:
        copy.wait()
    slot = out_ref.shape[2]
    index = pidx_ref[...]
    mask = is_row(index >> LO_BITS, PH)
    hot = one_hot_rows(index & (LO - 1), LO)
    jp = [jp_ref[k : k + 1, :] for k in range(6)]
    res = [res_ref[a : a + 1, :] for a in range(2)]
    grad = [-(jp[i] * res[0] + jp[3 + i] * res[1]) for i in range(3)]
    square = [jp[i] * jp[i] + jp[3 + i] * jp[3 + i] for i in range(3)]
    table = scatter_points(mask, hot, jnp.concatenate(grad + square, axis=0))
    rhs = table[: 3 * PH]
    diag = table[3 * PH :] + DAMPING
    pb_ref[...] = rhs
    pd_ref[...] = diag
    z = rhs / diag
    at = gather_points(mask, hot, z)
    u = [sum(jp[3 * a + i] * at[i] for i in range(3)) for a in range(2)]
    pu_ref[0:1, :] = u[0]
    pu_ref[1:2, :] = u[1]
    gamma = total_of(rhs * z)
    norm = total_of(z * z)
    scalars = jnp.concatenate([lanes(gamma, slot // 2), lanes(norm, slot // 2)], axis=1)
    cams = cidx_ref[...].astype(F32)
    for h in range(n_grp):
        cols = slice(h * slot, (h + 1) * slot)
        block = jnp.concatenate(
            [
                jc_ref[0:8, cols],
                jc_ref[9:17, cols],
                jc_ref[8:9, cols],
                jc_ref[17:18, cols],
                res[0][:, cols],
                res[1][:, cols],
                u[0][:, cols],
                u[1][:, cols],
                cams[:, cols],
                scalars,
            ],
            axis=0,
        )

        @pl.loop(0, n_z)
        def _(z_to, block=block, h=h):
            out_ref[h * n_z + z_to] = block


def read_blocks(ref, numbers):
    x = jnp.concatenate([ref[k] for k in numbers], axis=1)
    return x, x[22:23].astype(jnp.int32)


def chunk_of(chunk, per):
    return [chunk * per + k for k in range(per)]


def first_sums(ref, acc_ref, per, count, tail_rows):
    def body(chunk, carry):
        x, index = read_blocks(ref, chunk_of(chunk, per))
        hi, hot = index >> LO_BITS, one_hot_rows(index & (LO - 1), LO)
        j0, j1 = x[0:8], x[8:16]
        j08, j18, r0, r1 = x[16:17], x[17:18], x[18:19], x[19:20]
        acc_ref[...] += scatter_mixed(
            hi,
            hot,
            [-(j0 * r0 + j1 * r1), j0 * j0 + j1 * j1],
            [-(j08 * r0 + j18 * r1), j08 * j08 + j18 * j18],
            count,
            tail_rows,
        )
        return carry

    lax.fori_loop(0, ref.shape[0] // per, body, 0)


def own_sums_kernel(count, tail_rows, a_ref, acc_ref):
    acc_ref[...] = jnp.zeros(acc_ref.shape, F32)
    first_sums(a_ref, acc_ref, min(16, a_ref.shape[0]), count, tail_rows)


def camera_kernel(
    n_grp, n_z, count, tail_rows, a_ref, b_ref, start_ref,
    back_ref, tb_ref, td_ref, ts_ref,
    acc_ref, w_ref, zz_ref,
):
    blocks, _, slot = a_ref.shape
    per = min(8, blocks)
    chunks = blocks // per
    acc_ref[...] = start_ref[...]
    first_sums(b_ref, acc_ref, min(16, blocks), count, tail_rows)
    scalars = jnp.zeros((1, slot), F32)
    for ref in (a_ref, b_ref):
        scalars = scalars + jnp.sum(ref[:, 23, :], axis=0, keepdims=True)
    main = 8 * count
    half = acc_ref.shape[0] // 2
    for k in range(count):
        row = 16 * k
        tb_ref[8 * k : 8 * k + 8, :] = acc_ref[row : row + 8, :] + acc_ref[half + row : half + row + 8, :]
        row = 16 * k + 8
        td_ref[8 * k : 8 * k + 8, :] = (
            acc_ref[row : row + 8, :] + acc_ref[half + row : half + row + 8, :] + DAMPING
        )
    tb_ref[main:, :] = (
        acc_ref[2 * main : 2 * main + tail_rows, :]
        + acc_ref[half + 2 * main : half + 2 * main + tail_rows, :]
    )
    td_ref[main:, :] = (
        acc_ref[2 * main + tail_rows : half, :] + acc_ref[half + 2 * main + tail_rows :, :] + DAMPING
    )
    z = tb_ref[...] / td_ref[...]
    gamma = total_of(tb_ref[...] * z)
    norm = total_of(z * z)
    zz_ref[...] = stacked(z)
    ts_ref[...] = z
    acc_ref[0:half, :] = jnp.zeros((half, LO), F32)

    def second(ref, keep):
        def body(chunk, energy):
            numbers = chunk_of(chunk, per)
            x, index = read_blocks(ref, numbers)
            hi, hot = index >> LO_BITS, one_hot_rows(index & (LO - 1), LO)
            j0, j1 = x[0:8], x[8:16]
            j08, j18, u0, u1 = x[16:17], x[17:18], x[20:21], x[21:22]
            at, at8 = gather_mixed(hi, hot, zz_ref[...], count, tail_rows)
            w0 = jnp.sum(j0 * at, axis=0, keepdims=True) + j08 * at8
            w1 = jnp.sum(j1 * at, axis=0, keepdims=True) + j18 * at8
            if keep:
                for k, number in enumerate(numbers):
                    cols = slice(k * slot, (k + 1) * slot)
                    w_ref[number, 0:1, :] = w0[:, cols]
                    w_ref[number, 1:2, :] = w1[:, cols]
            e0, e1 = u0 + w0, u1 + w1
            acc_ref[0:half, :] += scatter_mixed(
                hi, hot, [j0 * e0 + j1 * e1], [j08 * e0 + j18 * e1], count, tail_rows
            )
            return energy + e0 * e0 + e1 * e1

        return body

    energy = jnp.zeros((1, per * slot), F32)
    energy = lax.fori_loop(0, chunks, second(a_ref, True), energy)
    energy = lax.fori_loop(0, chunks, second(b_ref, False), energy)
    ts_ref[...] += both(acc_ref[0:half, :])
    zz_ref[...] = stacked(ts_ref[...] / td_ref[...])
    share = 1.0 / n_grp
    gamma = gamma + share * scalars[:, 0:1]
    delta = norm + total_of(energy) + share * scalars[:, slot // 2 : slot // 2 + 1]
    mine = lax.axis_index("tile") // 2
    numbers = [g * n_z + mine for g in range(n_grp)]
    per = min(4, n_grp)
    for first in range(0, n_grp, per):
        some = numbers[first : first + per]
        x, index = read_blocks(a_ref, some)
        hi, hot = index >> LO_BITS, one_hot_rows(index & (LO - 1), LO)
        at, at8 = gather_mixed(hi, hot, zz_ref[...], count, tail_rows)
        v0 = jnp.sum(x[0:8] * at, axis=0, keepdims=True) + x[16:17] * at8
        v1 = jnp.sum(x[8:16] * at, axis=0, keepdims=True) + x[17:18] * at8
        for k in range(per):
            cols = slice(k * slot, (k + 1) * slot)
            g = first + k
            back_ref[g, 0:2, 0:slot] = w_ref[some[k], 0:2, :]
            back_ref[g, 2:3, 0:slot] = v0[:, cols]
            back_ref[g, 3:4, 0:slot] = v1[:, cols]
            back_ref[g, :, slot:] = lanes(jnp.concatenate([gamma, delta, gamma, delta], axis=0), 128)


def mine_kernel(main, tb_ref, td_ref, ts_ref, cb_ref, cd_ref, cs_ref):
    tile = lax.axis_index("tile")
    mine, core = tile // 2, tile % 2
    for source, target in ((tb_ref, cb_ref), (td_ref, cd_ref), (ts_ref, cs_ref)):
        own, own8 = [], []
        for k in range(3):
            rows = source[pl.ds(pl.multiple_of(8 * (3 * mine + k), 8), 8), :]
            tail = source[pl.ds(main + 3 * mine + k, 1), :]
            own += [rows[:, :128], rows[:, 128:]]
            own8 += [tail[:, :128], tail[:, 128:]]
        for m in range(3):
            cols = slice(m * 128, (m + 1) * 128)
            target[0:8, cols] = jnp.where(core == 0, own[m], own[m + 3])
            target[8:9, cols] = jnp.where(core == 0, own8[m], own8[m + 3])


def point_kernel(
    n_grp, back_ref, jp_ref, pidx_ref, pb_ref, pd_ref, pu_ref, cb_ref, cd_ref, cs_ref,
    out_ref, ps_ref, pe_ref, sc_ref,
):
    slot = back_ref.shape[2] - 128
    index = pidx_ref[...]
    mask = is_row(index >> LO_BITS, PH)
    hot = one_hot_rows(index & (LO - 1), LO)
    jp = [jp_ref[k : k + 1, :] for k in range(6)]
    scalars = back_ref[0, :, slot:]
    for h in range(1, n_grp):
        scalars = scalars + back_ref[h, :, slot:]
    gamma, delta = scalars[0:1, 0:1], scalars[1:2, 0:1]
    alpha = gamma / delta
    w = [
        jnp.concatenate([back_ref[h, r : r + 1, 0:slot] for h in range(n_grp)], axis=1) for r in range(4)
    ]
    rhs, diag = pb_ref[...], pd_ref[...]
    z = rhs / diag
    error = [pu_ref[a : a + 1, :] + w[a] for a in range(2)]
    s = z + scatter_points(mask, hot, jp_ref[0:3, :] * error[0] + jp_ref[3:6, :] * error[1])
    r1 = rhs - alpha * s
    z1 = r1 / diag
    at = gather_points(mask, hot, z1)
    error = [
        sum(jp[3 * a + i] * at[i] for i in range(3)) + (w[a] - alpha * w[2 + a]) for a in range(2)
    ]
    ps_ref[...] = s
    pe_ref[0:1, :] = error[0]
    pe_ref[1:2, :] = error[1]
    cr1 = cb_ref[...] - alpha * cs_ref[...]
    cz1 = cr1 / cd_ref[...]
    gamma1 = total_of(r1 * z1) + total_of(cr1 * cz1)
    delta1 = (
        total_of(error[0] * error[0] + error[1] * error[1]) + total_of(z1 * z1) + total_of(cz1 * cz1)
    )
    sc_ref[...] = lanes(jnp.concatenate([gamma, alpha], axis=0), 128)
    tail = lanes(jnp.concatenate([gamma1, delta1], axis=0), 128)
    per = out_ref.shape[0] // n_grp
    for h in range(n_grp):
        cols = slice(h * slot, (h + 1) * slot)
        block = jnp.concatenate([jnp.concatenate([e[:, cols] for e in error], axis=0), tail], axis=1)

        @pl.loop(0, per)
        def _(tile, block=block, h=h):
            out_ref[h * per + tile] = block


def last_point_sums_kernel(jp_ref, pidx_ref, pe_ref, pt_ref):
    index = pidx_ref[...]
    mask = is_row(index >> LO_BITS, PH)
    hot = one_hot_rows(index & (LO - 1), LO)
    terms = jp_ref[0:3, :] * pe_ref[0:1, :] + jp_ref[3:6, :] * pe_ref[1:2, :]
    pt_ref[...] = scatter_points(mask, hot, terms)


def final_kernel(
    err_ref, a_ref, b_ref, pb_ref, pd_ref, ps_ref, pt_ref, cb_ref, cd_ref, cs_ref, sc_ref,
    px_ref, cx_ref, pr_ref, cr_ref, acc_ref,
):
    blocks, _, slot = a_ref.shape
    per = min(8, blocks)
    chunks = blocks // per
    tile = lax.axis_index("tile")
    core = tile % 2
    acc_ref[...] = jnp.zeros(acc_ref.shape, F32)

    def body(ref, parity):
        def step(chunk, scalars):
            numbers = chunk_of(chunk, per)
            x, index = read_blocks(ref, numbers)
            errs = [err_ref[2 * k + parity] for k in numbers]
            e = jnp.concatenate([v[:, 0:slot] for v in errs], axis=1)
            for v in errs:
                scalars = scalars + v[:, slot:]
            index = index - tile * CAM_DEV
            hi = index >> 7
            hot = one_hot_rows(index & 127, 128)
            j0, j1 = x[0:8], x[8:16]
            e0, e1 = e[0:1], e[1:2]
            acc_ref[...] += scatter_mixed(
                hi, hot, [j0 * e0 + j1 * e1], [x[16:17] * e0 + x[17:18] * e1], 4, 16
            )
            return scalars

        return step

    scalars = lax.fori_loop(0, chunks, body(a_ref, core), jnp.zeros((2, 128), F32))
    scalars = lax.fori_loop(0, chunks, body(b_ref, 1 - core), scalars)
    gamma1, delta1 = scalars[0:1, 0:1], scalars[1:2, 0:1]
    gamma, alpha = sc_ref[0:1, 0:1], sc_ref[1:2, 0:1]
    ratio = gamma1 / gamma
    alpha1 = gamma1 / (delta1 - ratio * gamma1 / alpha)

    rhs, diag, s = pb_ref[...], pd_ref[...], ps_ref[...]
    z = rhs / diag
    r1 = rhs - alpha * s
    z1 = r1 / diag
    x = alpha * z + alpha1 * (z1 + ratio * z)
    r2 = r1 - alpha1 * (z1 + pt_ref[...] + ratio * s)
    for i in range(3):
        for hi in range(PH):
            row = i * PH + hi
            px_ref[i : i + 1, hi * LO : (hi + 1) * LO] = x[row : row + 1]
            pr_ref[i : i + 1, hi * LO : (hi + 1) * LO] = r2[row : row + 1]

    rhs, s = cb_ref[...], cs_ref[...]
    z = rhs / cd_ref[...]
    r1 = rhs - alpha * s
    z1 = r1 / cd_ref[...]
    cx_ref[...] = alpha * z + alpha1 * (z1 + ratio * z)
    sums = both(acc_ref[...])
    base = r1 - alpha1 * (z1 + ratio * s)
    for k in range(3):
        cols = slice(k * 128, (k + 1) * 128)
        cr_ref[0:8, cols] = base[0:8, cols] - alpha1 * sums[8 * k : 8 * k + 8, :]
        cr_ref[8:9, cols] = base[8:9, cols] - alpha1 * sums[32 + k : 33 + k, :]


def shape(*dims):
    return jax.ShapeDtypeStruct(dims, F32)


def replicated(jac_point, jac_cam, resid, point_index, cam_index):
    n_grp, n_tile = lax.axis_size("grp"), lax.axis_size("tile")
    n_z = n_tile // 2
    obs = jac_point.shape[1]
    slot = obs // n_grp
    blocks = n_grp * n_z
    count = CAM_DEV * n_tile // LO
    tail_rows = -(-count // 16) * 16
    rows = 8 * count + tail_rows
    groups = [[d * 2 + core for d in range(blocks)] for core in range(2)]
    swap = [(t, t ^ 1) for t in range(n_tile)]
    pidx, cidx = point_index.reshape(1, obs), cam_index.reshape(1, obs)

    hbm = pl.BlockSpec(memory_space=pltpu.HBM)
    packed, pb, pd, pu, jp, pidx = pl.pallas_call(
        functools.partial(pack_kernel, n_grp, n_z),
        in_specs=[hbm] * 5,
        out_shape=(
            shape(blocks, 24, slot),
            shape(3 * PH, LO),
            shape(3 * PH, LO),
            shape(2, obs),
            shape(6, obs),
            jax.ShapeDtypeStruct((1, obs), jnp.int32),
        ),
        scratch_shapes=[
            pltpu.VMEM((18, obs), F32),
            pltpu.VMEM((2, obs), F32),
            pltpu.VMEM((1, obs), jnp.int32),
            pltpu.SemaphoreType.DMA((5,)),
        ],
        compiler_params=PARAMS,
        name="pack",
    )(*(pltpu.with_memory_space_constraint(x, pltpu.HBM) for x in (jac_point, jac_cam, resid, pidx, cidx)))
    own = lax.all_to_all(packed, ("grp", "tile"), 0, 0, axis_index_groups=groups, tiled=True)
    other = lax.ppermute(own, "tile", swap)
    sums = pl.pallas_call(
        functools.partial(own_sums_kernel, count, tail_rows),
        out_shape=shape(4 * rows, LO),
        compiler_params=PARAMS,
        name="own_sums",
        cost_estimate=pl.CostEstimate(flops=2 * 10**9, bytes_accessed=10**6, transcendentals=0),
    )(own)
    table = shape(rows, LO)
    back, tb, td, ts = pl.pallas_call(
        functools.partial(camera_kernel, n_grp, n_z, count, tail_rows),
        out_shape=(shape(n_grp, 4, slot + 128), table, table, table),
        scratch_shapes=[
            pltpu.VMEM((4 * rows, LO), F32),
            pltpu.VMEM((blocks, 2, slot), F32),
            pltpu.VMEM((2 * rows, LO), BF16),
        ],
        compiler_params=PARAMS,
        name="cameras",
    )(own, other, sums)
    back = lax.all_to_all(back, "grp", 0, 0, tiled=True)
    cb, cd, cs = pl.pallas_call(
        functools.partial(mine_kernel, 8 * count),
        out_shape=(shape(9, CAM_DEV),) * 3,
        compiler_params=PARAMS,
        name="mine",
    )(tb, td, ts)
    errors, ps, pe, sc = pl.pallas_call(
        functools.partial(point_kernel, n_grp),
        out_shape=(
            shape(n_grp * n_tile, 2, slot + 128),
            shape(3 * PH, LO),
            shape(2, obs),
            shape(2, 128),
        ),
        compiler_params=PARAMS,
        name="points",
    )(back, jp, pidx, pb, pd, pu, cb, cd, cs)
    errors = lax.all_to_all(errors, ("grp", "tile"), 0, 0, tiled=True)
    pt = pl.pallas_call(
        last_point_sums_kernel,
        out_shape=shape(3 * PH, LO),
        compiler_params=PARAMS,
        name="last_point_sums",
    )(jp, pidx, pe)
    return pl.pallas_call(
        final_kernel,
        out_shape=(shape(3, P_DEV), shape(9, CAM_DEV), shape(3, P_DEV), shape(9, CAM_DEV)),
        scratch_shapes=[pltpu.VMEM((96, 128), F32)],
        compiler_params=PARAMS,
        name="finish",
    )(errors, own, other, pb, pd, ps, pt, cb, cd, cs, sc)


def eights(row):
    return jnp.broadcast_to(row, (8, row.shape[1]))


def row_numbers(width):
    return lax.broadcasted_iota(jnp.int32, (16, width), 0)


def as_16_bit(numbers):
    return numbers.astype(F32).astype(BF16)


def masked_rows(parts, masks):
    none = jnp.zeros(parts[0].shape, BF16)
    return jnp.concatenate([jnp.where(m, p, none) for p in parts for m in masks], axis=0)


def low_lanes(rows):
    return lax.broadcasted_iota(jnp.int32, (rows, HALF), 1) < SLOTS


def swap_lanes(v):
    return pltpu.roll(v, SLOTS, 1)


def point_sums(pidx_ref, jp_ref, res_ref):
    index = pidx_ref[...]
    mask = is_row(index >> LO_BITS, PH)
    hot = one_hot_rows(index & (LO - 1), LO)
    jp = jp_ref[0:3, :], jp_ref[3:6, :]
    grad = -(jp[0] * res_ref[0:1, :] + jp[1] * res_ref[1:2, :])
    square = jp[0] * jp[0] + jp[1] * jp[1]
    return scatter_points(mask, hot, jnp.concatenate([grad, square], axis=0)), mask, hot, jp


def start_copies(pairs, sems):
    copies = [pltpu.make_async_copy(a, b, sems.at[k]) for k, (a, b) in enumerate(pairs)]
    for copy in copies:
        copy.start()
    for copy in copies:
        copy.wait()


def route_kernel(
    n_grp, n_tile, jp_hbm, jc_hbm, res_hbm, pidx_hbm, cidx_hbm,
    out_ref, pb_ref, pd_ref, pu_ref, jp_ref, pidx_ref, place_ref, sc_ref,
    jc_ref, res_ref, cidx_ref, sems,
):
    width = cidx_ref.shape[1] // 4
    pairs = [(pidx_hbm, pidx_ref), (jp_hbm, jp_ref), (res_hbm, res_ref), (cidx_hbm, cidx_ref)]
    for k in range(4):
        part = pl.ds(k * width, width)
        pairs.append((jc_hbm.at[:, part], jc_ref.at[:, part]))
    start_copies(pairs, sems)
    slot = cidx_ref.shape[1] // n_grp
    cams = cidx_ref[...]
    owner = ((cams >> 7) * 171) >> 9
    local = (cams - owner * CAM_DEV).astype(F32)
    mine = is_row(owner, n_tile)
    ones = jnp.where(mine, 1.0, 0.0)
    stack = jnp.concatenate([ones[:, h * slot : (h + 1) * slot] for h in range(n_grp)], axis=0)
    before = lax.broadcasted_iota(jnp.int32, (slot, slot), 0)
    before = before < lax.broadcasted_iota(jnp.int32, (slot, slot), 1)
    counts = dot_nn(stack.astype(BF16), jnp.where(before, 1.0, 0.0).astype(BF16))
    counts = jnp.concatenate([counts[h * n_tile : (h + 1) * n_tile] for h in range(n_grp)], axis=1)
    rank = jnp.sum(jnp.where(mine, counts, 0.0), axis=0, keepdims=True)
    place_ref[0:1, :] = owner
    place_ref[1:2, :] = rank.astype(jnp.int32)
    over = jnp.max(jnp.where(rank >= FULL, 1.0, 0.0), axis=1, keepdims=True)
    rank = rank.astype(jnp.int32)
    hot_rank = one_hot_rows(rank, HALF)
    wide = sixteen(owner)
    numbers = row_numbers(owner.shape[1])
    core = lax.axis_index("tile") % 2
    upper, lower, others = core, 1 + core, 2 - 2 * core
    low = low_lanes(8)

    def route_main(h):
        cols = slice(h * slot, (h + 1) * slot)
        here = [wide[:, cols] == BF16(t) for t in range(n_tile)]
        parts = two_parts(jnp.concatenate([jc_ref[0:8, cols], jc_ref[9:17, cols]], axis=0))
        moved = both(dot_nt(masked_rows(parts, here), hot_rank[:, cols]))
        for t in range(n_tile):
            first, second = moved[16 * t : 16 * t + 8], moved[16 * t + 8 : 16 * t + 16]
            tile = jnp.where(low, first, swap_lanes(second))
            out_ref[3 * (h * n_tile + t) + upper] = tile[0:4]
            out_ref[3 * (h * n_tile + t) + lower] = tile[4:8]

    def route_rest(parts, here, h):
        cols = slice(h * slot, (h + 1) * slot)
        left = masked_rows([p[:, cols] for p in parts], [m[:, cols] for m in here])
        moved = both(dot_nt(left, hot_rank[:, cols]))
        for t in range(n_tile):
            rows = moved[8 * t : 8 * t + 8]
            tile = jnp.where(low[0:4], rows[0:4], swap_lanes(rows)[4:8])
            out_ref[3 * (h * n_tile + t) + others] = tile

    table, mask, hot, jp = point_sums(pidx_ref, jp_ref, res_ref)
    for h in range(n_grp):
        route_main(h)
    rhs, diag = table[: 3 * PH], table[3 * PH :] + DAMPING
    z = rhs / diag
    at = gather_points(mask, hot, z)
    pb_ref[...] = rhs
    pd_ref[...] = diag
    u = [sum(jp[a][i : i + 1] * at[i] for i in range(3)) for a in range(2)]
    pu_ref[0:1, :] = u[0]
    pu_ref[1:2, :] = u[1]
    sc_ref[...] = lanes(jnp.concatenate([total_of(rhs * z), total_of(z * z), over], axis=0), HALF)
    rows = [jc_ref[8:9, :], res_ref[0:1, :], local, u[0], jc_ref[17:18, :], res_ref[1:2, :], local, u[1]]
    parts = two_parts(jnp.concatenate(rows * 2, axis=0))
    here = [wide == as_16_bit((numbers >> 3) + t) for t in range(0, n_tile, 2)]
    for h in range(n_grp):
        route_rest(parts, here, h)


def unfold(even, odd):
    low = low_lanes(even.shape[0])
    return jnp.where(low, even, swap_lanes(odd)), jnp.where(low, swap_lanes(even), odd)


def unfold_rest(both_rows):
    low, swapped = low_lanes(4), swap_lanes(both_rows)
    return (
        jnp.where(low, both_rows[0:4], swapped[4:8]),
        jnp.where(low, swapped[0:4], both_rows[4:8]),
    )


def last_slot(v):
    return (lax.broadcasted_iota(jnp.int32, v.shape, 1) & (SLOTS - 1)) == FULL


def read_routed(ref, sources):
    main, rest = ([], []), ([], [])
    for s in sources[::2]:
        tile = 3 * (s // 2)
        pair = unfold(ref[tile], ref[tile + 2])
        pair_rest = unfold_rest(ref[tile + 1])
        for a in range(2):
            main[a].append(pair[a])
            rest[a].append(pair_rest[a])
    main = [jnp.concatenate(v, axis=1) for v in main]
    rest = [jnp.concatenate(v, axis=1) for v in rest]
    index = rest[0][2:3].astype(jnp.int32)
    return main, rest, (index >> 7).astype(F32), one_hot_rows(index & 127, 128)


OWN_ROWS = 32
STEP = 32


def scatter_two(hi, hot, first, second):
    wide, numbers = sixteen(hi), row_numbers(hi.shape[1])
    blocks = [wide == BF16(k) for k in range(3)]
    tail = wide == as_16_bit(numbers & 7)
    rows = two_parts(jnp.concatenate([first[0], second[0]], axis=0))
    tails = two_parts(jnp.concatenate([eights(first[1]), eights(second[1])], axis=0))
    none = jnp.zeros(wide.shape, BF16)
    pieces = []
    for part in range(2):
        pieces += [jnp.where(mask, rows[part], none) for mask in blocks]
        pieces.append(jnp.where(tail, tails[part], none))
    return both(dot_nt(jnp.concatenate(pieces, axis=0), hot))


def scatter_one(hi, hot, main, tail):
    wide, numbers = sixteen(hi), row_numbers(hi.shape[1])
    upper = wide == as_16_bit(numbers >> 3)
    lower = wide == as_16_bit(jnp.where(numbers < 8, 2, numbers - 8))
    rows = two_parts(jnp.concatenate([main, main], axis=0))
    tails = two_parts(jnp.concatenate([main, eights(tail)], axis=0))
    none = jnp.zeros(wide.shape, BF16)
    pieces = []
    for part in range(2):
        pieces += [jnp.where(upper, rows[part], none), jnp.where(lower, tails[part], none)]
    return both(dot_nt(jnp.concatenate(pieces, axis=0), hot))


def gather_own(hi, hot, table, main, rest):
    found = both(dot_nn(table, hot))
    block = eights(hi)
    at = jnp.where(block == 0, found[0:8], jnp.where(block == 1, found[8:16], found[16:24]))
    numbers = lax.broadcasted_iota(jnp.int32, block.shape, 0).astype(F32)
    tail = jnp.where(block == numbers, found[24:32], 0.0)
    return [
        jnp.sum(main[a] * at + eights(rest[a][0:1]) * tail, axis=0, keepdims=True) for a in range(2)
    ]


def scatter_j(hi, hot, main, rest, e):
    return scatter_one(
        hi, hot, main[0] * e[0] + main[1] * e[1], rest[0][0:1] * e[0] + rest[1][0:1] * e[1]
    )


def owner_kernel(in_ref, sc_ref, back_ref, tb_ref, td_ref, ts_ref, acc_ref, zz_ref, w_ref, *kept):
    devices = back_ref.shape[0]
    per = min(STEP, devices)
    steps = devices // per

    if steps == 1:
        main, rest, hi, hot = read_routed(in_ref, range(devices))
        kept[0][...] = hot
        for a in range(2):
            kept[1][8 * a : 8 * a + 8, :] = main[a]
            kept[1][16 + a : 17 + a, :] = rest[a][0:1]
        kept[1][18:19, :] = hi

        def loop(body, start):
            return body((main, rest, hi, hot), 0, start)
    else:

        def loop(body, start):
            def step(number, carry):
                return body(read_routed(in_ref, chunk_of(number, per)), number, carry)

            return lax.fori_loop(0, steps, step, start)

    def rhs_and_diag(slots, number, carry):
        main, rest, hi, hot = slots
        r = [rest[a][1:2] for a in range(2)]
        rhs = (-(main[0] * r[0] + main[1] * r[1]), -(rest[0][0:1] * r[0] + rest[1][0:1] * r[1]))
        square = (
            main[0] * main[0] + main[1] * main[1],
            rest[0][0:1] * rest[0][0:1] + rest[1][0:1] * rest[1][0:1],
        )
        acc_ref[...] += scatter_two(hi, hot, rhs, square)
        return carry

    acc_ref[...] = jnp.zeros(acc_ref.shape, F32)
    loop(rhs_and_diag, 0)
    rhs = jnp.concatenate([acc_ref[16 * k : 16 * k + 8, :] for k in range(4)], axis=0)
    diag = jnp.concatenate([acc_ref[16 * k + 8 : 16 * k + 16, :] for k in range(4)], axis=0) + DAMPING
    tb_ref[...] = rhs
    td_ref[...] = diag
    z = rhs / diag
    zz_ref[...] = stacked(z)
    acc_ref[0:OWN_ROWS, :] = z

    def apply(slots, number, energy):
        main, rest, hi, hot = slots
        w = gather_own(hi, hot, zz_ref[...], main, rest)
        e = [rest[a][3:4] + w[a] for a in range(2)]
        for a in range(2):
            w_ref[number, 2 * a : 2 * a + 1, :] = w[a]
        acc_ref[0:OWN_ROWS, :] += scatter_j(hi, hot, main, rest, e)
        return energy + e[0] * e[0] + e[1] * e[1]

    energy = loop(apply, jnp.zeros((1, per * SLOTS), F32))
    s = acc_ref[0:OWN_ROWS, :]
    ts_ref[...] = s
    zz_ref[...] = stacked(s / diag)
    gamma = sc_ref[0:1, :] + total_of(rhs * z)
    delta = sc_ref[1:2, :] + total_of(z * z) + total_of(energy)
    over = sc_ref[2:3, :]
    low = low_lanes(2)
    tail = jnp.where(
        low, jnp.concatenate([gamma, over], axis=0), jnp.concatenate([delta, over], axis=0)
    )

    def send(slots, number, carry):
        main, rest, hi, hot = slots
        v = gather_own(hi, hot, zz_ref[...], main, rest)
        for a in range(2):
            w_ref[number, 2 * a + 1 : 2 * a + 2, :] = v[a]
        w = w_ref[number]
        for k in range(per // 2):
            cols = slice(k * HALF, (k + 1) * HALF)
            first, second = w[0:2, cols], w[2:4, cols]
            even = jnp.where(low, first, swap_lanes(second))
            odd = jnp.where(low, swap_lanes(first), second)
            for t, tile in ((2 * k, even), (2 * k + 1, odd)):
                back_ref[number * per + t] = jnp.where(last_slot(tile), tail, tile)
        return carry

    loop(send, 0)


def halved(ref):
    return jnp.concatenate(
        [
            ref[i * PH : (i + 1) * PH, half * HALF : (half + 1) * HALF]
            for i in range(3)
            for half in range(2)
        ],
        axis=0,
    )


def routed_point_kernel(
    n_grp, n_tile, back_ref, jp_ref, pidx_ref, place_ref, pb_ref, pd_ref, pu_ref, cb_ref, cd_ref, cs_ref,
    out_ref, ps_ref, pe_ref, sc_ref, over_ref,
):
    slot = place_ref.shape[1] // n_grp
    index = pidx_ref[...]
    mask = is_row(((index >> 7) & 1) * PH + (index >> LO_BITS), 2 * PH)
    hot = one_hot_rows(index & (HALF - 1), HALF)
    jp = [jp_ref[k : k + 1, :] for k in range(6)]
    scalars = jnp.sum(back_ref[...], axis=0)
    scalars = scalars[0:4] + scalars[4:8]
    scalars = scalars[0:2] + scalars[2:4]
    gamma, delta = scalars[0:1, FULL : FULL + 1], scalars[0:1, HALF - 1 : HALF]
    over_ref[...] = lanes(scalars[1:2, FULL : FULL + 1], HALF)
    alpha = gamma / delta
    owner = place_ref[0:1, :]
    hot_rank = one_hot_rows(place_ref[1:2, :], HALF)
    numbers = lax.broadcasted_iota(jnp.int32, (2 * n_tile, slot), 0) >> 1
    terms = []
    for h in range(n_grp):
        cols = slice(h * slot, (h + 1) * slot)
        rows = jnp.concatenate([back_ref[h * n_tile // 4 + k] for k in range(n_tile // 4)], axis=0)
        rows = jnp.concatenate([rows, swap_lanes(rows)], axis=0)
        found = both(dot_nn(stacked(rows), hot_rank[:, cols]))
        here = numbers == owner[:, cols]
        of_a = []
        for a in range(2):
            mine = jnp.where(here, found[2 * n_tile * a : 2 * n_tile * (a + 1)], 0.0)
            mine = sum(mine[8 * k : 8 * k + 8] for k in range(n_tile // 4))
            mine = mine[0:4] + mine[4:8]
            of_a.append(mine[0:2] + mine[2:4])
        terms.append(jnp.concatenate(of_a, axis=0))
    terms = jnp.concatenate(terms, axis=1)
    w0 = [terms[2 * a : 2 * a + 1] for a in range(2)]
    w1 = [terms[2 * a + 1 : 2 * a + 2] for a in range(2)]
    rhs, diag = halved(pb_ref), halved(pd_ref)
    z = rhs / diag
    error = [pu_ref[a : a + 1, :] + w0[a] for a in range(2)]
    s = z + scatter_points(mask, hot, jp_ref[0:3, :] * error[0] + jp_ref[3:6, :] * error[1])
    r1 = rhs - alpha * s
    z1 = r1 / diag
    at = gather_points(mask, hot, z1)
    error = [sum(jp[3 * a + i] * at[i] for i in range(3)) + (w0[a] - alpha * w1[a]) for a in range(2)]
    for i in range(3):
        for half in range(2):
            row = (2 * i + half) * PH
            ps_ref[i * PH : (i + 1) * PH, half * HALF : (half + 1) * HALF] = s[row : row + PH]
    pe_ref[0:1, :] = error[0]
    pe_ref[1:2, :] = error[1]
    cr1 = cb_ref[...] - alpha * cs_ref[...]
    cz1 = cr1 / cd_ref[...]
    gamma1 = total_of(r1 * z1) + total_of(cr1 * cz1)
    delta1 = (
        total_of(error[0] * error[0] + error[1] * error[1]) + total_of(z1 * z1) + total_of(cz1 * cz1)
    )
    sc_ref[...] = lanes(jnp.concatenate([gamma, alpha], axis=0), HALF)
    tail = jnp.where(low_lanes(1), gamma1, delta1)
    wide, numbers = sixteen(owner), row_numbers(owner.shape[1])
    parts = two_parts(jnp.concatenate([eights(e) for e in error], axis=0))
    here = [wide == as_16_bit((numbers & 7) + t) for t in range(0, n_tile, 8)]
    left = masked_rows(parts, here)
    low = low_lanes(8)
    for h in range(n_grp):
        moved = both(dot_nt(left[:, h * slot : (h + 1) * slot], hot_rank[:, h * slot : (h + 1) * slot]))
        for t in range(0, n_tile, 8):
            tile = jnp.where(low, moved[2 * t : 2 * t + 8], swap_lanes(moved[2 * t + 8 : 2 * t + 16]))
            tile = jnp.where(last_slot(tile), tail, tile)
            for k in range(8):
                out_ref[h * n_tile + t + k] = tile[k : k + 1]


def point_results(alpha, alpha1, ratio, pb_ref, pd_ref, ps_ref, pt_ref, px_ref, pr_ref, copies):
    rhs, diag, s = pb_ref[...], pd_ref[...], ps_ref[...]
    z = rhs / diag
    r1 = rhs - alpha * s
    z1 = r1 / diag
    x = alpha * z + alpha1 * (z1 + ratio * z)
    r2 = r1 - alpha1 * (z1 + pt_ref[...] + ratio * s)
    for table, target, copy in ((x, px_ref, copies[0]), (r2, pr_ref, copies[1])):
        for i in range(3):
            for hi in range(PH):
                row = i * PH + hi
                target[i : i + 1, hi * LO : (hi + 1) * LO] = table[row : row + 1]
        copy.start()


def routed_final_kernel(
    err_ref, in_ref, jp_ref, pidx_ref, pe_ref, pb_ref, pd_ref, ps_ref, cb_ref, cd_ref, cs_ref, sc_ref, *rest_refs
):
    kept, outs, (px_ref, cx_ref, pr_ref, cr_ref, acc_ref, pt_ref, sems) = (
        rest_refs[:-11],
        rest_refs[-11:-7],
        rest_refs[-7:],
    )
    devices = err_ref.shape[0]
    per = min(STEP, devices)
    steps = devices // per

    def body(step, carry):
        sources = chunk_of(step, per)
        if kept:
            hot, rows = kept[0][...], kept[1]
            main = [rows[8 * a : 8 * a + 8, :] for a in range(2)]
            rest = [rows[16 + a : 17 + a, :] for a in range(2)]
            hi = rows[18:19, :]
        else:
            main, rest, hi, hot = read_routed(in_ref, sources)
        pairs = [unfold(err_ref[s], err_ref[t]) for s, t in zip(sources[::2], sources[1::2])]
        e = [jnp.concatenate([pair[a] for pair in pairs], axis=1) for a in range(2)]
        acc_ref[...] += scatter_j(hi, hot, main, rest, e)
        return carry

    acc_ref[...] = jnp.zeros(acc_ref.shape, F32)
    if steps == 1:
        body(0, 0)
    else:
        lax.fori_loop(0, steps, body, 0)
    index = pidx_ref[...]
    mask = is_row(((index >> 7) & 1) * PH + (index >> LO_BITS), 2 * PH)
    terms = jp_ref[0:3, :] * pe_ref[0:1, :] + jp_ref[3:6, :] * pe_ref[1:2, :]
    sums = scatter_points(mask, one_hot_rows(index & (HALF - 1), HALF), terms)
    for i in range(3):
        for half in range(2):
            row = (2 * i + half) * PH
            pt_ref[i * PH : (i + 1) * PH, half * HALF : (half + 1) * HALF] = sums[row : row + PH]
    scalars = jnp.sum(err_ref[...], axis=0)
    gamma1, delta1 = scalars[:, FULL : FULL + 1], scalars[:, HALF - 1 : HALF]
    gamma, alpha = sc_ref[0:1, 0:1], sc_ref[1:2, 0:1]
    ratio = gamma1 / gamma
    alpha1 = gamma1 / (delta1 - ratio * gamma1 / alpha)
    copies = [
        pltpu.make_async_copy(here, there, sems.at[k])
        for k, (here, there) in enumerate(zip((px_ref, cx_ref, pr_ref, cr_ref), outs))
    ]
    point_results(
        alpha, alpha1, ratio, pb_ref, pd_ref, ps_ref, pt_ref, px_ref, pr_ref, (copies[0], copies[2])
    )
    rhs, s = cb_ref[...], cs_ref[...]
    z = rhs / cd_ref[...]
    r1 = rhs - alpha * s
    z1 = r1 / cd_ref[...]
    x = alpha * z + alpha1 * (z1 + ratio * z)
    r2 = r1 - alpha1 * (z1 + acc_ref[...] + ratio * s)
    for table, target in ((x, cx_ref), (r2, cr_ref)):
        for k in range(3):
            cols = slice(k * 128, (k + 1) * 128)
            target[0:8, cols] = table[8 * k : 8 * k + 8]
            target[8:9, cols] = table[24 + k : 25 + k]
    copies[1].start()
    copies[3].start()
    for copy in copies:
        copy.wait()


def shards(jac_point, jac_cam, resid, point_index, cam_index):
    n_grp, n_tile = lax.axis_size("grp"), lax.axis_size("tile")
    devices = n_grp * n_tile
    obs = jac_point.shape[1]
    pidx, cidx = point_index.reshape(1, obs), cam_index.reshape(1, obs)
    hbm = pl.BlockSpec(memory_space=pltpu.HBM)
    ints = jax.ShapeDtypeStruct((1, obs), jnp.int32)
    places = jax.ShapeDtypeStruct((2, obs), jnp.int32)
    points = shape(3 * PH, LO)
    cameras = shape(OWN_ROWS, 128)
    routed, pb, pd, pu, jp, pidx_here, place, sc = pl.pallas_call(
        functools.partial(route_kernel, n_grp, n_tile),
        in_specs=[hbm] * 5,
        out_shape=(shape(3 * devices, 4, HALF), points, points, shape(2, obs), shape(6, obs), ints, places, shape(3, HALF)),
        scratch_shapes=[
            pltpu.VMEM((18, obs), F32),
            pltpu.VMEM((2, obs), F32),
            pltpu.VMEM((1, obs), jnp.int32),
            pltpu.SemaphoreType.DMA((8,)),
        ],
        compiler_params=PARAMS,
        name="route",
    )(*(pltpu.with_memory_space_constraint(x, pltpu.HBM) for x in (jac_point, jac_cam, resid, pidx, cidx)))
    routed = lax.all_to_all(routed, ("grp", "tile"), 0, 0, tiled=True).reshape(3 * devices // 2, 8, HALF)
    slots = devices * SLOTS
    per = min(STEP, devices)
    scratch = [
        pltpu.VMEM((2 * OWN_ROWS, 128), F32),
        pltpu.VMEM((2 * OWN_ROWS, 128), BF16),
        pltpu.VMEM((devices // per, 4, per * SLOTS), F32),
    ]
    kept_shapes = ()
    if devices == per:
        kept_shapes = (jax.ShapeDtypeStruct((128, slots), BF16), shape(24, slots))

    def owner(in_ref, sc_ref, back_ref, tb_ref, td_ref, ts_ref, *others):
        kept, work = others[: len(kept_shapes)], others[len(kept_shapes) :]
        owner_kernel(in_ref, sc_ref, back_ref, tb_ref, td_ref, ts_ref, *work, *kept)

    back, tb, td, ts, *kept = pl.pallas_call(
        owner,
        out_shape=(shape(devices, 2, HALF), cameras, cameras, cameras) + kept_shapes,
        scratch_shapes=scratch,
        compiler_params=PARAMS,
        name="owner",
    )(routed, sc)
    back = lax.all_to_all(back, ("grp", "tile"), 0, 0, tiled=True).reshape(devices // 4, 8, HALF)
    errors, ps, pe, sc, over = pl.pallas_call(
        functools.partial(routed_point_kernel, n_grp, n_tile),
        out_shape=(shape(devices, 1, HALF), points, shape(2, obs), shape(2, HALF), shape(1, HALF)),
        compiler_params=PARAMS,
        name="points",
    )(back, jp, pidx_here, place, pb, pd, pu, tb, td, ts)
    outputs = (shape(3, P_DEV), shape(9, CAM_DEV), shape(3, P_DEV), shape(9, CAM_DEV))

    def fits(*operands):
        errors = lax.all_to_all(operands[5], ("grp", "tile"), 0, 0, tiled=True)
        return pl.pallas_call(
            routed_final_kernel,
            out_shape=outputs,
            out_specs=[hbm] * 4,
            scratch_shapes=[pltpu.VMEM(v.shape, F32) for v in outputs]
            + [
                pltpu.VMEM((OWN_ROWS, 128), F32),
                pltpu.VMEM((3 * PH, LO), F32),
                pltpu.SemaphoreType.DMA((4,)),
            ],
            compiler_params=PARAMS,
            name="finish",
        )(errors, *operands[6:])

    def overflows(*operands):
        return tuple(replicated(*operands[:5]))

    over, *operands = lax.optimization_barrier(
        (
            over, jac_point, jac_cam, resid, point_index, cam_index,
            errors, routed, jp, pidx_here, pe, pb, pd, ps, tb, td, ts, sc, *kept,
        )
    )
    return lax.cond(over[0, 0] > 0, overflows, lambda *operands: tuple(fits(*operands)), *operands)


def solution(mesh):
    placed = (
        P(None, ("grp", "tile")),
        P(None, ("grp", "tile")),
        P(None, ("grp", "tile")),
        P(("grp", "tile")),
        P(("grp", "tile")),
    )
    return jax.shard_map(
        shards,
        mesh=mesh,
        in_specs=placed,
        out_specs=(P(None, ("grp", "tile")),) * 4,
        check_vma=False,
    )
```
